32 devices in a mesh: row: 4 (over y, x), col: 8 (over z, core).
Axes of the slice: x: 2, y: 2, z: 4, core: 2. Of those that a mesh axis runs over, the one named last changes fastest.
Arguments:
- state: float32 [3, 10, 131072], P(None, None, ('row', 'col')), may hold values from -6 to 6
- depth: float32 [131072], P(('row', 'col')), may hold values from 1 to 18
- metric: float32 [4, 131072], P(None, ('row', 'col')), may hold values from -4 to 4, as said below
- partner: int32 [131072], P(('row', 'col')), may hold values from -63 to 63, as said below
- refine: int32 [131072], P(('row', 'col')), may hold values from 0 to 1, as said below
- diff_ops: float32 [2, 10, 10], replicated, may hold values from -2 to 2
- lift: float32 [10, 12], replicated, may hold values from -1.75 to 1.75
- prolong: float32 [2, 10, 10], replicated, may hold values from -2 to 2
Outputs:
- refined: float32 [3, 10, 196608], P(None, None, ('row', 'col'))
The draws below stay inside these ranges and needn't reach their ends.
Inputs may be any that keep to these rules, and one draw needn't show every extreme that they name: `metric`: (r_x, r_y) and (s_x, s_y) are orthogonal and of equal length, between 1 and 4. Where partner[i] is not 0, j = i + partner[i] is a triangle with partner[j] = -partner[i]; an offset of size 63 occurs in every draw. `refine`: split the curve into sections of 4096 consecutive triangles. The refinements before section k number k * 2048 plus an offset between -1024 and 1024, and both ends of that range occur in every draw; all refinements together number 131072 / 2.
All inputs are finite; a program needn't handle non-finite values.
Results may differ from the reference program's by a relative error of at most 0.000076.
Values sent between devices are 32-bit elements; how exact they have to be, the bound alone decides.
No kernel may reach another device: no remote copies, remote signals or barrier semaphores. Data moves between devices by JAX's collectives and lax.ppermute only.
A program may use at most 64 MiB of HBM per device.

```python
import jax
import jax.numpy as jnp
import numpy as np
from jax import lax

E_DEV = 4096
RIM = 64
NE = 131072
NEW = 196608


def draw_depth(key, part):
    total = NE
    keys = jax.random.split(key, 3)
    position = jnp.arange(total, dtype=jnp.float32) / total
    center = jax.random.uniform(keys[1], (), jnp.float32, 0.0, 1.0)
    height = jax.random.uniform(keys[2], (), jnp.float32, 4.0, 8.0)
    bump = jnp.maximum(0.0, 1.0 - 8.0 * jnp.abs(position - center))
    trend = 1.0 + height * bump
    rough = jnp.exp(jax.random.uniform(keys[0], (total,), jnp.float32, 0.0, jnp.log(2.0)))
    return (trend * rough).astype(jnp.float32)


def draw_metric(key, part):
    total = NE
    keys = jax.random.split(key, 3)
    size = jnp.exp(jax.random.uniform(keys[0], (total,), jnp.float32, 0.0, jnp.log(4.0)))
    turn = jax.random.randint(keys[1], (total,), 0, 8).astype(jnp.float32) * (jnp.pi / 4.0)
    mirror = 1.0 - 2.0 * jax.random.randint(keys[2], (total,), 0, 2).astype(jnp.float32)
    cosine = size * jnp.cos(turn)
    sine = size * jnp.sin(turn)
    return jnp.stack([cosine, sine, -sine * mirror, cosine * mirror]).astype(jnp.float32)


def draw_partner(key, part):
    total = NE
    sections = NE // E_DEV
    keys = jax.random.split(key, 6)
    index = jnp.arange(total, dtype=jnp.int32)
    back_all = jax.random.randint(keys[0], (sections + 1,), 1, RIM)
    high = jax.random.randint(keys[1], (), 1, sections)
    low = 1 + (high - 1 + jax.random.randint(keys[2], (), 1, sections - 1)) % (sections - 1)
    back_all = back_all.at[high].set(1).at[low].set(RIM - 1)
    nearest = ((index + E_DEV // 2) // E_DEV).astype(jnp.int32)
    real_end = (nearest >= 1) & (nearest <= sections - 1)
    back = jnp.take(back_all, nearest)
    cross_start = nearest * E_DEV - back
    in_cross = real_end & (index >= cross_start) & (index < cross_start + RIM)
    after_cross = real_end & (index == cross_start + RIM)
    grid = (index % RIM == 0) & ~in_cross
    windows = total // RIM + 1
    quiet = jax.random.randint(keys[4], (windows,), 0, 8) == 0
    loose = (jax.random.randint(keys[3], (total,), 0, 3) == 0) & (index % 2 == 0) & (index % RIM != 0) & ~in_cross & ~quiet[index // RIM]
    mark = grid | in_cross & (index == cross_start) | after_cross | loose | (index == 0)
    start = lax.cummax(jnp.where(mark, index, 0))
    marked = jnp.where(mark, index, total)
    after = jnp.concatenate([marked[1:], jnp.full((1,), total, jnp.int32)])
    finish = lax.cummin(after, reverse=True)
    paired = start + finish - 1 - index
    coast_bits = jax.random.randint(keys[5], (total,), 0, 4) == 0
    coast = jnp.take(coast_bits, start) & ~in_cross
    return jnp.where(coast, 0, paired - index).astype(jnp.int32)


def shuffled(subkey):
    return jax.random.permutation(subkey, E_DEV)


def draw_refine(key, part):
    sections = NE // E_DEV
    keys = jax.random.split(key, 4)
    quarter = E_DEV // 4
    drift = jax.random.randint(keys[0], (sections + 1,), -quarter, quarter + 1)
    high = jax.random.randint(keys[1], (), 1, sections)
    low = 1 + (high - 1 + jax.random.randint(keys[2], (), 1, sections - 1)) % (sections - 1)
    drift = drift.at[high].set(quarter).at[low].set(-quarter)
    drift = drift.at[0].set(0).at[sections].set(0)
    amount = E_DEV // 2 + drift[1:] - drift[:-1]
    order = jax.vmap(shuffled)(jax.random.split(keys[3], sections))
    return (order < amount[:, None]).astype(jnp.int32).reshape(-1)


def block_levels(stream_key, shape, cuts, smallest, largest):
    loudness = 1.0
    for dim, blocks in cuts:
        draws = jax.random.uniform(jax.random.fold_in(jax.random.fold_in(stream_key, 6), dim), (blocks,), jnp.float32, smallest / len(cuts), largest / len(cuts))
        loudness = loudness * jnp.repeat(jnp.exp(draws), shape[dim] // blocks).reshape((-1,) + (1,) * (len(shape) - 1 - dim))
    return loudness


def scatter_about(stream_key, dims, spread, bound, pieces=(), kind=jnp.bfloat16):
    loudness = block_levels(stream_key, dims, pieces, -0.22, 0.18) if pieces else 1.0
    entries = jax.random.normal(stream_key, dims, jnp.float32) * spread * loudness
    return jnp.minimum(jnp.maximum(entries, -bound), bound).astype(kind)


def setup_inputs(seed: int = 0) -> dict:
    arg_keys = jax.random.split(jax.random.key(seed), 9)
    return {
        "state": scatter_about(arg_keys[0], (3, 10, NE), 1.0, 6.0, ((2, 32),), jnp.float32),
        "depth": draw_depth(jax.random.fold_in(arg_keys[8], 71), 0),
        "metric": draw_metric(jax.random.fold_in(arg_keys[8], 71), 0),
        "partner": draw_partner(jax.random.fold_in(arg_keys[8], 71), 0),
        "refine": draw_refine(jax.random.fold_in(arg_keys[8], 71), 0),
        "diff_ops": scatter_about(arg_keys[5], (2, 10, 10), 10 ** -0.5, 2.0, (), jnp.float32),
        "lift": scatter_about(arg_keys[6], (10, 12), 12 ** -0.5, 1.75, (), jnp.float32),
        "prolong": scatter_about(arg_keys[7], (2, 10, 10), 10 ** -0.5, 2.0, (), jnp.float32),
    }


GRAVITY = 9.81
COURANT = 0.5
FACE_NODES = (0, 1, 2, 3, 3, 6, 8, 9, 9, 7, 4, 0)
HIGH = lax.Precision.HIGHEST

def apply_ops(matrix, field):
    return jnp.einsum('ab,fbx->fax', matrix, field, precision=HIGH)

def normal_flux(values, speed_sq, normal_x, normal_y):
    return jnp.stack([values[1] * normal_x + values[2] * normal_y, speed_sq * values[0] * normal_x, speed_sq * values[0] * normal_y])

def face_vectors(metric):
    grad_rx, grad_ry, grad_sx, grad_sy = (metric[0], metric[1], metric[2], metric[3])
    return ((-grad_sx, -grad_sy), (grad_rx + grad_sx, grad_ry + grad_sy), (-grad_rx, -grad_ry))

def wave_rate(depth, metric):
    lengths = [jnp.sqrt(vx * vx + vy * vy) for vx, vy in face_vectors(metric)]
    return jnp.sqrt(GRAVITY * depth) * jnp.maximum(jnp.maximum(lengths[0], lengths[1]), lengths[2])

def tendency(state, depth, metric, outer, outer_depth, walls, diff_ops, lift):
    speed_sq = GRAVITY * depth
    grad_rx, grad_ry, grad_sx, grad_sy = (metric[0], metric[1], metric[2], metric[3])
    moved = jnp.stack([state[1], state[2], state[0]])
    along_r = apply_ops(diff_ops[0], moved)
    along_s = apply_ops(diff_ops[1], moved)
    vol_eta = -(grad_rx * along_r[0] + grad_sx * along_s[0] + grad_ry * along_r[1] + grad_sy * along_s[1])
    vol_mx = -speed_sq * (grad_rx * along_r[2] + grad_sx * along_s[2])
    vol_my = -speed_sq * (grad_ry * along_r[2] + grad_sy * along_s[2])
    inner = jnp.take(state, np.array(FACE_NODES), axis=1)
    jumps = []
    for edge_num, (vec_x, vec_y) in enumerate(face_vectors(metric)):
        length = jnp.sqrt(vec_x * vec_x + vec_y * vec_y)
        normal_x = vec_x / length
        normal_y = vec_y / length
        inside = inner[:, 4 * edge_num:4 * edge_num + 4, :]
        normal_m = inside[1] * normal_x + inside[2] * normal_y
        ghost = jnp.stack([inside[0], inside[1] - 2.0 * normal_m * normal_x, inside[2] - 2.0 * normal_m * normal_y])
        closed = walls[edge_num]
        outside = jnp.where(closed, ghost, outer[edge_num])
        outside_sq = jnp.where(closed, speed_sq, GRAVITY * outer_depth[edge_num])
        flux_in = normal_flux(inside, speed_sq, normal_x, normal_y)
        flux_out = normal_flux(outside, outside_sq, normal_x, normal_y)
        wave_top = jnp.sqrt(jnp.maximum(speed_sq, outside_sq))
        common = 0.5 * (flux_in + flux_out) - 0.5 * wave_top * (outside - inside)
        jumps.append(length * (flux_in - common))
    surface = apply_ops(lift, jnp.concatenate(jumps, axis=1))
    return jnp.stack([vol_eta, vol_mx, vol_my]) + surface

def neighbour_values(current, depth, partner):
    total = current.shape[2]
    index = jnp.arange(total, dtype=jnp.int32)
    traces = jnp.take(current, np.array(FACE_NODES), axis=1)
    zero_col = jnp.zeros((3, 4, 1), current.dtype)
    from_prev = jnp.concatenate([zero_col, traces[:, 7:3:-1, :-1]], axis=2)
    from_next = jnp.concatenate([traces[:, 3::-1, 1:], zero_col], axis=2)
    safe = jnp.clip(index + partner.astype(jnp.int32), 0, total - 1).astype(jnp.int32)
    from_pair = jnp.take(traces[:, 11:7:-1, :], safe, axis=2)
    depth_prev = jnp.concatenate([depth[:1], depth[:-1]])
    depth_next = jnp.concatenate([depth[1:], depth[-1:]])
    depth_pair = jnp.take(depth, safe)
    walls = (index == 0, index == total - 1, partner == 0)
    return ((from_prev, from_next, from_pair), (depth_prev, depth_next, depth_pair), walls)

def reference(state, depth, metric, partner, refine, diff_ops, lift, prolong):
    step = COURANT / jnp.max(wave_rate(depth, metric))

    def rhs(current):
        outer, outer_depth, walls = neighbour_values(current, depth, partner)
        return tendency(current, depth, metric, outer, outer_depth, walls, diff_ops, lift)
    first = state + step * rhs(state)
    second = 0.5 * state + 0.5 * (first + step * rhs(first))
    counts = (1 + refine).astype(jnp.int32)
    ends = jnp.cumsum(counts).astype(jnp.int32)
    starts = ends - counts
    slots = jnp.arange(NEW, dtype=jnp.int32)
    parent = jnp.searchsorted(ends, slots, side='right').astype(jnp.int32)
    which = slots - jnp.take(starts, parent)
    child_one = jnp.where(refine == 1, apply_ops(prolong[0], second), second)
    child_two = apply_ops(prolong[1], second)
    return jnp.where(which == 0, jnp.take(child_one, parent, axis=2), jnp.take(child_two, parent, axis=2))
```

```python
import functools

import jax
import jax.numpy as jnp
from jax import lax
from jax.experimental import pallas as pl
from jax.experimental.pallas import tpu as pltpu
from jax.sharding import PartitionSpec as P

GRAVITY = 9.81
COURANT = 0.5
HIGH = lax.Precision.HIGHEST
LANES = 128
AXES = ("row", "col")
FACES = ((0, 1, 2, 3), (3, 6, 8, 9), (9, 7, 4, 0))
PACK = 40
WIDE = 48
PAD = 8

VMEM = pl.BlockSpec(memory_space=pltpu.VMEM)
SMEM = pl.BlockSpec(memory_space=pltpu.SMEM)
PARAMS = pltpu.CompilerParams(vmem_limit_bytes=48 * 1024 * 1024)


class Sizes:
    def __init__(self, cells):
        self.cells = cells
        self.blocks = cells // LANES
        self.margin = cells // 4 // LANES
        self.halo = self.margin + 1
        self.pre = -(-self.halo // 8) * 8
        self.rows = self.blocks + 2 * self.pre
        self.tall = self.rows + 2 * PAD
        self.slots = 3 * self.blocks // 2
        self.keep = self.pre - self.margin


def split_metric(metric_ref, spread, blocks):
    for block in range(blocks):
        spread[8 * block : 8 * block + 4, :] = metric_ref[:, LANES * block : LANES * (block + 1)]
    return [spread[pl.ds(comp, blocks, stride=8), :] for comp in range(4)]


def pack_kernel(
    sizes, state_ref, depth_ref, metric_ref, partner_ref, refine_ref, stats_ref, head_ref, tail_ref, spread
):
    blocks, halo = sizes.blocks, sizes.halo
    rx, ry, sx, sy = split_metric(metric_ref, spread, blocks)
    depth = depth_ref[...]
    refine = refine_ref[...].astype(jnp.float32)
    faces = ((sx, sy), (rx + sx, ry + sy), (rx, ry))
    lengths = [jnp.sqrt(vx * vx + vy * vy) for vx, vy in faces]
    rate = jnp.sqrt(GRAVITY * depth) * jnp.maximum(jnp.maximum(lengths[0], lengths[1]), lengths[2])
    top = jnp.max(jnp.max(rate, axis=0, keepdims=True), axis=1, keepdims=True)
    extra = jnp.sum(jnp.sum(refine, axis=0, keepdims=True), axis=1, keepdims=True)
    shape = stats_ref.shape
    lane = lax.broadcasted_iota(jnp.int32, shape, 1)
    stats_ref[...] = jnp.where(
        lane < LANES // 2, jnp.broadcast_to(top, shape), jnp.broadcast_to(extra, shape)
    )
    partner = partner_ref[...].astype(jnp.float32)
    for ref, start in ((head_ref, 0), (tail_ref, blocks - halo)):
        for block in range(halo):
            lo = LANES * (start + block)
            for field in range(3):
                at = PACK * block + 10 * field
                ref[at : at + 10, :] = state_ref[field, :, lo : lo + LANES]
        for num, dense in enumerate((depth, rx, ry, sx, sy, partner, refine)):
            ref[pl.ds(30 + num, halo, stride=PACK), :] = dense[start : start + halo]


def pair_index(partner):
    lane = lax.broadcasted_iota(jnp.int32, partner.shape, 1)
    target = lane + partner.astype(jnp.int32)
    return target & (LANES - 1), (target >= 0) & (target < LANES)


def lane_gather(values, index):
    return jnp.take_along_axis(values, index, axis=1, mode="promise_in_bounds")


def outer_values(load, index, inside):
    shape = index.shape
    lane = lax.broadcasted_iota(jnp.int32, shape, 1)

    def prev(item):
        return pltpu.roll(jnp.where(lane == LANES - 1, load(item, -1), load(item, 0)), 1, 1)

    def after(item):
        return pltpu.roll(jnp.where(lane == 0, load(item, 1), load(item, 0)), LANES - 1, 1)

    def across(item):
        other = jnp.where(lane < LANES // 2, load(item, 1), load(item, -1))
        return jnp.where(inside, lane_gather(load(item, 0), index), lane_gather(other, index))

    return prev, after, across


def wall_masks(sizes, group, place, count, partner):
    shape = partner.shape
    lane = lax.broadcasted_iota(jnp.int32, shape, 1)
    row = lax.broadcasted_iota(jnp.int32, shape, 0) + 8 * group
    first = (lane == 0) & (row == sizes.pre) & (place == 0)
    last = (lane == LANES - 1) & (row == sizes.pre + sizes.blocks - 1) & (place == count - 1)
    return first, last, partner == 0


def tendency(load, geo, walls, index, inside, diff_ref, lift_ref):
    speed_sq, rx, ry, sx, sy = geo[:5]
    outer_sq, waves, ghosts = geo[5:8], geo[8:11], geo[11:14]
    own = [[load(10 * field + node, 0) for node in range(10)] for field in range(3)]
    eta, mom_x, mom_y = own
    flow_r = [-(rx * mom_x[b] + ry * mom_y[b]) for b in range(10)]
    flow_s = [-(sx * mom_x[b] + sy * mom_y[b]) for b in range(10)]
    half_r = (0.5 * rx, 0.5 * ry)
    half_s = (0.5 * sx, 0.5 * sy)
    vectors = (
        (-half_s[0], -half_s[1]),
        (half_r[0] + half_s[0], half_r[1] + half_s[1]),
        (-half_r[0], -half_r[1]),
    )
    fetch = outer_values(load, index, inside)
    jumps = ([], [], [])
    for face in range(3):
        vec_x, vec_y = vectors[face]
        theirs = FACES[(1, 0, 2)[face]]
        wall = walls[face]
        for j in range(4):
            node, match = FACES[face][j], theirs[3 - j]
            in_eta, in_x, in_y = eta[node], mom_x[node], mom_y[node]
            ext_eta, ext_x, ext_y = [fetch[face](10 * field + match) for field in range(3)]
            bounce = (in_x * vec_x + in_y * vec_y) * ghosts[face]
            d_eta = jnp.where(wall, 0.0, in_eta - ext_eta)
            d_x = jnp.where(wall, bounce * vec_x, in_x - ext_x)
            d_y = jnp.where(wall, bounce * vec_y, in_y - ext_y)
            head = jnp.where(wall, 0.0, speed_sq * in_eta - outer_sq[face] * ext_eta)
            jumps[0].append(d_x * vec_x + d_y * vec_y - waves[face] * d_eta)
            jumps[1].append(head * vec_x - waves[face] * d_x)
            jumps[2].append(head * vec_y - waves[face] * d_y)
    pull = (-speed_sq * rx, -speed_sq * ry)
    push = (-speed_sq * sx, -speed_sq * sy)
    out = [[None] * 10 for _ in range(3)]
    for a in range(10):
        total = along_r = along_s = None
        for b in range(10):
            d_r, d_s = diff_ref[0, a, b], diff_ref[1, a, b]
            term = d_r * flow_r[b] + d_s * flow_s[b]
            total = term if b == 0 else total + term
            along_r = d_r * eta[b] if b == 0 else along_r + d_r * eta[b]
            along_s = d_s * eta[b] if b == 0 else along_s + d_s * eta[b]
        sums = [total, pull[0] * along_r + push[0] * along_s, pull[1] * along_r + push[1] * along_s]
        for q in range(12):
            weight = lift_ref[a, q]
            for field in range(3):
                sums[field] = sums[field] + weight * jumps[field][q]
        for field in range(3):
            out[field][a] = sums[field]
    return [out[field][a] for field in range(3) for a in range(10)]


def first_kernel(
    sizes, state_ref, depth_ref, metric_ref, partner_ref, refine_ref, before_ref, after_ref, diff_ref, lift_ref,
    cur, rate_ref, geo_ref, spread, wide, aux,
):
    blocks, halo, pre = sizes.blocks, sizes.halo, sizes.pre
    top, bottom = PAD + pre, PAD + pre + blocks
    place = lax.axis_index(AXES)
    count = lax.axis_size(AXES)
    metric = split_metric(metric_ref, spread, blocks)
    dense = [depth_ref[...], *metric, partner_ref[...].astype(jnp.float32), refine_ref[...].astype(jnp.float32)]
    for num in range(7):
        aux[num, top - halo : top, :] = before_ref[pl.ds(30 + num, halo, stride=PACK), :]
        aux[num, top:bottom, :] = dense[num]
        aux[num, bottom : bottom + halo, :] = after_ref[pl.ds(30 + num, halo, stride=PACK), :]
    for block in range(blocks):
        for field in range(3):
            at = WIDE * block + 16 * field
            wide[at : at + 10, :] = state_ref[field, :, LANES * block : LANES * (block + 1)]
    for field in range(3):
        for node in range(10):
            item = 10 * field + node
            cur[item, top - halo : top, :] = before_ref[pl.ds(item, halo, stride=PACK), :]
            cur[item, top:bottom, :] = wide[pl.ds(16 * field + node, blocks, stride=WIDE), :]
            cur[item, bottom : bottom + halo, :] = after_ref[pl.ds(item, halo, stride=PACK), :]

    def step(group, carry):
        base = PAD + 8 * group

        def load_aux(item, shift):
            return aux[item, pl.ds(base + shift, 8), :]

        def load(item, shift):
            return cur[item, pl.ds(base + shift, 8), :]

        depth, rx, ry, sx, sy, partner, refine = [load_aux(num, 0) for num in range(7)]
        index, inside = pair_index(partner)
        fetch = outer_values(load_aux, index, inside)
        walls = wall_masks(sizes, group, place, count, partner)
        speed_sq = GRAVITY * depth
        outer_sq = [jnp.where(walls[k], speed_sq, GRAVITY * fetch[k](0)) for k in range(3)]
        faces = ((sx, sy), (rx + sx, ry + sy), (rx, ry))
        squares = [vx * vx + vy * vy for vx, vy in faces]
        waves = [
            0.5 * jnp.sqrt(squares[k]) * jnp.sqrt(jnp.maximum(speed_sq, outer_sq[k])) for k in range(3)
        ]
        ghosts = [8.0 / squares[k] for k in range(3)]
        geo = [speed_sq, rx, ry, sx, sy, *outer_sq, *waves, *ghosts]
        rates = tendency(load, geo, walls, index, inside, diff_ref, lift_ref)
        at = pl.ds(pl.multiple_of(8 * group, 8), 8)
        for num, value in enumerate([*geo, partner, refine]):
            geo_ref[num, at, :] = value
        for item in range(30):
            rate_ref[item, at, :] = rates[item]
        return carry

    lax.fori_loop(0, sizes.rows // 8, step, 0)


def second_kernel(
    sizes, cur, rate_ref, geo_ref, stats_ref, diff_ref, lift_ref, prolong_ref, out_ref,
    first, ends_ref, place_v, place_s, wide, weights, gathered, index_ref, sem,
):
    slots, keep, rows = sizes.slots, sizes.keep, sizes.rows
    place = lax.axis_index(AXES)
    count = lax.axis_size(AXES)
    stats = stats_ref[...]
    lane_n = lax.broadcasted_iota(jnp.int32, stats.shape, 1)
    dev_n = lax.broadcasted_iota(jnp.int32, stats.shape, 0)
    rate = jnp.where(lane_n < LANES // 2, stats, 0.0)
    top = jnp.max(jnp.max(rate, axis=0, keepdims=True), axis=1, keepdims=True)
    gone = jnp.where((lane_n == LANES - 1) & (dev_n < place), stats, 0.0)
    earlier = jnp.sum(jnp.sum(gone, axis=0, keepdims=True), axis=1, keepdims=True)
    step = COURANT / top
    wide[...] = jnp.zeros(wide.shape, jnp.float32)
    refine = geo_ref[15, keep : keep + slots, :]
    counts = (1.0 + refine).astype(jnp.bfloat16)
    row_i = lax.broadcasted_iota(jnp.int32, (LANES, LANES), 0)
    col_i = lax.broadcasted_iota(jnp.int32, (LANES, LANES), 1)
    upper = (row_i <= col_i).astype(jnp.bfloat16)
    within = jnp.dot(counts, upper, preferred_element_type=jnp.float32)
    whole = jnp.dot(counts, jnp.ones((LANES, LANES), jnp.bfloat16), preferred_element_type=jnp.float32)
    row_s = lax.broadcasted_iota(jnp.int32, (slots, slots), 0)
    col_s = lax.broadcasted_iota(jnp.int32, (slots, slots), 1)
    lower = (col_s < row_s).astype(jnp.bfloat16)
    before = jnp.dot(lower, whole.astype(jnp.bfloat16), preferred_element_type=jnp.float32)
    own = before[sizes.margin : sizes.margin + 1, :]
    start = earlier - (place * (sizes.cells // 2)).astype(jnp.float32)
    ends = within + before + (start - own)
    ends_ref[:slots, :] = 2.0 * ends + refine
    ends_ref[slots:, :] = jnp.full((8, LANES), 1e9, jnp.float32)
    full = before + whole + (start - own)
    first_slot = LANES * lax.broadcasted_iota(jnp.int32, (slots, LANES), 1).astype(jnp.float32)
    lead = jnp.sum((full <= first_slot).astype(jnp.float32), axis=0, keepdims=True)
    lead = jnp.clip(lead.astype(jnp.int32), 0, slots - 1)
    place_v[...] = jnp.broadcast_to(lead, (8, LANES))
    copy = pltpu.make_async_copy(place_v, place_s, sem)
    copy.start()

    for item in range(30):
        first[item, PAD : PAD + rows, :] = cur[item, PAD : PAD + rows, :] + step * rate_ref[item]

    def stage(group, carry):
        base = PAD + 8 * group
        at = pl.ds(pl.multiple_of(8 * group, 8), 8)

        def load(item, shift):
            return first[item, pl.ds(base + shift, 8), :]

        geo = [geo_ref[num, at, :] for num in range(14)]
        partner = geo_ref[14, at, :]
        index, inside = pair_index(partner)
        walls = wall_masks(sizes, group, place, count, partner)
        rates = tendency(load, geo, walls, index, inside, diff_ref, lift_ref)
        lead_row = (8 * group - keep) * WIDE
        for field in range(3):
            for node in range(10):
                item = 10 * field + node
                old = cur[item, pl.ds(pl.multiple_of(base, 8), 8), :]
                new = 0.5 * old + 0.5 * (load(item, 0) + step * rates[item])
                wide[pl.ds(lead_row + 16 * field + node, 8, stride=WIDE), :] = new
        return carry

    lax.fori_loop(keep // 8, (keep + slots) // 8, stage, 0)

    weights[...] = jnp.zeros(weights.shape, jnp.float32)
    for child in range(2):
        for field in range(3):
            weights[
                WIDE * child + 16 * field : WIDE * child + 16 * field + 10, 16 * field : 16 * field + 10
            ] = prolong_ref[child]
    copy.wait()
    for slot in range(slots):
        lead_at = place_s[0, slot]
        index_ref[0, slot : slot + 1, :] = ends_ref[pl.ds(lead_at, 1), :]
        index_ref[1, slot : slot + 1, :] = ends_ref[pl.ds(lead_at + 1, 1), :]
    near, far = index_ref[0], index_ref[1]
    slot_no = LANES * lax.broadcasted_iota(jnp.int32, (slots, LANES), 0) + lax.broadcasted_iota(
        jnp.int32, (slots, LANES), 1
    )
    goal = (2 * slot_no + 1).astype(jnp.float32)
    beyond = jnp.broadcast_to(near[:, LANES - 1 :], (slots, LANES)) <= goal

    def pick(index):
        return jnp.where(beyond, lane_gather(far, index), lane_gather(near, index))

    found = jnp.zeros((slots, LANES), jnp.int32)
    size = LANES // 2
    while size:
        passed = pick(found + (size - 1)) <= goal
        found = jnp.where(passed, found + size, found)
        size //= 2
    mine = pick(found).astype(jnp.int32)
    split = mine & 1
    begin = (mine >> 1) - 1 - split
    kind = split * (1 + slot_no - begin)
    index_ref[0] = found.astype(jnp.float32)
    index_ref[1] = kind.astype(jnp.float32)
    index_ref[2] = beyond.astype(jnp.float32)
    for slot in range(slots):
        lead_at = place_s[0, slot] * WIDE
        lane_idx = jnp.broadcast_to(index_ref[0, slot : slot + 1, :], (WIDE, LANES)).astype(jnp.int32)
        passed = jnp.broadcast_to(index_ref[2, slot : slot + 1, :], (WIDE, LANES)) > 0.5
        one = wide[pl.ds(pl.multiple_of(lead_at, WIDE), WIDE), :]
        two = wide[pl.ds(pl.multiple_of(lead_at + WIDE, WIDE), WIDE), :]
        gathered[:, LANES * slot : LANES * (slot + 1)] = jnp.where(
            passed, lane_gather(two, lane_idx), lane_gather(one, lane_idx)
        )
    matrix = weights[...]
    chunk = 8 * LANES
    for part in range(slots // 8):
        span = slice(chunk * part, chunk * (part + 1))
        values = gathered[:, span]
        children = jnp.dot(matrix, values, precision=HIGH, preferred_element_type=jnp.float32)
        for sub in range(8):
            slot = 8 * part + sub
            cut = slice(LANES * sub, LANES * (sub + 1))
            tag = jnp.broadcast_to(index_ref[1, slot : slot + 1, :], (16, LANES))
            for field in range(3):
                at = slice(16 * field, 16 * field + 16)
                second = slice(WIDE + 16 * field, WIDE + 16 * field + 16)
                value = jnp.where(
                    tag < 0.5,
                    values[at, cut],
                    jnp.where(tag < 1.5, children[at, cut], children[second, cut]),
                )
                out_ref[field, :, LANES * slot : LANES * (slot + 1)] = value[:10]


def shards(state, depth, metric, partner, refine, diff_ops, lift, prolong):
    sizes = Sizes(state.shape[2])
    count = lax.axis_size(AXES)
    blocks, rows, slots = sizes.blocks, sizes.rows, sizes.slots
    depth, partner, refine = [x.reshape(blocks, LANES) for x in (depth, partner, refine)]
    f32 = jnp.float32
    packed = jax.ShapeDtypeStruct((PACK * sizes.halo, LANES), f32)
    stats, head, tail = pl.pallas_call(
        functools.partial(pack_kernel, sizes),
        name="pack",
        out_shape=(jax.ShapeDtypeStruct((count, LANES), f32), packed, packed),
        in_specs=[VMEM] * 5,
        out_specs=(VMEM,) * 3,
        scratch_shapes=[pltpu.VMEM((8 * blocks, LANES), f32)],
        compiler_params=PARAMS,
    )(state, depth, metric, partner, refine)
    before = lax.ppermute(tail, AXES, [(i, (i + 1) % count) for i in range(count)])
    after = lax.ppermute(head, AXES, [((i + 1) % count, i) for i in range(count)])
    stats = lax.all_to_all(stats, AXES, 0, 0, tiled=True)
    cur, rates, geo = pl.pallas_call(
        functools.partial(first_kernel, sizes),
        name="first_stage",
        out_shape=(
            jax.ShapeDtypeStruct((30, sizes.tall, LANES), f32),
            jax.ShapeDtypeStruct((30, rows, LANES), f32),
            jax.ShapeDtypeStruct((16, rows, LANES), f32),
        ),
        in_specs=[VMEM] * 7 + [SMEM] * 2,
        out_specs=(VMEM,) * 3,
        scratch_shapes=[
            pltpu.VMEM((8 * blocks, LANES), f32),
            pltpu.VMEM((WIDE * blocks, LANES), f32),
            pltpu.VMEM((7, sizes.tall, LANES), f32),
        ],
        compiler_params=PARAMS,
    )(state, depth, metric, partner, refine, before, after, diff_ops, lift)
    return pl.pallas_call(
        functools.partial(second_kernel, sizes),
        name="second_stage_refine",
        out_shape=jax.ShapeDtypeStruct((3, 10, LANES * slots), f32),
        in_specs=[VMEM] * 4 + [SMEM] * 2 + [VMEM],
        out_specs=VMEM,
        scratch_shapes=[
            pltpu.VMEM((30, sizes.tall, LANES), f32),
            pltpu.VMEM((slots + 8, LANES), f32),
            pltpu.VMEM((8, LANES), jnp.int32),
            pltpu.SMEM((8, LANES), jnp.int32),
            pltpu.VMEM((WIDE * (slots + 1), LANES), f32),
            pltpu.VMEM((2 * WIDE, WIDE), f32),
            pltpu.VMEM((WIDE, LANES * slots), f32),
            pltpu.VMEM((3, slots, LANES), f32),
            pltpu.SemaphoreType.DMA,
        ],
        compiler_params=PARAMS,
    )(cur, rates, geo, stats, diff_ops, lift, prolong)


def solution(mesh):
    return jax.shard_map(
        shards,
        mesh=mesh,
        in_specs=(
            P(None, None, AXES),
            P(AXES),
            P(None, AXES),
            P(AXES),
            P(AXES),
            P(),
            P(),
            P(),
        ),
        out_specs=P(None, None, AXES),
        check_vma=False,
    )
```

```python
import functools

import jax
import jax.numpy as jnp
from jax import lax
from jax.experimental import pallas as pl
from jax.experimental.pallas import tpu as pltpu
from jax.sharding import PartitionSpec as P

GRAVITY = 9.81
COURANT = 0.5
HIGH = lax.Precision.HIGHEST
LANES = 128
AXES = ("row", "col")
FACES = ((0, 1, 2, 3), (3, 6, 8, 9), (9, 7, 4, 0))
PACK = 40
WIDE = 32
PAD = 8

VMEM = pl.BlockSpec(memory_space=pltpu.VMEM)
HBM = pl.BlockSpec(memory_space=pltpu.HBM)
PARAMS = pltpu.CompilerParams(vmem_limit_bytes=48 * 1024 * 1024)


class Sizes:
    def __init__(self, cells):
        self.cells = cells
        self.blocks = cells // LANES
        self.margin = cells // 4 // LANES
        self.halo = self.margin + 1
        self.rows = -(-(self.blocks + 2 * self.halo) // 8) * 8
        self.tall = self.rows + 2 * PAD
        self.slots = 3 * self.blocks // 2
        self.keep = self.halo - self.margin


def fetch_all(pairs, sems):
    copies = [pltpu.make_async_copy(src, dst, sems.at[num]) for num, (src, dst) in enumerate(pairs)]
    for copy in copies:
        copy.start()
    return copies


def split_metric(metric_ref, spread, blocks):
    for block in range(blocks):
        spread[8 * block : 8 * block + 4, :] = metric_ref[:, LANES * block : LANES * (block + 1)]
    return [spread[pl.ds(comp, blocks, stride=8), :] for comp in range(4)]


def pack_kernel(
    sizes, state_hbm, depth_hbm, metric_hbm, partner_hbm, refine_hbm, stats_ref, head_ref, tail_ref,
    state_head, state_tail, depth_ref, metric_ref, partner_ref, refine_ref, spread, sems,
):
    blocks, halo = sizes.blocks, sizes.halo
    wide = LANES * halo
    copies = fetch_all(
        (
            (depth_hbm, depth_ref),
            (metric_hbm, metric_ref),
            (refine_hbm, refine_ref),
            (partner_hbm, partner_ref),
            (state_hbm.at[:, :, 0:wide], state_head),
            (state_hbm.at[:, :, sizes.cells - wide : sizes.cells], state_tail),
        ),
        sems,
    )
    for copy in copies:
        copy.wait()
    rx, ry, sx, sy = split_metric(metric_ref, spread, blocks)
    depth = depth_ref[...]
    refine = refine_ref[...].astype(jnp.float32)
    faces = ((sx, sy), (rx + sx, ry + sy), (rx, ry))
    lengths = [jnp.sqrt(vx * vx + vy * vy) for vx, vy in faces]
    rate = jnp.sqrt(GRAVITY * depth) * jnp.maximum(jnp.maximum(lengths[0], lengths[1]), lengths[2])
    top = jnp.max(jnp.max(rate, axis=0, keepdims=True), axis=1, keepdims=True)
    extra = jnp.sum(jnp.sum(refine, axis=0, keepdims=True), axis=1, keepdims=True)
    shape = stats_ref.shape
    lane = lax.broadcasted_iota(jnp.int32, shape, 1)
    stats_ref[...] = jnp.where(
        lane < LANES // 2, jnp.broadcast_to(top, shape), jnp.broadcast_to(extra, shape)
    )
    partner = partner_ref[...].astype(jnp.float32)
    for ref, source, start in ((head_ref, state_head, 0), (tail_ref, state_tail, blocks - halo)):
        pack_state(source, ref, halo)
        for num, dense in enumerate((depth, rx, ry, sx, sy, partner, refine)):
            ref[pl.ds(4 * num + 3, halo, stride=PACK), :] = dense[start : start + halo]


def pack_state(source, target, blocks):
    for block in range(blocks):
        for node in range(10):
            at = PACK * block + 4 * node
            target[at : at + 3, :] = source[node, :, LANES * block : LANES * (block + 1)]


def pair_index(partner):
    lane = lax.broadcasted_iota(jnp.int32, partner.shape, 1)
    target = lane + partner.astype(jnp.int32)
    return target & (LANES - 1), (target >= 0) & (target < LANES)


def lane_gather(values, index):
    return jnp.take_along_axis(values, index, axis=1, mode="promise_in_bounds")


def outer_values(load, index, inside):
    shape = index.shape
    lane = lax.broadcasted_iota(jnp.int32, shape, 1)

    def prev(item):
        return pltpu.roll(jnp.where(lane == LANES - 1, load(item, -1), load(item, 0)), 1, 1)

    def after(item):
        return pltpu.roll(jnp.where(lane == 0, load(item, 1), load(item, 0)), LANES - 1, 1)

    def across(item):
        other = jnp.where(lane < LANES // 2, load(item, 1), load(item, -1))
        return jnp.where(inside, lane_gather(load(item, 0), index), lane_gather(other, index))

    return prev, after, across


def wall_masks(sizes, start, place, count, partner):
    shape = partner.shape
    lane = lax.broadcasted_iota(jnp.int32, shape, 1)
    row = lax.broadcasted_iota(jnp.int32, shape, 0) + start
    first = (lane == 0) & (row == sizes.halo) & (place == 0)
    last = (lane == LANES - 1) & (row == sizes.halo + sizes.blocks - 1) & (place == count - 1)
    return first, last, partner == 0


def tendency(load, geo, walls, index, inside, diff_ref, lift_ref):
    speed_sq, rx, ry, sx, sy = geo[:5]
    outer_sq, waves, ghosts = geo[5:8], geo[8:11], geo[11:14]
    own = [[load(10 * field + node, 0) for node in range(10)] for field in range(3)]
    eta, mom_x, mom_y = own
    flow_r = [-(rx * mom_x[b] + ry * mom_y[b]) for b in range(10)]
    flow_s = [-(sx * mom_x[b] + sy * mom_y[b]) for b in range(10)]
    half_r = (0.5 * rx, 0.5 * ry)
    half_s = (0.5 * sx, 0.5 * sy)
    vectors = (
        (-half_s[0], -half_s[1]),
        (half_r[0] + half_s[0], half_r[1] + half_s[1]),
        (-half_r[0], -half_r[1]),
    )
    fetch = outer_values(load, index, inside)
    jumps = ([], [], [])
    for face in range(3):
        vec_x, vec_y = vectors[face]
        theirs = FACES[(1, 0, 2)[face]]
        wall = walls[face]
        for j in range(4):
            node, match = FACES[face][j], theirs[3 - j]
            in_eta, in_x, in_y = eta[node], mom_x[node], mom_y[node]
            ext_eta, ext_x, ext_y = [fetch[face](10 * field + match) for field in range(3)]
            bounce = (in_x * vec_x + in_y * vec_y) * ghosts[face]
            d_eta = jnp.where(wall, 0.0, in_eta - ext_eta)
            d_x = jnp.where(wall, bounce * vec_x, in_x - ext_x)
            d_y = jnp.where(wall, bounce * vec_y, in_y - ext_y)
            head = jnp.where(wall, 0.0, speed_sq * in_eta - outer_sq[face] * ext_eta)
            jumps[0].append(d_x * vec_x + d_y * vec_y - waves[face] * d_eta)
            jumps[1].append(head * vec_x - waves[face] * d_x)
            jumps[2].append(head * vec_y - waves[face] * d_y)
    pull = (-speed_sq * rx, -speed_sq * ry)
    push = (-speed_sq * sx, -speed_sq * sy)
    out = [[None] * 10 for _ in range(3)]
    for a in range(10):
        total = along_r = along_s = None
        for b in range(10):
            d_r, d_s = diff_ref[a, 0, b], diff_ref[a, 1, b]
            term = d_r * flow_r[b] + d_s * flow_s[b]
            total = term if b == 0 else total + term
            along_r = d_r * eta[b] if b == 0 else along_r + d_r * eta[b]
            along_s = d_s * eta[b] if b == 0 else along_s + d_s * eta[b]
        sums = [total, pull[0] * along_r + push[0] * along_s, pull[1] * along_r + push[1] * along_s]
        for q in range(12):
            weight = lift_ref[a, q]
            for field in range(3):
                sums[field] = sums[field] + weight * jumps[field][q]
        for field in range(3):
            out[field][a] = sums[field]
    return [out[field][a] for field in range(3) for a in range(10)]


def first_kernel(
    sizes, state_hbm, depth_hbm, metric_hbm, partner_hbm, refine_hbm, before_hbm, after_hbm, diff_hbm, lift_hbm,
    cur, rate_ref, geo_ref,
    state_ref, depth_ref, metric_ref, partner_ref, refine_ref, before_ref, after_ref, diff_ref, lift_ref,
    spread, wide, aux, sems,
):
    blocks, halo = sizes.blocks, sizes.halo
    top, bottom = PAD + halo, PAD + halo + blocks
    place = lax.axis_index(AXES)
    count = lax.axis_size(AXES)
    copies = fetch_all(
        (
            (metric_hbm, metric_ref),
            (state_hbm, state_ref),
            (depth_hbm, depth_ref),
            (partner_hbm, partner_ref),
            (refine_hbm, refine_ref),
            (before_hbm, before_ref),
            (after_hbm, after_ref),
            (diff_hbm, diff_ref),
            (lift_hbm, lift_ref),
        ),
        sems,
    )
    for copy in copies:
        copy.wait()
    metric = split_metric(metric_ref, spread, blocks)
    dense = [depth_ref[...], *metric, partner_ref[...].astype(jnp.float32), refine_ref[...].astype(jnp.float32)]
    pack_state(state_ref, wide, blocks)
    for num in range(7):
        at = 4 * num + 3
        aux[num, top - halo : top, :] = before_ref[pl.ds(at, halo, stride=PACK), :]
        aux[num, top:bottom, :] = dense[num]
        aux[num, bottom : bottom + halo, :] = after_ref[pl.ds(at, halo, stride=PACK), :]
    for field in range(3):
        for node in range(10):
            item = 10 * field + node
            at = 4 * node + field
            cur[item, top - halo : top, :] = before_ref[pl.ds(at, halo, stride=PACK), :]
            cur[item, top:bottom, :] = wide[pl.ds(at, blocks, stride=PACK), :]
            cur[item, bottom : bottom + halo, :] = after_ref[pl.ds(at, halo, stride=PACK), :]

    def step(group, carry):
        base = PAD + 8 * group

        def load_aux(item, shift):
            return aux[item, pl.ds(base + shift, 8), :]

        def load(item, shift):
            return cur[item, pl.ds(base + shift, 8), :]

        depth, rx, ry, sx, sy, partner, refine = [load_aux(num, 0) for num in range(7)]
        index, inside = pair_index(partner)
        fetch = outer_values(load_aux, index, inside)
        walls = wall_masks(sizes, 8 * group, place, count, partner)
        speed_sq = GRAVITY * depth
        outer_sq = [jnp.where(walls[k], speed_sq, GRAVITY * fetch[k](0)) for k in range(3)]
        faces = ((sx, sy), (rx + sx, ry + sy), (rx, ry))
        squares = [vx * vx + vy * vy for vx, vy in faces]
        waves = [
            0.5 * jnp.sqrt(squares[k]) * jnp.sqrt(jnp.maximum(speed_sq, outer_sq[k])) for k in range(3)
        ]
        ghosts = [8.0 / squares[k] for k in range(3)]
        geo = [speed_sq, rx, ry, sx, sy, *outer_sq, *waves, *ghosts]
        rates = tendency(load, geo, walls, index, inside, diff_ref, lift_ref)
        at = pl.ds(pl.multiple_of(8 * group, 8), 8)
        for num, value in enumerate([*geo, partner, refine]):
            geo_ref[num, at, :] = value
        for item in range(30):
            rate_ref[item, at, :] = rates[item]
        return carry

    lax.fori_loop(0, sizes.rows // 8, step, 0)


def child_matrix(prolong_ref):
    f32 = jnp.float32
    node_r = lax.broadcasted_iota(jnp.int32, (PACK, 10), 0) // 4
    spread_r = (node_r == lax.broadcasted_iota(jnp.int32, (PACK, 10), 1)).astype(f32)
    item_c = lax.broadcasted_iota(jnp.int32, (10, WIDE), 1)
    spread_c = (item_c % 10 == lax.broadcasted_iota(jnp.int32, (10, WIDE), 0)).astype(f32)
    row = lax.broadcasted_iota(jnp.int32, (PACK, WIDE), 0)
    col = lax.broadcasted_iota(jnp.int32, (PACK, WIDE), 1)
    same = row % 4 == col // 10
    parts = []
    for child in range(2):
        left = jnp.dot(spread_r, prolong_ref[:, child, :], precision=HIGH, preferred_element_type=f32)
        full = jnp.dot(left, spread_c, precision=HIGH, preferred_element_type=f32)
        parts.append(jnp.where(same, full, 0.0))
    parts.append((same & (row // 4 == col % 10)).astype(f32))
    whole = jnp.concatenate(parts, axis=0)
    rounded = whole.astype(jnp.bfloat16)
    rest = (whole - rounded.astype(f32)).astype(jnp.bfloat16)
    return jnp.concatenate([rounded, rounded, rounded, rest], axis=1)


def second_kernel(
    sizes, cur, rate_ref, geo_ref, stats_hbm, diff_hbm, lift_hbm, prolong_hbm, out_hbm,
    stats_ref, diff_ref, lift_ref, prolong_ref, out_ref,
    first, ends_ref, place_v, place_s, wide, weights, gathered, index_ref, sems, out_sems, sem,
):
    slots, keep, rows = sizes.slots, sizes.keep, sizes.rows
    place = lax.axis_index(AXES)
    count = lax.axis_size(AXES)
    copies = fetch_all(
        ((stats_hbm, stats_ref), (prolong_hbm, prolong_ref), (diff_hbm, diff_ref), (lift_hbm, lift_ref)), sems
    )
    for item in (30, 31):
        wide[pl.ds(item, slots + 1, stride=WIDE), :] = jnp.zeros((slots + 1, LANES), jnp.float32)
    for copy in copies:
        copy.wait()
    weights[...] = child_matrix(prolong_ref)
    stats = stats_ref[...]
    lane_n = lax.broadcasted_iota(jnp.int32, stats.shape, 1)
    dev_n = lax.broadcasted_iota(jnp.int32, stats.shape, 0)
    rate = jnp.where(lane_n < LANES // 2, stats, 0.0)
    top = jnp.max(jnp.max(rate, axis=0, keepdims=True), axis=1, keepdims=True)
    gone = jnp.where((lane_n == LANES - 1) & (dev_n < place), stats, 0.0)
    earlier = jnp.sum(jnp.sum(gone, axis=0, keepdims=True), axis=1, keepdims=True)
    step = COURANT / top
    refine = geo_ref[15, keep : keep + slots, :]
    counts = (1.0 + refine).astype(jnp.bfloat16)
    row_i = lax.broadcasted_iota(jnp.int32, (LANES, LANES), 0)
    col_i = lax.broadcasted_iota(jnp.int32, (LANES, LANES), 1)
    upper = (row_i <= col_i).astype(jnp.bfloat16)
    within = jnp.dot(counts, upper, preferred_element_type=jnp.float32)
    whole = jnp.dot(counts, jnp.ones((LANES, LANES), jnp.bfloat16), preferred_element_type=jnp.float32)
    row_s = lax.broadcasted_iota(jnp.int32, (slots, slots), 0)
    col_s = lax.broadcasted_iota(jnp.int32, (slots, slots), 1)
    lower = (col_s < row_s).astype(jnp.bfloat16)
    before = jnp.dot(lower, whole.astype(jnp.bfloat16), preferred_element_type=jnp.float32)
    own = before[sizes.margin : sizes.margin + 1, :]
    start = earlier - (place * (sizes.cells // 2)).astype(jnp.float32)
    ends = within + before + (start - own)
    ends_ref[:slots, :] = 2.0 * ends + refine
    ends_ref[slots:, :] = jnp.full((8, LANES), 1e9, jnp.float32)
    full = before + whole + (start - own)
    first_slot = LANES * lax.broadcasted_iota(jnp.int32, (slots, LANES), 1).astype(jnp.float32)
    lead = jnp.sum((full <= first_slot).astype(jnp.float32), axis=0, keepdims=True)
    lead = jnp.clip(lead.astype(jnp.int32), 0, slots - 1)
    place_v[...] = jnp.broadcast_to(lead, (8, LANES))
    copy = pltpu.make_async_copy(place_v, place_s, sem)
    copy.start()

    for item in range(30):
        first[item, PAD : PAD + rows, :] = cur[item, PAD : PAD + rows, :] + step * rate_ref[item]

    def stage(group, carry):
        base = PAD + keep + 8 * group
        at = pl.ds(8 * group + keep, 8)

        def load(item, shift):
            return first[item, pl.ds(base + shift, 8), :]

        geo = [geo_ref[num, at, :] for num in range(14)]
        partner = geo_ref[14, at, :]
        index, inside = pair_index(partner)
        walls = wall_masks(sizes, 8 * group + keep, place, count, partner)
        rates = tendency(load, geo, walls, index, inside, diff_ref, lift_ref)
        lead_row = 8 * WIDE * group
        for field in range(3):
            for node in range(10):
                item = 10 * field + node
                old = cur[item, pl.ds(base, 8), :]
                new = 0.5 * old + 0.5 * (load(item, 0) + step * rates[item])
                wide[pl.ds(lead_row + item, 8, stride=WIDE), :] = new
        return carry

    lax.fori_loop(0, slots // 8, stage, 0)

    copy.wait()
    for slot in range(slots):
        lead_at = place_s[0, slot]
        index_ref[0, slot : slot + 1, :] = ends_ref[pl.ds(lead_at, 1), :]
        index_ref[1, slot : slot + 1, :] = ends_ref[pl.ds(lead_at + 1, 1), :]
    near, far = index_ref[0], index_ref[1]
    slot_no = LANES * lax.broadcasted_iota(jnp.int32, (slots, LANES), 0) + lax.broadcasted_iota(
        jnp.int32, (slots, LANES), 1
    )
    goal = (2 * slot_no + 1).astype(jnp.float32)
    beyond = jnp.broadcast_to(near[:, LANES - 1 :], (slots, LANES)) <= goal

    def pick(index):
        return jnp.where(beyond, lane_gather(far, index), lane_gather(near, index))

    found = jnp.zeros((slots, LANES), jnp.int32)
    size = LANES // 2
    while size:
        passed = pick(found + (size - 1)) <= goal
        found = jnp.where(passed, found + size, found)
        size //= 2
    mine = pick(found).astype(jnp.int32)
    split = mine & 1
    begin = (mine >> 1) - 1 - split
    kind = split * (1 + slot_no - begin)
    index_ref[0] = found.astype(jnp.float32)
    index_ref[1] = kind.astype(jnp.float32)
    index_ref[2] = beyond.astype(jnp.float32)
    for slot in range(slots):
        lead_at = place_s[0, slot] * WIDE
        lane_idx = jnp.broadcast_to(index_ref[0, slot : slot + 1, :], (WIDE, LANES)).astype(jnp.int32)
        passed = jnp.broadcast_to(index_ref[2, slot : slot + 1, :], (WIDE, LANES)) > 0.5
        one = wide[pl.ds(pl.multiple_of(lead_at, WIDE), WIDE), :]
        two = wide[pl.ds(pl.multiple_of(lead_at + WIDE, WIDE), WIDE), :]
        gathered[:, LANES * slot : LANES * (slot + 1)] = jnp.where(
            passed, lane_gather(two, lane_idx), lane_gather(one, lane_idx)
        )
    matrix = weights[...]
    chunk = 8 * LANES
    results = []
    for part in range(slots // 8):
        span = slice(chunk * part, chunk * (part + 1))
        values = gathered[:, span]
        high = values.astype(jnp.bfloat16)
        rest = values - high.astype(jnp.float32)
        low = rest.astype(jnp.bfloat16)
        last = (rest - low.astype(jnp.float32)).astype(jnp.bfloat16)
        stack = jnp.concatenate([high, low, last, high], axis=0)
        children = jnp.dot(matrix, stack, preferred_element_type=jnp.float32)
        for sub in range(8):
            slot = 8 * part + sub
            cut = slice(LANES * sub, LANES * (sub + 1))
            tag = jnp.broadcast_to(index_ref[1, slot : slot + 1, :], (PACK, LANES))
            value = jnp.where(
                tag < 0.5,
                children[2 * PACK :, cut],
                jnp.where(tag < 1.5, children[:PACK, cut], children[PACK : 2 * PACK, cut]),
            )
            for node in range(10):
                out_ref[node, :, LANES * slot : LANES * (slot + 1)] = value[4 * node : 4 * node + 3]
        result = pltpu.make_async_copy(out_ref.at[:, :, span], out_hbm.at[:, :, span], out_sems.at[part])
        result.start()
        results.append(result)
    for result in results:
        result.wait()


def shards(state, depth, metric, partner, refine, diff_ops, lift, prolong):
    sizes = Sizes(state.shape[2])
    count = lax.axis_size(AXES)
    blocks, rows, slots, halo = sizes.blocks, sizes.rows, sizes.slots, sizes.halo
    depth, partner, refine = [x.reshape(blocks, LANES) for x in (depth, partner, refine)]
    state, diff_ops, prolong = [jnp.transpose(x, (1, 0, 2)) for x in (state, diff_ops, prolong)]
    f32, i32 = jnp.float32, jnp.int32
    packed = jax.ShapeDtypeStruct((PACK * halo, LANES), f32)
    dense = [
        pltpu.VMEM((blocks, LANES), f32),
        pltpu.VMEM(metric.shape, f32),
        pltpu.VMEM((blocks, LANES), i32),
        pltpu.VMEM((blocks, LANES), i32),
    ]
    stats, head, tail = pl.pallas_call(
        functools.partial(pack_kernel, sizes),
        name="pack",
        out_shape=(jax.ShapeDtypeStruct((count, LANES), f32), packed, packed),
        in_specs=[HBM] * 5,
        out_specs=(VMEM,) * 3,
        scratch_shapes=[
            pltpu.VMEM((10, 3, LANES * halo), f32),
            pltpu.VMEM((10, 3, LANES * halo), f32),
            *dense,
            pltpu.VMEM((8 * blocks, LANES), f32),
            pltpu.SemaphoreType.DMA((6,)),
        ],
        compiler_params=PARAMS,
    )(state, depth, metric, partner, refine)
    before = lax.ppermute(tail, AXES, [(i, i + 1) for i in range(count - 1)])
    after = lax.ppermute(head, AXES, [(i + 1, i) for i in range(count - 1)])
    stats = lax.all_to_all(stats, AXES, 0, 0, tiled=True)
    operators = [pltpu.SMEM(diff_ops.shape, f32), pltpu.SMEM(lift.shape, f32)]
    cur, rates, geo = pl.pallas_call(
        functools.partial(first_kernel, sizes),
        name="first_stage",
        out_shape=(
            jax.ShapeDtypeStruct((30, sizes.tall, LANES), f32),
            jax.ShapeDtypeStruct((30, rows, LANES), f32),
            jax.ShapeDtypeStruct((16, rows, LANES), f32),
        ),
        in_specs=[HBM] * 9,
        out_specs=(VMEM,) * 3,
        scratch_shapes=[
            pltpu.VMEM(state.shape, f32),
            *dense,
            pltpu.VMEM(before.shape, f32),
            pltpu.VMEM(after.shape, f32),
            *operators,
            pltpu.VMEM((8 * blocks, LANES), f32),
            pltpu.VMEM((PACK * blocks, LANES), f32),
            pltpu.VMEM((7, sizes.tall, LANES), f32),
            pltpu.SemaphoreType.DMA((9,)),
        ],
        compiler_params=PARAMS,
    )(state, depth, metric, partner, refine, before, after, diff_ops, lift)
    refined = pl.pallas_call(
        functools.partial(second_kernel, sizes),
        name="second_stage_refine",
        out_shape=jax.ShapeDtypeStruct((10, 3, LANES * slots), f32),
        in_specs=[VMEM] * 3 + [HBM] * 4,
        out_specs=HBM,
        scratch_shapes=[
            pltpu.VMEM(stats.shape, f32),
            *operators,
            pltpu.VMEM(prolong.shape, f32),
            pltpu.VMEM((10, 3, LANES * slots), f32),
            pltpu.VMEM((30, sizes.tall, LANES), f32),
            pltpu.VMEM((slots + 8, LANES), f32),
            pltpu.VMEM((8, LANES), i32),
            pltpu.SMEM((8, LANES), i32),
            pltpu.VMEM((WIDE * (slots + 1), LANES), f32),
            pltpu.VMEM((3 * PACK, 4 * WIDE), jnp.bfloat16),
            pltpu.VMEM((WIDE, LANES * slots), f32),
            pltpu.VMEM((3, slots, LANES), f32),
            pltpu.SemaphoreType.DMA((4,)),
            pltpu.SemaphoreType.DMA((slots // 8,)),
            pltpu.SemaphoreType.DMA,
        ],
        compiler_params=PARAMS,
    )(cur, rates, geo, stats, diff_ops, lift, prolong)
    return jnp.transpose(refined, (1, 0, 2))


def solution(mesh):
    return jax.shard_map(
        shards,
        mesh=mesh,
        in_specs=(
            P(None, None, AXES),
            P(AXES),
            P(None, AXES),
            P(AXES),
            P(AXES),
            P(),
            P(),
            P(),
        ),
        out_specs=P(None, None, AXES),
        check_vma=False,
    )
```

```python
import functools

import jax
import jax.numpy as jnp
from jax import lax
from jax.experimental import pallas as pl
from jax.experimental.pallas import tpu as pltpu
from jax.sharding import PartitionSpec as P

GRAVITY = 9.81
COURANT = 0.5
HIGH = lax.Precision.HIGHEST
LANES = 128
AXES = ("row", "col")
FACES = ((0, 1, 2, 3), (3, 6, 8, 9), (9, 7, 4, 0))
PACK = 40
WIDE = 32
PAD = 8

VMEM = pl.BlockSpec(memory_space=pltpu.VMEM)
HBM = pl.BlockSpec(memory_space=pltpu.HBM)
PARAMS = pltpu.CompilerParams(vmem_limit_bytes=48 * 1024 * 1024)


class Sizes:
    def __init__(self, cells):
        self.cells = cells
        self.blocks = cells // LANES
        self.margin = cells // 4 // LANES
        self.halo = self.margin + 1
        self.rows = -(-(self.blocks + 2 * self.halo) // 8) * 8
        self.tall = self.rows + 2 * PAD
        self.slots = 3 * self.blocks // 2
        self.keep = self.halo - self.margin


def fetch_all(pairs, sems):
    copies = [pltpu.make_async_copy(src, dst, sems.at[num]) for num, (src, dst) in enumerate(pairs)]
    for copy in copies:
        copy.start()
    return copies


def split_metric(metric_ref, spread, blocks):
    for block in range(blocks):
        spread[8 * block : 8 * block + 4, :] = metric_ref[:, LANES * block : LANES * (block + 1)]
    return [spread[pl.ds(comp, blocks, stride=8), :] for comp in range(4)]


def pack_kernel(
    sizes, state_hbm, depth_hbm, metric_hbm, partner_hbm, refine_hbm, stats_ref, head_ref, tail_ref,
    state_head, state_tail, depth_ref, metric_ref, partner_ref, refine_ref, spread, sems,
):
    blocks, halo = sizes.blocks, sizes.halo
    wide = LANES * halo
    copies = fetch_all(
        (
            (depth_hbm, depth_ref),
            (metric_hbm, metric_ref),
            (refine_hbm, refine_ref),
            (partner_hbm, partner_ref),
            (state_hbm.at[:, :, 0:wide], state_head),
            (state_hbm.at[:, :, sizes.cells - wide : sizes.cells], state_tail),
        ),
        sems,
    )
    for copy in copies:
        copy.wait()
    rx, ry, sx, sy = split_metric(metric_ref, spread, blocks)
    depth = depth_ref[...]
    refine = refine_ref[...].astype(jnp.float32)
    faces = ((sx, sy), (rx + sx, ry + sy), (rx, ry))
    lengths = [jnp.sqrt(vx * vx + vy * vy) for vx, vy in faces]
    rate = jnp.sqrt(GRAVITY * depth) * jnp.maximum(jnp.maximum(lengths[0], lengths[1]), lengths[2])
    top = jnp.max(jnp.max(rate, axis=0, keepdims=True), axis=1, keepdims=True)
    extra = jnp.sum(jnp.sum(refine, axis=0, keepdims=True), axis=1, keepdims=True)
    shape = stats_ref.shape
    lane = lax.broadcasted_iota(jnp.int32, shape, 1)
    stats_ref[...] = jnp.where(
        lane < LANES // 2, jnp.broadcast_to(top, shape), jnp.broadcast_to(extra, shape)
    )
    partner = partner_ref[...].astype(jnp.float32)
    for ref, source, start in ((head_ref, state_head, 0), (tail_ref, state_tail, blocks - halo)):
        pack_state(source, ref, halo)
        for num, dense in enumerate((depth, rx, ry, sx, sy, partner, refine)):
            ref[pl.ds(4 * num + 3, halo, stride=PACK), :] = dense[start : start + halo]


def pack_state(source, target, blocks):
    for block in range(blocks):
        for node in range(10):
            at = PACK * block + 4 * node
            target[at : at + 3, :] = source[node, :, LANES * block : LANES * (block + 1)]


def pair_index(partner):
    lane = lax.broadcasted_iota(jnp.int32, partner.shape, 1)
    target = lane + partner.astype(jnp.int32)
    return target & (LANES - 1), (target >= 0) & (target < LANES)


def lane_gather(values, index):
    return jnp.take_along_axis(values, index, axis=1, mode="promise_in_bounds")


def outer_values(load, index, inside):
    shape = index.shape
    lane = lax.broadcasted_iota(jnp.int32, shape, 1)

    def prev(item):
        return pltpu.roll(jnp.where(lane == LANES - 1, load(item, -1), load(item, 0)), 1, 1)

    def after(item):
        return pltpu.roll(jnp.where(lane == 0, load(item, 1), load(item, 0)), LANES - 1, 1)

    def across(item):
        other = jnp.where(lane < LANES // 2, load(item, 1), load(item, -1))
        return jnp.where(inside, lane_gather(load(item, 0), index), lane_gather(other, index))

    return prev, after, across


def wall_masks(sizes, start, place, count, partner):
    shape = partner.shape
    lane = lax.broadcasted_iota(jnp.int32, shape, 1)
    row = lax.broadcasted_iota(jnp.int32, shape, 0) + start
    first = (lane == 0) & (row == sizes.halo) & (place == 0)
    last = (lane == LANES - 1) & (row == sizes.halo + sizes.blocks - 1) & (place == count - 1)
    return first, last, partner == 0


def tendency(load, geo, walls, index, inside, diff_ref, lift_ref):
    speed_sq, rx, ry, sx, sy = geo[:5]
    outer_sq, waves, ghosts = geo[5:8], geo[8:11], geo[11:14]
    own = [[load(10 * field + node, 0) for node in range(10)] for field in range(3)]
    eta, mom_x, mom_y = own
    flow_r = [-(rx * mom_x[b] + ry * mom_y[b]) for b in range(10)]
    flow_s = [-(sx * mom_x[b] + sy * mom_y[b]) for b in range(10)]
    half_r = (0.5 * rx, 0.5 * ry)
    half_s = (0.5 * sx, 0.5 * sy)
    vectors = (
        (-half_s[0], -half_s[1]),
        (half_r[0] + half_s[0], half_r[1] + half_s[1]),
        (-half_r[0], -half_r[1]),
    )
    fetch = outer_values(load, index, inside)
    jumps = ([], [], [])
    for face in range(3):
        vec_x, vec_y = vectors[face]
        theirs = FACES[(1, 0, 2)[face]]
        wall = walls[face]
        for j in range(4):
            node, match = FACES[face][j], theirs[3 - j]
            in_eta, in_x, in_y = eta[node], mom_x[node], mom_y[node]
            ext_eta, ext_x, ext_y = [fetch[face](10 * field + match) for field in range(3)]
            bounce = (in_x * vec_x + in_y * vec_y) * ghosts[face]
            d_eta = jnp.where(wall, 0.0, in_eta - ext_eta)
            d_x = jnp.where(wall, bounce * vec_x, in_x - ext_x)
            d_y = jnp.where(wall, bounce * vec_y, in_y - ext_y)
            head = jnp.where(wall, 0.0, speed_sq * in_eta - outer_sq[face] * ext_eta)
            jumps[0].append(d_x * vec_x + d_y * vec_y - waves[face] * d_eta)
            jumps[1].append(head * vec_x - waves[face] * d_x)
            jumps[2].append(head * vec_y - waves[face] * d_y)
    pull = (-speed_sq * rx, -speed_sq * ry)
    push = (-speed_sq * sx, -speed_sq * sy)
    out = [[None] * 10 for _ in range(3)]
    for a in range(10):
        total = along_r = along_s = None
        for b in range(10):
            d_r, d_s = diff_ref[a, 0, b], diff_ref[a, 1, b]
            term = d_r * flow_r[b] + d_s * flow_s[b]
            total = term if b == 0 else total + term
            along_r = d_r * eta[b] if b == 0 else along_r + d_r * eta[b]
            along_s = d_s * eta[b] if b == 0 else along_s + d_s * eta[b]
        sums = [total, pull[0] * along_r + push[0] * along_s, pull[1] * along_r + push[1] * along_s]
        for q in range(12):
            weight = lift_ref[a, q]
            for field in range(3):
                sums[field] = sums[field] + weight * jumps[field][q]
        for field in range(3):
            out[field][a] = sums[field]
    return [out[field][a] for field in range(3) for a in range(10)]


def first_kernel(
    sizes, state_hbm, depth_hbm, metric_hbm, partner_hbm, refine_hbm, before_ref, after_ref, diff_hbm, lift_hbm,
    cur, rate_ref, geo_ref,
    state_ref, depth_ref, metric_ref, partner_ref, refine_ref, diff_ref, lift_ref,
    spread, wide, aux, sems,
):
    blocks, halo = sizes.blocks, sizes.halo
    top, bottom = PAD + halo, PAD + halo + blocks
    place = lax.axis_index(AXES)
    count = lax.axis_size(AXES)
    copies = fetch_all(
        (
            (metric_hbm, metric_ref),
            (state_hbm, state_ref),
            (depth_hbm, depth_ref),
            (partner_hbm, partner_ref),
            (refine_hbm, refine_ref),
            (diff_hbm, diff_ref),
            (lift_hbm, lift_ref),
        ),
        sems,
    )
    for copy in copies:
        copy.wait()
    metric = split_metric(metric_ref, spread, blocks)
    dense = [depth_ref[...], *metric, partner_ref[...].astype(jnp.float32), refine_ref[...].astype(jnp.float32)]
    pack_state(state_ref, wide, blocks)
    for num in range(7):
        at = 4 * num + 3
        aux[num, top - halo : top, :] = before_ref[pl.ds(at, halo, stride=PACK), :]
        aux[num, top:bottom, :] = dense[num]
        aux[num, bottom : bottom + halo, :] = after_ref[pl.ds(at, halo, stride=PACK), :]
    for field in range(3):
        for node in range(10):
            item = 10 * field + node
            at = 4 * node + field
            cur[item, top - halo : top, :] = before_ref[pl.ds(at, halo, stride=PACK), :]
            cur[item, top:bottom, :] = wide[pl.ds(at, blocks, stride=PACK), :]
            cur[item, bottom : bottom + halo, :] = after_ref[pl.ds(at, halo, stride=PACK), :]

    def step(group, carry):
        base = PAD + 8 * group

        def load_aux(item, shift):
            return aux[item, pl.ds(base + shift, 8), :]

        def load(item, shift):
            return cur[item, pl.ds(base + shift, 8), :]

        depth, rx, ry, sx, sy, partner, refine = [load_aux(num, 0) for num in range(7)]
        index, inside = pair_index(partner)
        fetch = outer_values(load_aux, index, inside)
        walls = wall_masks(sizes, 8 * group, place, count, partner)
        speed_sq = GRAVITY * depth
        outer_sq = [jnp.where(walls[k], speed_sq, GRAVITY * fetch[k](0)) for k in range(3)]
        faces = ((sx, sy), (rx + sx, ry + sy), (rx, ry))
        squares = [vx * vx + vy * vy for vx, vy in faces]
        waves = [
            0.5 * jnp.sqrt(squares[k]) * jnp.sqrt(jnp.maximum(speed_sq, outer_sq[k])) for k in range(3)
        ]
        ghosts = [8.0 / squares[k] for k in range(3)]
        geo = [speed_sq, rx, ry, sx, sy, *outer_sq, *waves, *ghosts]
        rates = tendency(load, geo, walls, index, inside, diff_ref, lift_ref)
        at = pl.ds(pl.multiple_of(8 * group, 8), 8)
        for num, value in enumerate([*geo, partner, refine]):
            geo_ref[num, at, :] = value
        for item in range(30):
            rate_ref[item, at, :] = rates[item]
        return carry

    lax.fori_loop(0, sizes.rows // 8, step, 0)


def child_matrix(prolong_ref):
    f32 = jnp.float32
    node_r = lax.broadcasted_iota(jnp.int32, (PACK, 10), 0) // 4
    spread_r = (node_r == lax.broadcasted_iota(jnp.int32, (PACK, 10), 1)).astype(f32)
    item_c = lax.broadcasted_iota(jnp.int32, (10, WIDE), 1)
    spread_c = (item_c % 10 == lax.broadcasted_iota(jnp.int32, (10, WIDE), 0)).astype(f32)
    row = lax.broadcasted_iota(jnp.int32, (PACK, WIDE), 0)
    col = lax.broadcasted_iota(jnp.int32, (PACK, WIDE), 1)
    same = row % 4 == col // 10
    parts = []
    for child in range(2):
        left = jnp.dot(spread_r, prolong_ref[:, child, :], precision=HIGH, preferred_element_type=f32)
        full = jnp.dot(left, spread_c, precision=HIGH, preferred_element_type=f32)
        parts.append(jnp.where(same, full, 0.0))
    parts.append((same & (row // 4 == col % 10)).astype(f32))
    whole = jnp.concatenate(parts, axis=0)
    rounded = whole.astype(jnp.bfloat16)
    rest = (whole - rounded.astype(f32)).astype(jnp.bfloat16)
    return jnp.concatenate([rounded, rounded, rounded, rest], axis=1)


def second_kernel(
    sizes, cur, rate_ref, geo_ref, stats_ref, diff_hbm, lift_hbm, prolong_hbm, out_hbm,
    diff_ref, lift_ref, prolong_ref, out_ref,
    first, ends_ref, place_v, place_s, wide, weights, gathered, index_ref, sems, out_sems, sem,
):
    slots, keep, rows = sizes.slots, sizes.keep, sizes.rows
    place = lax.axis_index(AXES)
    count = lax.axis_size(AXES)
    copies = fetch_all(
        ((prolong_hbm, prolong_ref), (diff_hbm, diff_ref), (lift_hbm, lift_ref)), sems
    )
    for item in (30, 31):
        wide[pl.ds(item, slots + 1, stride=WIDE), :] = jnp.zeros((slots + 1, LANES), jnp.float32)
    for copy in copies:
        copy.wait()
    weights[...] = child_matrix(prolong_ref)
    stats = stats_ref[...]
    lane_n = lax.broadcasted_iota(jnp.int32, stats.shape, 1)
    dev_n = lax.broadcasted_iota(jnp.int32, stats.shape, 0)
    rate = jnp.where(lane_n < LANES // 2, stats, 0.0)
    top = jnp.max(jnp.max(rate, axis=0, keepdims=True), axis=1, keepdims=True)
    gone = jnp.where((lane_n == LANES - 1) & (dev_n < place), stats, 0.0)
    earlier = jnp.sum(jnp.sum(gone, axis=0, keepdims=True), axis=1, keepdims=True)
    step = COURANT / top
    refine = geo_ref[15, keep : keep + slots, :]
    counts = (1.0 + refine).astype(jnp.bfloat16)
    row_i = lax.broadcasted_iota(jnp.int32, (LANES, LANES), 0)
    col_i = lax.broadcasted_iota(jnp.int32, (LANES, LANES), 1)
    upper = (row_i <= col_i).astype(jnp.bfloat16)
    within = jnp.dot(counts, upper, preferred_element_type=jnp.float32)
    whole = jnp.dot(counts, jnp.ones((LANES, LANES), jnp.bfloat16), preferred_element_type=jnp.float32)
    row_s = lax.broadcasted_iota(jnp.int32, (slots, slots), 0)
    col_s = lax.broadcasted_iota(jnp.int32, (slots, slots), 1)
    lower = (col_s < row_s).astype(jnp.bfloat16)
    before = jnp.dot(lower, whole.astype(jnp.bfloat16), preferred_element_type=jnp.float32)
    own = before[sizes.margin : sizes.margin + 1, :]
    start = earlier - (place * (sizes.cells // 2)).astype(jnp.float32)
    ends = within + before + (start - own)
    ends_ref[:slots, :] = 2.0 * ends + refine
    ends_ref[slots:, :] = jnp.full((8, LANES), 1e9, jnp.float32)
    full = before + whole + (start - own)
    first_slot = LANES * lax.broadcasted_iota(jnp.int32, (slots, LANES), 1).astype(jnp.float32)
    lead = jnp.sum((full <= first_slot).astype(jnp.float32), axis=0, keepdims=True)
    lead = jnp.clip(lead.astype(jnp.int32), 0, slots - 1)
    place_v[...] = jnp.broadcast_to(lead, (8, LANES))
    copy = pltpu.make_async_copy(place_v, place_s, sem)
    copy.start()

    for item in range(30):
        first[item, PAD : PAD + rows, :] = cur[item, PAD : PAD + rows, :] + step * rate_ref[item]

    def stage(group, carry):
        base = PAD + keep + 8 * group
        at = pl.ds(8 * group + keep, 8)

        def load(item, shift):
            return first[item, pl.ds(base + shift, 8), :]

        geo = [geo_ref[num, at, :] for num in range(14)]
        partner = geo_ref[14, at, :]
        index, inside = pair_index(partner)
        walls = wall_masks(sizes, 8 * group + keep, place, count, partner)
        rates = tendency(load, geo, walls, index, inside, diff_ref, lift_ref)
        lead_row = 8 * WIDE * group
        for field in range(3):
            for node in range(10):
                item = 10 * field + node
                old = cur[item, pl.ds(base, 8), :]
                new = 0.5 * old + 0.5 * (load(item, 0) + step * rates[item])
                wide[pl.ds(lead_row + item, 8, stride=WIDE), :] = new
        return carry

    lax.fori_loop(0, slots // 8, stage, 0)

    copy.wait()
    for slot in range(slots):
        lead_at = place_s[0, slot]
        index_ref[0, slot : slot + 1, :] = ends_ref[pl.ds(lead_at, 1), :]
        index_ref[1, slot : slot + 1, :] = ends_ref[pl.ds(lead_at + 1, 1), :]
    near, far = index_ref[0], index_ref[1]
    slot_no = LANES * lax.broadcasted_iota(jnp.int32, (slots, LANES), 0) + lax.broadcasted_iota(
        jnp.int32, (slots, LANES), 1
    )
    goal = (2 * slot_no + 1).astype(jnp.float32)
    beyond = jnp.broadcast_to(near[:, LANES - 1 :], (slots, LANES)) <= goal

    def pick(index):
        return jnp.where(beyond, lane_gather(far, index), lane_gather(near, index))

    found = jnp.zeros((slots, LANES), jnp.int32)
    size = LANES // 2
    while size:
        passed = pick(found + (size - 1)) <= goal
        found = jnp.where(passed, found + size, found)
        size //= 2
    mine = pick(found).astype(jnp.int32)
    split = mine & 1
    begin = (mine >> 1) - 1 - split
    kind = split * (1 + slot_no - begin)
    index_ref[0] = found.astype(jnp.float32)
    index_ref[1] = kind.astype(jnp.float32)
    index_ref[2] = beyond.astype(jnp.float32)
    for slot in range(slots):
        lead_at = place_s[0, slot] * WIDE
        lane_idx = jnp.broadcast_to(index_ref[0, slot : slot + 1, :], (WIDE, LANES)).astype(jnp.int32)
        passed = jnp.broadcast_to(index_ref[2, slot : slot + 1, :], (WIDE, LANES)) > 0.5
        one = wide[pl.ds(pl.multiple_of(lead_at, WIDE), WIDE), :]
        two = wide[pl.ds(pl.multiple_of(lead_at + WIDE, WIDE), WIDE), :]
        gathered[:, LANES * slot : LANES * (slot + 1)] = jnp.where(
            passed, lane_gather(two, lane_idx), lane_gather(one, lane_idx)
        )
    matrix = weights[...]
    chunk = 8 * LANES
    results = []
    for part in range(slots // 8):
        span = slice(chunk * part, chunk * (part + 1))
        values = gathered[:, span]
        high = values.astype(jnp.bfloat16)
        rest = values - high.astype(jnp.float32)
        low = rest.astype(jnp.bfloat16)
        last = (rest - low.astype(jnp.float32)).astype(jnp.bfloat16)
        stack = jnp.concatenate([high, low, last, high], axis=0)
        children = jnp.dot(matrix, stack, preferred_element_type=jnp.float32)
        for sub in range(8):
            slot = 8 * part + sub
            cut = slice(LANES * sub, LANES * (sub + 1))
            tag = jnp.broadcast_to(index_ref[1, slot : slot + 1, :], (PACK, LANES))
            value = jnp.where(
                tag < 0.5,
                children[2 * PACK :, cut],
                jnp.where(tag < 1.5, children[:PACK, cut], children[PACK : 2 * PACK, cut]),
            )
            for node in range(10):
                out_ref[node, :, LANES * slot : LANES * (slot + 1)] = value[4 * node : 4 * node + 3]
        result = pltpu.make_async_copy(out_ref.at[:, :, span], out_hbm.at[:, :, span], out_sems.at[part])
        result.start()
        results.append(result)
    for result in results:
        result.wait()


def shards(state, depth, metric, partner, refine, diff_ops, lift, prolong):
    sizes = Sizes(state.shape[2])
    count = lax.axis_size(AXES)
    blocks, rows, slots, halo = sizes.blocks, sizes.rows, sizes.slots, sizes.halo
    depth, partner, refine = [x.reshape(blocks, LANES) for x in (depth, partner, refine)]
    state, diff_ops, prolong = [jnp.transpose(x, (1, 0, 2)) for x in (state, diff_ops, prolong)]
    state, depth, metric, partner, refine, diff_ops, lift, prolong = [
        pltpu.with_memory_space_constraint(x, pltpu.HBM)
        for x in (state, depth, metric, partner, refine, diff_ops, lift, prolong)
    ]
    f32, i32 = jnp.float32, jnp.int32
    packed = jax.ShapeDtypeStruct((PACK * halo, LANES), f32)
    dense = [
        pltpu.VMEM((blocks, LANES), f32),
        pltpu.VMEM(metric.shape, f32),
        pltpu.VMEM((blocks, LANES), i32),
        pltpu.VMEM((blocks, LANES), i32),
    ]
    stats, head, tail = pl.pallas_call(
        functools.partial(pack_kernel, sizes),
        name="pack",
        out_shape=(jax.ShapeDtypeStruct((count, LANES), f32), packed, packed),
        in_specs=[HBM] * 5,
        out_specs=(VMEM,) * 3,
        scratch_shapes=[
            pltpu.VMEM((10, 3, LANES * halo), f32),
            pltpu.VMEM((10, 3, LANES * halo), f32),
            *dense,
            pltpu.VMEM((8 * blocks, LANES), f32),
            pltpu.SemaphoreType.DMA((6,)),
        ],
        compiler_params=PARAMS,
    )(state, depth, metric, partner, refine)
    before = lax.ppermute(tail, AXES, [(i, i + 1) for i in range(count - 1)])
    after = lax.ppermute(head, AXES, [(i + 1, i) for i in range(count - 1)])
    stats = lax.all_to_all(stats, AXES, 0, 0, tiled=True)
    before, after, stats = [
        pltpu.with_memory_space_constraint(x, pltpu.VMEM) for x in (before, after, stats)
    ]
    operators = [pltpu.SMEM(diff_ops.shape, f32), pltpu.SMEM(lift.shape, f32)]
    cur, rates, geo = pl.pallas_call(
        functools.partial(first_kernel, sizes),
        name="first_stage",
        out_shape=(
            jax.ShapeDtypeStruct((30, sizes.tall, LANES), f32),
            jax.ShapeDtypeStruct((30, rows, LANES), f32),
            jax.ShapeDtypeStruct((16, rows, LANES), f32),
        ),
        in_specs=[HBM] * 5 + [VMEM] * 2 + [HBM] * 2,
        out_specs=(VMEM,) * 3,
        scratch_shapes=[
            pltpu.VMEM(state.shape, f32),
            *dense,
            *operators,
            pltpu.VMEM((8 * blocks, LANES), f32),
            pltpu.VMEM((PACK * blocks, LANES), f32),
            pltpu.VMEM((7, sizes.tall, LANES), f32),
            pltpu.SemaphoreType.DMA((7,)),
        ],
        compiler_params=PARAMS,
    )(state, depth, metric, partner, refine, before, after, diff_ops, lift)
    refined = pl.pallas_call(
        functools.partial(second_kernel, sizes),
        name="second_stage_refine",
        out_shape=jax.ShapeDtypeStruct((10, 3, LANES * slots), f32),
        in_specs=[VMEM] * 4 + [HBM] * 3,
        out_specs=HBM,
        scratch_shapes=[
            *operators,
            pltpu.VMEM(prolong.shape, f32),
            pltpu.VMEM((10, 3, LANES * slots), f32),
            pltpu.VMEM((30, sizes.tall, LANES), f32),
            pltpu.VMEM((slots + 8, LANES), f32),
            pltpu.VMEM((8, LANES), i32),
            pltpu.SMEM((8, LANES), i32),
            pltpu.VMEM((WIDE * (slots + 1), LANES), f32),
            pltpu.VMEM((3 * PACK, 4 * WIDE), jnp.bfloat16),
            pltpu.VMEM((WIDE, LANES * slots), f32),
            pltpu.VMEM((3, slots, LANES), f32),
            pltpu.SemaphoreType.DMA((3,)),
            pltpu.SemaphoreType.DMA((slots // 8,)),
            pltpu.SemaphoreType.DMA,
        ],
        compiler_params=PARAMS,
    )(cur, rates, geo, stats, diff_ops, lift, prolong)
    return jnp.transpose(refined, (1, 0, 2))


def solution(mesh):
    return jax.shard_map(
        shards,
        mesh=mesh,
        in_specs=(
            P(None, None, AXES),
            P(AXES),
            P(None, AXES),
            P(AXES),
            P(AXES),
            P(),
            P(),
            P(),
        ),
        out_specs=P(None, None, AXES),
        check_vma=False,
    )
```

```python
import functools

import jax
import jax.numpy as jnp
from jax import lax
from jax.experimental import pallas as pl
from jax.experimental.pallas import tpu as pltpu
from jax.sharding import PartitionSpec as P

GRAVITY = 9.81
COURANT = 0.5
HIGH = lax.Precision.HIGHEST
LANES = 128
AXES = ("row", "col")
FACES = ((0, 1, 2, 3), (3, 6, 8, 9), (9, 7, 4, 0))
PACK = 40
WIDE = 32
PAD = 8

VMEM = pl.BlockSpec(memory_space=pltpu.VMEM)
HBM = pl.BlockSpec(memory_space=pltpu.HBM)
PARAMS = pltpu.CompilerParams(vmem_limit_bytes=48 * 1024 * 1024)


class Sizes:
    def __init__(self, cells):
        self.cells = cells
        self.blocks = cells // LANES
        self.margin = cells // 4 // LANES
        self.halo = self.margin + 1
        self.rows = -(-(self.blocks + 2 * self.halo) // 8) * 8
        self.tall = self.rows + 2 * PAD
        self.slots = 3 * self.blocks // 2
        self.keep = self.halo - self.margin


def fetch_all(pairs, sems):
    copies = [pltpu.make_async_copy(src, dst, sems.at[num]) for num, (src, dst) in enumerate(pairs)]
    for copy in copies:
        copy.start()
    return copies


def split_metric(metric_ref, spread, blocks):
    for block in range(blocks):
        spread[8 * block : 8 * block + 4, :] = metric_ref[:, LANES * block : LANES * (block + 1)]
    return [spread[pl.ds(comp, blocks, stride=8), :] for comp in range(4)]


def pack_kernel(
    sizes, state_hbm, depth_hbm, metric_hbm, partner_hbm, refine_hbm, stats_ref, even_ref, odd_ref,
    state_even, state_odd, depth_ref, metric_ref, partner_ref, refine_ref, spread, sems,
):
    blocks, halo = sizes.blocks, sizes.halo
    wide = LANES * halo
    late = blocks - halo
    even = (lax.axis_index(AXES) + 1) % 2 * late
    odd = late - even
    copies = fetch_all(
        (
            (depth_hbm, depth_ref),
            (metric_hbm, metric_ref),
            (refine_hbm, refine_ref),
            (partner_hbm, partner_ref),
            (state_hbm.at[:, :, pl.ds(pl.multiple_of(LANES * even, LANES), wide)], state_even),
            (state_hbm.at[:, :, pl.ds(pl.multiple_of(LANES * odd, LANES), wide)], state_odd),
        ),
        sems,
    )
    for copy in copies:
        copy.wait()
    rx, ry, sx, sy = split_metric(metric_ref, spread, blocks)
    depth = depth_ref[...]
    refine = refine_ref[...].astype(jnp.float32)
    faces = ((sx, sy), (rx + sx, ry + sy), (rx, ry))
    lengths = [jnp.sqrt(vx * vx + vy * vy) for vx, vy in faces]
    rate = jnp.sqrt(GRAVITY * depth) * jnp.maximum(jnp.maximum(lengths[0], lengths[1]), lengths[2])
    top = jnp.max(jnp.max(rate, axis=0, keepdims=True), axis=1, keepdims=True)
    extra = jnp.sum(jnp.sum(refine, axis=0, keepdims=True), axis=1, keepdims=True)
    shape = stats_ref.shape
    lane = lax.broadcasted_iota(jnp.int32, shape, 1)
    stats_ref[...] = jnp.where(
        lane < LANES // 2, jnp.broadcast_to(top, shape), jnp.broadcast_to(extra, shape)
    )
    for ref, source, start in ((even_ref, state_even, even), (odd_ref, state_odd, odd)):
        pack_state(source, ref, halo)
        at = pl.ds(start, halo)
        dense = [depth_ref[at, :]]
        dense += [spread[pl.ds(8 * start + comp, halo, stride=8), :] for comp in range(4)]
        dense += [partner_ref[at, :].astype(jnp.float32), refine_ref[at, :].astype(jnp.float32)]
        for num, value in enumerate(dense):
            ref[pl.ds(4 * num + 3, halo, stride=PACK), :] = value


def pack_state(source, target, blocks):
    for block in range(blocks):
        for node in range(10):
            at = PACK * block + 4 * node
            target[at : at + 3, :] = source[node, :, LANES * block : LANES * (block + 1)]


def pair_index(partner):
    lane = lax.broadcasted_iota(jnp.int32, partner.shape, 1)
    target = lane + partner.astype(jnp.int32)
    return target & (LANES - 1), (target >= 0) & (target < LANES)


def lane_gather(values, index):
    return jnp.take_along_axis(values, index, axis=1, mode="promise_in_bounds")


def outer_values(load, index, inside):
    shape = index.shape
    lane = lax.broadcasted_iota(jnp.int32, shape, 1)

    def prev(item):
        return pltpu.roll(jnp.where(lane == LANES - 1, load(item, -1), load(item, 0)), 1, 1)

    def after(item):
        return pltpu.roll(jnp.where(lane == 0, load(item, 1), load(item, 0)), LANES - 1, 1)

    def across(item):
        other = jnp.where(lane < LANES // 2, load(item, 1), load(item, -1))
        return jnp.where(inside, lane_gather(load(item, 0), index), lane_gather(other, index))

    return prev, after, across


def wall_masks(sizes, start, place, count, partner):
    shape = partner.shape
    lane = lax.broadcasted_iota(jnp.int32, shape, 1)
    row = lax.broadcasted_iota(jnp.int32, shape, 0) + start
    first = (lane == 0) & (row == sizes.halo) & (place == 0)
    last = (lane == LANES - 1) & (row == sizes.halo + sizes.blocks - 1) & (place == count - 1)
    return first, last, partner == 0


def tendency(load, geo, walls, index, inside, diff_ref, lift_ref):
    speed_sq, rx, ry, sx, sy = geo[:5]
    outer_sq, waves, ghosts = geo[5:8], geo[8:11], geo[11:14]
    own = [[load(10 * field + node, 0) for node in range(10)] for field in range(3)]
    eta, mom_x, mom_y = own
    flow_r = [-(rx * mom_x[b] + ry * mom_y[b]) for b in range(10)]
    flow_s = [-(sx * mom_x[b] + sy * mom_y[b]) for b in range(10)]
    half_r = (0.5 * rx, 0.5 * ry)
    half_s = (0.5 * sx, 0.5 * sy)
    vectors = (
        (-half_s[0], -half_s[1]),
        (half_r[0] + half_s[0], half_r[1] + half_s[1]),
        (-half_r[0], -half_r[1]),
    )
    fetch = outer_values(load, index, inside)
    jumps = ([], [], [])
    for face in range(3):
        vec_x, vec_y = vectors[face]
        theirs = FACES[(1, 0, 2)[face]]
        wall = walls[face]
        for j in range(4):
            node, match = FACES[face][j], theirs[3 - j]
            in_eta, in_x, in_y = eta[node], mom_x[node], mom_y[node]
            ext_eta, ext_x, ext_y = [fetch[face](10 * field + match) for field in range(3)]
            bounce = (in_x * vec_x + in_y * vec_y) * ghosts[face]
            d_eta = jnp.where(wall, 0.0, in_eta - ext_eta)
            d_x = jnp.where(wall, bounce * vec_x, in_x - ext_x)
            d_y = jnp.where(wall, bounce * vec_y, in_y - ext_y)
            head = jnp.where(wall, 0.0, speed_sq * in_eta - outer_sq[face] * ext_eta)
            jumps[0].append(d_x * vec_x + d_y * vec_y - waves[face] * d_eta)
            jumps[1].append(head * vec_x - waves[face] * d_x)
            jumps[2].append(head * vec_y - waves[face] * d_y)
    pull = (-speed_sq * rx, -speed_sq * ry)
    push = (-speed_sq * sx, -speed_sq * sy)
    out = [[None] * 10 for _ in range(3)]
    for a in range(10):
        total = along_r = along_s = None
        for b in range(10):
            d_r, d_s = diff_ref[a, 0, b], diff_ref[a, 1, b]
            term = d_r * flow_r[b] + d_s * flow_s[b]
            total = term if b == 0 else total + term
            along_r = d_r * eta[b] if b == 0 else along_r + d_r * eta[b]
            along_s = d_s * eta[b] if b == 0 else along_s + d_s * eta[b]
        sums = [total, pull[0] * along_r + push[0] * along_s, pull[1] * along_r + push[1] * along_s]
        for q in range(12):
            weight = lift_ref[a, q]
            for field in range(3):
                sums[field] = sums[field] + weight * jumps[field][q]
        for field in range(3):
            out[field][a] = sums[field]
    return [out[field][a] for field in range(3) for a in range(10)]


def first_kernel(
    sizes, state_hbm, depth_hbm, metric_hbm, partner_hbm, refine_hbm, even_ref, odd_ref, diff_hbm, lift_hbm,
    cur, rate_ref, geo_ref,
    state_ref, depth_ref, metric_ref, partner_ref, refine_ref, diff_ref, lift_ref,
    spread, wide, aux, sems,
):
    blocks, halo = sizes.blocks, sizes.halo
    top, bottom = PAD + halo, PAD + halo + blocks
    place = lax.axis_index(AXES)
    count = lax.axis_size(AXES)
    copies = fetch_all(
        (
            (metric_hbm, metric_ref),
            (state_hbm, state_ref),
            (depth_hbm, depth_ref),
            (partner_hbm, partner_ref),
            (refine_hbm, refine_ref),
            (diff_hbm, diff_ref),
            (lift_hbm, lift_ref),
        ),
        sems,
    )
    for copy in copies:
        copy.wait()
    metric = split_metric(metric_ref, spread, blocks)
    dense = [depth_ref[...], *metric, partner_ref[...].astype(jnp.float32), refine_ref[...].astype(jnp.float32)]
    pack_state(state_ref, wide, blocks)
    even = place % 2 == 0

    def set_halo(target, num, row):
        by_even = even_ref[pl.ds(row, halo, stride=PACK), :]
        by_odd = odd_ref[pl.ds(row, halo, stride=PACK), :]
        target[num, top - halo : top, :] = jnp.where(even, by_odd, by_even)
        target[num, bottom : bottom + halo, :] = jnp.where(even, by_even, by_odd)

    for num in range(7):
        set_halo(aux, num, 4 * num + 3)
        aux[num, top:bottom, :] = dense[num]
    for field in range(3):
        for node in range(10):
            item = 10 * field + node
            set_halo(cur, item, 4 * node + field)
            cur[item, top:bottom, :] = wide[pl.ds(4 * node + field, blocks, stride=PACK), :]

    def step(group, carry):
        base = PAD + 8 * group

        def load_aux(item, shift):
            return aux[item, pl.ds(base + shift, 8), :]

        def load(item, shift):
            return cur[item, pl.ds(base + shift, 8), :]

        depth, rx, ry, sx, sy, partner, refine = [load_aux(num, 0) for num in range(7)]
        index, inside = pair_index(partner)
        fetch = outer_values(load_aux, index, inside)
        walls = wall_masks(sizes, 8 * group, place, count, partner)
        speed_sq = GRAVITY * depth
        outer_sq = [jnp.where(walls[k], speed_sq, GRAVITY * fetch[k](0)) for k in range(3)]
        faces = ((sx, sy), (rx + sx, ry + sy), (rx, ry))
        squares = [vx * vx + vy * vy for vx, vy in faces]
        waves = [
            0.5 * jnp.sqrt(squares[k]) * jnp.sqrt(jnp.maximum(speed_sq, outer_sq[k])) for k in range(3)
        ]
        ghosts = [8.0 / squares[k] for k in range(3)]
        geo = [speed_sq, rx, ry, sx, sy, *outer_sq, *waves, *ghosts]
        rates = tendency(load, geo, walls, index, inside, diff_ref, lift_ref)
        at = pl.ds(pl.multiple_of(8 * group, 8), 8)
        for num, value in enumerate([*geo, partner, refine]):
            geo_ref[num, at, :] = value
        for item in range(30):
            rate_ref[item, at, :] = rates[item]
        return carry

    lax.fori_loop(0, sizes.rows // 8, step, 0)


def child_matrix(prolong_ref):
    f32 = jnp.float32
    node_r = lax.broadcasted_iota(jnp.int32, (PACK, 10), 0) // 4
    spread_r = (node_r == lax.broadcasted_iota(jnp.int32, (PACK, 10), 1)).astype(f32)
    item_c = lax.broadcasted_iota(jnp.int32, (10, WIDE), 1)
    spread_c = (item_c % 10 == lax.broadcasted_iota(jnp.int32, (10, WIDE), 0)).astype(f32)
    row = lax.broadcasted_iota(jnp.int32, (PACK, WIDE), 0)
    col = lax.broadcasted_iota(jnp.int32, (PACK, WIDE), 1)
    same = row % 4 == col // 10
    parts = []
    for child in range(2):
        left = jnp.dot(spread_r, prolong_ref[:, child, :], precision=HIGH, preferred_element_type=f32)
        full = jnp.dot(left, spread_c, precision=HIGH, preferred_element_type=f32)
        parts.append(jnp.where(same, full, 0.0))
    parts.append((same & (row // 4 == col % 10)).astype(f32))
    whole = jnp.concatenate(parts, axis=0)
    rounded = whole.astype(jnp.bfloat16)
    rest = (whole - rounded.astype(f32)).astype(jnp.bfloat16)
    return jnp.concatenate([rounded, rounded, rounded, rest], axis=1)


def second_kernel(
    sizes, cur, rate_ref, geo_ref, stats_hbm, diff_hbm, lift_hbm, prolong_hbm, out_hbm,
    stats_ref, diff_ref, lift_ref, prolong_ref, out_ref,
    first, ends_ref, place_v, place_s, wide, weights, gathered, index_ref, sems, out_sems, sem,
):
    slots, keep, rows = sizes.slots, sizes.keep, sizes.rows
    place = lax.axis_index(AXES)
    count = lax.axis_size(AXES)
    copies = fetch_all(
        ((prolong_hbm, prolong_ref), (stats_hbm, stats_ref), (diff_hbm, diff_ref), (lift_hbm, lift_ref)), sems
    )
    for item in (30, 31):
        wide[pl.ds(item, slots + 1, stride=WIDE), :] = jnp.zeros((slots + 1, LANES), jnp.float32)
    copies[0].wait()
    weights[...] = child_matrix(prolong_ref)
    for copy in copies[1:]:
        copy.wait()
    stats = stats_ref[...]
    lane_n = lax.broadcasted_iota(jnp.int32, stats.shape, 1)
    row_n = lax.broadcasted_iota(jnp.int32, stats.shape, 0)
    rate = jnp.where(lane_n < LANES // 2, stats, 0.0)
    top = jnp.max(jnp.max(rate, axis=0, keepdims=True), axis=1, keepdims=True)
    gone = jnp.where((lane_n == LANES - 1) & (row_n % 8 == 0) & (row_n < 8 * place), stats, 0.0)
    earlier = jnp.sum(jnp.sum(gone, axis=0, keepdims=True), axis=1, keepdims=True)
    step = COURANT / top
    refine = geo_ref[15, keep : keep + slots, :]
    counts = (1.0 + refine).astype(jnp.bfloat16)
    row_i = lax.broadcasted_iota(jnp.int32, (LANES, LANES), 0)
    col_i = lax.broadcasted_iota(jnp.int32, (LANES, LANES), 1)
    upper = (row_i <= col_i).astype(jnp.bfloat16)
    within = jnp.dot(counts, upper, preferred_element_type=jnp.float32)
    whole = jnp.dot(counts, jnp.ones((LANES, LANES), jnp.bfloat16), preferred_element_type=jnp.float32)
    row_s = lax.broadcasted_iota(jnp.int32, (slots, slots), 0)
    col_s = lax.broadcasted_iota(jnp.int32, (slots, slots), 1)
    lower = (col_s < row_s).astype(jnp.bfloat16)
    before = jnp.dot(lower, whole.astype(jnp.bfloat16), preferred_element_type=jnp.float32)
    own = before[sizes.margin : sizes.margin + 1, :]
    start = earlier - (place * (sizes.cells // 2)).astype(jnp.float32)
    ends = within + before + (start - own)
    ends_ref[:slots, :] = 2.0 * ends + refine
    ends_ref[slots:, :] = jnp.full((8, LANES), 1e9, jnp.float32)
    full = before + whole + (start - own)
    first_slot = LANES * lax.broadcasted_iota(jnp.int32, (slots, LANES), 1).astype(jnp.float32)
    lead = jnp.sum((full <= first_slot).astype(jnp.float32), axis=0, keepdims=True)
    lead = jnp.clip(lead.astype(jnp.int32), 0, slots - 1)
    place_v[...] = jnp.broadcast_to(lead, (8, LANES))
    copy = pltpu.make_async_copy(place_v, place_s, sem)
    copy.start()

    for item in range(30):
        first[item, PAD : PAD + rows, :] = cur[item, PAD : PAD + rows, :] + step * rate_ref[item]

    def stage(group, carry):
        base = PAD + keep + 8 * group
        at = pl.ds(8 * group + keep, 8)

        def load(item, shift):
            return first[item, pl.ds(base + shift, 8), :]

        geo = [geo_ref[num, at, :] for num in range(14)]
        partner = geo_ref[14, at, :]
        index, inside = pair_index(partner)
        walls = wall_masks(sizes, 8 * group + keep, place, count, partner)
        rates = tendency(load, geo, walls, index, inside, diff_ref, lift_ref)
        lead_row = 8 * WIDE * group
        for field in range(3):
            for node in range(10):
                item = 10 * field + node
                old = cur[item, pl.ds(base, 8), :]
                new = 0.5 * old + 0.5 * (load(item, 0) + step * rates[item])
                wide[pl.ds(lead_row + item, 8, stride=WIDE), :] = new
        return carry

    lax.fori_loop(0, slots // 8, stage, 0)

    copy.wait()
    for slot in range(slots):
        lead_at = place_s[0, slot]
        index_ref[0, slot : slot + 1, :] = ends_ref[pl.ds(lead_at, 1), :]
        index_ref[1, slot : slot + 1, :] = ends_ref[pl.ds(lead_at + 1, 1), :]
    near, far = index_ref[0], index_ref[1]
    slot_no = LANES * lax.broadcasted_iota(jnp.int32, (slots, LANES), 0) + lax.broadcasted_iota(
        jnp.int32, (slots, LANES), 1
    )
    goal = (2 * slot_no + 1).astype(jnp.float32)
    beyond = jnp.broadcast_to(near[:, LANES - 1 :], (slots, LANES)) <= goal

    def pick(index):
        return jnp.where(beyond, lane_gather(far, index), lane_gather(near, index))

    found = jnp.zeros((slots, LANES), jnp.int32)
    size = LANES // 2
    while size:
        passed = pick(found + (size - 1)) <= goal
        found = jnp.where(passed, found + size, found)
        size //= 2
    mine = pick(found).astype(jnp.int32)
    split = mine & 1
    begin = (mine >> 1) - 1 - split
    kind = split * (1 + slot_no - begin)
    index_ref[0] = found.astype(jnp.float32)
    index_ref[1] = kind.astype(jnp.float32)
    index_ref[2] = beyond.astype(jnp.float32)
    for slot in range(slots):
        lead_at = place_s[0, slot] * WIDE
        lane_idx = jnp.broadcast_to(index_ref[0, slot : slot + 1, :], (WIDE, LANES)).astype(jnp.int32)
        passed = jnp.broadcast_to(index_ref[2, slot : slot + 1, :], (WIDE, LANES)) > 0.5
        one = wide[pl.ds(pl.multiple_of(lead_at, WIDE), WIDE), :]
        two = wide[pl.ds(pl.multiple_of(lead_at + WIDE, WIDE), WIDE), :]
        gathered[:, LANES * slot : LANES * (slot + 1)] = jnp.where(
            passed, lane_gather(two, lane_idx), lane_gather(one, lane_idx)
        )
    matrix = weights[...]
    chunk = 8 * LANES
    results = []
    for part in range(slots // 8):
        span = slice(chunk * part, chunk * (part + 1))
        values = gathered[:, span]
        high = values.astype(jnp.bfloat16)
        rest = values - high.astype(jnp.float32)
        low = rest.astype(jnp.bfloat16)
        last = (rest - low.astype(jnp.float32)).astype(jnp.bfloat16)
        stack = jnp.concatenate([high, low, last, high], axis=0)
        children = jnp.dot(matrix, stack, preferred_element_type=jnp.float32)
        for sub in range(8):
            slot = 8 * part + sub
            cut = slice(LANES * sub, LANES * (sub + 1))
            tag = jnp.broadcast_to(index_ref[1, slot : slot + 1, :], (PACK, LANES))
            value = jnp.where(
                tag < 0.5,
                children[2 * PACK :, cut],
                jnp.where(tag < 1.5, children[:PACK, cut], children[PACK : 2 * PACK, cut]),
            )
            for node in range(10):
                out_ref[node, :, LANES * slot : LANES * (slot + 1)] = value[4 * node : 4 * node + 3]
        result = pltpu.make_async_copy(out_ref.at[:, :, span], out_hbm.at[:, :, span], out_sems.at[part])
        result.start()
        results.append(result)
    for result in results:
        result.wait()


def swaps(start, count):
    pairs = [(i, i + 1) for i in range(start, count - 1, 2)]
    return pairs + [(j, i) for i, j in pairs]


def shards(state, depth, metric, partner, refine, diff_ops, lift, prolong):
    sizes = Sizes(state.shape[2])
    count = lax.axis_size(AXES)
    blocks, rows, slots, halo = sizes.blocks, sizes.rows, sizes.slots, sizes.halo
    depth, partner, refine = [x.reshape(blocks, LANES) for x in (depth, partner, refine)]
    state, diff_ops, prolong = [jnp.transpose(x, (1, 0, 2)) for x in (state, diff_ops, prolong)]
    state, depth, metric, partner, refine, diff_ops, lift, prolong = [
        pltpu.with_memory_space_constraint(x, pltpu.HBM)
        for x in (state, depth, metric, partner, refine, diff_ops, lift, prolong)
    ]
    f32, i32 = jnp.float32, jnp.int32
    packed = jax.ShapeDtypeStruct((PACK * halo, LANES), f32)
    dense = [
        pltpu.VMEM((blocks, LANES), f32),
        pltpu.VMEM(metric.shape, f32),
        pltpu.VMEM((blocks, LANES), i32),
        pltpu.VMEM((blocks, LANES), i32),
    ]
    stats, even, odd = pl.pallas_call(
        functools.partial(pack_kernel, sizes),
        name="pack",
        out_shape=(jax.ShapeDtypeStruct((8, LANES), f32), packed, packed),
        in_specs=[HBM] * 5,
        out_specs=(VMEM,) * 3,
        scratch_shapes=[
            pltpu.VMEM((10, 3, LANES * halo), f32),
            pltpu.VMEM((10, 3, LANES * halo), f32),
            *dense,
            pltpu.VMEM((8 * blocks, LANES), f32),
            pltpu.SemaphoreType.DMA((6,)),
        ],
        compiler_params=PARAMS,
    )(state, depth, metric, partner, refine)
    stats = lax.all_gather(stats, AXES, tiled=True)
    even = lax.ppermute(even, AXES, swaps(0, count))
    odd = lax.ppermute(odd, AXES, swaps(1, count))
    even, odd = [pltpu.with_memory_space_constraint(x, pltpu.VMEM) for x in (even, odd)]
    stats = pltpu.with_memory_space_constraint(stats, pltpu.HBM)
    operators = [pltpu.SMEM(diff_ops.shape, f32), pltpu.SMEM(lift.shape, f32)]
    cur, rates, geo = pl.pallas_call(
        functools.partial(first_kernel, sizes),
        name="first_stage",
        out_shape=(
            jax.ShapeDtypeStruct((30, sizes.tall, LANES), f32),
            jax.ShapeDtypeStruct((30, rows, LANES), f32),
            jax.ShapeDtypeStruct((16, rows, LANES), f32),
        ),
        in_specs=[HBM] * 5 + [VMEM] * 2 + [HBM] * 2,
        out_specs=(VMEM,) * 3,
        scratch_shapes=[
            pltpu.VMEM(state.shape, f32),
            *dense,
            *operators,
            pltpu.VMEM((8 * blocks, LANES), f32),
            pltpu.VMEM((PACK * blocks, LANES), f32),
            pltpu.VMEM((7, sizes.tall, LANES), f32),
            pltpu.SemaphoreType.DMA((7,)),
        ],
        compiler_params=PARAMS,
    )(state, depth, metric, partner, refine, even, odd, diff_ops, lift)
    refined = pl.pallas_call(
        functools.partial(second_kernel, sizes),
        name="second_stage_refine",
        out_shape=jax.ShapeDtypeStruct((10, 3, LANES * slots), f32),
        in_specs=[VMEM] * 3 + [HBM] * 4,
        out_specs=HBM,
        scratch_shapes=[
            pltpu.VMEM(stats.shape, f32),
            *operators,
            pltpu.VMEM(prolong.shape, f32),
            pltpu.VMEM((10, 3, LANES * slots), f32),
            pltpu.VMEM((30, sizes.tall, LANES), f32),
            pltpu.VMEM((slots + 8, LANES), f32),
            pltpu.VMEM((8, LANES), i32),
            pltpu.SMEM((8, LANES), i32),
            pltpu.VMEM((WIDE * (slots + 1), LANES), f32),
            pltpu.VMEM((3 * PACK, 4 * WIDE), jnp.bfloat16),
            pltpu.VMEM((WIDE, LANES * slots), f32),
            pltpu.VMEM((3, slots, LANES), f32),
            pltpu.SemaphoreType.DMA((4,)),
            pltpu.SemaphoreType.DMA((slots // 8,)),
            pltpu.SemaphoreType.DMA,
        ],
        compiler_params=PARAMS,
    )(cur, rates, geo, stats, diff_ops, lift, prolong)
    return jnp.transpose(refined, (1, 0, 2))


def solution(mesh):
    return jax.shard_map(
        shards,
        mesh=mesh,
        in_specs=(
            P(None, None, AXES),
            P(AXES),
            P(None, AXES),
            P(AXES),
            P(AXES),
            P(),
            P(),
            P(),
        ),
        out_specs=P(None, None, AXES),
        check_vma=False,
    )
```

```python
import functools

import jax
import jax.numpy as jnp
from jax import lax
from jax.experimental import pallas as pl
from jax.experimental.pallas import tpu as pltpu
from jax.sharding import PartitionSpec as P

GRAVITY = 9.81
COURANT = 0.5
HIGH = lax.Precision.HIGHEST
LANES = 128
AXES = ("row", "col")
FACES = ((0, 1, 2, 3), (3, 6, 8, 9), (9, 7, 4, 0))
PACK = 40
WIDE = 32
PAD = 8

VMEM = pl.BlockSpec(memory_space=pltpu.VMEM)
HBM = pl.BlockSpec(memory_space=pltpu.HBM)
PARAMS = pltpu.CompilerParams(vmem_limit_bytes=48 * 1024 * 1024)


class Sizes:
    def __init__(self, cells):
        self.cells = cells
        self.blocks = cells // LANES
        self.margin = cells // 4 // LANES
        self.halo = self.margin + 1
        self.rows = -(-(self.blocks + 2 * self.halo) // 8) * 8
        self.tall = self.rows + 2 * PAD
        self.slots = 3 * self.blocks // 2
        self.keep = self.halo - self.margin


def fetch_all(pairs, sems):
    copies = [pltpu.make_async_copy(src, dst, sems.at[num]) for num, (src, dst) in enumerate(pairs)]
    for copy in copies:
        copy.start()
    return copies


def split_metric(metric_ref, spread, blocks):
    for block in range(blocks):
        spread[8 * block : 8 * block + 4, :] = metric_ref[:, LANES * block : LANES * (block + 1)]
    return [spread[pl.ds(comp, blocks, stride=8), :] for comp in range(4)]


def pack_kernel(
    sizes, state_hbm, depth_hbm, metric_hbm, partner_hbm, refine_hbm, stats_ref, even_ref, odd_ref,
    state_even, state_odd, depth_ref, metric_ref, partner_ref, refine_ref, spread, sems,
):
    blocks, halo = sizes.blocks, sizes.halo
    wide = LANES * halo
    late = blocks - halo
    even = (lax.axis_index(AXES) + 1) % 2 * late
    odd = late - even
    copies = fetch_all(
        (
            (depth_hbm, depth_ref),
            (metric_hbm, metric_ref),
            (refine_hbm, refine_ref),
            (partner_hbm, partner_ref),
            (state_hbm.at[:, :, pl.ds(pl.multiple_of(LANES * even, LANES), wide)], state_even),
            (state_hbm.at[:, :, pl.ds(pl.multiple_of(LANES * odd, LANES), wide)], state_odd),
        ),
        sems,
    )
    for copy in copies:
        copy.wait()
    rx, ry, sx, sy = split_metric(metric_ref, spread, blocks)
    depth = depth_ref[...]
    refine = refine_ref[...].astype(jnp.float32)
    faces = ((sx, sy), (rx + sx, ry + sy), (rx, ry))
    lengths = [jnp.sqrt(vx * vx + vy * vy) for vx, vy in faces]
    rate = jnp.sqrt(GRAVITY * depth) * jnp.maximum(jnp.maximum(lengths[0], lengths[1]), lengths[2])
    top = jnp.max(jnp.max(rate, axis=0, keepdims=True), axis=1, keepdims=True)
    extra = jnp.sum(jnp.sum(refine, axis=0, keepdims=True), axis=1, keepdims=True)
    shape = stats_ref.shape
    lane = lax.broadcasted_iota(jnp.int32, shape, 1)
    stats_ref[...] = jnp.where(
        lane < LANES // 2, jnp.broadcast_to(top, shape), jnp.broadcast_to(extra, shape)
    )
    for ref, source, start in ((even_ref, state_even, even), (odd_ref, state_odd, odd)):
        pack_state(source, ref, halo)
        at = pl.ds(start, halo)
        dense = [depth_ref[at, :]]
        dense += [spread[pl.ds(8 * start + comp, halo, stride=8), :] for comp in range(4)]
        dense += [partner_ref[at, :].astype(jnp.float32), refine_ref[at, :].astype(jnp.float32)]
        for num, value in enumerate(dense):
            ref[pl.ds(4 * num + 3, halo, stride=PACK), :] = value


def pack_state(source, target, blocks):
    for block in range(blocks):
        for node in range(10):
            at = PACK * block + 4 * node
            target[at : at + 3, :] = source[node, :, LANES * block : LANES * (block + 1)]


def pair_index(partner):
    lane = lax.broadcasted_iota(jnp.int32, partner.shape, 1)
    target = lane + partner.astype(jnp.int32)
    return target & (LANES - 1), (target >= 0) & (target < LANES)


def lane_gather(values, index):
    return jnp.take_along_axis(values, index, axis=1, mode="promise_in_bounds")


def outer_values(load, index, inside):
    shape = index.shape
    lane = lax.broadcasted_iota(jnp.int32, shape, 1)

    def prev(item):
        return pltpu.roll(jnp.where(lane == LANES - 1, load(item, -1), load(item, 0)), 1, 1)

    def after(item):
        return pltpu.roll(jnp.where(lane == 0, load(item, 1), load(item, 0)), LANES - 1, 1)

    def across(item):
        other = jnp.where(lane < LANES // 2, load(item, 1), load(item, -1))
        return jnp.where(inside, lane_gather(load(item, 0), index), lane_gather(other, index))

    return prev, after, across


def wall_masks(sizes, start, place, count, partner):
    shape = partner.shape
    lane = lax.broadcasted_iota(jnp.int32, shape, 1)
    row = lax.broadcasted_iota(jnp.int32, shape, 0) + start
    first = (lane == 0) & (row == sizes.halo) & (place == 0)
    last = (lane == LANES - 1) & (row == sizes.halo + sizes.blocks - 1) & (place == count - 1)
    return first, last, partner == 0


def tendency(load, geo, walls, index, inside, diff_ref, lift_ref):
    speed_sq, rx, ry, sx, sy = geo[:5]
    outer_sq, waves, ghosts = geo[5:8], geo[8:11], geo[11:14]
    own = [[load(10 * field + node, 0) for node in range(10)] for field in range(3)]
    eta, mom_x, mom_y = own
    flow_r = [-(rx * mom_x[b] + ry * mom_y[b]) for b in range(10)]
    flow_s = [-(sx * mom_x[b] + sy * mom_y[b]) for b in range(10)]
    half_r = (0.5 * rx, 0.5 * ry)
    half_s = (0.5 * sx, 0.5 * sy)
    vectors = (
        (-half_s[0], -half_s[1]),
        (half_r[0] + half_s[0], half_r[1] + half_s[1]),
        (-half_r[0], -half_r[1]),
    )
    fetch = outer_values(load, index, inside)
    jumps = ([], [], [])
    for face in range(3):
        vec_x, vec_y = vectors[face]
        theirs = FACES[(1, 0, 2)[face]]
        wall = walls[face]
        for j in range(4):
            node, match = FACES[face][j], theirs[3 - j]
            in_eta, in_x, in_y = eta[node], mom_x[node], mom_y[node]
            ext_eta, ext_x, ext_y = [fetch[face](10 * field + match) for field in range(3)]
            bounce = (in_x * vec_x + in_y * vec_y) * ghosts[face]
            d_eta = jnp.where(wall, 0.0, in_eta - ext_eta)
            d_x = jnp.where(wall, bounce * vec_x, in_x - ext_x)
            d_y = jnp.where(wall, bounce * vec_y, in_y - ext_y)
            head = jnp.where(wall, 0.0, speed_sq * in_eta - outer_sq[face] * ext_eta)
            jumps[0].append(d_x * vec_x + d_y * vec_y - waves[face] * d_eta)
            jumps[1].append(head * vec_x - waves[face] * d_x)
            jumps[2].append(head * vec_y - waves[face] * d_y)
    pull = (-speed_sq * rx, -speed_sq * ry)
    push = (-speed_sq * sx, -speed_sq * sy)
    out = [[None] * 10 for _ in range(3)]
    for a in range(10):
        total = along_r = along_s = None
        for b in range(10):
            d_r, d_s = diff_ref[a, 0, b], diff_ref[a, 1, b]
            term = d_r * flow_r[b] + d_s * flow_s[b]
            total = term if b == 0 else total + term
            along_r = d_r * eta[b] if b == 0 else along_r + d_r * eta[b]
            along_s = d_s * eta[b] if b == 0 else along_s + d_s * eta[b]
        sums = [total, pull[0] * along_r + push[0] * along_s, pull[1] * along_r + push[1] * along_s]
        for q in range(12):
            weight = lift_ref[a, q]
            for field in range(3):
                sums[field] = sums[field] + weight * jumps[field][q]
        for field in range(3):
            out[field][a] = sums[field]
    return [out[field][a] for field in range(3) for a in range(10)]


def first_kernel(
    sizes, state_hbm, depth_hbm, metric_hbm, partner_hbm, refine_hbm, even_ref, odd_ref, diff_hbm, lift_hbm,
    cur, rate_ref, geo_ref,
    state_ref, depth_ref, metric_ref, partner_ref, refine_ref, diff_ref, lift_ref,
    spread, wide, aux, sems,
):
    blocks, halo = sizes.blocks, sizes.halo
    top, bottom = PAD + halo, PAD + halo + blocks
    place = lax.axis_index(AXES)
    count = lax.axis_size(AXES)
    copies = fetch_all(
        (
            (metric_hbm, metric_ref),
            (state_hbm, state_ref),
            (depth_hbm, depth_ref),
            (partner_hbm, partner_ref),
            (refine_hbm, refine_ref),
            (diff_hbm, diff_ref),
            (lift_hbm, lift_ref),
        ),
        sems,
    )
    for copy in copies:
        copy.wait()
    metric = split_metric(metric_ref, spread, blocks)
    dense = [depth_ref[...], *metric, partner_ref[...].astype(jnp.float32), refine_ref[...].astype(jnp.float32)]
    pack_state(state_ref, wide, blocks)
    even = place % 2 == 0

    def set_halo(target, num, row):
        by_even = even_ref[pl.ds(row, halo, stride=PACK), :]
        by_odd = odd_ref[pl.ds(row, halo, stride=PACK), :]
        target[num, top - halo : top, :] = jnp.where(even, by_odd, by_even)
        target[num, bottom : bottom + halo, :] = jnp.where(even, by_even, by_odd)

    for num in range(7):
        set_halo(aux, num, 4 * num + 3)
        aux[num, top:bottom, :] = dense[num]
    for field in range(3):
        for node in range(10):
            item = 10 * field + node
            set_halo(cur, item, 4 * node + field)
            cur[item, top:bottom, :] = wide[pl.ds(4 * node + field, blocks, stride=PACK), :]

    def step(group, carry):
        base = PAD + 8 * group

        def load_aux(item, shift):
            return aux[item, pl.ds(base + shift, 8), :]

        def load(item, shift):
            return cur[item, pl.ds(base + shift, 8), :]

        depth, rx, ry, sx, sy, partner, refine = [load_aux(num, 0) for num in range(7)]
        index, inside = pair_index(partner)
        fetch = outer_values(load_aux, index, inside)
        walls = wall_masks(sizes, 8 * group, place, count, partner)
        speed_sq = GRAVITY * depth
        outer_sq = [jnp.where(walls[k], speed_sq, GRAVITY * fetch[k](0)) for k in range(3)]
        faces = ((sx, sy), (rx + sx, ry + sy), (rx, ry))
        squares = [vx * vx + vy * vy for vx, vy in faces]
        waves = [
            0.5 * jnp.sqrt(squares[k]) * jnp.sqrt(jnp.maximum(speed_sq, outer_sq[k])) for k in range(3)
        ]
        ghosts = [8.0 / squares[k] for k in range(3)]
        geo = [speed_sq, rx, ry, sx, sy, *outer_sq, *waves, *ghosts]
        rates = tendency(load, geo, walls, index, inside, diff_ref, lift_ref)
        at = pl.ds(pl.multiple_of(8 * group, 8), 8)
        for num, value in enumerate([*geo, partner, refine]):
            geo_ref[num, at, :] = value
        for item in range(30):
            rate_ref[item, at, :] = rates[item]
        return carry

    lax.fori_loop(0, sizes.rows // 8, step, 0)


def child_matrix(prolong_ref):
    f32 = jnp.float32
    node_r = lax.broadcasted_iota(jnp.int32, (PACK, 10), 0) // 4
    spread_r = (node_r == lax.broadcasted_iota(jnp.int32, (PACK, 10), 1)).astype(f32)
    item_c = lax.broadcasted_iota(jnp.int32, (10, WIDE), 1)
    spread_c = (item_c % 10 == lax.broadcasted_iota(jnp.int32, (10, WIDE), 0)).astype(f32)
    row = lax.broadcasted_iota(jnp.int32, (PACK, WIDE), 0)
    col = lax.broadcasted_iota(jnp.int32, (PACK, WIDE), 1)
    same = row % 4 == col // 10
    parts = []
    for child in range(2):
        left = jnp.dot(spread_r, prolong_ref[:, child, :], precision=HIGH, preferred_element_type=f32)
        full = jnp.dot(left, spread_c, precision=HIGH, preferred_element_type=f32)
        parts.append(jnp.where(same, full, 0.0))
    parts.append((same & (row // 4 == col % 10)).astype(f32))
    whole = jnp.concatenate(parts, axis=0)
    rounded = whole.astype(jnp.bfloat16)
    rest = (whole - rounded.astype(f32)).astype(jnp.bfloat16)
    return jnp.concatenate([rounded, rounded, rounded, rest], axis=1)


def second_kernel(
    sizes, cur, rate_ref, geo_ref, stats_hbm, diff_hbm, lift_hbm, prolong_hbm, out_hbm,
    stats_ref, diff_ref, lift_ref, prolong_ref, out_ref,
    first, ends_ref, place_v, place_s, wide, weights, gathered, index_ref, sems, out_sems, sem,
):
    slots, keep, rows = sizes.slots, sizes.keep, sizes.rows
    place = lax.axis_index(AXES)
    count = lax.axis_size(AXES)
    copies = fetch_all(
        ((prolong_hbm, prolong_ref), (stats_hbm, stats_ref), (diff_hbm, diff_ref), (lift_hbm, lift_ref)), sems
    )
    for item in (30, 31):
        wide[pl.ds(item, slots + 1, stride=WIDE), :] = jnp.zeros((slots + 1, LANES), jnp.float32)
    copies[0].wait()
    weights[...] = child_matrix(prolong_ref)
    for copy in copies[1:]:
        copy.wait()
    stats = stats_ref[...]
    lane_n = lax.broadcasted_iota(jnp.int32, stats.shape, 1)
    row_n = lax.broadcasted_iota(jnp.int32, stats.shape, 0)
    rate = jnp.where(lane_n < LANES // 2, stats, 0.0)
    top = jnp.max(jnp.max(rate, axis=0, keepdims=True), axis=1, keepdims=True)
    gone = jnp.where((lane_n == LANES - 1) & (row_n % 8 == 0) & (row_n < 8 * place), stats, 0.0)
    earlier = jnp.sum(jnp.sum(gone, axis=0, keepdims=True), axis=1, keepdims=True)
    step = COURANT / top
    refine = geo_ref[15, keep : keep + slots, :]
    counts = (1.0 + refine).astype(jnp.bfloat16)
    row_i = lax.broadcasted_iota(jnp.int32, (LANES, LANES), 0)
    col_i = lax.broadcasted_iota(jnp.int32, (LANES, LANES), 1)
    upper = (row_i <= col_i).astype(jnp.bfloat16)
    within = jnp.dot(counts, upper, preferred_element_type=jnp.float32)
    whole = jnp.dot(counts, jnp.ones((LANES, LANES), jnp.bfloat16), preferred_element_type=jnp.float32)
    row_s = lax.broadcasted_iota(jnp.int32, (slots, slots), 0)
    col_s = lax.broadcasted_iota(jnp.int32, (slots, slots), 1)
    lower = (col_s < row_s).astype(jnp.bfloat16)
    before = jnp.dot(lower, whole.astype(jnp.bfloat16), preferred_element_type=jnp.float32)
    own = before[sizes.margin : sizes.margin + 1, :]
    start = earlier - (place * (sizes.cells // 2)).astype(jnp.float32)
    ends = within + before + (start - own)
    ends_ref[:slots, :] = 2.0 * ends + refine
    ends_ref[slots:, :] = jnp.full((8, LANES), 1e9, jnp.float32)
    full = before + whole + (start - own)
    first_slot = LANES * lax.broadcasted_iota(jnp.int32, (slots, LANES), 1).astype(jnp.float32)
    lead = jnp.sum((full <= first_slot).astype(jnp.float32), axis=0, keepdims=True)
    lead = jnp.clip(lead.astype(jnp.int32), 0, slots - 1)
    place_v[...] = jnp.broadcast_to(lead, (8, LANES))
    copy = pltpu.make_async_copy(place_v, place_s, sem)
    copy.start()

    for item in range(30):
        first[item, PAD : PAD + rows, :] = cur[item, PAD : PAD + rows, :] + step * rate_ref[item]

    def stage(group, carry):
        base = PAD + keep + 8 * group
        at = pl.ds(8 * group + keep, 8)

        def load(item, shift):
            return first[item, pl.ds(base + shift, 8), :]

        geo = [geo_ref[num, at, :] for num in range(14)]
        partner = geo_ref[14, at, :]
        index, inside = pair_index(partner)
        walls = wall_masks(sizes, 8 * group + keep, place, count, partner)
        rates = tendency(load, geo, walls, index, inside, diff_ref, lift_ref)
        lead_row = 8 * WIDE * group
        for field in range(3):
            for node in range(10):
                item = 10 * field + node
                old = cur[item, pl.ds(base, 8), :]
                new = 0.5 * old + 0.5 * (load(item, 0) + step * rates[item])
                wide[pl.ds(lead_row + item, 8, stride=WIDE), :] = new
        return carry

    lax.fori_loop(0, slots // 8, stage, 0)

    copy.wait()
    for slot in range(slots):
        lead_at = place_s[0, slot]
        index_ref[0, slot : slot + 1, :] = ends_ref[pl.ds(lead_at, 1), :]
        index_ref[1, slot : slot + 1, :] = ends_ref[pl.ds(lead_at + 1, 1), :]
    near, far = index_ref[0], index_ref[1]
    slot_no = LANES * lax.broadcasted_iota(jnp.int32, (slots, LANES), 0) + lax.broadcasted_iota(
        jnp.int32, (slots, LANES), 1
    )
    goal = (2 * slot_no + 1).astype(jnp.float32)
    beyond = jnp.broadcast_to(near[:, LANES - 1 :], (slots, LANES)) <= goal

    def pick(index):
        return jnp.where(beyond, lane_gather(far, index), lane_gather(near, index))

    found = jnp.zeros((slots, LANES), jnp.int32)
    size = LANES // 2
    while size:
        passed = pick(found + (size - 1)) <= goal
        found = jnp.where(passed, found + size, found)
        size //= 2
    mine = pick(found).astype(jnp.int32)
    split = mine & 1
    begin = (mine >> 1) - 1 - split
    kind = split * (1 + slot_no - begin)
    index_ref[0] = found.astype(jnp.float32)
    index_ref[1] = kind.astype(jnp.float32)
    index_ref[2] = beyond.astype(jnp.float32)
    for slot in range(slots):
        lead_at = place_s[0, slot] * WIDE
        lane_idx = jnp.broadcast_to(index_ref[0, slot : slot + 1, :], (WIDE, LANES)).astype(jnp.int32)
        passed = jnp.broadcast_to(index_ref[2, slot : slot + 1, :], (WIDE, LANES)) > 0.5
        one = wide[pl.ds(pl.multiple_of(lead_at, WIDE), WIDE), :]
        two = wide[pl.ds(pl.multiple_of(lead_at + WIDE, WIDE), WIDE), :]
        gathered[:, LANES * slot : LANES * (slot + 1)] = jnp.where(
            passed, lane_gather(two, lane_idx), lane_gather(one, lane_idx)
        )
    matrix = weights[...]
    chunk = 8 * LANES
    results = []
    for part in range(slots // 8):
        span = slice(chunk * part, chunk * (part + 1))
        values = gathered[:, span]
        high = values.astype(jnp.bfloat16)
        rest = values - high.astype(jnp.float32)
        low = rest.astype(jnp.bfloat16)
        last = (rest - low.astype(jnp.float32)).astype(jnp.bfloat16)
        stack = jnp.concatenate([high, low, last, high], axis=0)
        children = jnp.dot(matrix, stack, preferred_element_type=jnp.float32)
        for sub in range(8):
            slot = 8 * part + sub
            cut = slice(LANES * sub, LANES * (sub + 1))
            tag = jnp.broadcast_to(index_ref[1, slot : slot + 1, :], (PACK, LANES))
            value = jnp.where(
                tag < 0.5,
                children[2 * PACK :, cut],
                jnp.where(tag < 1.5, children[:PACK, cut], children[PACK : 2 * PACK, cut]),
            )
            for node in range(10):
                out_ref[node, :, LANES * slot : LANES * (slot + 1)] = value[4 * node : 4 * node + 3]
        result = pltpu.make_async_copy(out_ref.at[:, :, span], out_hbm.at[:, :, span], out_sems.at[part])
        result.start()
        results.append(result)
    for result in results:
        result.wait()


def swaps(start, count):
    pairs = [(i, i + 1) for i in range(start, count - 1, 2)]
    return pairs + [(j, i) for i, j in pairs]


def shards(state, depth, metric, partner, refine, diff_ops, lift, prolong):
    sizes = Sizes(state.shape[2])
    count = lax.axis_size(AXES)
    blocks, rows, slots, halo = sizes.blocks, sizes.rows, sizes.slots, sizes.halo
    depth, partner, refine = [x.reshape(blocks, LANES) for x in (depth, partner, refine)]
    state, diff_ops, prolong = [jnp.transpose(x, (1, 0, 2)) for x in (state, diff_ops, prolong)]
    state, depth, metric, partner, refine, diff_ops, lift, prolong = [
        pltpu.with_memory_space_constraint(x, pltpu.HBM)
        for x in (state, depth, metric, partner, refine, diff_ops, lift, prolong)
    ]
    f32, i32 = jnp.float32, jnp.int32
    packed = jax.ShapeDtypeStruct((PACK * halo, LANES), f32)
    dense = [
        pltpu.VMEM((blocks, LANES), f32),
        pltpu.VMEM(metric.shape, f32),
        pltpu.VMEM((blocks, LANES), i32),
        pltpu.VMEM((blocks, LANES), i32),
    ]
    stats, even, odd = pl.pallas_call(
        functools.partial(pack_kernel, sizes),
        name="pack",
        out_shape=(jax.ShapeDtypeStruct((8 * count, LANES), f32), packed, packed),
        in_specs=[HBM] * 5,
        out_specs=(VMEM,) * 3,
        scratch_shapes=[
            pltpu.VMEM((10, 3, LANES * halo), f32),
            pltpu.VMEM((10, 3, LANES * halo), f32),
            *dense,
            pltpu.VMEM((8 * blocks, LANES), f32),
            pltpu.SemaphoreType.DMA((6,)),
        ],
        compiler_params=PARAMS,
    )(state, depth, metric, partner, refine)
    stats = lax.all_to_all(stats, AXES, 0, 0, tiled=True)
    even = lax.ppermute(even, AXES, swaps(0, count))
    odd = lax.ppermute(odd, AXES, swaps(1, count))
    even, odd = [pltpu.with_memory_space_constraint(x, pltpu.VMEM) for x in (even, odd)]
    stats = pltpu.with_memory_space_constraint(stats, pltpu.HBM)
    operators = [pltpu.SMEM(diff_ops.shape, f32), pltpu.SMEM(lift.shape, f32)]
    cur, rates, geo = pl.pallas_call(
        functools.partial(first_kernel, sizes),
        name="first_stage",
        cost_estimate=pl.CostEstimate(flops=1024, transcendentals=0, bytes_accessed=1024),
        out_shape=(
            jax.ShapeDtypeStruct((30, sizes.tall, LANES), f32),
            jax.ShapeDtypeStruct((30, rows, LANES), f32),
            jax.ShapeDtypeStruct((16, rows, LANES), f32),
        ),
        in_specs=[HBM] * 5 + [VMEM] * 2 + [HBM] * 2,
        out_specs=(VMEM,) * 3,
        scratch_shapes=[
            pltpu.VMEM(state.shape, f32),
            *dense,
            *operators,
            pltpu.VMEM((8 * blocks, LANES), f32),
            pltpu.VMEM((PACK * blocks, LANES), f32),
            pltpu.VMEM((7, sizes.tall, LANES), f32),
            pltpu.SemaphoreType.DMA((7,)),
        ],
        compiler_params=PARAMS,
    )(state, depth, metric, partner, refine, even, odd, diff_ops, lift)
    refined = pl.pallas_call(
        functools.partial(second_kernel, sizes),
        name="second_stage_refine",
        out_shape=jax.ShapeDtypeStruct((10, 3, LANES * slots), f32),
        in_specs=[VMEM] * 3 + [HBM] * 4,
        out_specs=HBM,
        scratch_shapes=[
            pltpu.VMEM(stats.shape, f32),
            *operators,
            pltpu.VMEM(prolong.shape, f32),
            pltpu.VMEM((10, 3, LANES * slots), f32),
            pltpu.VMEM((30, sizes.tall, LANES), f32),
            pltpu.VMEM((slots + 8, LANES), f32),
            pltpu.VMEM((8, LANES), i32),
            pltpu.SMEM((8, LANES), i32),
            pltpu.VMEM((WIDE * (slots + 1), LANES), f32),
            pltpu.VMEM((3 * PACK, 4 * WIDE), jnp.bfloat16),
            pltpu.VMEM((WIDE, LANES * slots), f32),
            pltpu.VMEM((3, slots, LANES), f32),
            pltpu.SemaphoreType.DMA((4,)),
            pltpu.SemaphoreType.DMA((slots // 8,)),
            pltpu.SemaphoreType.DMA,
        ],
        compiler_params=PARAMS,
    )(cur, rates, geo, stats, diff_ops, lift, prolong)
    return jnp.transpose(refined, (1, 0, 2))


def solution(mesh):
    return jax.shard_map(
        shards,
        mesh=mesh,
        in_specs=(
            P(None, None, AXES),
            P(AXES),
            P(None, AXES),
            P(AXES),
            P(AXES),
            P(),
            P(),
            P(),
        ),
        out_specs=P(None, None, AXES),
        check_vma=False,
    )
```

```python
import functools

import jax
import jax.numpy as jnp
from jax import lax
from jax.experimental import pallas as pl
from jax.experimental.pallas import tpu as pltpu
from jax.sharding import PartitionSpec as P

GRAVITY = 9.81
COURANT = 0.5
HIGH = lax.Precision.HIGHEST
LANES = 128
AXES = ("row", "col")
FACES = ((0, 1, 2, 3), (3, 6, 8, 9), (9, 7, 4, 0))
PACK = 40
WIDE = 32
PAD = 8

VMEM = pl.BlockSpec(memory_space=pltpu.VMEM)
HBM = pl.BlockSpec(memory_space=pltpu.HBM)
PARAMS = pltpu.CompilerParams(vmem_limit_bytes=48 * 1024 * 1024)


class Sizes:
    def __init__(self, cells):
        self.cells = cells
        self.blocks = cells // LANES
        self.margin = cells // 4 // LANES
        self.halo = self.margin + 1
        self.rows = -(-(self.blocks + 2 * self.halo) // 8) * 8
        self.tall = self.rows + 2 * PAD
        self.slots = 3 * self.blocks // 2
        self.keep = self.halo - self.margin


def fetch_all(pairs, sems):
    copies = [pltpu.make_async_copy(src, dst, sems.at[num]) for num, (src, dst) in enumerate(pairs)]
    for copy in copies:
        copy.start()
    return copies


def split_metric(metric_ref, spread, blocks):
    for block in range(blocks):
        spread[8 * block : 8 * block + 4, :] = metric_ref[:, LANES * block : LANES * (block + 1)]
    return [spread[pl.ds(comp, blocks, stride=8), :] for comp in range(4)]


def pack_kernel(
    sizes, state_hbm, depth_hbm, metric_hbm, partner_hbm, refine_hbm, stats_hbm, even_ref, odd_ref,
    stats_ref, state_even, state_odd, depth_ref, metric_ref, partner_ref, refine_ref, spread, sems, sem,
):
    blocks, halo = sizes.blocks, sizes.halo
    wide = LANES * halo
    late = blocks - halo
    even = (lax.axis_index(AXES) + 1) % 2 * late
    odd = late - even
    copies = fetch_all(
        (
            (depth_hbm, depth_ref),
            (metric_hbm, metric_ref),
            (refine_hbm, refine_ref),
            (partner_hbm, partner_ref),
            (state_hbm.at[:, :, pl.ds(pl.multiple_of(LANES * even, LANES), wide)], state_even),
            (state_hbm.at[:, :, pl.ds(pl.multiple_of(LANES * odd, LANES), wide)], state_odd),
        ),
        sems,
    )
    for copy in copies[:3]:
        copy.wait()
    rx, ry, sx, sy = split_metric(metric_ref, spread, blocks)
    depth = depth_ref[...]
    refine = refine_ref[...].astype(jnp.float32)
    faces = ((sx, sy), (rx + sx, ry + sy), (rx, ry))
    lengths = [jnp.sqrt(vx * vx + vy * vy) for vx, vy in faces]
    rate = jnp.sqrt(GRAVITY * depth) * jnp.maximum(jnp.maximum(lengths[0], lengths[1]), lengths[2])
    top = jnp.max(jnp.max(rate, axis=0, keepdims=True), axis=1, keepdims=True)
    extra = jnp.sum(jnp.sum(refine, axis=0, keepdims=True), axis=1, keepdims=True)
    shape = stats_ref.shape
    lane = lax.broadcasted_iota(jnp.int32, shape, 1)
    stats_ref[...] = jnp.where(
        lane < LANES // 2, jnp.broadcast_to(top, shape), jnp.broadcast_to(extra, shape)
    )
    sent = pltpu.make_async_copy(stats_ref, stats_hbm, sem)
    sent.start()
    for copy in copies[3:]:
        copy.wait()
    for ref, source, start in ((even_ref, state_even, even), (odd_ref, state_odd, odd)):
        pack_state(source, ref, halo)
        at = pl.ds(start, halo)
        dense = [depth_ref[at, :]]
        dense += [spread[pl.ds(8 * start + comp, halo, stride=8), :] for comp in range(4)]
        dense += [partner_ref[at, :].astype(jnp.float32), refine_ref[at, :].astype(jnp.float32)]
        for num, value in enumerate(dense):
            ref[pl.ds(4 * num + 3, halo, stride=PACK), :] = value
    sent.wait()


def pack_state(source, target, blocks):
    for block in range(blocks):
        for node in range(10):
            at = PACK * block + 4 * node
            target[at : at + 3, :] = source[node, :, LANES * block : LANES * (block + 1)]


def pair_index(partner):
    lane = lax.broadcasted_iota(jnp.int32, partner.shape, 1)
    target = lane + partner.astype(jnp.int32)
    return target & (LANES - 1), (target >= 0) & (target < LANES)


def lane_gather(values, index):
    return jnp.take_along_axis(values, index, axis=1, mode="promise_in_bounds")


def outer_values(load, index, inside):
    shape = index.shape
    lane = lax.broadcasted_iota(jnp.int32, shape, 1)

    def prev(item):
        return pltpu.roll(jnp.where(lane == LANES - 1, load(item, -1), load(item, 0)), 1, 1)

    def after(item):
        return pltpu.roll(jnp.where(lane == 0, load(item, 1), load(item, 0)), LANES - 1, 1)

    def across(item):
        other = jnp.where(lane < LANES // 2, load(item, 1), load(item, -1))
        return jnp.where(inside, lane_gather(load(item, 0), index), lane_gather(other, index))

    return prev, after, across


def wall_masks(sizes, start, place, count, partner):
    shape = partner.shape
    lane = lax.broadcasted_iota(jnp.int32, shape, 1)
    row = lax.broadcasted_iota(jnp.int32, shape, 0) + start
    first = (lane == 0) & (row == sizes.halo) & (place == 0)
    last = (lane == LANES - 1) & (row == sizes.halo + sizes.blocks - 1) & (place == count - 1)
    return first, last, partner == 0


def tendency(load, geo, walls, index, inside, diff_ref, lift_ref):
    speed_sq, rx, ry, sx, sy = geo[:5]
    outer_sq, waves, ghosts = geo[5:8], geo[8:11], geo[11:14]
    own = [[load(10 * field + node, 0) for node in range(10)] for field in range(3)]
    eta, mom_x, mom_y = own
    flow_r = [-(rx * mom_x[b] + ry * mom_y[b]) for b in range(10)]
    flow_s = [-(sx * mom_x[b] + sy * mom_y[b]) for b in range(10)]
    half_r = (0.5 * rx, 0.5 * ry)
    half_s = (0.5 * sx, 0.5 * sy)
    vectors = (
        (-half_s[0], -half_s[1]),
        (half_r[0] + half_s[0], half_r[1] + half_s[1]),
        (-half_r[0], -half_r[1]),
    )
    fetch = outer_values(load, index, inside)
    jumps = ([], [], [])
    for face in range(3):
        vec_x, vec_y = vectors[face]
        theirs = FACES[(1, 0, 2)[face]]
        wall = walls[face]
        for j in range(4):
            node, match = FACES[face][j], theirs[3 - j]
            in_eta, in_x, in_y = eta[node], mom_x[node], mom_y[node]
            ext_eta, ext_x, ext_y = [fetch[face](10 * field + match) for field in range(3)]
            bounce = (in_x * vec_x + in_y * vec_y) * ghosts[face]
            d_eta = jnp.where(wall, 0.0, in_eta - ext_eta)
            d_x = jnp.where(wall, bounce * vec_x, in_x - ext_x)
            d_y = jnp.where(wall, bounce * vec_y, in_y - ext_y)
            head = jnp.where(wall, 0.0, speed_sq * in_eta - outer_sq[face] * ext_eta)
            jumps[0].append(d_x * vec_x + d_y * vec_y - waves[face] * d_eta)
            jumps[1].append(head * vec_x - waves[face] * d_x)
            jumps[2].append(head * vec_y - waves[face] * d_y)
    pull = (-speed_sq * rx, -speed_sq * ry)
    push = (-speed_sq * sx, -speed_sq * sy)
    out = [[None] * 10 for _ in range(3)]
    for a in range(10):
        total = along_r = along_s = None
        for b in range(10):
            d_r, d_s = diff_ref[a, 0, b], diff_ref[a, 1, b]
            term = d_r * flow_r[b] + d_s * flow_s[b]
            total = term if b == 0 else total + term
            along_r = d_r * eta[b] if b == 0 else along_r + d_r * eta[b]
            along_s = d_s * eta[b] if b == 0 else along_s + d_s * eta[b]
        sums = [total, pull[0] * along_r + push[0] * along_s, pull[1] * along_r + push[1] * along_s]
        for q in range(12):
            weight = lift_ref[a, q]
            for field in range(3):
                sums[field] = sums[field] + weight * jumps[field][q]
        for field in range(3):
            out[field][a] = sums[field]
    return [out[field][a] for field in range(3) for a in range(10)]


def child_matrix(prolong_ref):
    f32 = jnp.float32
    node_r = lax.broadcasted_iota(jnp.int32, (PACK, 10), 0) // 4
    spread_r = (node_r == lax.broadcasted_iota(jnp.int32, (PACK, 10), 1)).astype(f32)
    item_c = lax.broadcasted_iota(jnp.int32, (10, WIDE), 1)
    spread_c = (item_c % 10 == lax.broadcasted_iota(jnp.int32, (10, WIDE), 0)).astype(f32)
    row = lax.broadcasted_iota(jnp.int32, (PACK, WIDE), 0)
    col = lax.broadcasted_iota(jnp.int32, (PACK, WIDE), 1)
    same = row % 4 == col // 10
    parts = []
    for child in range(2):
        left = jnp.dot(spread_r, prolong_ref[:, child, :], precision=HIGH, preferred_element_type=f32)
        full = jnp.dot(left, spread_c, precision=HIGH, preferred_element_type=f32)
        parts.append(jnp.where(same, full, 0.0))
    parts.append((same & (row // 4 == col % 10)).astype(f32))
    whole = jnp.concatenate(parts, axis=0)
    rounded = whole.astype(jnp.bfloat16)
    rest = (whole - rounded.astype(f32)).astype(jnp.bfloat16)
    return jnp.concatenate([rounded, rounded, rounded, rest], axis=1)


def sum_children(sizes, refine, ends_ref):
    slots, f32 = sizes.slots, jnp.float32
    counts = (1.0 + refine).astype(jnp.bfloat16)
    row_i = lax.broadcasted_iota(jnp.int32, (LANES, LANES), 0)
    col_i = lax.broadcasted_iota(jnp.int32, (LANES, LANES), 1)
    upper = (row_i <= col_i).astype(jnp.bfloat16)
    within = jnp.dot(counts, upper, preferred_element_type=f32)
    whole = jnp.dot(counts, jnp.ones((LANES, LANES), jnp.bfloat16), preferred_element_type=f32)
    row_s = lax.broadcasted_iota(jnp.int32, (slots, slots), 0)
    col_s = lax.broadcasted_iota(jnp.int32, (slots, slots), 1)
    lower = (col_s < row_s).astype(jnp.bfloat16)
    before = jnp.dot(lower, whole.astype(jnp.bfloat16), preferred_element_type=f32)
    before = before - before[sizes.margin : sizes.margin + 1, :]
    ends_ref[0] = 2.0 * (within + before) + refine
    ends_ref[1] = before + whole


def first_kernel(
    sizes, state_hbm, depth_hbm, metric_hbm, partner_hbm, refine_hbm, even_ref, odd_ref, diff_hbm, lift_hbm, prolong_hbm,
    cur, rate_ref, geo_ref, weights, ends_ref,
    state_ref, depth_ref, metric_ref, partner_ref, refine_ref, diff_ref, lift_ref, prolong_ref,
    spread, wide, aux, sems,
):
    blocks, halo = sizes.blocks, sizes.halo
    top, bottom = PAD + halo, PAD + halo + blocks
    place = lax.axis_index(AXES)
    count = lax.axis_size(AXES)
    copies = fetch_all(
        (
            (metric_hbm, metric_ref),
            (state_hbm, state_ref),
            (depth_hbm, depth_ref),
            (partner_hbm, partner_ref),
            (refine_hbm, refine_ref),
            (diff_hbm, diff_ref),
            (lift_hbm, lift_ref),
            (prolong_hbm, prolong_ref),
        ),
        sems,
    )
    for copy in copies:
        copy.wait()
    metric = split_metric(metric_ref, spread, blocks)
    dense = [depth_ref[...], *metric, partner_ref[...].astype(jnp.float32), refine_ref[...].astype(jnp.float32)]
    pack_state(state_ref, wide, blocks)
    even = place % 2 == 0

    def set_halo(target, num, row):
        by_even = even_ref[pl.ds(row, halo, stride=PACK), :]
        by_odd = odd_ref[pl.ds(row, halo, stride=PACK), :]
        target[num, top - halo : top, :] = jnp.where(even, by_odd, by_even)
        target[num, bottom : bottom + halo, :] = jnp.where(even, by_even, by_odd)

    for num in range(7):
        set_halo(aux, num, 4 * num + 3)
        aux[num, top:bottom, :] = dense[num]
    for field in range(3):
        for node in range(10):
            item = 10 * field + node
            set_halo(cur, item, 4 * node + field)
            cur[item, top:bottom, :] = wide[pl.ds(4 * node + field, blocks, stride=PACK), :]

    weights[...] = child_matrix(prolong_ref)
    begin = PAD + sizes.keep
    sum_children(sizes, aux[6, begin : begin + sizes.slots, :], ends_ref)

    def step(group, carry):
        base = PAD + 8 * group

        def load_aux(item, shift):
            return aux[item, pl.ds(base + shift, 8), :]

        def load(item, shift):
            return cur[item, pl.ds(base + shift, 8), :]

        depth, rx, ry, sx, sy, partner = [load_aux(num, 0) for num in range(6)]
        index, inside = pair_index(partner)
        fetch = outer_values(load_aux, index, inside)
        walls = wall_masks(sizes, 8 * group, place, count, partner)
        speed_sq = GRAVITY * depth
        outer_sq = [jnp.where(walls[k], speed_sq, GRAVITY * fetch[k](0)) for k in range(3)]
        faces = ((sx, sy), (rx + sx, ry + sy), (rx, ry))
        squares = [vx * vx + vy * vy for vx, vy in faces]
        waves = [
            0.5 * jnp.sqrt(squares[k]) * jnp.sqrt(jnp.maximum(speed_sq, outer_sq[k])) for k in range(3)
        ]
        ghosts = [8.0 / squares[k] for k in range(3)]
        geo = [speed_sq, rx, ry, sx, sy, *outer_sq, *waves, *ghosts]
        rates = tendency(load, geo, walls, index, inside, diff_ref, lift_ref)
        at = pl.ds(pl.multiple_of(8 * group, 8), 8)
        for num, value in enumerate([*geo, partner]):
            geo_ref[num, at, :] = value
        for item in range(30):
            rate_ref[item, at, :] = rates[item]
        return carry

    lax.fori_loop(0, sizes.rows // 8, step, 0)


def second_kernel(
    sizes, cur, rate_ref, geo_ref, weights, base_ref, stats_ref, diff_hbm, lift_hbm, out_hbm,
    diff_ref, lift_ref, out_ref, first, ends_ref, place_v, place_s, wide, pair_ref, gathered, index_ref,
    sems, out_sems, sem,
):
    slots, keep, rows = sizes.slots, sizes.keep, sizes.rows
    place = lax.axis_index(AXES)
    count = lax.axis_size(AXES)
    copies = fetch_all(((diff_hbm, diff_ref), (lift_hbm, lift_ref)), sems)
    stats = stats_ref[...]
    half = LANES // 2
    row_n = lax.broadcasted_iota(jnp.int32, stats.shape, 0)
    top = jnp.max(stats, axis=0, keepdims=True)
    earlier = jnp.sum(jnp.where(row_n < place, stats, 0.0), axis=0, keepdims=True)
    left = lax.broadcasted_iota(jnp.int32, (1, LANES), 1) < half
    top = jnp.where(left, top, pltpu.roll(top, half, 1))
    earlier = jnp.where(left, pltpu.roll(earlier, half, 1), earlier)
    step = COURANT / top
    start = earlier - (place * (sizes.cells // 2)).astype(jnp.float32)
    ends_ref[:slots, :] = base_ref[0] + 2.0 * start
    ends_ref[slots:, :] = jnp.full((8, LANES), 1e9, jnp.float32)
    first_slot = LANES * lax.broadcasted_iota(jnp.int32, (slots, LANES), 1).astype(jnp.float32)
    lead = jnp.sum((base_ref[1] + start <= first_slot).astype(jnp.float32), axis=0, keepdims=True)
    lead = jnp.clip(lead.astype(jnp.int32), 0, slots - 1)
    place_v[...] = jnp.broadcast_to(lead, (8, LANES))
    copy = pltpu.make_async_copy(place_v, place_s, sem)
    copy.start()
    for item in (30, 31):
        wide[pl.ds(item, slots + 1, stride=WIDE), :] = jnp.zeros((slots + 1, LANES), jnp.float32)

    for item in range(30):
        first[item, PAD : PAD + rows, :] = cur[item, PAD : PAD + rows, :] + step * rate_ref[item]

    copy.wait()
    for fetched in copies:
        fetched.wait()

    def search(group):
        for sub in range(8):
            lead_at = place_s[0, 8 * group + sub]
            pair_ref[0, sub : sub + 1, :] = ends_ref[pl.ds(lead_at, 1), :]
            pair_ref[1, sub : sub + 1, :] = ends_ref[pl.ds(lead_at + 1, 1), :]
        near, far = pair_ref[0], pair_ref[1]
        row = lax.broadcasted_iota(jnp.int32, (8, LANES), 0) + 8 * group
        slot_no = LANES * row + lax.broadcasted_iota(jnp.int32, (8, LANES), 1)
        goal = (2 * slot_no + 1).astype(jnp.float32)
        beyond = jnp.broadcast_to(near[:, LANES - 1 :], (8, LANES)) <= goal

        def pick(index):
            return jnp.where(beyond, lane_gather(far, index), lane_gather(near, index))

        found = jnp.zeros((8, LANES), jnp.int32)
        size = LANES // 2
        while size:
            passed = pick(found + (size - 1)) <= goal
            found = jnp.where(passed, found + size, found)
            size //= 2
        mine = pick(found).astype(jnp.int32)
        split = mine & 1
        begin = (mine >> 1) - 1 - split
        at = pl.ds(pl.multiple_of(8 * group, 8), 8)
        index_ref[0, at, :] = found.astype(jnp.float32)
        index_ref[1, at, :] = (split * (1 + slot_no - begin)).astype(jnp.float32)
        index_ref[2, at, :] = beyond.astype(jnp.float32)

    def stage(group, carry):
        search(group)
        base = PAD + keep + 8 * group
        at = pl.ds(8 * group + keep, 8)

        def load(item, shift):
            return first[item, pl.ds(base + shift, 8), :]

        geo = [geo_ref[num, at, :] for num in range(14)]
        partner = geo_ref[14, at, :]
        index, inside = pair_index(partner)
        walls = wall_masks(sizes, 8 * group + keep, place, count, partner)
        rates = tendency(load, geo, walls, index, inside, diff_ref, lift_ref)
        lead_row = 8 * WIDE * group
        for field in range(3):
            for node in range(10):
                item = 10 * field + node
                old = cur[item, pl.ds(base, 8), :]
                new = 0.5 * old + 0.5 * (load(item, 0) + step * rates[item])
                wide[pl.ds(lead_row + item, 8, stride=WIDE), :] = new
        return carry

    lax.fori_loop(0, slots // 8, stage, 0)

    for slot in range(slots):
        lead_at = place_s[0, slot] * WIDE
        lane_idx = jnp.broadcast_to(index_ref[0, slot : slot + 1, :], (WIDE, LANES)).astype(jnp.int32)
        passed = jnp.broadcast_to(index_ref[2, slot : slot + 1, :], (WIDE, LANES)) > 0.5
        one = wide[pl.ds(pl.multiple_of(lead_at, WIDE), WIDE), :]
        two = wide[pl.ds(pl.multiple_of(lead_at + WIDE, WIDE), WIDE), :]
        gathered[:, LANES * slot : LANES * (slot + 1)] = jnp.where(
            passed, lane_gather(two, lane_idx), lane_gather(one, lane_idx)
        )
    matrix = weights[...]
    chunk = 8 * LANES
    results = []
    for part in range(slots // 8):
        span = slice(chunk * part, chunk * (part + 1))
        values = gathered[:, span]
        high = values.astype(jnp.bfloat16)
        rest = values - high.astype(jnp.float32)
        low = rest.astype(jnp.bfloat16)
        last = (rest - low.astype(jnp.float32)).astype(jnp.bfloat16)
        stack = jnp.concatenate([high, low, last, high], axis=0)
        children = jnp.dot(matrix, stack, preferred_element_type=jnp.float32)
        for sub in range(8):
            slot = 8 * part + sub
            cut = slice(LANES * sub, LANES * (sub + 1))
            tag = jnp.broadcast_to(index_ref[1, slot : slot + 1, :], (PACK, LANES))
            value = jnp.where(
                tag < 0.5,
                children[2 * PACK :, cut],
                jnp.where(tag < 1.5, children[:PACK, cut], children[PACK : 2 * PACK, cut]),
            )
            for node in range(10):
                out_ref[node, :, LANES * slot : LANES * (slot + 1)] = value[4 * node : 4 * node + 3]
        result = pltpu.make_async_copy(out_ref.at[:, :, span], out_hbm.at[:, :, span], out_sems.at[part])
        result.start()
        results.append(result)
    for result in results:
        result.wait()


def swaps(start, count):
    pairs = [(i, i + 1) for i in range(start, count - 1, 2)]
    return pairs + [(j, i) for i, j in pairs]


def shards(state, depth, metric, partner, refine, diff_ops, lift, prolong):
    sizes = Sizes(state.shape[2])
    count = lax.axis_size(AXES)
    blocks, rows, slots, halo = sizes.blocks, sizes.rows, sizes.slots, sizes.halo
    depth, partner, refine = [x.reshape(blocks, LANES) for x in (depth, partner, refine)]
    state, diff_ops, prolong = [jnp.transpose(x, (1, 0, 2)) for x in (state, diff_ops, prolong)]
    state, depth, metric, partner, refine, diff_ops, lift, prolong = [
        pltpu.with_memory_space_constraint(x, pltpu.HBM)
        for x in (state, depth, metric, partner, refine, diff_ops, lift, prolong)
    ]
    f32, i32 = jnp.float32, jnp.int32
    packed = jax.ShapeDtypeStruct((PACK * halo, LANES), f32)
    dense = [
        pltpu.VMEM((blocks, LANES), f32),
        pltpu.VMEM(metric.shape, f32),
        pltpu.VMEM((blocks, LANES), i32),
        pltpu.VMEM((blocks, LANES), i32),
    ]
    stats, even, odd = pl.pallas_call(
        functools.partial(pack_kernel, sizes),
        name="pack",
        out_shape=(jax.ShapeDtypeStruct((count, LANES), f32), packed, packed),
        in_specs=[HBM] * 5,
        out_specs=(HBM, VMEM, VMEM),
        scratch_shapes=[
            pltpu.VMEM((count, LANES), f32),
            pltpu.VMEM((10, 3, LANES * halo), f32),
            pltpu.VMEM((10, 3, LANES * halo), f32),
            *dense,
            pltpu.VMEM((8 * blocks, LANES), f32),
            pltpu.SemaphoreType.DMA((6,)),
            pltpu.SemaphoreType.DMA,
        ],
        compiler_params=PARAMS,
    )(state, depth, metric, partner, refine)
    even = lax.ppermute(even, AXES, swaps(0, count))
    odd = lax.ppermute(odd, AXES, swaps(1, count))
    stats = lax.all_to_all(stats, AXES, 0, 0, tiled=True)
    even, odd, stats = [pltpu.with_memory_space_constraint(x, pltpu.VMEM) for x in (even, odd, stats)]
    operators = [pltpu.SMEM(diff_ops.shape, f32), pltpu.SMEM(lift.shape, f32)]
    cur, rates, geo, weights, ends = pl.pallas_call(
        functools.partial(first_kernel, sizes),
        name="first_stage",
        out_shape=(
            jax.ShapeDtypeStruct((30, sizes.tall, LANES), f32),
            jax.ShapeDtypeStruct((30, rows, LANES), f32),
            jax.ShapeDtypeStruct((15, rows, LANES), f32),
            jax.ShapeDtypeStruct((3 * PACK, 4 * WIDE), jnp.bfloat16),
            jax.ShapeDtypeStruct((2, slots, LANES), f32),
        ),
        in_specs=[HBM] * 5 + [VMEM] * 2 + [HBM] * 3,
        out_specs=(VMEM,) * 5,
        scratch_shapes=[
            pltpu.VMEM(state.shape, f32),
            *dense,
            *operators,
            pltpu.VMEM(prolong.shape, f32),
            pltpu.VMEM((8 * blocks, LANES), f32),
            pltpu.VMEM((PACK * blocks, LANES), f32),
            pltpu.VMEM((7, sizes.tall, LANES), f32),
            pltpu.SemaphoreType.DMA((8,)),
        ],
        compiler_params=PARAMS,
    )(state, depth, metric, partner, refine, even, odd, diff_ops, lift, prolong)
    refined = pl.pallas_call(
        functools.partial(second_kernel, sizes),
        name="second_stage_refine",
        out_shape=jax.ShapeDtypeStruct((10, 3, LANES * slots), f32),
        in_specs=[VMEM] * 6 + [HBM] * 2,
        out_specs=HBM,
        scratch_shapes=[
            *operators,
            pltpu.VMEM((10, 3, LANES * slots), f32),
            pltpu.VMEM((30, sizes.tall, LANES), f32),
            pltpu.VMEM((slots + 8, LANES), f32),
            pltpu.VMEM((8, LANES), i32),
            pltpu.SMEM((8, LANES), i32),
            pltpu.VMEM((WIDE * (slots + 1), LANES), f32),
            pltpu.VMEM((2, 8, LANES), f32),
            pltpu.VMEM((WIDE, LANES * slots), f32),
            pltpu.VMEM((3, slots, LANES), f32),
            pltpu.SemaphoreType.DMA((2,)),
            pltpu.SemaphoreType.DMA((slots // 8,)),
            pltpu.SemaphoreType.DMA,
        ],
        compiler_params=PARAMS,
    )(cur, rates, geo, weights, ends, stats, diff_ops, lift)
    return jnp.transpose(refined, (1, 0, 2))


def solution(mesh):
    return jax.shard_map(
        shards,
        mesh=mesh,
        in_specs=(
            P(None, None, AXES),
            P(AXES),
            P(None, AXES),
            P(AXES),
            P(AXES),
            P(),
            P(),
            P(),
        ),
        out_specs=P(None, None, AXES),
        check_vma=False,
    )
```

```python
import functools

import jax
import jax.numpy as jnp
from jax import lax
from jax.experimental import pallas as pl
from jax.experimental.pallas import tpu as pltpu
from jax.sharding import PartitionSpec as P

GRAVITY = 9.81
COURANT = 0.5
HIGH = lax.Precision.HIGHEST
LANES = 128
AXES = ("row", "col")
FACES = ((0, 1, 2, 3), (3, 6, 8, 9), (9, 7, 4, 0))
PACK = 40
WIDE = 32
PAD = 8

VMEM = pl.BlockSpec(memory_space=pltpu.VMEM)
HBM = pl.BlockSpec(memory_space=pltpu.HBM)
PARAMS = pltpu.CompilerParams(vmem_limit_bytes=48 * 1024 * 1024)


class Sizes:
    def __init__(self, cells):
        self.cells = cells
        self.blocks = cells // LANES
        self.margin = cells // 4 // LANES
        self.halo = self.margin + 1
        self.rows = -(-(self.blocks + 2 * self.halo) // 8) * 8
        self.tall = self.rows + 2 * PAD
        self.slots = 3 * self.blocks // 2
        self.keep = self.halo - self.margin


def fetch_all(pairs, sems):
    copies = [pltpu.make_async_copy(src, dst, sems.at[num]) for num, (src, dst) in enumerate(pairs)]
    for copy in copies:
        copy.start()
    return copies


def split_metric(metric_ref, spread, blocks):
    for block in range(blocks):
        spread[8 * block : 8 * block + 4, :] = metric_ref[:, LANES * block : LANES * (block + 1)]
    return [spread[pl.ds(comp, blocks, stride=8), :] for comp in range(4)]


def pack_kernel(
    sizes, state_hbm, depth_hbm, metric_hbm, partner_hbm, refine_hbm, stats_hbm, even_ref, odd_ref,
    stats_ref, state_even, state_odd, depth_ref, metric_ref, partner_ref, refine_ref, spread, sems, sem,
):
    blocks, halo = sizes.blocks, sizes.halo
    wide = LANES * halo
    late = blocks - halo
    even = (lax.axis_index(AXES) + 1) % 2 * late
    odd = late - even
    copies = fetch_all(
        (
            (depth_hbm, depth_ref),
            (metric_hbm, metric_ref),
            (refine_hbm, refine_ref),
            (partner_hbm, partner_ref),
            (state_hbm.at[:, :, pl.ds(pl.multiple_of(LANES * even, LANES), wide)], state_even),
            (state_hbm.at[:, :, pl.ds(pl.multiple_of(LANES * odd, LANES), wide)], state_odd),
        ),
        sems,
    )
    for copy in copies[:3]:
        copy.wait()
    rx, ry, sx, sy = split_metric(metric_ref, spread, blocks)
    depth = depth_ref[...]
    refine = refine_ref[...].astype(jnp.float32)
    faces = ((sx, sy), (rx + sx, ry + sy), (rx, ry))
    lengths = [jnp.sqrt(vx * vx + vy * vy) for vx, vy in faces]
    rate = jnp.sqrt(GRAVITY * depth) * jnp.maximum(jnp.maximum(lengths[0], lengths[1]), lengths[2])
    top = jnp.max(jnp.max(rate, axis=0, keepdims=True), axis=1, keepdims=True)
    extra = jnp.sum(jnp.sum(refine, axis=0, keepdims=True), axis=1, keepdims=True)
    shape = stats_ref.shape
    lane = lax.broadcasted_iota(jnp.int32, shape, 1)
    stats_ref[...] = jnp.where(
        lane < LANES // 2, jnp.broadcast_to(top, shape), jnp.broadcast_to(extra, shape)
    )
    sent = pltpu.make_async_copy(stats_ref, stats_hbm, sem)
    sent.start()
    for copy in copies[3:]:
        copy.wait()
    for ref, source, start in ((even_ref, state_even, even), (odd_ref, state_odd, odd)):
        pack_state(source, ref, halo)
        at = pl.ds(start, halo)
        dense = [depth_ref[at, :]]
        dense += [spread[pl.ds(8 * start + comp, halo, stride=8), :] for comp in range(4)]
        dense += [partner_ref[at, :].astype(jnp.float32), refine_ref[at, :].astype(jnp.float32)]
        for num, value in enumerate(dense):
            ref[pl.ds(4 * num + 3, halo, stride=PACK), :] = value
    sent.wait()


def pack_state(source, target, blocks):
    for block in range(blocks):
        for node in range(10):
            at = PACK * block + 4 * node
            target[at : at + 3, :] = source[node, :, LANES * block : LANES * (block + 1)]


def pair_index(partner):
    lane = lax.broadcasted_iota(jnp.int32, partner.shape, 1)
    target = lane + partner.astype(jnp.int32)
    return target & (LANES - 1), (target >= 0) & (target < LANES)


def lane_gather(values, index):
    return jnp.take_along_axis(values, index, axis=1, mode="promise_in_bounds")


def outer_values(load, index, inside):
    shape = index.shape
    lane = lax.broadcasted_iota(jnp.int32, shape, 1)

    def prev(item):
        return pltpu.roll(jnp.where(lane == LANES - 1, load(item, -1), load(item, 0)), 1, 1)

    def after(item):
        return pltpu.roll(jnp.where(lane == 0, load(item, 1), load(item, 0)), LANES - 1, 1)

    def across(item):
        other = jnp.where(lane < LANES // 2, load(item, 1), load(item, -1))
        return jnp.where(inside, lane_gather(load(item, 0), index), lane_gather(other, index))

    return prev, after, across


def wall_masks(sizes, start, place, count, partner):
    shape = partner.shape
    lane = lax.broadcasted_iota(jnp.int32, shape, 1)
    row = lax.broadcasted_iota(jnp.int32, shape, 0) + start
    first = (lane == 0) & (row == sizes.halo) & (place == 0)
    last = (lane == LANES - 1) & (row == sizes.halo + sizes.blocks - 1) & (place == count - 1)
    return first, last, partner == 0


def tendency(load, geo, walls, index, inside, diff_ref, lift_ref):
    speed_sq, rx, ry, sx, sy = geo[:5]
    outer_sq, waves, ghosts = geo[5:8], geo[8:11], geo[11:14]
    own = [[load(10 * field + node, 0) for node in range(10)] for field in range(3)]
    eta, mom_x, mom_y = own
    flow_r = [-(rx * mom_x[b] + ry * mom_y[b]) for b in range(10)]
    flow_s = [-(sx * mom_x[b] + sy * mom_y[b]) for b in range(10)]
    half_r = (0.5 * rx, 0.5 * ry)
    half_s = (0.5 * sx, 0.5 * sy)
    vectors = (
        (-half_s[0], -half_s[1]),
        (half_r[0] + half_s[0], half_r[1] + half_s[1]),
        (-half_r[0], -half_r[1]),
    )
    fetch = outer_values(load, index, inside)
    jumps = ([], [], [])
    for face in range(3):
        vec_x, vec_y = vectors[face]
        theirs = FACES[(1, 0, 2)[face]]
        wall = walls[face]
        for j in range(4):
            node, match = FACES[face][j], theirs[3 - j]
            in_eta, in_x, in_y = eta[node], mom_x[node], mom_y[node]
            ext_eta, ext_x, ext_y = [fetch[face](10 * field + match) for field in range(3)]
            bounce = (in_x * vec_x + in_y * vec_y) * ghosts[face]
            d_eta = jnp.where(wall, 0.0, in_eta - ext_eta)
            d_x = jnp.where(wall, bounce * vec_x, in_x - ext_x)
            d_y = jnp.where(wall, bounce * vec_y, in_y - ext_y)
            head = jnp.where(wall, 0.0, speed_sq * in_eta - outer_sq[face] * ext_eta)
            jumps[0].append(d_x * vec_x + d_y * vec_y - waves[face] * d_eta)
            jumps[1].append(head * vec_x - waves[face] * d_x)
            jumps[2].append(head * vec_y - waves[face] * d_y)
    pull = (-speed_sq * rx, -speed_sq * ry)
    push = (-speed_sq * sx, -speed_sq * sy)
    out = [[None] * 10 for _ in range(3)]
    for a in range(10):
        total = along_r = along_s = None
        for b in range(10):
            d_r, d_s = diff_ref[a, 0, b], diff_ref[a, 1, b]
            term = d_r * flow_r[b] + d_s * flow_s[b]
            total = term if b == 0 else total + term
            along_r = d_r * eta[b] if b == 0 else along_r + d_r * eta[b]
            along_s = d_s * eta[b] if b == 0 else along_s + d_s * eta[b]
        sums = [total, pull[0] * along_r + push[0] * along_s, pull[1] * along_r + push[1] * along_s]
        for q in range(12):
            weight = lift_ref[a, q]
            for field in range(3):
                sums[field] = sums[field] + weight * jumps[field][q]
        for field in range(3):
            out[field][a] = sums[field]
    return [out[field][a] for field in range(3) for a in range(10)]


def child_matrix(prolong_ref):
    f32 = jnp.float32
    node_r = lax.broadcasted_iota(jnp.int32, (PACK, 10), 0) // 4
    spread_r = (node_r == lax.broadcasted_iota(jnp.int32, (PACK, 10), 1)).astype(f32)
    item_c = lax.broadcasted_iota(jnp.int32, (10, WIDE), 1)
    spread_c = (item_c % 10 == lax.broadcasted_iota(jnp.int32, (10, WIDE), 0)).astype(f32)
    row = lax.broadcasted_iota(jnp.int32, (PACK, WIDE), 0)
    col = lax.broadcasted_iota(jnp.int32, (PACK, WIDE), 1)
    same = row % 4 == col // 10
    parts = []
    for child in range(2):
        left = jnp.dot(spread_r, prolong_ref[:, child, :], precision=HIGH, preferred_element_type=f32)
        full = jnp.dot(left, spread_c, precision=HIGH, preferred_element_type=f32)
        parts.append(jnp.where(same, full, 0.0))
    parts.append((same & (row // 4 == col % 10)).astype(f32))
    whole = jnp.concatenate(parts, axis=0)
    rounded = whole.astype(jnp.bfloat16)
    rest = (whole - rounded.astype(f32)).astype(jnp.bfloat16)
    return jnp.concatenate([rounded, rounded, rounded, rest], axis=1)


def sum_children(sizes, refine, ends_ref):
    slots, f32 = sizes.slots, jnp.float32
    counts = (1.0 + refine).astype(jnp.bfloat16)
    row_i = lax.broadcasted_iota(jnp.int32, (LANES, LANES), 0)
    col_i = lax.broadcasted_iota(jnp.int32, (LANES, LANES), 1)
    upper = (row_i <= col_i).astype(jnp.bfloat16)
    within = jnp.dot(counts, upper, preferred_element_type=f32)
    whole = jnp.dot(counts, jnp.ones((LANES, LANES), jnp.bfloat16), preferred_element_type=f32)
    row_s = lax.broadcasted_iota(jnp.int32, (slots, slots), 0)
    col_s = lax.broadcasted_iota(jnp.int32, (slots, slots), 1)
    lower = (col_s < row_s).astype(jnp.bfloat16)
    before = jnp.dot(lower, whole.astype(jnp.bfloat16), preferred_element_type=f32)
    before = before - before[sizes.margin : sizes.margin + 1, :]
    ends_ref[0] = 2.0 * (within + before) + refine
    ends_ref[1] = before + whole


def first_kernel(
    sizes, state_hbm, depth_hbm, metric_hbm, partner_hbm, refine_hbm, odd_ref, even_ref, diff_hbm, lift_hbm, prolong_hbm,
    cur, rate_ref, twice_ref, weights, ends_ref,
    geo_ref, state_ref, depth_ref, metric_ref, partner_ref, refine_ref, diff_ref, lift_ref, prolong_ref,
    spread, wide, aux, sems,
):
    blocks, halo = sizes.blocks, sizes.halo
    top, bottom = PAD + halo, PAD + halo + blocks
    place = lax.axis_index(AXES)
    count = lax.axis_size(AXES)
    copies = fetch_all(
        (
            (metric_hbm, metric_ref),
            (state_hbm, state_ref),
            (depth_hbm, depth_ref),
            (partner_hbm, partner_ref),
            (refine_hbm, refine_ref),
            (diff_hbm, diff_ref),
            (lift_hbm, lift_ref),
            (prolong_hbm, prolong_ref),
        ),
        sems,
    )
    for copy in copies:
        copy.wait()
    metric = split_metric(metric_ref, spread, blocks)
    dense = [depth_ref[...], *metric, partner_ref[...].astype(jnp.float32), refine_ref[...].astype(jnp.float32)]
    pack_state(state_ref, wide, blocks)
    even = place % 2 == 0

    def set_halo(target, num, row):
        by_even = even_ref[pl.ds(row, halo, stride=PACK), :]
        by_odd = odd_ref[pl.ds(row, halo, stride=PACK), :]
        target[num, top - halo : top, :] = jnp.where(even, by_odd, by_even)
        target[num, bottom : bottom + halo, :] = jnp.where(even, by_even, by_odd)

    for num in range(7):
        set_halo(aux, num, 4 * num + 3)
        aux[num, top:bottom, :] = dense[num]
    for field in range(3):
        for node in range(10):
            item = 10 * field + node
            set_halo(cur, item, 4 * node + field)
            cur[item, top:bottom, :] = wide[pl.ds(4 * node + field, blocks, stride=PACK), :]

    weights[...] = child_matrix(prolong_ref)
    begin = PAD + sizes.keep
    sum_children(sizes, aux[6, begin : begin + sizes.slots, :], ends_ref)

    def step(group, carry):
        base = PAD + 8 * group

        def load_aux(item, shift):
            return aux[item, pl.ds(base + shift, 8), :]

        def load(item, shift):
            return cur[item, pl.ds(base + shift, 8), :]

        depth, rx, ry, sx, sy, partner = [load_aux(num, 0) for num in range(6)]
        index, inside = pair_index(partner)
        fetch = outer_values(load_aux, index, inside)
        walls = wall_masks(sizes, 8 * group, place, count, partner)
        speed_sq = GRAVITY * depth
        outer_sq = [jnp.where(walls[k], speed_sq, GRAVITY * fetch[k](0)) for k in range(3)]
        faces = ((sx, sy), (rx + sx, ry + sy), (rx, ry))
        squares = [vx * vx + vy * vy for vx, vy in faces]
        waves = [
            0.5 * jnp.sqrt(squares[k]) * jnp.sqrt(jnp.maximum(speed_sq, outer_sq[k])) for k in range(3)
        ]
        ghosts = [8.0 / squares[k] for k in range(3)]
        geo = [speed_sq, rx, ry, sx, sy, *outer_sq, *waves, *ghosts]
        rates = tendency(load, geo, walls, index, inside, diff_ref, lift_ref)
        at = pl.ds(pl.multiple_of(8 * group, 8), 8)
        for num, value in enumerate([*geo, partner]):
            geo_ref[num, at, :] = value
        for item in range(30):
            rate_ref[item, pl.ds(base, 8), :] = rates[item]
        return carry

    lax.fori_loop(0, sizes.rows // 8, step, 0)

    def again(group, carry):
        row = 8 * group + sizes.keep
        at = pl.ds(row, 8)

        def load(item, shift):
            return rate_ref[item, pl.ds(PAD + row + shift, 8), :]

        geo = [geo_ref[num, at, :] for num in range(14)]
        partner = geo_ref[14, at, :]
        index, inside = pair_index(partner)
        walls = wall_masks(sizes, row, place, count, partner)
        rates = tendency(load, geo, walls, index, inside, diff_ref, lift_ref)
        for item in range(30):
            twice_ref[item, pl.ds(pl.multiple_of(8 * group, 8), 8), :] = rates[item]
        return carry

    lax.fori_loop(0, sizes.slots // 8, again, 0)


def refine_kernel(
    sizes, cur, rate_ref, twice_ref, weights, base_ref, stats_ref, out_hbm,
    out_ref, ends_ref, place_v, place_s, wide, gathered, index_ref, out_sems, sem,
):
    slots, keep = sizes.slots, sizes.keep
    place = lax.axis_index(AXES)
    stats = stats_ref[...]
    half = LANES // 2
    row_n = lax.broadcasted_iota(jnp.int32, stats.shape, 0)
    top = jnp.max(stats, axis=0, keepdims=True)
    earlier = jnp.sum(jnp.where(row_n < place, stats, 0.0), axis=0, keepdims=True)
    left = lax.broadcasted_iota(jnp.int32, (1, LANES), 1) < half
    top = jnp.where(left, top, pltpu.roll(top, half, 1))
    earlier = jnp.where(left, pltpu.roll(earlier, half, 1), earlier)
    step = COURANT / top
    half_square = 0.5 * step * step
    start = earlier - (place * (sizes.cells // 2)).astype(jnp.float32)
    ends_ref[:slots, :] = base_ref[0] + 2.0 * start
    ends_ref[slots:, :] = jnp.full((8, LANES), 1e9, jnp.float32)
    first_slot = LANES * lax.broadcasted_iota(jnp.int32, (slots, LANES), 1).astype(jnp.float32)
    lead = jnp.sum((base_ref[1] + start <= first_slot).astype(jnp.float32), axis=0, keepdims=True)
    lead = jnp.clip(lead.astype(jnp.int32), 0, slots - 1)
    place_v[...] = jnp.broadcast_to(lead, (8, LANES))
    copy = pltpu.make_async_copy(place_v, place_s, sem)
    copy.start()
    for item in range(30):
        now = slice(PAD + keep, PAD + keep + slots)
        value = cur[item, now, :] + step * rate_ref[item, now, :] + half_square * twice_ref[item]
        wide[pl.ds(item, slots, stride=WIDE), :] = value
    for item in (30, 31):
        wide[pl.ds(item, slots + 1, stride=WIDE), :] = jnp.zeros((slots + 1, LANES), jnp.float32)
    copy.wait()
    for slot in range(slots):
        lead_at = place_s[0, slot]
        index_ref[0, slot : slot + 1, :] = ends_ref[pl.ds(lead_at, 1), :]
        index_ref[1, slot : slot + 1, :] = ends_ref[pl.ds(lead_at + 1, 1), :]
    near, far = index_ref[0], index_ref[1]
    lane = lax.broadcasted_iota(jnp.int32, (slots, LANES), 1)
    slot_no = LANES * lax.broadcasted_iota(jnp.int32, (slots, LANES), 0) + lane
    goal = (2 * slot_no + 1).astype(jnp.float32)
    beyond = jnp.broadcast_to(near[:, LANES - 1 :], (slots, LANES)) <= goal

    def pick(index):
        return jnp.where(beyond, lane_gather(far, index), lane_gather(near, index))

    found = jnp.zeros((slots, LANES), jnp.int32)
    size = LANES // 2
    while size:
        passed = pick(found + (size - 1)) <= goal
        found = jnp.where(passed, found + size, found)
        size //= 2
    mine = pick(found).astype(jnp.int32)
    split = mine & 1
    begin = (mine >> 1) - 1 - split
    kind = split * (1 + slot_no - begin)
    index_ref[0] = found.astype(jnp.float32)
    index_ref[1] = kind.astype(jnp.float32)
    index_ref[2] = (lane < jnp.broadcast_to(found[:, 0:1], (slots, LANES))).astype(jnp.float32)
    for slot in range(slots):
        lead_at = place_s[0, slot] * WIDE
        lane_idx = jnp.broadcast_to(index_ref[0, slot : slot + 1, :], (8, LANES)).astype(jnp.int32)
        ahead = jnp.broadcast_to(index_ref[2, slot : slot + 1, :], (8, LANES)) > 0.5
        for part in range(0, WIDE, 8):
            one = wide[pl.ds(pl.multiple_of(lead_at + part, 8), 8), :]
            two = wide[pl.ds(pl.multiple_of(lead_at + WIDE + part, 8), 8), :]
            gathered[part : part + 8, LANES * slot : LANES * (slot + 1)] = lane_gather(
                jnp.where(ahead, two, one), lane_idx
            )
    matrix = weights[...]
    chunk = 8 * LANES
    results = []
    for part in range(slots // 8):
        span = slice(chunk * part, chunk * (part + 1))
        values = gathered[:, span]
        high = values.astype(jnp.bfloat16)
        rest = values - high.astype(jnp.float32)
        low = rest.astype(jnp.bfloat16)
        last = (rest - low.astype(jnp.float32)).astype(jnp.bfloat16)
        stack = jnp.concatenate([high, low, last, high], axis=0)
        children = jnp.dot(matrix, stack, preferred_element_type=jnp.float32)
        for sub in range(8):
            slot = 8 * part + sub
            cut = slice(LANES * sub, LANES * (sub + 1))
            tag = jnp.broadcast_to(index_ref[1, slot : slot + 1, :], (PACK, LANES))
            value = jnp.where(
                tag < 0.5,
                children[2 * PACK :, cut],
                jnp.where(tag < 1.5, children[:PACK, cut], children[PACK : 2 * PACK, cut]),
            )
            for node in range(10):
                out_ref[node, :, LANES * slot : LANES * (slot + 1)] = value[4 * node : 4 * node + 3]
        result = pltpu.make_async_copy(out_ref.at[:, :, span], out_hbm.at[:, :, span], out_sems.at[part])
        result.start()
        results.append(result)
    for result in results:
        result.wait()


def swaps(start, count):
    pairs = [(i, i + 1) for i in range(start, count - 1, 2)]
    return pairs + [(j, i) for i, j in pairs]


def shards(state, depth, metric, partner, refine, diff_ops, lift, prolong):
    sizes = Sizes(state.shape[2])
    count = lax.axis_size(AXES)
    blocks, rows, slots, halo = sizes.blocks, sizes.rows, sizes.slots, sizes.halo
    depth, partner, refine = [x.reshape(blocks, LANES) for x in (depth, partner, refine)]
    state, diff_ops, prolong = [jnp.transpose(x, (1, 0, 2)) for x in (state, diff_ops, prolong)]
    state, depth, metric, partner, refine, diff_ops, lift, prolong = [
        pltpu.with_memory_space_constraint(x, pltpu.HBM)
        for x in (state, depth, metric, partner, refine, diff_ops, lift, prolong)
    ]
    f32, i32 = jnp.float32, jnp.int32
    packed = jax.ShapeDtypeStruct((PACK * halo, LANES), f32)
    dense = [
        pltpu.VMEM((blocks, LANES), f32),
        pltpu.VMEM(metric.shape, f32),
        pltpu.VMEM((blocks, LANES), i32),
        pltpu.VMEM((blocks, LANES), i32),
    ]
    stats, even, odd = pl.pallas_call(
        functools.partial(pack_kernel, sizes),
        name="pack",
        out_shape=(jax.ShapeDtypeStruct((count, LANES), f32), packed, packed),
        in_specs=[HBM] * 5,
        out_specs=(HBM, VMEM, VMEM),
        scratch_shapes=[
            pltpu.VMEM((count, LANES), f32),
            pltpu.VMEM((10, 3, LANES * halo), f32),
            pltpu.VMEM((10, 3, LANES * halo), f32),
            *dense,
            pltpu.VMEM((8 * blocks, LANES), f32),
            pltpu.SemaphoreType.DMA((6,)),
            pltpu.SemaphoreType.DMA,
        ],
        compiler_params=PARAMS,
    )(state, depth, metric, partner, refine)
    odd = lax.ppermute(odd, AXES, swaps(1, count))
    even = lax.ppermute(even, AXES, swaps(0, count))
    stats = lax.all_to_all(stats, AXES, 0, 0, tiled=True)
    even, odd, stats = [pltpu.with_memory_space_constraint(x, pltpu.VMEM) for x in (even, odd, stats)]
    cur, rates, twice, weights, ends = pl.pallas_call(
        functools.partial(first_kernel, sizes),
        name="rates_twice",
        out_shape=(
            jax.ShapeDtypeStruct((30, sizes.tall, LANES), f32),
            jax.ShapeDtypeStruct((30, sizes.tall, LANES), f32),
            jax.ShapeDtypeStruct((30, slots, LANES), f32),
            jax.ShapeDtypeStruct((3 * PACK, 4 * WIDE), jnp.bfloat16),
            jax.ShapeDtypeStruct((2, slots, LANES), f32),
        ),
        in_specs=[HBM] * 5 + [VMEM] * 2 + [HBM] * 3,
        out_specs=(VMEM,) * 5,
        scratch_shapes=[
            pltpu.VMEM((15, rows, LANES), f32),
            pltpu.VMEM(state.shape, f32),
            *dense,
            pltpu.SMEM(diff_ops.shape, f32),
            pltpu.SMEM(lift.shape, f32),
            pltpu.VMEM(prolong.shape, f32),
            pltpu.VMEM((8 * blocks, LANES), f32),
            pltpu.VMEM((PACK * blocks, LANES), f32),
            pltpu.VMEM((7, sizes.tall, LANES), f32),
            pltpu.SemaphoreType.DMA((8,)),
        ],
        compiler_params=PARAMS,
    )(state, depth, metric, partner, refine, odd, even, diff_ops, lift, prolong)
    refined = pl.pallas_call(
        functools.partial(refine_kernel, sizes),
        name="sum_and_refine",
        out_shape=jax.ShapeDtypeStruct((10, 3, LANES * slots), f32),
        in_specs=[VMEM] * 6,
        out_specs=HBM,
        scratch_shapes=[
            pltpu.VMEM((10, 3, LANES * slots), f32),
            pltpu.VMEM((slots + 8, LANES), f32),
            pltpu.VMEM((8, LANES), i32),
            pltpu.SMEM((8, LANES), i32),
            pltpu.VMEM((WIDE * (slots + 1), LANES), f32),
            pltpu.VMEM((WIDE, LANES * slots), f32),
            pltpu.VMEM((3, slots, LANES), f32),
            pltpu.SemaphoreType.DMA((slots // 8,)),
            pltpu.SemaphoreType.DMA,
        ],
        compiler_params=PARAMS,
    )(cur, rates, twice, weights, ends, stats)
    return jnp.transpose(refined, (1, 0, 2))


def solution(mesh):
    return jax.shard_map(
        shards,
        mesh=mesh,
        in_specs=(
            P(None, None, AXES),
            P(AXES),
            P(None, AXES),
            P(AXES),
            P(AXES),
            P(),
            P(),
            P(),
        ),
        out_specs=P(None, None, AXES),
        check_vma=False,
    )
```

```python
import functools

import jax
import jax.numpy as jnp
from jax import lax
from jax.experimental import pallas as pl
from jax.experimental.pallas import tpu as pltpu
from jax.sharding import PartitionSpec as P

GRAVITY = 9.81
COURANT = 0.5
HIGH = lax.Precision.HIGHEST
LANES = 128
AXES = ("row", "col")
FACES = ((0, 1, 2, 3), (3, 6, 8, 9), (9, 7, 4, 0))
PACK = 40
SENT = 37
WIDE = 32
PAD = 8

VMEM = pl.BlockSpec(memory_space=pltpu.VMEM)
HBM = pl.BlockSpec(memory_space=pltpu.HBM)
PARAMS = pltpu.CompilerParams(vmem_limit_bytes=48 * 1024 * 1024)


class Sizes:
    def __init__(self, cells):
        self.cells = cells
        self.blocks = cells // LANES
        self.margin = cells // 4 // LANES
        self.halo = self.margin + 1
        self.tall = self.blocks + 2 * PAD
        self.side = self.halo + 3
        self.strip = -(-2 * self.side // 8) * 8
        self.strip_tall = self.strip + 2 * PAD
        self.slots = 3 * self.blocks // 2


def fetch_all(pairs, sems):
    copies = [pltpu.make_async_copy(src, dst, sems.at[num]) for num, (src, dst) in enumerate(pairs)]
    for copy in copies:
        copy.start()
    return copies


def split_metric(metric_ref, spread, blocks):
    for block in range(blocks):
        spread[8 * block : 8 * block + 4, :] = metric_ref[:, LANES * block : LANES * (block + 1)]
    return [spread[pl.ds(comp, blocks, stride=8), :] for comp in range(4)]


def pack_kernel(
    sizes, state_hbm, depth_hbm, metric_hbm, partner_hbm, refine_hbm, stats_hbm, even_ref, odd_ref,
    stats_ref, state_even, state_odd, depth_ref, metric_ref, partner_ref, refine_ref, spread, sems, sem,
):
    blocks, halo = sizes.blocks, sizes.halo
    wide = LANES * halo
    late = blocks - halo
    even = (lax.axis_index(AXES) + 1) % 2 * late
    odd = late - even
    copies = fetch_all(
        (
            (depth_hbm, depth_ref),
            (metric_hbm, metric_ref),
            (refine_hbm, refine_ref),
            (partner_hbm, partner_ref),
            (state_hbm.at[:, :, pl.ds(pl.multiple_of(LANES * even, LANES), wide)], state_even),
            (state_hbm.at[:, :, pl.ds(pl.multiple_of(LANES * odd, LANES), wide)], state_odd),
        ),
        sems,
    )
    for copy in copies[:3]:
        copy.wait()
    rx, ry, sx, sy = split_metric(metric_ref, spread, blocks)
    depth = depth_ref[...]
    refine = refine_ref[...].astype(jnp.float32)
    faces = ((sx, sy), (rx + sx, ry + sy), (rx, ry))
    lengths = [jnp.sqrt(vx * vx + vy * vy) for vx, vy in faces]
    rate = jnp.sqrt(GRAVITY * depth) * jnp.maximum(jnp.maximum(lengths[0], lengths[1]), lengths[2])
    top = jnp.max(jnp.max(rate, axis=0, keepdims=True), axis=1, keepdims=True)
    extra = jnp.sum(jnp.sum(refine, axis=0, keepdims=True), axis=1, keepdims=True)
    shape = stats_ref.shape
    lane = lax.broadcasted_iota(jnp.int32, shape, 1)
    stats_ref[...] = jnp.where(
        lane < LANES // 2, jnp.broadcast_to(top, shape), jnp.broadcast_to(extra, shape)
    )
    sent = pltpu.make_async_copy(stats_ref, stats_hbm, sem)
    sent.start()
    for copy in copies[3:]:
        copy.wait()
    for ref, source, start in ((even_ref, state_even, even), (odd_ref, state_odd, odd)):
        pack_state(source, ref, halo, SENT, 3)
        at = pl.ds(start, halo)
        dense = [depth_ref[at, :]]
        dense += [spread[pl.ds(8 * start + comp, halo, stride=8), :] for comp in range(4)]
        dense += [partner_ref[at, :].astype(jnp.float32), refine_ref[at, :].astype(jnp.float32)]
        for num, value in enumerate(dense):
            ref[pl.ds(30 + num, halo, stride=SENT), :] = value
    sent.wait()


def pack_state(source, target, blocks, height, width):
    for block in range(blocks):
        for node in range(10):
            at = height * block + width * node
            target[at : at + 3, :] = source[node, :, LANES * block : LANES * (block + 1)]


def pair_index(partner):
    lane = lax.broadcasted_iota(jnp.int32, partner.shape, 1)
    target = lane + partner.astype(jnp.int32)
    return target & (LANES - 1), (target >= 0) & (target < LANES)


def lane_gather(values, index):
    return jnp.take_along_axis(values, index, axis=1, mode="promise_in_bounds")


def outer_values(load, index, inside):
    shape = index.shape
    lane = lax.broadcasted_iota(jnp.int32, shape, 1)

    def prev(item):
        return pltpu.roll(jnp.where(lane == LANES - 1, load(item, -1), load(item, 0)), 1, 1)

    def after(item):
        return pltpu.roll(jnp.where(lane == 0, load(item, 1), load(item, 0)), LANES - 1, 1)

    def across(item):
        other = jnp.where(lane < LANES // 2, load(item, 1), load(item, -1))
        return jnp.where(inside, lane_gather(load(item, 0), index), lane_gather(other, index))

    return prev, after, across


def wall_masks(start, first_row, last_row, place, count, partner):
    shape = partner.shape
    lane = lax.broadcasted_iota(jnp.int32, shape, 1)
    row = lax.broadcasted_iota(jnp.int32, shape, 0) + start
    first = (lane == 0) & (row == first_row) & (place == 0)
    last = (lane == LANES - 1) & (row == last_row) & (place == count - 1)
    return first, last, partner == 0


def tendency(load, geo, walls, index, inside, diff_ref, lift_ref):
    speed_sq, rx, ry, sx, sy = geo[:5]
    outer_sq, waves, ghosts = geo[5:8], geo[8:11], geo[11:14]
    own = [[load(10 * field + node, 0) for node in range(10)] for field in range(3)]
    eta, mom_x, mom_y = own
    flow_r = [-(rx * mom_x[b] + ry * mom_y[b]) for b in range(10)]
    flow_s = [-(sx * mom_x[b] + sy * mom_y[b]) for b in range(10)]
    half_r = (0.5 * rx, 0.5 * ry)
    half_s = (0.5 * sx, 0.5 * sy)
    vectors = (
        (-half_s[0], -half_s[1]),
        (half_r[0] + half_s[0], half_r[1] + half_s[1]),
        (-half_r[0], -half_r[1]),
    )
    fetch = outer_values(load, index, inside)
    jumps = ([], [], [])
    for face in range(3):
        vec_x, vec_y = vectors[face]
        theirs = FACES[(1, 0, 2)[face]]
        wall = walls[face]
        for j in range(4):
            node, match = FACES[face][j], theirs[3 - j]
            in_eta, in_x, in_y = eta[node], mom_x[node], mom_y[node]
            ext_eta, ext_x, ext_y = [fetch[face](10 * field + match) for field in range(3)]
            bounce = (in_x * vec_x + in_y * vec_y) * ghosts[face]
            d_eta = jnp.where(wall, 0.0, in_eta - ext_eta)
            d_x = jnp.where(wall, bounce * vec_x, in_x - ext_x)
            d_y = jnp.where(wall, bounce * vec_y, in_y - ext_y)
            head = jnp.where(wall, 0.0, speed_sq * in_eta - outer_sq[face] * ext_eta)
            jumps[0].append(d_x * vec_x + d_y * vec_y - waves[face] * d_eta)
            jumps[1].append(head * vec_x - waves[face] * d_x)
            jumps[2].append(head * vec_y - waves[face] * d_y)
    pull = (-speed_sq * rx, -speed_sq * ry)
    push = (-speed_sq * sx, -speed_sq * sy)
    out = [[None] * 10 for _ in range(3)]
    for a in range(10):
        total = along_r = along_s = None
        for b in range(10):
            d_r, d_s = diff_ref[a, 0, b], diff_ref[a, 1, b]
            term = d_r * flow_r[b] + d_s * flow_s[b]
            total = term if b == 0 else total + term
            along_r = d_r * eta[b] if b == 0 else along_r + d_r * eta[b]
            along_s = d_s * eta[b] if b == 0 else along_s + d_s * eta[b]
        sums = [total, pull[0] * along_r + push[0] * along_s, pull[1] * along_r + push[1] * along_s]
        for q in range(12):
            weight = lift_ref[a, q]
            for field in range(3):
                sums[field] = sums[field] + weight * jumps[field][q]
        for field in range(3):
            out[field][a] = sums[field]
    return [out[field][a] for field in range(3) for a in range(10)]


def child_matrix(prolong_ref):
    f32 = jnp.float32
    node_r = lax.broadcasted_iota(jnp.int32, (PACK, 10), 0) // 4
    spread_r = (node_r == lax.broadcasted_iota(jnp.int32, (PACK, 10), 1)).astype(f32)
    item_c = lax.broadcasted_iota(jnp.int32, (10, WIDE), 1)
    spread_c = (item_c % 10 == lax.broadcasted_iota(jnp.int32, (10, WIDE), 0)).astype(f32)
    row = lax.broadcasted_iota(jnp.int32, (PACK, WIDE), 0)
    col = lax.broadcasted_iota(jnp.int32, (PACK, WIDE), 1)
    same = row % 4 == col // 10
    parts = []
    for child in range(2):
        left = jnp.dot(spread_r, prolong_ref[:, child, :], precision=HIGH, preferred_element_type=f32)
        full = jnp.dot(left, spread_c, precision=HIGH, preferred_element_type=f32)
        parts.append(jnp.where(same, full, 0.0))
    parts.append((same & (row // 4 == col % 10)).astype(f32))
    whole = jnp.concatenate(parts, axis=0)
    rounded = whole.astype(jnp.bfloat16)
    rest = (whole - rounded.astype(f32)).astype(jnp.bfloat16)
    return jnp.concatenate([rounded, rounded, rounded, rest], axis=1)


def sum_children(sizes, refine, ends_ref):
    slots, f32 = sizes.slots, jnp.float32
    counts = (1.0 + refine).astype(jnp.bfloat16)
    row_i = lax.broadcasted_iota(jnp.int32, (LANES, LANES), 0)
    col_i = lax.broadcasted_iota(jnp.int32, (LANES, LANES), 1)
    upper = (row_i <= col_i).astype(jnp.bfloat16)
    within = jnp.dot(counts, upper, preferred_element_type=f32)
    whole = jnp.dot(counts, jnp.ones((LANES, LANES), jnp.bfloat16), preferred_element_type=f32)
    row_s = lax.broadcasted_iota(jnp.int32, (slots, slots), 0)
    col_s = lax.broadcasted_iota(jnp.int32, (slots, slots), 1)
    lower = (col_s < row_s).astype(jnp.bfloat16)
    before = jnp.dot(lower, whole.astype(jnp.bfloat16), preferred_element_type=f32)
    before = before - before[sizes.margin : sizes.margin + 1, :]
    ends_ref[0] = 2.0 * (within + before) + refine
    ends_ref[1] = before + whole


def rates_of_state(groups, ends, cur, aux, diff_ref, lift_ref, geo_ref, rate_ref):
    place, count = lax.axis_index(AXES), lax.axis_size(AXES)

    def step(group, carry):
        base = PAD + 8 * group

        def load_aux(item, shift):
            return aux[item, pl.ds(base + shift, 8), :]

        def load(item, shift):
            return cur[item, pl.ds(base + shift, 8), :]

        depth, rx, ry, sx, sy, partner = [load_aux(num, 0) for num in range(6)]
        index, inside = pair_index(partner)
        fetch = outer_values(load_aux, index, inside)
        walls = wall_masks(8 * group, *ends, place, count, partner)
        speed_sq = GRAVITY * depth
        outer_sq = [jnp.where(walls[k], speed_sq, GRAVITY * fetch[k](0)) for k in range(3)]
        faces = ((sx, sy), (rx + sx, ry + sy), (rx, ry))
        squares = [vx * vx + vy * vy for vx, vy in faces]
        waves = [
            0.5 * jnp.sqrt(squares[k]) * jnp.sqrt(jnp.maximum(speed_sq, outer_sq[k])) for k in range(3)
        ]
        ghosts = [8.0 / squares[k] for k in range(3)]
        geo = [speed_sq, rx, ry, sx, sy, *outer_sq, *waves, *ghosts]
        rates = tendency(load, geo, walls, index, inside, diff_ref, lift_ref)
        at = pl.ds(pl.multiple_of(8 * group, 8), 8)
        for num, value in enumerate([*geo, partner]):
            geo_ref[num, at, :] = value
        for item in range(30):
            rate_ref[item, pl.ds(pl.multiple_of(base, 8), 8), :] = rates[item]
        return carry

    lax.fori_loop(0, groups, step, 0)


def rates_of_rates(groups, ends, rate_ref, diff_ref, lift_ref, geo_ref, twice_ref):
    place, count = lax.axis_index(AXES), lax.axis_size(AXES)

    def step(group, carry):
        base = PAD + 8 * group
        at = pl.ds(pl.multiple_of(8 * group, 8), 8)

        def load(item, shift):
            return rate_ref[item, pl.ds(base + shift, 8), :]

        geo = [geo_ref[num, at, :] for num in range(14)]
        partner = geo_ref[14, at, :]
        index, inside = pair_index(partner)
        walls = wall_masks(8 * group, *ends, place, count, partner)
        rates = tendency(load, geo, walls, index, inside, diff_ref, lift_ref)
        for item in range(30):
            twice_ref[item, at, :] = rates[item]
        return carry

    lax.fori_loop(0, groups, step, 0)


def own_kernel(
    sizes, state_hbm, depth_hbm, metric_hbm, partner_hbm, refine_hbm, diff_hbm, lift_hbm, prolong_hbm,
    cur, aux, rate_ref, twice_ref, weights,
    geo_ref, state_ref, depth_ref, metric_ref, partner_ref, refine_ref, diff_ref, lift_ref, prolong_ref,
    spread, wide, sems,
):
    blocks = sizes.blocks
    now = slice(PAD, PAD + blocks)
    copies = fetch_all(
        (
            (metric_hbm, metric_ref),
            (state_hbm, state_ref),
            (depth_hbm, depth_ref),
            (partner_hbm, partner_ref),
            (refine_hbm, refine_ref),
            (diff_hbm, diff_ref),
            (lift_hbm, lift_ref),
            (prolong_hbm, prolong_ref),
        ),
        sems,
    )
    for copy in copies:
        copy.wait()
    metric = split_metric(metric_ref, spread, blocks)
    dense = [depth_ref[...], *metric, partner_ref[...].astype(jnp.float32), refine_ref[...].astype(jnp.float32)]
    for num in range(7):
        aux[num, now, :] = dense[num]
    pack_state(state_ref, wide, blocks, PACK, 4)
    for field in range(3):
        for node in range(10):
            cur[10 * field + node, now, :] = wide[pl.ds(4 * node + field, blocks, stride=PACK), :]
    weights[...] = child_matrix(prolong_ref)
    ends = (0, blocks - 1)
    rates_of_state(blocks // 8, ends, cur, aux, diff_ref, lift_ref, geo_ref, rate_ref)
    rates_of_rates(blocks // 8, ends, rate_ref, diff_ref, lift_ref, geo_ref, twice_ref)


def strip_kernel(
    sizes, cur_own, aux_own, rate_own, odd_ref, even_ref, diff_hbm, lift_hbm,
    cur, rate_ref, twice_ref, ends_ref, aux, geo_ref, diff_ref, lift_ref, refine_ref, sems,
):
    blocks, halo, side, margin = sizes.blocks, sizes.halo, sizes.side, sizes.margin
    copies = fetch_all(((diff_hbm, diff_ref), (lift_hbm, lift_ref)), sems)
    even = lax.axis_index(AXES) % 2 == 0

    def fill(target, source, num, row):
        by_even = even_ref[pl.ds(row, halo, stride=SENT), :]
        by_odd = odd_ref[pl.ds(row, halo, stride=SENT), :]
        target[num, PAD : PAD + halo, :] = jnp.where(even, by_odd, by_even)
        target[num, PAD + halo : PAD + side, :] = source[num, PAD : PAD + 3, :]
        target[num, PAD + side : PAD + side + 3, :] = source[num, PAD + blocks - 3 : PAD + blocks, :]
        target[num, PAD + side + 3 : PAD + 2 * side, :] = jnp.where(even, by_even, by_odd)

    for num in range(7):
        fill(aux, aux_own, num, 30 + num)
    for field in range(3):
        for node in range(10):
            fill(cur, cur_own, 10 * field + node, 3 * node + field)
    refine_ref[:margin, :] = aux[6, PAD + 1 : PAD + 1 + margin, :]
    refine_ref[margin : margin + blocks, :] = aux_own[6, PAD : PAD + blocks, :]
    refine_ref[margin + blocks :, :] = aux[6, PAD + side + 3 : PAD + side + 3 + margin, :]
    sum_children(sizes, refine_ref[...], ends_ref)
    for copy in copies:
        copy.wait()
    ends = (halo, side + 2)
    rates_of_state(sizes.strip // 8, ends, cur, aux, diff_ref, lift_ref, geo_ref, rate_ref)
    for item in range(30):
        for row, block in ((side - 1, 2), (side, blocks - 3)):
            rate_ref[item, PAD + row : PAD + row + 1, :] = rate_own[item, PAD + block : PAD + block + 1, :]
    rates_of_rates(sizes.strip // 8, ends, rate_ref, diff_ref, lift_ref, geo_ref, twice_ref)


def refine_kernel(
    sizes, cur_own, rate_own, twice_own, cur, rate_ref, twice_ref, weights, base_ref, stats_ref, out_hbm,
    out_ref, ends_ref, place_v, place_s, wide, gathered, index_ref, out_sems, sem,
):
    slots, blocks, side, outer = sizes.slots, sizes.blocks, sizes.side, sizes.margin + 2
    place = lax.axis_index(AXES)
    stats = stats_ref[...]
    half = LANES // 2
    row_n = lax.broadcasted_iota(jnp.int32, stats.shape, 0)
    top = jnp.max(stats, axis=0, keepdims=True)
    earlier = jnp.sum(jnp.where(row_n < place, stats, 0.0), axis=0, keepdims=True)
    left = lax.broadcasted_iota(jnp.int32, (1, LANES), 1) < half
    top = jnp.where(left, top, pltpu.roll(top, half, 1))
    earlier = jnp.where(left, pltpu.roll(earlier, half, 1), earlier)
    step = COURANT / top
    half_square = 0.5 * step * step
    start = earlier - (place * (sizes.cells // 2)).astype(jnp.float32)
    ends_ref[:slots, :] = base_ref[0] + 2.0 * start
    ends_ref[slots:, :] = jnp.full((8, LANES), 1e9, jnp.float32)
    first_slot = LANES * lax.broadcasted_iota(jnp.int32, (slots, LANES), 1).astype(jnp.float32)
    lead = jnp.sum((base_ref[1] + start <= first_slot).astype(jnp.float32), axis=0, keepdims=True)
    lead = jnp.clip(lead.astype(jnp.int32), 0, slots - 1)
    place_v[...] = jnp.broadcast_to(lead, (8, LANES))
    copy = pltpu.make_async_copy(place_v, place_s, sem)
    copy.start()
    for item in range(30):
        for to, rows, start_row, refs in (
            (0, outer, 1, (cur, rate_ref, twice_ref)),
            (outer, blocks - 4, 2, (cur_own, rate_own, twice_own)),
            (slots - outer, outer, side + 1, (cur, rate_ref, twice_ref)),
        ):
            now = slice(PAD + start_row, PAD + start_row + rows)
            once = refs[0][item, now, :] + step * refs[1][item, now, :]
            value = once + half_square * refs[2][item, start_row : start_row + rows, :]
            wide[pl.ds(WIDE * to + item, rows, stride=WIDE), :] = value
    for item in (30, 31):
        wide[pl.ds(item, slots + 1, stride=WIDE), :] = jnp.zeros((slots + 1, LANES), jnp.float32)
    copy.wait()
    for slot in range(slots):
        lead_at = place_s[0, slot]
        index_ref[0, slot : slot + 1, :] = ends_ref[pl.ds(lead_at, 1), :]
        index_ref[1, slot : slot + 1, :] = ends_ref[pl.ds(lead_at + 1, 1), :]
    near, far = index_ref[0], index_ref[1]
    lane = lax.broadcasted_iota(jnp.int32, (slots, LANES), 1)
    slot_no = LANES * lax.broadcasted_iota(jnp.int32, (slots, LANES), 0) + lane
    goal = (2 * slot_no + 1).astype(jnp.float32)
    beyond = jnp.broadcast_to(near[:, LANES - 1 :], (slots, LANES)) <= goal

    def pick(index):
        return jnp.where(beyond, lane_gather(far, index), lane_gather(near, index))

    found = jnp.zeros((slots, LANES), jnp.int32)
    size = LANES // 2
    while size:
        passed = pick(found + (size - 1)) <= goal
        found = jnp.where(passed, found + size, found)
        size //= 2
    mine = pick(found).astype(jnp.int32)
    split = mine & 1
    begin = (mine >> 1) - 1 - split
    kind = split * (1 + slot_no - begin)
    index_ref[0] = found.astype(jnp.float32)
    index_ref[1] = kind.astype(jnp.float32)
    index_ref[2] = (lane < jnp.broadcast_to(found[:, 0:1], (slots, LANES))).astype(jnp.float32)
    for slot in range(slots):
        lead_at = place_s[0, slot] * WIDE
        lane_idx = jnp.broadcast_to(index_ref[0, slot : slot + 1, :], (8, LANES)).astype(jnp.int32)
        ahead = jnp.broadcast_to(index_ref[2, slot : slot + 1, :], (8, LANES)) > 0.5
        for part in range(0, WIDE, 8):
            one = wide[pl.ds(pl.multiple_of(lead_at + part, 8), 8), :]
            two = wide[pl.ds(pl.multiple_of(lead_at + WIDE + part, 8), 8), :]
            gathered[part : part + 8, LANES * slot : LANES * (slot + 1)] = lane_gather(
                jnp.where(ahead, two, one), lane_idx
            )
    matrix = weights[...]
    chunk = 8 * LANES
    results = []
    for part in range(slots // 8):
        span = slice(chunk * part, chunk * (part + 1))
        values = gathered[:, span]
        high = values.astype(jnp.bfloat16)
        rest = values - high.astype(jnp.float32)
        low = rest.astype(jnp.bfloat16)
        last = (rest - low.astype(jnp.float32)).astype(jnp.bfloat16)
        stack = jnp.concatenate([high, low, last, high], axis=0)
        children = jnp.dot(matrix, stack, preferred_element_type=jnp.float32)
        for sub in range(8):
            slot = 8 * part + sub
            cut = slice(LANES * sub, LANES * (sub + 1))
            tag = jnp.broadcast_to(index_ref[1, slot : slot + 1, :], (PACK, LANES))
            value = jnp.where(
                tag < 0.5,
                children[2 * PACK :, cut],
                jnp.where(tag < 1.5, children[:PACK, cut], children[PACK : 2 * PACK, cut]),
            )
            for node in range(10):
                out_ref[node, :, LANES * slot : LANES * (slot + 1)] = value[4 * node : 4 * node + 3]
        result = pltpu.make_async_copy(out_ref.at[:, :, span], out_hbm.at[:, :, span], out_sems.at[part])
        result.start()
        results.append(result)
    for result in results:
        result.wait()


def swaps(start, count):
    pairs = [(i, i + 1) for i in range(start, count - 1, 2)]
    return pairs + [(j, i) for i, j in pairs]


def shards(state, depth, metric, partner, refine, diff_ops, lift, prolong):
    sizes = Sizes(state.shape[2])
    count = lax.axis_size(AXES)
    blocks, slots, halo = sizes.blocks, sizes.slots, sizes.halo
    depth, partner, refine = [x.reshape(blocks, LANES) for x in (depth, partner, refine)]
    state, diff_ops, prolong = [jnp.transpose(x, (1, 0, 2)) for x in (state, diff_ops, prolong)]
    state, depth, metric, partner, refine, diff_ops, lift, prolong = [
        pltpu.with_memory_space_constraint(x, pltpu.HBM)
        for x in (state, depth, metric, partner, refine, diff_ops, lift, prolong)
    ]
    f32, i32 = jnp.float32, jnp.int32
    packed = jax.ShapeDtypeStruct((SENT * halo, LANES), f32)
    dense = [
        pltpu.VMEM((blocks, LANES), f32),
        pltpu.VMEM(metric.shape, f32),
        pltpu.VMEM((blocks, LANES), i32),
        pltpu.VMEM((blocks, LANES), i32),
    ]
    operators = [pltpu.SMEM(diff_ops.shape, f32), pltpu.SMEM(lift.shape, f32)]
    stats, even, odd = pl.pallas_call(
        functools.partial(pack_kernel, sizes),
        name="pack",
        out_shape=(jax.ShapeDtypeStruct((count, LANES), f32), packed, packed),
        in_specs=[HBM] * 5,
        out_specs=(HBM, VMEM, VMEM),
        scratch_shapes=[
            pltpu.VMEM((count, LANES), f32),
            pltpu.VMEM((10, 3, LANES * halo), f32),
            pltpu.VMEM((10, 3, LANES * halo), f32),
            *dense,
            pltpu.VMEM((8 * blocks, LANES), f32),
            pltpu.SemaphoreType.DMA((6,)),
            pltpu.SemaphoreType.DMA,
        ],
        compiler_params=PARAMS,
    )(state, depth, metric, partner, refine)
    odd = lax.ppermute(odd, AXES, swaps(1, count))
    even = lax.ppermute(even, AXES, swaps(0, count))
    stats = lax.all_to_all(stats, AXES, 0, 0, tiled=True)
    even, odd, stats = [pltpu.with_memory_space_constraint(x, pltpu.VMEM) for x in (even, odd, stats)]
    cur, aux, rates, twice, weights = pl.pallas_call(
        functools.partial(own_kernel, sizes),
        name="own_rates",
        cost_estimate=pl.CostEstimate(flops=1 << 24, transcendentals=1 << 16, bytes_accessed=1 << 24),
        out_shape=(
            jax.ShapeDtypeStruct((30, sizes.tall, LANES), f32),
            jax.ShapeDtypeStruct((7, sizes.tall, LANES), f32),
            jax.ShapeDtypeStruct((30, sizes.tall, LANES), f32),
            jax.ShapeDtypeStruct((30, blocks, LANES), f32),
            jax.ShapeDtypeStruct((3 * PACK, 4 * WIDE), jnp.bfloat16),
        ),
        in_specs=[HBM] * 8,
        out_specs=(VMEM,) * 5,
        scratch_shapes=[
            pltpu.VMEM((15, blocks, LANES), f32),
            pltpu.VMEM(state.shape, f32),
            *dense,
            *operators,
            pltpu.VMEM(prolong.shape, f32),
            pltpu.VMEM((8 * blocks, LANES), f32),
            pltpu.VMEM((PACK * blocks, LANES), f32),
            pltpu.SemaphoreType.DMA((8,)),
        ],
        compiler_params=PARAMS,
    )(state, depth, metric, partner, refine, diff_ops, lift, prolong)
    strip_cur, strip_rates, strip_twice, ends = pl.pallas_call(
        functools.partial(strip_kernel, sizes),
        name="strip_rates",
        cost_estimate=pl.CostEstimate(flops=1024, transcendentals=0, bytes_accessed=1024),
        out_shape=(
            jax.ShapeDtypeStruct((30, sizes.strip_tall, LANES), f32),
            jax.ShapeDtypeStruct((30, sizes.strip_tall, LANES), f32),
            jax.ShapeDtypeStruct((30, sizes.strip, LANES), f32),
            jax.ShapeDtypeStruct((2, slots, LANES), f32),
        ),
        in_specs=[VMEM] * 5 + [HBM] * 2,
        out_specs=(VMEM,) * 4,
        scratch_shapes=[
            pltpu.VMEM((7, sizes.strip_tall, LANES), f32),
            pltpu.VMEM((15, sizes.strip, LANES), f32),
            *operators,
            pltpu.VMEM((slots, LANES), f32),
            pltpu.SemaphoreType.DMA((2,)),
        ],
        compiler_params=PARAMS,
    )(cur, aux, rates, odd, even, diff_ops, lift)
    refined = pl.pallas_call(
        functools.partial(refine_kernel, sizes),
        name="sum_and_refine",
        out_shape=jax.ShapeDtypeStruct((10, 3, LANES * slots), f32),
        in_specs=[VMEM] * 9,
        out_specs=HBM,
        scratch_shapes=[
            pltpu.VMEM((10, 3, LANES * slots), f32),
            pltpu.VMEM((slots + 8, LANES), f32),
            pltpu.VMEM((8, LANES), i32),
            pltpu.SMEM((8, LANES), i32),
            pltpu.VMEM((WIDE * (slots + 1), LANES), f32),
            pltpu.VMEM((WIDE, LANES * slots), f32),
            pltpu.VMEM((3, slots, LANES), f32),
            pltpu.SemaphoreType.DMA((slots // 8,)),
            pltpu.SemaphoreType.DMA,
        ],
        compiler_params=PARAMS,
    )(cur, rates, twice, strip_cur, strip_rates, strip_twice, weights, ends, stats)
    return jnp.transpose(refined, (1, 0, 2))


def solution(mesh):
    return jax.shard_map(
        shards,
        mesh=mesh,
        in_specs=(
            P(None, None, AXES),
            P(AXES),
            P(None, AXES),
            P(AXES),
            P(AXES),
            P(),
            P(),
            P(),
        ),
        out_specs=P(None, None, AXES),
        check_vma=False,
    )
```

```python
import functools

import jax
import jax.numpy as jnp
from jax import lax
from jax.experimental import pallas as pl
from jax.experimental.pallas import tpu as pltpu
from jax.sharding import PartitionSpec as P

GRAVITY = 9.81
COURANT = 0.5
HIGH = lax.Precision.HIGHEST
LANES = 128
AXES = ("row", "col")
FACES = ((0, 1, 2, 3), (3, 6, 8, 9), (9, 7, 4, 0))
PACK = 40
SENT = 37
WIDE = 32
PAD = 8

VMEM = pl.BlockSpec(memory_space=pltpu.VMEM)
HBM = pl.BlockSpec(memory_space=pltpu.HBM)
PARAMS = pltpu.CompilerParams(vmem_limit_bytes=48 * 1024 * 1024)


class Sizes:
    def __init__(self, cells):
        self.cells = cells
        self.blocks = cells // LANES
        self.margin = cells // 4 // LANES
        self.halo = self.margin + 1
        self.rows = -(-(self.blocks + 2 * self.halo) // 8) * 8
        self.tall = self.rows + 2 * PAD
        self.slots = 3 * self.blocks // 2
        self.keep = self.halo - self.margin


def fetch_all(pairs, sems):
    copies = [pltpu.make_async_copy(src, dst, sems.at[num]) for num, (src, dst) in enumerate(pairs)]
    for copy in copies:
        copy.start()
    return copies


def split_metric(metric_ref, spread, blocks):
    for block in range(blocks):
        spread[8 * block : 8 * block + 4, :] = metric_ref[:, LANES * block : LANES * (block + 1)]
    return [spread[pl.ds(comp, blocks, stride=8), :] for comp in range(4)]


def pack_kernel(
    sizes, state_hbm, depth_hbm, metric_hbm, partner_hbm, refine_hbm, stats_hbm, even_ref, odd_ref,
    stats_ref, state_even, state_odd, depth_ref, metric_ref, partner_ref, refine_ref, spread, sems, sem,
):
    blocks, halo = sizes.blocks, sizes.halo
    wide = LANES * halo
    late = blocks - halo
    even = (lax.axis_index(AXES) + 1) % 2 * late
    odd = late - even
    copies = fetch_all(
        (
            (depth_hbm, depth_ref),
            (metric_hbm, metric_ref),
            (refine_hbm, refine_ref),
            (partner_hbm, partner_ref),
            (state_hbm.at[:, :, pl.ds(pl.multiple_of(LANES * even, LANES), wide)], state_even),
            (state_hbm.at[:, :, pl.ds(pl.multiple_of(LANES * odd, LANES), wide)], state_odd),
        ),
        sems,
    )
    for copy in copies[:3]:
        copy.wait()
    rx, ry, sx, sy = split_metric(metric_ref, spread, blocks)
    depth = depth_ref[...]
    refine = refine_ref[...].astype(jnp.float32)
    faces = ((sx, sy), (rx + sx, ry + sy), (rx, ry))
    lengths = [jnp.sqrt(vx * vx + vy * vy) for vx, vy in faces]
    rate = jnp.sqrt(GRAVITY * depth) * jnp.maximum(jnp.maximum(lengths[0], lengths[1]), lengths[2])
    top = jnp.max(jnp.max(rate, axis=0, keepdims=True), axis=1, keepdims=True)
    extra = jnp.sum(jnp.sum(refine, axis=0, keepdims=True), axis=1, keepdims=True)
    shape = stats_ref.shape
    lane = lax.broadcasted_iota(jnp.int32, shape, 1)
    stats_ref[...] = jnp.where(
        lane < LANES // 2, jnp.broadcast_to(top, shape), jnp.broadcast_to(extra, shape)
    )
    sent = pltpu.make_async_copy(stats_ref, stats_hbm, sem)
    sent.start()
    for copy in copies[3:]:
        copy.wait()
    for ref, source, start in ((even_ref, state_even, even), (odd_ref, state_odd, odd)):
        pack_state(source, ref, halo, SENT, 3)
        at = pl.ds(start, halo)
        dense = [depth_ref[at, :]]
        dense += [spread[pl.ds(8 * start + comp, halo, stride=8), :] for comp in range(4)]
        dense += [partner_ref[at, :].astype(jnp.float32), refine_ref[at, :].astype(jnp.float32)]
        for num, value in enumerate(dense):
            ref[pl.ds(30 + num, halo, stride=SENT), :] = value
    sent.wait()


def pack_state(source, target, blocks, height, width):
    for block in range(blocks):
        for node in range(10):
            at = height * block + width * node
            target[at : at + 3, :] = source[node, :, LANES * block : LANES * (block + 1)]


def pair_index(partner):
    lane = lax.broadcasted_iota(jnp.int32, partner.shape, 1)
    target = lane + partner.astype(jnp.int32)
    return target & (LANES - 1), (target >= 0) & (target < LANES)


def lane_gather(values, index):
    return jnp.take_along_axis(values, index, axis=1, mode="promise_in_bounds")


def outer_values(load, index, inside):
    shape = index.shape
    lane = lax.broadcasted_iota(jnp.int32, shape, 1)

    def prev(item):
        return pltpu.roll(jnp.where(lane == LANES - 1, load(item, -1), load(item, 0)), 1, 1)

    def after(item):
        return pltpu.roll(jnp.where(lane == 0, load(item, 1), load(item, 0)), LANES - 1, 1)

    def across(item):
        other = jnp.where(lane < LANES // 2, load(item, 1), load(item, -1))
        return jnp.where(inside, lane_gather(load(item, 0), index), lane_gather(other, index))

    return prev, after, across


def wall_masks(sizes, start, place, count, partner):
    shape = partner.shape
    lane = lax.broadcasted_iota(jnp.int32, shape, 1)
    row = lax.broadcasted_iota(jnp.int32, shape, 0) + start
    first = (lane == 0) & (row == sizes.halo) & (place == 0)
    last = (lane == LANES - 1) & (row == sizes.halo + sizes.blocks - 1) & (place == count - 1)
    return first, last, partner == 0


def volume_matrix(diff_ref):
    d_r, d_s = diff_ref[:, 0, :], diff_ref[:, 1, :]
    zero = jnp.zeros((10, 10), jnp.float32)
    whole = jnp.concatenate(
        [
            jnp.concatenate([-d_r, -d_s, zero, jnp.zeros((10, 2), jnp.float32)], axis=1),
            jnp.concatenate([zero, zero, d_r, jnp.zeros((10, 2), jnp.float32)], axis=1),
            jnp.concatenate([zero, zero, d_s, jnp.zeros((10, 2), jnp.float32)], axis=1),
            jnp.zeros((2, WIDE), jnp.float32),
        ],
        axis=0,
    )
    rounded = whole.astype(jnp.bfloat16)
    rest = (whole - rounded.astype(jnp.float32)).astype(jnp.bfloat16)
    return jnp.concatenate([rounded, rounded, rest], axis=1)


def by_matrix(matrix, rows, laid, results):
    for num, value in enumerate(rows):
        laid[pl.ds(num, 8, stride=WIDE), :] = value
    blocks = [laid[WIDE * sub : WIDE * (sub + 1), :] for sub in range(8)]
    values = jnp.concatenate(blocks, axis=1)
    high = values.astype(jnp.bfloat16)
    low = (values - high.astype(jnp.float32)).astype(jnp.bfloat16)
    stack = jnp.concatenate([high, low, high], axis=0)
    products = jnp.dot(matrix, stack, preferred_element_type=jnp.float32)
    for sub in range(8):
        results[WIDE * sub : WIDE * (sub + 1), :] = products[:, LANES * sub : LANES * (sub + 1)]
    return [results[pl.ds(num, 8, stride=WIDE), :] for num in range(len(rows))]


def tendency(load, geo, walls, index, inside, volume, lift_ref):
    speed_sq, rx, ry, sx, sy = geo[:5]
    outer_sq, waves, ghosts = geo[5:8], geo[8:11], geo[11:14]
    own = [[load(10 * field + node, 0) for node in range(10)] for field in range(3)]
    eta, mom_x, mom_y = own
    flow_r = [rx * mom_x[b] + ry * mom_y[b] for b in range(10)]
    flow_s = [sx * mom_x[b] + sy * mom_y[b] for b in range(10)]
    products = by_matrix(volume[0][...], flow_r + flow_s + eta, *volume[1:])
    inflow, along_r, along_s = products[:10], products[10:20], products[20:]
    half_r = (0.5 * rx, 0.5 * ry)
    half_s = (0.5 * sx, 0.5 * sy)
    vectors = (
        (-half_s[0], -half_s[1]),
        (half_r[0] + half_s[0], half_r[1] + half_s[1]),
        (-half_r[0], -half_r[1]),
    )
    fetch = outer_values(load, index, inside)
    jumps = ([], [], [])
    for face in range(3):
        vec_x, vec_y = vectors[face]
        theirs = FACES[(1, 0, 2)[face]]
        wall = walls[face]
        for j in range(4):
            node, match = FACES[face][j], theirs[3 - j]
            in_eta, in_x, in_y = eta[node], mom_x[node], mom_y[node]
            ext_eta, ext_x, ext_y = [fetch[face](10 * field + match) for field in range(3)]
            bounce = (in_x * vec_x + in_y * vec_y) * ghosts[face]
            d_eta = jnp.where(wall, 0.0, in_eta - ext_eta)
            d_x = jnp.where(wall, bounce * vec_x, in_x - ext_x)
            d_y = jnp.where(wall, bounce * vec_y, in_y - ext_y)
            head = jnp.where(wall, 0.0, speed_sq * in_eta - outer_sq[face] * ext_eta)
            jumps[0].append(d_x * vec_x + d_y * vec_y - waves[face] * d_eta)
            jumps[1].append(head * vec_x - waves[face] * d_x)
            jumps[2].append(head * vec_y - waves[face] * d_y)
    pull = (-speed_sq * rx, -speed_sq * ry)
    push = (-speed_sq * sx, -speed_sq * sy)
    out = [[None] * 10 for _ in range(3)]
    for a in range(10):
        sums = [
            inflow[a],
            pull[0] * along_r[a] + push[0] * along_s[a],
            pull[1] * along_r[a] + push[1] * along_s[a],
        ]
        for q in range(12):
            weight = lift_ref[a, q]
            for field in range(3):
                sums[field] = sums[field] + weight * jumps[field][q]
        for field in range(3):
            out[field][a] = sums[field]
    return [out[field][a] for field in range(3) for a in range(10)]


def child_matrix(prolong_ref):
    f32 = jnp.float32
    node_r = lax.broadcasted_iota(jnp.int32, (PACK, 10), 0) // 4
    spread_r = (node_r == lax.broadcasted_iota(jnp.int32, (PACK, 10), 1)).astype(f32)
    item_c = lax.broadcasted_iota(jnp.int32, (10, WIDE), 1)
    spread_c = (item_c % 10 == lax.broadcasted_iota(jnp.int32, (10, WIDE), 0)).astype(f32)
    row = lax.broadcasted_iota(jnp.int32, (PACK, WIDE), 0)
    col = lax.broadcasted_iota(jnp.int32, (PACK, WIDE), 1)
    same = row % 4 == col // 10
    parts = []
    for child in range(2):
        left = jnp.dot(spread_r, prolong_ref[:, child, :], precision=HIGH, preferred_element_type=f32)
        full = jnp.dot(left, spread_c, precision=HIGH, preferred_element_type=f32)
        parts.append(jnp.where(same, full, 0.0))
    parts.append((same & (row // 4 == col % 10)).astype(f32))
    whole = jnp.concatenate(parts, axis=0)
    rounded = whole.astype(jnp.bfloat16)
    rest = (whole - rounded.astype(f32)).astype(jnp.bfloat16)
    return jnp.concatenate([rounded, rounded, rounded, rest], axis=1)


def sum_children(sizes, refine, ends_ref):
    slots, f32 = sizes.slots, jnp.float32
    counts = (1.0 + refine).astype(jnp.bfloat16)
    row_i = lax.broadcasted_iota(jnp.int32, (LANES, LANES), 0)
    col_i = lax.broadcasted_iota(jnp.int32, (LANES, LANES), 1)
    upper = (row_i <= col_i).astype(jnp.bfloat16)
    within = jnp.dot(counts, upper, preferred_element_type=f32)
    whole = jnp.dot(counts, jnp.ones((LANES, LANES), jnp.bfloat16), preferred_element_type=f32)
    row_s = lax.broadcasted_iota(jnp.int32, (slots, slots), 0)
    col_s = lax.broadcasted_iota(jnp.int32, (slots, slots), 1)
    lower = (col_s < row_s).astype(jnp.bfloat16)
    before = jnp.dot(lower, whole.astype(jnp.bfloat16), preferred_element_type=f32)
    before = before - before[sizes.margin : sizes.margin + 1, :]
    ends_ref[0] = 2.0 * (within + before) + refine
    ends_ref[1] = before + whole


def first_kernel(
    sizes, state_hbm, depth_hbm, metric_hbm, partner_hbm, refine_hbm, odd_ref, even_ref, diff_hbm, lift_hbm, prolong_hbm,
    cur, rate_ref, twice_ref, weights, ends_ref,
    geo_ref, state_ref, depth_ref, metric_ref, partner_ref, refine_ref, diff_ref, lift_ref, prolong_ref,
    spread, wide, aux, matrix, laid, results, sems,
):
    blocks, halo = sizes.blocks, sizes.halo
    top, bottom = PAD + halo, PAD + halo + blocks
    place = lax.axis_index(AXES)
    count = lax.axis_size(AXES)
    copies = fetch_all(
        (
            (metric_hbm, metric_ref),
            (state_hbm, state_ref),
            (depth_hbm, depth_ref),
            (partner_hbm, partner_ref),
            (refine_hbm, refine_ref),
            (diff_hbm, diff_ref),
            (lift_hbm, lift_ref),
            (prolong_hbm, prolong_ref),
        ),
        sems,
    )
    for copy in copies:
        copy.wait()
    metric = split_metric(metric_ref, spread, blocks)
    dense = [depth_ref[...], *metric, partner_ref[...].astype(jnp.float32), refine_ref[...].astype(jnp.float32)]
    pack_state(state_ref, wide, blocks, PACK, 4)
    even = place % 2 == 0

    def set_halo(target, num, row):
        by_even = even_ref[pl.ds(row, halo, stride=SENT), :]
        by_odd = odd_ref[pl.ds(row, halo, stride=SENT), :]
        target[num, top - halo : top, :] = jnp.where(even, by_odd, by_even)
        target[num, bottom : bottom + halo, :] = jnp.where(even, by_even, by_odd)

    for num in range(7):
        set_halo(aux, num, 30 + num)
        aux[num, top:bottom, :] = dense[num]
    for field in range(3):
        for node in range(10):
            item = 10 * field + node
            set_halo(cur, item, 3 * node + field)
            cur[item, top:bottom, :] = wide[pl.ds(4 * node + field, blocks, stride=PACK), :]

    weights[...] = child_matrix(prolong_ref)
    matrix[...] = volume_matrix(diff_ref)
    for row in (30, 31):
        laid[pl.ds(row, 8, stride=WIDE), :] = jnp.zeros((8, LANES), jnp.float32)
    volume = (matrix, laid, results)
    begin = PAD + sizes.keep
    sum_children(sizes, aux[6, begin : begin + sizes.slots, :], ends_ref)

    def step(group, carry):
        base = PAD + 8 * group

        def load_aux(item, shift):
            return aux[item, pl.ds(base + shift, 8), :]

        def load(item, shift):
            return cur[item, pl.ds(base + shift, 8), :]

        depth, rx, ry, sx, sy, partner = [load_aux(num, 0) for num in range(6)]
        index, inside = pair_index(partner)
        fetch = outer_values(load_aux, index, inside)
        walls = wall_masks(sizes, 8 * group, place, count, partner)
        speed_sq = GRAVITY * depth
        outer_sq = [jnp.where(walls[k], speed_sq, GRAVITY * fetch[k](0)) for k in range(3)]
        faces = ((sx, sy), (rx + sx, ry + sy), (rx, ry))
        squares = [vx * vx + vy * vy for vx, vy in faces]
        waves = [
            0.5 * jnp.sqrt(squares[k]) * jnp.sqrt(jnp.maximum(speed_sq, outer_sq[k])) for k in range(3)
        ]
        ghosts = [8.0 / squares[k] for k in range(3)]
        geo = [speed_sq, rx, ry, sx, sy, *outer_sq, *waves, *ghosts]
        rates = tendency(load, geo, walls, index, inside, volume, lift_ref)
        at = pl.ds(pl.multiple_of(8 * group, 8), 8)
        for num, value in enumerate([*geo, partner]):
            geo_ref[num, at, :] = value
        for item in range(30):
            rate_ref[item, pl.ds(base, 8), :] = rates[item]
        return carry

    lax.fori_loop(0, sizes.rows // 8, step, 0)

    def again(group, carry):
        row = 8 * group + sizes.keep
        at = pl.ds(row, 8)

        def load(item, shift):
            return rate_ref[item, pl.ds(PAD + row + shift, 8), :]

        geo = [geo_ref[num, at, :] for num in range(14)]
        partner = geo_ref[14, at, :]
        index, inside = pair_index(partner)
        walls = wall_masks(sizes, row, place, count, partner)
        rates = tendency(load, geo, walls, index, inside, volume, lift_ref)
        for item in range(30):
            twice_ref[item, pl.ds(pl.multiple_of(8 * group, 8), 8), :] = rates[item]
        return carry

    lax.fori_loop(0, sizes.slots // 8, again, 0)


def refine_kernel(
    sizes, cur, rate_ref, twice_ref, weights, base_ref, stats_ref, out_hbm,
    out_ref, ends_ref, place_v, place_s, wide, gathered, index_ref, out_sems, sem,
):
    slots, keep = sizes.slots, sizes.keep
    place = lax.axis_index(AXES)
    stats = stats_ref[...]
    half = LANES // 2
    row_n = lax.broadcasted_iota(jnp.int32, stats.shape, 0)
    top = jnp.max(stats, axis=0, keepdims=True)
    earlier = jnp.sum(jnp.where(row_n < place, stats, 0.0), axis=0, keepdims=True)
    left = lax.broadcasted_iota(jnp.int32, (1, LANES), 1) < half
    top = jnp.where(left, top, pltpu.roll(top, half, 1))
    earlier = jnp.where(left, pltpu.roll(earlier, half, 1), earlier)
    step = COURANT / top
    half_square = 0.5 * step * step
    start = earlier - (place * (sizes.cells // 2)).astype(jnp.float32)
    ends_ref[:slots, :] = base_ref[0] + 2.0 * start
    ends_ref[slots:, :] = jnp.full((8, LANES), 1e9, jnp.float32)
    first_slot = LANES * lax.broadcasted_iota(jnp.int32, (slots, LANES), 1).astype(jnp.float32)
    lead = jnp.sum((base_ref[1] + start <= first_slot).astype(jnp.float32), axis=0, keepdims=True)
    lead = jnp.clip(lead.astype(jnp.int32), 0, slots - 1)
    place_v[...] = jnp.broadcast_to(lead, (8, LANES))
    copy = pltpu.make_async_copy(place_v, place_s, sem)
    copy.start()
    for item in range(30):
        now = slice(PAD + keep, PAD + keep + slots)
        value = cur[item, now, :] + step * rate_ref[item, now, :] + half_square * twice_ref[item]
        wide[pl.ds(item, slots, stride=WIDE), :] = value
    for item in (30, 31):
        wide[pl.ds(item, slots + 1, stride=WIDE), :] = jnp.zeros((slots + 1, LANES), jnp.float32)
    copy.wait()
    for slot in range(slots):
        lead_at = place_s[0, slot]
        index_ref[0, slot : slot + 1, :] = ends_ref[pl.ds(lead_at, 1), :]
        index_ref[1, slot : slot + 1, :] = ends_ref[pl.ds(lead_at + 1, 1), :]
    near, far = index_ref[0], index_ref[1]
    lane = lax.broadcasted_iota(jnp.int32, (slots, LANES), 1)
    slot_no = LANES * lax.broadcasted_iota(jnp.int32, (slots, LANES), 0) + lane
    goal = (2 * slot_no + 1).astype(jnp.float32)
    beyond = jnp.broadcast_to(near[:, LANES - 1 :], (slots, LANES)) <= goal

    def pick(index):
        return jnp.where(beyond, lane_gather(far, index), lane_gather(near, index))

    found = jnp.zeros((slots, LANES), jnp.int32)
    size = LANES // 2
    while size:
        passed = pick(found + (size - 1)) <= goal
        found = jnp.where(passed, found + size, found)
        size //= 2
    mine = pick(found).astype(jnp.int32)
    split = mine & 1
    begin = (mine >> 1) - 1 - split
    kind = split * (1 + slot_no - begin)
    index_ref[0] = found.astype(jnp.float32)
    index_ref[1] = kind.astype(jnp.float32)
    index_ref[2] = (lane < jnp.broadcast_to(found[:, 0:1], (slots, LANES))).astype(jnp.float32)
    for slot in range(slots):
        lead_at = place_s[0, slot] * WIDE
        lane_idx = jnp.broadcast_to(index_ref[0, slot : slot + 1, :], (8, LANES)).astype(jnp.int32)
        ahead = jnp.broadcast_to(index_ref[2, slot : slot + 1, :], (8, LANES)) > 0.5
        for part in range(0, WIDE, 8):
            one = wide[pl.ds(pl.multiple_of(lead_at + part, 8), 8), :]
            two = wide[pl.ds(pl.multiple_of(lead_at + WIDE + part, 8), 8), :]
            gathered[part : part + 8, LANES * slot : LANES * (slot + 1)] = lane_gather(
                jnp.where(ahead, two, one), lane_idx
            )
    matrix = weights[...]
    chunk = 8 * LANES
    results = []
    for part in range(slots // 8):
        span = slice(chunk * part, chunk * (part + 1))
        values = gathered[:, span]
        high = values.astype(jnp.bfloat16)
        rest = values - high.astype(jnp.float32)
        low = rest.astype(jnp.bfloat16)
        last = (rest - low.astype(jnp.float32)).astype(jnp.bfloat16)
        stack = jnp.concatenate([high, low, last, high], axis=0)
        children = jnp.dot(matrix, stack, preferred_element_type=jnp.float32)
        for sub in range(8):
            slot = 8 * part + sub
            cut = slice(LANES * sub, LANES * (sub + 1))
            tag = jnp.broadcast_to(index_ref[1, slot : slot + 1, :], (PACK, LANES))
            value = jnp.where(
                tag < 0.5,
                children[2 * PACK :, cut],
                jnp.where(tag < 1.5, children[:PACK, cut], children[PACK : 2 * PACK, cut]),
            )
            for node in range(10):
                out_ref[node, :, LANES * slot : LANES * (slot + 1)] = value[4 * node : 4 * node + 3]
        result = pltpu.make_async_copy(out_ref.at[:, :, span], out_hbm.at[:, :, span], out_sems.at[part])
        result.start()
        results.append(result)
    for result in results:
        result.wait()


def swaps(start, count):
    pairs = [(i, i + 1) for i in range(start, count - 1, 2)]
    return pairs + [(j, i) for i, j in pairs]


def shards(state, depth, metric, partner, refine, diff_ops, lift, prolong):
    sizes = Sizes(state.shape[2])
    count = lax.axis_size(AXES)
    blocks, rows, slots, halo = sizes.blocks, sizes.rows, sizes.slots, sizes.halo
    depth, partner, refine = [x.reshape(blocks, LANES) for x in (depth, partner, refine)]
    state, diff_ops, prolong = [jnp.transpose(x, (1, 0, 2)) for x in (state, diff_ops, prolong)]
    state, depth, metric, partner, refine, diff_ops, lift, prolong = [
        pltpu.with_memory_space_constraint(x, pltpu.HBM)
        for x in (state, depth, metric, partner, refine, diff_ops, lift, prolong)
    ]
    f32, i32 = jnp.float32, jnp.int32
    packed = jax.ShapeDtypeStruct((SENT * halo, LANES), f32)
    dense = [
        pltpu.VMEM((blocks, LANES), f32),
        pltpu.VMEM(metric.shape, f32),
        pltpu.VMEM((blocks, LANES), i32),
        pltpu.VMEM((blocks, LANES), i32),
    ]
    stats, even, odd = pl.pallas_call(
        functools.partial(pack_kernel, sizes),
        name="pack",
        out_shape=(jax.ShapeDtypeStruct((count, LANES), f32), packed, packed),
        in_specs=[HBM] * 5,
        out_specs=(HBM, VMEM, VMEM),
        scratch_shapes=[
            pltpu.VMEM((count, LANES), f32),
            pltpu.VMEM((10, 3, LANES * halo), f32),
            pltpu.VMEM((10, 3, LANES * halo), f32),
            *dense,
            pltpu.VMEM((8 * blocks, LANES), f32),
            pltpu.SemaphoreType.DMA((6,)),
            pltpu.SemaphoreType.DMA,
        ],
        compiler_params=PARAMS,
    )(state, depth, metric, partner, refine)
    odd = lax.ppermute(odd, AXES, swaps(1, count))
    even = lax.ppermute(even, AXES, swaps(0, count))
    stats = lax.all_to_all(stats, AXES, 0, 0, tiled=True)
    even, odd, stats = [pltpu.with_memory_space_constraint(x, pltpu.VMEM) for x in (even, odd, stats)]
    cur, rates, twice, weights, ends = pl.pallas_call(
        functools.partial(first_kernel, sizes),
        name="rates_twice",
        out_shape=(
            jax.ShapeDtypeStruct((30, sizes.tall, LANES), f32),
            jax.ShapeDtypeStruct((30, sizes.tall, LANES), f32),
            jax.ShapeDtypeStruct((30, slots, LANES), f32),
            jax.ShapeDtypeStruct((3 * PACK, 4 * WIDE), jnp.bfloat16),
            jax.ShapeDtypeStruct((2, slots, LANES), f32),
        ),
        in_specs=[HBM] * 5 + [VMEM] * 2 + [HBM] * 3,
        out_specs=(VMEM,) * 5,
        scratch_shapes=[
            pltpu.VMEM((15, rows, LANES), f32),
            pltpu.VMEM(state.shape, f32),
            *dense,
            pltpu.VMEM(diff_ops.shape, f32),
            pltpu.SMEM(lift.shape, f32),
            pltpu.VMEM(prolong.shape, f32),
            pltpu.VMEM((8 * blocks, LANES), f32),
            pltpu.VMEM((PACK * blocks, LANES), f32),
            pltpu.VMEM((7, sizes.tall, LANES), f32),
            pltpu.VMEM((WIDE, 3 * WIDE), jnp.bfloat16),
            pltpu.VMEM((8 * WIDE, LANES), f32),
            pltpu.VMEM((8 * WIDE, LANES), f32),
            pltpu.SemaphoreType.DMA((8,)),
        ],
        compiler_params=PARAMS,
    )(state, depth, metric, partner, refine, odd, even, diff_ops, lift, prolong)
    refined = pl.pallas_call(
        functools.partial(refine_kernel, sizes),
        name="sum_and_refine",
        out_shape=jax.ShapeDtypeStruct((10, 3, LANES * slots), f32),
        in_specs=[VMEM] * 6,
        out_specs=HBM,
        scratch_shapes=[
            pltpu.VMEM((10, 3, LANES * slots), f32),
            pltpu.VMEM((slots + 8, LANES), f32),
            pltpu.VMEM((8, LANES), i32),
            pltpu.SMEM((8, LANES), i32),
            pltpu.VMEM((WIDE * (slots + 1), LANES), f32),
            pltpu.VMEM((WIDE, LANES * slots), f32),
            pltpu.VMEM((3, slots, LANES), f32),
            pltpu.SemaphoreType.DMA((slots // 8,)),
            pltpu.SemaphoreType.DMA,
        ],
        compiler_params=PARAMS,
    )(cur, rates, twice, weights, ends, stats)
    return jnp.transpose(refined, (1, 0, 2))


def solution(mesh):
    return jax.shard_map(
        shards,
        mesh=mesh,
        in_specs=(
            P(None, None, AXES),
            P(AXES),
            P(None, AXES),
            P(AXES),
            P(AXES),
            P(),
            P(),
            P(),
        ),
        out_specs=P(None, None, AXES),
        check_vma=False,
    )
```

```python
import functools

import jax
import jax.numpy as jnp
from jax import lax
from jax.experimental import pallas as pl
from jax.experimental.pallas import tpu as pltpu
from jax.sharding import PartitionSpec as P

GRAVITY = 9.81
COURANT = 0.5
HIGH = lax.Precision.HIGHEST
LANES = 128
AXES = ("row", "col")
FACES = ((0, 1, 2, 3), (3, 6, 8, 9), (9, 7, 4, 0))
PACK = 40
LAID = 41
SENT = 37
WIDE = 32
STEP = 33
PAD = 8

VMEM = pl.BlockSpec(memory_space=pltpu.VMEM)
HBM = pl.BlockSpec(memory_space=pltpu.HBM)
PARAMS = pltpu.CompilerParams(vmem_limit_bytes=48 * 1024 * 1024)


class Sizes:
    def __init__(self, cells):
        self.cells = cells
        self.blocks = cells // LANES
        self.margin = cells // 4 // LANES
        self.halo = self.margin + 1
        self.rows = -(-(self.blocks + 2 * self.halo) // 8) * 8
        self.tall = self.rows + 2 * PAD
        self.slots = 3 * self.blocks // 2
        self.keep = self.halo - self.margin


def fetch_all(pairs, sems):
    copies = [pltpu.make_async_copy(src, dst, sems.at[num]) for num, (src, dst) in enumerate(pairs)]
    for copy in copies:
        copy.start()
    return copies


def split_metric(metric_ref, spread, blocks):
    for block in range(blocks):
        spread[8 * block : 8 * block + 4, :] = metric_ref[:, LANES * block : LANES * (block + 1)]
    return [spread[pl.ds(comp, blocks, stride=8), :] for comp in range(4)]


def pack_kernel(
    sizes, state_hbm, depth_hbm, metric_hbm, partner_hbm, refine_hbm, stats_hbm, even_ref, odd_ref,
    stats_ref, state_even, state_odd, depth_ref, metric_ref, partner_ref, refine_ref, spread, sems, sem,
):
    blocks, halo = sizes.blocks, sizes.halo
    wide = LANES * halo
    late = blocks - halo
    even = (lax.axis_index(AXES) + 1) % 2 * late
    odd = late - even
    copies = fetch_all(
        (
            (depth_hbm, depth_ref),
            (metric_hbm, metric_ref),
            (refine_hbm, refine_ref),
            (partner_hbm, partner_ref),
            (state_hbm.at[:, :, pl.ds(pl.multiple_of(LANES * even, LANES), wide)], state_even),
            (state_hbm.at[:, :, pl.ds(pl.multiple_of(LANES * odd, LANES), wide)], state_odd),
        ),
        sems,
    )
    for copy in copies[:3]:
        copy.wait()
    rx, ry, sx, sy = split_metric(metric_ref, spread, blocks)
    depth = depth_ref[...]
    refine = refine_ref[...].astype(jnp.float32)
    faces = ((sx, sy), (rx + sx, ry + sy), (rx, ry))
    lengths = [jnp.sqrt(vx * vx + vy * vy) for vx, vy in faces]
    rate = jnp.sqrt(GRAVITY * depth) * jnp.maximum(jnp.maximum(lengths[0], lengths[1]), lengths[2])
    top = jnp.max(jnp.max(rate, axis=0, keepdims=True), axis=1, keepdims=True)
    extra = jnp.sum(jnp.sum(refine, axis=0, keepdims=True), axis=1, keepdims=True)
    shape = stats_ref.shape
    lane = lax.broadcasted_iota(jnp.int32, shape, 1)
    stats_ref[...] = jnp.where(
        lane < LANES // 2, jnp.broadcast_to(top, shape), jnp.broadcast_to(extra, shape)
    )
    sent = pltpu.make_async_copy(stats_ref, stats_hbm, sem)
    sent.start()
    for copy in copies[3:]:
        copy.wait()
    for ref, source, start in ((even_ref, state_even, even), (odd_ref, state_odd, odd)):
        pack_state(source, ref, halo, SENT, 3)
        at = pl.ds(start, halo)
        dense = [depth_ref[at, :]]
        dense += [spread[pl.ds(8 * start + comp, halo, stride=8), :] for comp in range(4)]
        dense += [partner_ref[at, :].astype(jnp.float32), refine_ref[at, :].astype(jnp.float32)]
        for num, value in enumerate(dense):
            ref[pl.ds(30 + num, halo, stride=SENT), :] = value
    sent.wait()


def pack_state(source, target, blocks, height, width):
    for block in range(blocks):
        for node in range(10):
            at = height * block + width * node
            target[at : at + 3, :] = source[node, :, LANES * block : LANES * (block + 1)]


def pair_index(partner):
    lane = lax.broadcasted_iota(jnp.int32, partner.shape, 1)
    target = lane + partner.astype(jnp.int32)
    return target & (LANES - 1), (target >= 0) & (target < LANES)


def lane_gather(values, index):
    return jnp.take_along_axis(values, index, axis=1, mode="promise_in_bounds")


def outer_values(load, index, inside):
    shape = index.shape
    lane = lax.broadcasted_iota(jnp.int32, shape, 1)

    def prev(item):
        return pltpu.roll(jnp.where(lane == LANES - 1, load(item, -1), load(item, 0)), 1, 1)

    def after(item):
        return pltpu.roll(jnp.where(lane == 0, load(item, 1), load(item, 0)), LANES - 1, 1)

    def across(item):
        other = jnp.where(lane < LANES // 2, load(item, 1), load(item, -1))
        return jnp.where(inside, lane_gather(load(item, 0), index), lane_gather(other, index))

    return prev, after, across


def wall_masks(sizes, start, place, count, partner):
    shape = partner.shape
    lane = lax.broadcasted_iota(jnp.int32, shape, 1)
    row = lax.broadcasted_iota(jnp.int32, shape, 0) + start
    first = (lane == 0) & (row == sizes.halo) & (place == 0)
    last = (lane == LANES - 1) & (row == sizes.halo + sizes.blocks - 1) & (place == count - 1)
    return first, last, partner == 0


def tendency(load, geo, walls, index, inside, diff_ref, lift_ref):
    speed_sq, rx, ry, sx, sy = geo[:5]
    outer_sq, waves, ghosts = geo[5:8], geo[8:11], geo[11:14]
    own = [[load(10 * field + node, 0) for node in range(10)] for field in range(3)]
    eta, mom_x, mom_y = own
    flow_r = [-(rx * mom_x[b] + ry * mom_y[b]) for b in range(10)]
    flow_s = [-(sx * mom_x[b] + sy * mom_y[b]) for b in range(10)]
    half_r = (0.5 * rx, 0.5 * ry)
    half_s = (0.5 * sx, 0.5 * sy)
    vectors = (
        (-half_s[0], -half_s[1]),
        (half_r[0] + half_s[0], half_r[1] + half_s[1]),
        (-half_r[0], -half_r[1]),
    )
    fetch = outer_values(load, index, inside)
    jumps = ([], [], [])
    for face in range(3):
        vec_x, vec_y = vectors[face]
        theirs = FACES[(1, 0, 2)[face]]
        wall = walls[face]
        for j in range(4):
            node, match = FACES[face][j], theirs[3 - j]
            in_eta, in_x, in_y = eta[node], mom_x[node], mom_y[node]
            ext_eta, ext_x, ext_y = [fetch[face](10 * field + match) for field in range(3)]
            bounce = (in_x * vec_x + in_y * vec_y) * ghosts[face]
            d_eta = jnp.where(wall, 0.0, in_eta - ext_eta)
            d_x = jnp.where(wall, bounce * vec_x, in_x - ext_x)
            d_y = jnp.where(wall, bounce * vec_y, in_y - ext_y)
            head = jnp.where(wall, 0.0, speed_sq * in_eta - outer_sq[face] * ext_eta)
            jumps[0].append(d_x * vec_x + d_y * vec_y - waves[face] * d_eta)
            jumps[1].append(head * vec_x - waves[face] * d_x)
            jumps[2].append(head * vec_y - waves[face] * d_y)
    pull = (-speed_sq * rx, -speed_sq * ry)
    push = (-speed_sq * sx, -speed_sq * sy)
    out = [[None] * 10 for _ in range(3)]
    for a in range(10):
        total = along_r = along_s = None
        for b in range(10):
            d_r, d_s = diff_ref[a, 0, b], diff_ref[a, 1, b]
            term = d_r * flow_r[b] + d_s * flow_s[b]
            total = term if b == 0 else total + term
            along_r = d_r * eta[b] if b == 0 else along_r + d_r * eta[b]
            along_s = d_s * eta[b] if b == 0 else along_s + d_s * eta[b]
        sums = [total, pull[0] * along_r + push[0] * along_s, pull[1] * along_r + push[1] * along_s]
        for q in range(12):
            weight = lift_ref[a, q]
            for field in range(3):
                sums[field] = sums[field] + weight * jumps[field][q]
        for field in range(3):
            out[field][a] = sums[field]
    return [out[field][a] for field in range(3) for a in range(10)]


def child_matrix(prolong_ref):
    f32 = jnp.float32
    node_r = lax.broadcasted_iota(jnp.int32, (PACK, 10), 0) // 4
    spread_r = (node_r == lax.broadcasted_iota(jnp.int32, (PACK, 10), 1)).astype(f32)
    item_c = lax.broadcasted_iota(jnp.int32, (10, WIDE), 1)
    spread_c = (item_c % 10 == lax.broadcasted_iota(jnp.int32, (10, WIDE), 0)).astype(f32)
    row = lax.broadcasted_iota(jnp.int32, (PACK, WIDE), 0)
    col = lax.broadcasted_iota(jnp.int32, (PACK, WIDE), 1)
    same = row % 4 == col // 10
    parts = []
    for child in range(2):
        left = jnp.dot(spread_r, prolong_ref[:, child, :], precision=HIGH, preferred_element_type=f32)
        full = jnp.dot(left, spread_c, precision=HIGH, preferred_element_type=f32)
        parts.append(jnp.where(same, full, 0.0))
    parts.append((same & (row // 4 == col % 10)).astype(f32))
    whole = jnp.concatenate(parts, axis=0)
    rounded = whole.astype(jnp.bfloat16)
    rest = (whole - rounded.astype(f32)).astype(jnp.bfloat16)
    return jnp.concatenate([rounded, rounded, rounded, rest], axis=1)


def sum_children(sizes, refine, ends_ref):
    slots, f32 = sizes.slots, jnp.float32
    counts = (1.0 + refine).astype(jnp.bfloat16)
    row_i = lax.broadcasted_iota(jnp.int32, (LANES, LANES), 0)
    col_i = lax.broadcasted_iota(jnp.int32, (LANES, LANES), 1)
    upper = (row_i <= col_i).astype(jnp.bfloat16)
    within = jnp.dot(counts, upper, preferred_element_type=f32)
    whole = jnp.dot(counts, jnp.ones((LANES, LANES), jnp.bfloat16), preferred_element_type=f32)
    row_s = lax.broadcasted_iota(jnp.int32, (slots, slots), 0)
    col_s = lax.broadcasted_iota(jnp.int32, (slots, slots), 1)
    lower = (col_s < row_s).astype(jnp.bfloat16)
    before = jnp.dot(lower, whole.astype(jnp.bfloat16), preferred_element_type=f32)
    before = before - before[sizes.margin : sizes.margin + 1, :]
    ends_ref[0] = 2.0 * (within + before) + refine
    ends_ref[1] = before + whole


def prep_kernel(
    sizes, state_hbm, depth_hbm, metric_hbm, partner_hbm, refine_hbm, cur, aux,
    state_ref, depth_ref, metric_ref, partner_ref, refine_ref, spread, wide, sems,
):
    blocks = sizes.blocks
    copies = fetch_all(
        (
            (metric_hbm, metric_ref),
            (state_hbm, state_ref),
            (depth_hbm, depth_ref),
            (partner_hbm, partner_ref),
            (refine_hbm, refine_ref),
        ),
        sems,
    )
    for copy in copies:
        copy.wait()
    metric = split_metric(metric_ref, spread, blocks)
    dense = [depth_ref[...], *metric, partner_ref[...].astype(jnp.float32), refine_ref[...].astype(jnp.float32)]
    for num in range(7):
        aux[num] = dense[num]
    pack_state(state_ref, wide, blocks, LAID, 4)
    for field in range(3):
        for node in range(10):
            cur[10 * field + node] = wide[pl.ds(4 * node + field, blocks, stride=LAID), :]


def first_kernel(
    sizes, cur_own, aux_own, odd_ref, even_ref, diff_hbm, lift_hbm, prolong_hbm,
    cur, rate_ref, twice_ref, weights, ends_ref,
    geo_ref, aux, diff_ref, lift_ref, prolong_ref, sems,
):
    blocks, halo = sizes.blocks, sizes.halo
    top, bottom = PAD + halo, PAD + halo + blocks
    place = lax.axis_index(AXES)
    count = lax.axis_size(AXES)
    copies = fetch_all(((diff_hbm, diff_ref), (lift_hbm, lift_ref), (prolong_hbm, prolong_ref)), sems)
    even = place % 2 == 0

    def set_halo(target, num, row):
        by_even = even_ref[pl.ds(row, halo, stride=SENT), :]
        by_odd = odd_ref[pl.ds(row, halo, stride=SENT), :]
        target[num, top - halo : top, :] = jnp.where(even, by_odd, by_even)
        target[num, bottom : bottom + halo, :] = jnp.where(even, by_even, by_odd)

    for num in range(7):
        set_halo(aux, num, 30 + num)
        aux[num, top:bottom, :] = aux_own[num]
    for field in range(3):
        for node in range(10):
            item = 10 * field + node
            set_halo(cur, item, 3 * node + field)
            cur[item, top:bottom, :] = cur_own[item]

    for copy in copies:
        copy.wait()
    weights[...] = child_matrix(prolong_ref)
    begin = PAD + sizes.keep
    sum_children(sizes, aux[6, begin : begin + sizes.slots, :], ends_ref)

    def step(group, carry):
        base = PAD + 8 * group

        def load_aux(item, shift):
            return aux[item, pl.ds(base + shift, 8), :]

        def load(item, shift):
            return cur[item, pl.ds(base + shift, 8), :]

        depth, rx, ry, sx, sy, partner = [load_aux(num, 0) for num in range(6)]
        index, inside = pair_index(partner)
        fetch = outer_values(load_aux, index, inside)
        walls = wall_masks(sizes, 8 * group, place, count, partner)
        speed_sq = GRAVITY * depth
        outer_sq = [jnp.where(walls[k], speed_sq, GRAVITY * fetch[k](0)) for k in range(3)]
        faces = ((sx, sy), (rx + sx, ry + sy), (rx, ry))
        squares = [vx * vx + vy * vy for vx, vy in faces]
        waves = [
            0.5 * jnp.sqrt(squares[k]) * jnp.sqrt(jnp.maximum(speed_sq, outer_sq[k])) for k in range(3)
        ]
        ghosts = [8.0 / squares[k] for k in range(3)]
        geo = [speed_sq, rx, ry, sx, sy, *outer_sq, *waves, *ghosts]
        rates = tendency(load, geo, walls, index, inside, diff_ref, lift_ref)
        at = pl.ds(pl.multiple_of(8 * group, 8), 8)
        for num, value in enumerate([*geo, partner]):
            geo_ref[num, at, :] = value
        for item in range(30):
            rate_ref[item, pl.ds(base, 8), :] = rates[item]
        return carry

    lax.fori_loop(0, sizes.rows // 8, step, 0)

    def again(group, carry):
        row = 8 * group + sizes.keep
        at = pl.ds(row, 8)

        def load(item, shift):
            return rate_ref[item, pl.ds(PAD + row + shift, 8), :]

        geo = [geo_ref[num, at, :] for num in range(14)]
        partner = geo_ref[14, at, :]
        index, inside = pair_index(partner)
        walls = wall_masks(sizes, row, place, count, partner)
        rates = tendency(load, geo, walls, index, inside, diff_ref, lift_ref)
        for item in range(30):
            twice_ref[item, pl.ds(pl.multiple_of(8 * group, 8), 8), :] = rates[item]
        return carry

    lax.fori_loop(0, sizes.slots // 8, again, 0)


def refine_kernel(
    sizes, cur, rate_ref, twice_ref, weights, base_ref, stats_ref, out_hbm,
    out_ref, ends_ref, place_v, place_s, wide, index_ref, out_sems, sem,
):
    slots, keep = sizes.slots, sizes.keep
    place = lax.axis_index(AXES)
    stats = stats_ref[...]
    half = LANES // 2
    row_n = lax.broadcasted_iota(jnp.int32, stats.shape, 0)
    top = jnp.max(stats, axis=0, keepdims=True)
    earlier = jnp.sum(jnp.where(row_n < place, stats, 0.0), axis=0, keepdims=True)
    left = lax.broadcasted_iota(jnp.int32, (1, LANES), 1) < half
    top = jnp.where(left, top, pltpu.roll(top, half, 1))
    earlier = jnp.where(left, pltpu.roll(earlier, half, 1), earlier)
    step = COURANT / top
    half_square = 0.5 * step * step
    start = earlier - (place * (sizes.cells // 2)).astype(jnp.float32)
    ends_ref[:slots, :] = base_ref[0] + 2.0 * start
    ends_ref[slots:, :] = jnp.full((8, LANES), 1e9, jnp.float32)
    first_slot = LANES * lax.broadcasted_iota(jnp.int32, (slots, LANES), 1).astype(jnp.float32)
    lead = jnp.sum((base_ref[1] + start <= first_slot).astype(jnp.float32), axis=0, keepdims=True)
    lead = jnp.clip(lead.astype(jnp.int32), 0, slots - 1)
    place_v[...] = jnp.broadcast_to(lead, (8, LANES))
    copy = pltpu.make_async_copy(place_v, place_s, sem)
    copy.start()
    for item in range(30):
        now = slice(PAD + keep, PAD + keep + slots)
        value = cur[item, now, :] + step * rate_ref[item, now, :] + half_square * twice_ref[item]
        wide[pl.ds(item, slots, stride=STEP), :] = value
    for item in (30, 31):
        wide[pl.ds(item, slots + 1, stride=STEP), :] = jnp.zeros((slots + 1, LANES), jnp.float32)
    copy.wait()
    for slot in range(slots):
        lead_at = place_s[0, slot]
        index_ref[0, slot : slot + 1, :] = ends_ref[pl.ds(lead_at, 1), :]
        index_ref[1, slot : slot + 1, :] = ends_ref[pl.ds(lead_at + 1, 1), :]
    near, far = index_ref[0], index_ref[1]
    lane = lax.broadcasted_iota(jnp.int32, (slots, LANES), 1)
    slot_no = LANES * lax.broadcasted_iota(jnp.int32, (slots, LANES), 0) + lane
    goal = (2 * slot_no + 1).astype(jnp.float32)
    beyond = jnp.broadcast_to(near[:, LANES - 1 :], (slots, LANES)) <= goal

    def pick(index):
        return jnp.where(beyond, lane_gather(far, index), lane_gather(near, index))

    found = jnp.zeros((slots, LANES), jnp.int32)
    size = LANES // 2
    while size:
        passed = pick(found + (size - 1)) <= goal
        found = jnp.where(passed, found + size, found)
        size //= 2
    mine = pick(found).astype(jnp.int32)
    split = mine & 1
    begin = (mine >> 1) - 1 - split
    kind = split * (1 + slot_no - begin)
    index_ref[0] = found.astype(jnp.float32)
    index_ref[1] = kind.astype(jnp.float32)
    index_ref[2] = (lane < jnp.broadcast_to(found[:, 0:1], (slots, LANES))).astype(jnp.float32)
    matrix = weights[...]
    chunk = 8 * LANES
    results = []
    for part in range(slots // 8):
        span = slice(chunk * part, chunk * (part + 1))
        columns = []
        for slot in range(8 * part, 8 * part + 8):
            lead_at = place_s[0, slot] * STEP
            lane_idx = jnp.broadcast_to(index_ref[0, slot : slot + 1, :], (8, LANES)).astype(jnp.int32)
            ahead = jnp.broadcast_to(index_ref[2, slot : slot + 1, :], (8, LANES)) > 0.5
            tiles = []
            for row in range(0, WIDE, 8):
                one = wide[pl.ds(lead_at + row, 8), :]
                two = wide[pl.ds(lead_at + STEP + row, 8), :]
                tiles.append(lane_gather(jnp.where(ahead, two, one), lane_idx))
            columns.append(jnp.concatenate(tiles, axis=0))
        values = jnp.concatenate(columns, axis=1)
        high = values.astype(jnp.bfloat16)
        rest = values - high.astype(jnp.float32)
        low = rest.astype(jnp.bfloat16)
        last = (rest - low.astype(jnp.float32)).astype(jnp.bfloat16)
        stack = jnp.concatenate([high, low, last, high], axis=0)
        children = jnp.dot(matrix, stack, preferred_element_type=jnp.float32)
        for sub in range(8):
            slot = 8 * part + sub
            cut = slice(LANES * sub, LANES * (sub + 1))
            tag = jnp.broadcast_to(index_ref[1, slot : slot + 1, :], (PACK, LANES))
            value = jnp.where(
                tag < 0.5,
                children[2 * PACK :, cut],
                jnp.where(tag < 1.5, children[:PACK, cut], children[PACK : 2 * PACK, cut]),
            )
            for node in range(10):
                out_ref[node, :, LANES * slot : LANES * (slot + 1)] = value[4 * node : 4 * node + 3]
        result = pltpu.make_async_copy(out_ref.at[:, :, span], out_hbm.at[:, :, span], out_sems.at[part])
        result.start()
        results.append(result)
    for result in results:
        result.wait()


def swaps(start, count):
    pairs = [(i, i + 1) for i in range(start, count - 1, 2)]
    return pairs + [(j, i) for i, j in pairs]


def shards(state, depth, metric, partner, refine, diff_ops, lift, prolong):
    sizes = Sizes(state.shape[2])
    count = lax.axis_size(AXES)
    blocks, rows, slots, halo = sizes.blocks, sizes.rows, sizes.slots, sizes.halo
    depth, partner, refine = [x.reshape(blocks, LANES) for x in (depth, partner, refine)]
    state, diff_ops, prolong = [jnp.transpose(x, (1, 0, 2)) for x in (state, diff_ops, prolong)]
    state, depth, metric, partner, refine, diff_ops, lift, prolong = [
        pltpu.with_memory_space_constraint(x, pltpu.HBM)
        for x in (state, depth, metric, partner, refine, diff_ops, lift, prolong)
    ]
    f32, i32 = jnp.float32, jnp.int32
    packed = jax.ShapeDtypeStruct((SENT * halo, LANES), f32)
    dense = [
        pltpu.VMEM((blocks, LANES), f32),
        pltpu.VMEM(metric.shape, f32),
        pltpu.VMEM((blocks, LANES), i32),
        pltpu.VMEM((blocks, LANES), i32),
    ]
    stats, even, odd = pl.pallas_call(
        functools.partial(pack_kernel, sizes),
        name="pack",
        out_shape=(jax.ShapeDtypeStruct((count, LANES), f32), packed, packed),
        in_specs=[HBM] * 5,
        out_specs=(HBM, VMEM, VMEM),
        scratch_shapes=[
            pltpu.VMEM((count, LANES), f32),
            pltpu.VMEM((10, 3, LANES * halo), f32),
            pltpu.VMEM((10, 3, LANES * halo), f32),
            *dense,
            pltpu.VMEM((8 * blocks, LANES), f32),
            pltpu.SemaphoreType.DMA((6,)),
            pltpu.SemaphoreType.DMA,
        ],
        compiler_params=PARAMS,
    )(state, depth, metric, partner, refine)
    odd = lax.ppermute(odd, AXES, swaps(1, count))
    even = lax.ppermute(even, AXES, swaps(0, count))
    stats = lax.all_to_all(stats, AXES, 0, 0, tiled=True)
    even, odd, stats = [pltpu.with_memory_space_constraint(x, pltpu.VMEM) for x in (even, odd, stats)]
    cur, aux = pl.pallas_call(
        functools.partial(prep_kernel, sizes),
        name="lay_out",
        cost_estimate=pl.CostEstimate(flops=1 << 24, transcendentals=1 << 16, bytes_accessed=1 << 24),
        out_shape=(
            jax.ShapeDtypeStruct((30, blocks, LANES), f32),
            jax.ShapeDtypeStruct((7, blocks, LANES), f32),
        ),
        in_specs=[HBM] * 5,
        out_specs=(VMEM,) * 2,
        scratch_shapes=[
            pltpu.VMEM(state.shape, f32),
            *dense,
            pltpu.VMEM((8 * blocks, LANES), f32),
            pltpu.VMEM((LAID * blocks, LANES), f32),
            pltpu.SemaphoreType.DMA((5,)),
        ],
        compiler_params=PARAMS,
    )(state, depth, metric, partner, refine)
    cur, rates, twice, weights, ends = pl.pallas_call(
        functools.partial(first_kernel, sizes),
        name="rates_twice",
        cost_estimate=pl.CostEstimate(flops=1024, transcendentals=0, bytes_accessed=1024),
        out_shape=(
            jax.ShapeDtypeStruct((30, sizes.tall, LANES), f32),
            jax.ShapeDtypeStruct((30, sizes.tall, LANES), f32),
            jax.ShapeDtypeStruct((30, slots, LANES), f32),
            jax.ShapeDtypeStruct((3 * PACK, 4 * WIDE), jnp.bfloat16),
            jax.ShapeDtypeStruct((2, slots, LANES), f32),
        ),
        in_specs=[VMEM] * 4 + [HBM] * 3,
        out_specs=(VMEM,) * 5,
        scratch_shapes=[
            pltpu.VMEM((15, rows, LANES), f32),
            pltpu.VMEM((7, sizes.tall, LANES), f32),
            pltpu.SMEM(diff_ops.shape, f32),
            pltpu.SMEM(lift.shape, f32),
            pltpu.VMEM(prolong.shape, f32),
            pltpu.SemaphoreType.DMA((3,)),
        ],
        compiler_params=PARAMS,
    )(cur, aux, odd, even, diff_ops, lift, prolong)
    refined = pl.pallas_call(
        functools.partial(refine_kernel, sizes),
        name="sum_and_refine",
        out_shape=jax.ShapeDtypeStruct((10, 3, LANES * slots), f32),
        in_specs=[VMEM] * 6,
        out_specs=HBM,
        scratch_shapes=[
            pltpu.VMEM((10, 3, LANES * slots), f32),
            pltpu.VMEM((slots + 8, LANES), f32),
            pltpu.VMEM((8, LANES), i32),
            pltpu.SMEM((8, LANES), i32),
            pltpu.VMEM((STEP * (slots + 1), LANES), f32),
            pltpu.VMEM((3, slots, LANES), f32),
            pltpu.SemaphoreType.DMA((slots // 8,)),
            pltpu.SemaphoreType.DMA,
        ],
        compiler_params=PARAMS,
    )(cur, rates, twice, weights, ends, stats)
    return jnp.transpose(refined, (1, 0, 2))


def solution(mesh):
    return jax.shard_map(
        shards,
        mesh=mesh,
        in_specs=(
            P(None, None, AXES),
            P(AXES),
            P(None, AXES),
            P(AXES),
            P(AXES),
            P(),
            P(),
            P(),
        ),
        out_specs=P(None, None, AXES),
        check_vma=False,
    )
```

```python
import functools

import jax
import jax.numpy as jnp
from jax import lax
from jax.experimental import pallas as pl
from jax.experimental.pallas import tpu as pltpu
from jax.sharding import PartitionSpec as P

GRAVITY = 9.81
COURANT = 0.5
HIGH = lax.Precision.HIGHEST
LANES = 128
AXES = ("row", "col")
FACES = ((0, 1, 2, 3), (3, 6, 8, 9), (9, 7, 4, 0))
PACK = 40
LAID = 41
SENT = 37
WIDE = 32
STEP = 33
PAD = 8

VMEM = pl.BlockSpec(memory_space=pltpu.VMEM)
HBM = pl.BlockSpec(memory_space=pltpu.HBM)
PARAMS = pltpu.CompilerParams(vmem_limit_bytes=48 * 1024 * 1024)


class Sizes:
    def __init__(self, cells):
        self.cells = cells
        self.blocks = cells // LANES
        self.margin = cells // 4 // LANES
        self.halo = self.margin + 1
        self.rows = -(-(self.blocks + 2 * self.halo) // 8) * 8
        self.tall = self.rows + 2 * PAD
        self.slots = 3 * self.blocks // 2
        self.keep = self.halo - self.margin


def fetch_all(pairs, sems):
    copies = [pltpu.make_async_copy(src, dst, sems.at[num]) for num, (src, dst) in enumerate(pairs)]
    for copy in copies:
        copy.start()
    return copies


def split_metric(metric_ref, spread, blocks):
    for block in range(blocks):
        spread[8 * block : 8 * block + 4, :] = metric_ref[:, LANES * block : LANES * (block + 1)]
    return [spread[pl.ds(comp, blocks, stride=8), :] for comp in range(4)]


def pack_kernel(
    sizes, state_hbm, depth_hbm, metric_hbm, partner_hbm, refine_hbm, stats_hbm, even_ref, odd_ref,
    stats_ref, state_even, state_odd, depth_ref, metric_ref, partner_ref, refine_ref, spread, sems, sem,
):
    blocks, halo = sizes.blocks, sizes.halo
    wide = LANES * halo
    late = blocks - halo
    even = (lax.axis_index(AXES) + 1) % 2 * late
    odd = late - even
    copies = fetch_all(
        (
            (depth_hbm, depth_ref),
            (metric_hbm, metric_ref),
            (refine_hbm, refine_ref),
            (partner_hbm, partner_ref),
            (state_hbm.at[:, :, pl.ds(pl.multiple_of(LANES * even, LANES), wide)], state_even),
            (state_hbm.at[:, :, pl.ds(pl.multiple_of(LANES * odd, LANES), wide)], state_odd),
        ),
        sems,
    )
    for copy in copies[:3]:
        copy.wait()
    rx, ry, sx, sy = split_metric(metric_ref, spread, blocks)
    depth = depth_ref[...]
    refine = refine_ref[...].astype(jnp.float32)
    faces = ((sx, sy), (rx + sx, ry + sy), (rx, ry))
    lengths = [jnp.sqrt(vx * vx + vy * vy) for vx, vy in faces]
    rate = jnp.sqrt(GRAVITY * depth) * jnp.maximum(jnp.maximum(lengths[0], lengths[1]), lengths[2])
    top = jnp.max(jnp.max(rate, axis=0, keepdims=True), axis=1, keepdims=True)
    extra = jnp.sum(jnp.sum(refine, axis=0, keepdims=True), axis=1, keepdims=True)
    shape = stats_ref.shape
    lane = lax.broadcasted_iota(jnp.int32, shape, 1)
    stats_ref[...] = jnp.where(
        lane < LANES // 2, jnp.broadcast_to(top, shape), jnp.broadcast_to(extra, shape)
    )
    sent = pltpu.make_async_copy(stats_ref, stats_hbm, sem)
    sent.start()
    for copy in copies[3:]:
        copy.wait()
    for ref, source, start in ((even_ref, state_even, even), (odd_ref, state_odd, odd)):
        pack_state(source, ref, halo, SENT, 3)
        at = pl.ds(start, halo)
        dense = [depth_ref[at, :]]
        dense += [spread[pl.ds(8 * start + comp, halo, stride=8), :] for comp in range(4)]
        dense += [partner_ref[at, :].astype(jnp.float32), refine_ref[at, :].astype(jnp.float32)]
        for num, value in enumerate(dense):
            ref[pl.ds(30 + num, halo, stride=SENT), :] = value
    sent.wait()


def pack_state(source, target, blocks, height, width):
    for block in range(blocks):
        for node in range(10):
            at = height * block + width * node
            target[at : at + 3, :] = source[node, :, LANES * block : LANES * (block + 1)]


def pair_index(partner):
    lane = lax.broadcasted_iota(jnp.int32, partner.shape, 1)
    target = lane + partner.astype(jnp.int32)
    return target & (LANES - 1), (target >= 0) & (target < LANES)


def lane_gather(values, index):
    return jnp.take_along_axis(values, index, axis=1, mode="promise_in_bounds")


def outer_values(load, index, inside):
    shape = index.shape
    lane = lax.broadcasted_iota(jnp.int32, shape, 1)

    def prev(item):
        return pltpu.roll(jnp.where(lane == LANES - 1, load(item, -1), load(item, 0)), 1, 1)

    def after(item):
        return pltpu.roll(jnp.where(lane == 0, load(item, 1), load(item, 0)), LANES - 1, 1)

    def across(item):
        other = jnp.where(lane < LANES // 2, load(item, 1), load(item, -1))
        return jnp.where(inside, lane_gather(load(item, 0), index), lane_gather(other, index))

    return prev, after, across


def wall_masks(sizes, start, place, count, partner):
    shape = partner.shape
    lane = lax.broadcasted_iota(jnp.int32, shape, 1)
    row = lax.broadcasted_iota(jnp.int32, shape, 0) + start
    first = (lane == 0) & (row == sizes.halo) & (place == 0)
    last = (lane == LANES - 1) & (row == sizes.halo + sizes.blocks - 1) & (place == count - 1)
    return first, last, partner == 0


def tendency(load, geo, walls, index, inside, diff_ref, lift_ref):
    speed_sq, rx, ry, sx, sy = geo[:5]
    outer_sq, waves, ghosts = geo[5:8], geo[8:11], geo[11:14]
    inflow, along_r, along_s = [None] * 10, [None] * 10, [None] * 10

    def add(total, term):
        return term if total is None else total + term

    for b in range(10):
        eta, mom_x, mom_y = [load(10 * field + b, 0) for field in range(3)]
        flow_r = -(rx * mom_x + ry * mom_y)
        flow_s = -(sx * mom_x + sy * mom_y)
        for a in range(10):
            d_r, d_s = diff_ref[a, 0, b], diff_ref[a, 1, b]
            inflow[a] = add(inflow[a], d_r * flow_r + d_s * flow_s)
            along_r[a] = add(along_r[a], d_r * eta)
            along_s[a] = add(along_s[a], d_s * eta)
    pull = (-speed_sq * rx, -speed_sq * ry)
    push = (-speed_sq * sx, -speed_sq * sy)
    sums = [inflow] + [[pull[k] * along_r[a] + push[k] * along_s[a] for a in range(10)] for k in range(2)]
    half_r = (0.5 * rx, 0.5 * ry)
    half_s = (0.5 * sx, 0.5 * sy)
    vectors = (
        (-half_s[0], -half_s[1]),
        (half_r[0] + half_s[0], half_r[1] + half_s[1]),
        (-half_r[0], -half_r[1]),
    )
    fetch = outer_values(load, index, inside)
    for face in range(3):
        vec_x, vec_y = vectors[face]
        theirs = FACES[(1, 0, 2)[face]]
        wall = walls[face]
        for j in range(4):
            node, match = FACES[face][j], theirs[3 - j]
            in_eta, in_x, in_y = [load(10 * field + node, 0) for field in range(3)]
            ext_eta, ext_x, ext_y = [fetch[face](10 * field + match) for field in range(3)]
            bounce = (in_x * vec_x + in_y * vec_y) * ghosts[face]
            d_eta = jnp.where(wall, 0.0, in_eta - ext_eta)
            d_x = jnp.where(wall, bounce * vec_x, in_x - ext_x)
            d_y = jnp.where(wall, bounce * vec_y, in_y - ext_y)
            head = jnp.where(wall, 0.0, speed_sq * in_eta - outer_sq[face] * ext_eta)
            jumps = (
                d_x * vec_x + d_y * vec_y - waves[face] * d_eta,
                head * vec_x - waves[face] * d_x,
                head * vec_y - waves[face] * d_y,
            )
            for a in range(10):
                weight = lift_ref[a, 4 * face + j]
                for field in range(3):
                    sums[field][a] = sums[field][a] + weight * jumps[field]
    return [sums[field][a] for field in range(3) for a in range(10)]


def child_matrix(prolong_ref):
    f32 = jnp.float32
    node_r = lax.broadcasted_iota(jnp.int32, (PACK, 10), 0) // 4
    spread_r = (node_r == lax.broadcasted_iota(jnp.int32, (PACK, 10), 1)).astype(f32)
    item_c = lax.broadcasted_iota(jnp.int32, (10, WIDE), 1)
    spread_c = (item_c % 10 == lax.broadcasted_iota(jnp.int32, (10, WIDE), 0)).astype(f32)
    row = lax.broadcasted_iota(jnp.int32, (PACK, WIDE), 0)
    col = lax.broadcasted_iota(jnp.int32, (PACK, WIDE), 1)
    same = row % 4 == col // 10
    parts = []
    for child in range(2):
        left = jnp.dot(spread_r, prolong_ref[:, child, :], precision=HIGH, preferred_element_type=f32)
        full = jnp.dot(left, spread_c, precision=HIGH, preferred_element_type=f32)
        parts.append(jnp.where(same, full, 0.0))
    parts.append((same & (row // 4 == col % 10)).astype(f32))
    whole = jnp.concatenate(parts, axis=0)
    rounded = whole.astype(jnp.bfloat16)
    rest = (whole - rounded.astype(f32)).astype(jnp.bfloat16)
    return jnp.concatenate([rounded, rounded, rest], axis=1)


def sum_children(sizes, refine, ends_ref, lines_ref):
    slots, f32 = sizes.slots, jnp.float32
    counts = (1.0 + refine).astype(jnp.bfloat16)
    row_i = lax.broadcasted_iota(jnp.int32, (LANES, LANES), 0)
    col_i = lax.broadcasted_iota(jnp.int32, (LANES, LANES), 1)
    upper = (row_i <= col_i).astype(jnp.bfloat16)
    within = jnp.dot(counts, upper, preferred_element_type=f32)
    whole = jnp.dot(counts, jnp.ones((LANES, LANES), jnp.bfloat16), preferred_element_type=f32)
    row_s = lax.broadcasted_iota(jnp.int32, (slots, slots), 0)
    col_s = lax.broadcasted_iota(jnp.int32, (slots, slots), 1)
    lower = (col_s < row_s).astype(jnp.bfloat16)
    before = jnp.dot(lower, whole.astype(jnp.bfloat16), preferred_element_type=f32)
    before = before - before[sizes.margin : sizes.margin + 1, :]
    ends_ref[0] = 2.0 * (within + before) + refine
    ends_ref[1] = before + whole
    ones = jnp.ones((8, LANES), jnp.bfloat16)
    sums = lax.dot_general(ones, counts, (((1,), (1,)), ((), ())), preferred_element_type=f32)
    gap = lax.broadcasted_iota(jnp.int32, (slots, LANES), 1) - lax.broadcasted_iota(jnp.int32, (slots, LANES), 0)
    lines = [
        jnp.dot(sums.astype(jnp.bfloat16), (gap >= least).astype(jnp.bfloat16), preferred_element_type=f32)
        for least in (2, 1, 0)
    ]
    own = lines[1][:, sizes.margin : sizes.margin + 1]
    for num in range(3):
        lines_ref[num] = lines[num] - own


def prep_kernel(
    sizes, state_hbm, depth_hbm, metric_hbm, partner_hbm, refine_hbm, cur, aux,
    state_ref, depth_ref, metric_ref, partner_ref, refine_ref, spread, wide, sems,
):
    blocks = sizes.blocks
    copies = fetch_all(
        (
            (metric_hbm, metric_ref),
            (state_hbm, state_ref),
            (depth_hbm, depth_ref),
            (partner_hbm, partner_ref),
            (refine_hbm, refine_ref),
        ),
        sems,
    )
    for copy in copies:
        copy.wait()
    metric = split_metric(metric_ref, spread, blocks)
    dense = [depth_ref[...], *metric, partner_ref[...].astype(jnp.float32), refine_ref[...].astype(jnp.float32)]
    for num in range(7):
        aux[num] = dense[num]
    pack_state(state_ref, wide, blocks, LAID, 4)
    for field in range(3):
        for node in range(10):
            cur[10 * field + node] = wide[pl.ds(4 * node + field, blocks, stride=LAID), :]


def first_kernel(
    sizes, cur_own, aux_own, odd_ref, even_ref, diff_hbm, lift_hbm, prolong_hbm,
    cur, rate_ref, twice_ref, weights, ends_ref, lines_ref,
    geo_ref, aux, diff_ref, lift_ref, prolong_ref, sems,
):
    blocks, halo = sizes.blocks, sizes.halo
    top, bottom = PAD + halo, PAD + halo + blocks
    place = lax.axis_index(AXES)
    count = lax.axis_size(AXES)
    copies = fetch_all(((diff_hbm, diff_ref), (lift_hbm, lift_ref), (prolong_hbm, prolong_ref)), sems)
    even = place % 2 == 0

    def set_halo(target, num, row):
        by_even = even_ref[pl.ds(row, halo, stride=SENT), :]
        by_odd = odd_ref[pl.ds(row, halo, stride=SENT), :]
        target[num, top - halo : top, :] = jnp.where(even, by_odd, by_even)
        target[num, bottom : bottom + halo, :] = jnp.where(even, by_even, by_odd)

    for num in range(7):
        set_halo(aux, num, 30 + num)
        aux[num, top:bottom, :] = aux_own[num]
    for field in range(3):
        for node in range(10):
            item = 10 * field + node
            set_halo(cur, item, 3 * node + field)
            cur[item, top:bottom, :] = cur_own[item]

    for copy in copies:
        copy.wait()
    weights[...] = child_matrix(prolong_ref)
    begin = PAD + sizes.keep
    sum_children(sizes, aux[6, begin : begin + sizes.slots, :], ends_ref, lines_ref)

    def step(group, carry):
        base = PAD + 8 * group

        def load_aux(item, shift):
            return aux[item, pl.ds(base + shift, 8), :]

        def load(item, shift):
            return cur[item, pl.ds(base + shift, 8), :]

        depth, rx, ry, sx, sy, partner = [load_aux(num, 0) for num in range(6)]
        index, inside = pair_index(partner)
        fetch = outer_values(load_aux, index, inside)
        walls = wall_masks(sizes, 8 * group, place, count, partner)
        speed_sq = GRAVITY * depth
        outer_sq = [jnp.where(walls[k], speed_sq, GRAVITY * fetch[k](0)) for k in range(3)]
        faces = ((sx, sy), (rx + sx, ry + sy), (rx, ry))
        squares = [vx * vx + vy * vy for vx, vy in faces]
        waves = [
            0.5 * jnp.sqrt(squares[k]) * jnp.sqrt(jnp.maximum(speed_sq, outer_sq[k])) for k in range(3)
        ]
        ghosts = [8.0 / squares[k] for k in range(3)]
        geo = [speed_sq, rx, ry, sx, sy, *outer_sq, *waves, *ghosts]
        rates = tendency(load, geo, walls, index, inside, diff_ref, lift_ref)
        at = pl.ds(pl.multiple_of(8 * group, 8), 8)
        for num, value in enumerate([*geo, partner]):
            geo_ref[num, at, :] = value
        for item in range(30):
            rate_ref[item, pl.ds(base, 8), :] = rates[item]
        return carry

    lax.fori_loop(0, sizes.rows // 8, step, 0)

    def again(group, carry):
        row = 8 * group + sizes.keep
        at = pl.ds(row, 8)

        def load(item, shift):
            return rate_ref[item, pl.ds(PAD + row + shift, 8), :]

        geo = [geo_ref[num, at, :] for num in range(14)]
        partner = geo_ref[14, at, :]
        index, inside = pair_index(partner)
        walls = wall_masks(sizes, row, place, count, partner)
        rates = tendency(load, geo, walls, index, inside, diff_ref, lift_ref)
        for item in range(30):
            twice_ref[item, pl.ds(pl.multiple_of(8 * group, 8), 8), :] = rates[item]
        return carry

    lax.fori_loop(0, sizes.slots // 8, again, 0)


def refine_kernel(
    sizes, cur, rate_ref, twice_ref, weights, base_ref, lines_ref, stats_ref, out_hbm,
    out_ref, place_v, place_s, wide, index_ref, out_sems, sem,
):
    slots, keep = sizes.slots, sizes.keep
    place = lax.axis_index(AXES)
    stats = stats_ref[...]
    half = LANES // 2
    row_n = lax.broadcasted_iota(jnp.int32, stats.shape, 0)
    top = jnp.max(stats, axis=0, keepdims=True)
    earlier = jnp.sum(jnp.where(row_n < place, stats, 0.0), axis=0, keepdims=True)
    left = lax.broadcasted_iota(jnp.int32, (1, LANES), 1) < half
    top = jnp.where(left, top, pltpu.roll(top, half, 1))
    earlier = jnp.where(left, pltpu.roll(earlier, half, 1), earlier)
    step = COURANT / top
    half_square = 0.5 * step * step
    start = earlier - (place * (sizes.cells // 2)).astype(jnp.float32)
    first_slot = LANES * lax.broadcasted_iota(jnp.int32, (slots, LANES), 1).astype(jnp.float32)
    lead = jnp.sum((base_ref[1] + start <= first_slot).astype(jnp.float32), axis=0, keepdims=True)
    lead = jnp.clip(lead.astype(jnp.int32), 0, slots - 1)
    place_v[...] = jnp.broadcast_to(lead, (8, LANES))
    copy = pltpu.make_async_copy(place_v, place_s, sem)
    copy.start()
    for item in range(30):
        now = slice(PAD + keep, PAD + keep + slots)
        value = cur[item, now, :] + step * rate_ref[item, now, :] + half_square * twice_ref[item]
        wide[pl.ds(item, slots, stride=STEP), :] = value
    for item in (30, 31):
        wide[pl.ds(item, slots + 1, stride=STEP), :] = jnp.zeros((slots + 1, LANES), jnp.float32)
    slot_start = LANES * lax.broadcasted_iota(jnp.int32, (slots, LANES), 0).astype(jnp.float32)
    begun = [lines_ref[num, 0:1, :] + start <= slot_start for num in range(3)]
    near, far = [
        2.0 * start
        + jnp.dot(
            (begun[num] & ~begun[num + 1]).astype(jnp.float32)[:, :slots],
            base_ref[0],
            precision=HIGH,
            preferred_element_type=jnp.float32,
        )
        for num in (1, 0)
    ]
    lane = lax.broadcasted_iota(jnp.int32, (slots, LANES), 1)
    slot_no = LANES * lax.broadcasted_iota(jnp.int32, (slots, LANES), 0) + lane
    goal = (2 * slot_no + 1).astype(jnp.float32)
    beyond = jnp.broadcast_to(near[:, LANES - 1 :], (slots, LANES)) <= goal

    def pick(index):
        return jnp.where(beyond, lane_gather(far, index), lane_gather(near, index))

    found = jnp.zeros((slots, LANES), jnp.int32)
    size = LANES // 2
    while size:
        passed = pick(found + (size - 1)) <= goal
        found = jnp.where(passed, found + size, found)
        size //= 2
    mine = pick(found).astype(jnp.int32)
    split = mine & 1
    begin = (mine >> 1) - 1 - split
    kind = split * (1 + slot_no - begin)
    index_ref[0] = found.astype(jnp.float32)
    index_ref[1] = kind.astype(jnp.float32)
    index_ref[2] = (lane < jnp.broadcast_to(found[:, 0:1], (slots, LANES))).astype(jnp.float32)
    copy.wait()
    matrix = weights[...]
    chunk = 8 * LANES
    results = []
    for part in range(slots // 8):
        span = slice(chunk * part, chunk * (part + 1))
        columns = []
        for slot in range(8 * part, 8 * part + 8):
            lead_at = place_s[0, slot] * STEP
            lane_idx = jnp.broadcast_to(index_ref[0, slot : slot + 1, :], (8, LANES)).astype(jnp.int32)
            ahead = jnp.broadcast_to(index_ref[2, slot : slot + 1, :], (8, LANES)) > 0.5
            tiles = []
            for row in range(0, WIDE, 8):
                one = wide[pl.ds(lead_at + row, 8), :]
                two = wide[pl.ds(lead_at + STEP + row, 8), :]
                tiles.append(lane_gather(jnp.where(ahead, two, one), lane_idx))
            columns.append(jnp.concatenate(tiles, axis=0))
        values = jnp.concatenate(columns, axis=1)
        high = values.astype(jnp.bfloat16)
        low = (values - high.astype(jnp.float32)).astype(jnp.bfloat16)
        stack = jnp.concatenate([high, low, high], axis=0)
        children = jnp.dot(matrix, stack, preferred_element_type=jnp.float32)
        for sub in range(8):
            slot = 8 * part + sub
            cut = slice(LANES * sub, LANES * (sub + 1))
            tag = jnp.broadcast_to(index_ref[1, slot : slot + 1, :], (PACK, LANES))
            value = jnp.where(
                tag < 0.5,
                children[2 * PACK :, cut],
                jnp.where(tag < 1.5, children[:PACK, cut], children[PACK : 2 * PACK, cut]),
            )
            for node in range(10):
                out_ref[node, :, LANES * slot : LANES * (slot + 1)] = value[4 * node : 4 * node + 3]
        result = pltpu.make_async_copy(out_ref.at[:, :, span], out_hbm.at[:, :, span], out_sems.at[part])
        result.start()
        results.append(result)
    for result in results:
        result.wait()


def swaps(start, count):
    pairs = [(i, i + 1) for i in range(start, count - 1, 2)]
    return pairs + [(j, i) for i, j in pairs]


def shards(state, depth, metric, partner, refine, diff_ops, lift, prolong):
    sizes = Sizes(state.shape[2])
    count = lax.axis_size(AXES)
    blocks, rows, slots, halo = sizes.blocks, sizes.rows, sizes.slots, sizes.halo
    depth, partner, refine = [x.reshape(blocks, LANES) for x in (depth, partner, refine)]
    state, diff_ops, prolong = [jnp.transpose(x, (1, 0, 2)) for x in (state, diff_ops, prolong)]
    state, depth, metric, partner, refine, diff_ops, lift, prolong = [
        pltpu.with_memory_space_constraint(x, pltpu.HBM)
        for x in (state, depth, metric, partner, refine, diff_ops, lift, prolong)
    ]
    f32, i32 = jnp.float32, jnp.int32
    packed = jax.ShapeDtypeStruct((SENT * halo, LANES), f32)
    dense = [
        pltpu.VMEM((blocks, LANES), f32),
        pltpu.VMEM(metric.shape, f32),
        pltpu.VMEM((blocks, LANES), i32),
        pltpu.VMEM((blocks, LANES), i32),
    ]
    stats, even, odd = pl.pallas_call(
        functools.partial(pack_kernel, sizes),
        name="pack",
        out_shape=(jax.ShapeDtypeStruct((count, LANES), f32), packed, packed),
        in_specs=[HBM] * 5,
        out_specs=(HBM, VMEM, VMEM),
        scratch_shapes=[
            pltpu.VMEM((count, LANES), f32),
            pltpu.VMEM((10, 3, LANES * halo), f32),
            pltpu.VMEM((10, 3, LANES * halo), f32),
            *dense,
            pltpu.VMEM((8 * blocks, LANES), f32),
            pltpu.SemaphoreType.DMA((6,)),
            pltpu.SemaphoreType.DMA,
        ],
        compiler_params=PARAMS,
    )(state, depth, metric, partner, refine)
    odd = lax.ppermute(odd, AXES, swaps(1, count))
    even = lax.ppermute(even, AXES, swaps(0, count))
    stats = lax.all_to_all(stats, AXES, 0, 0, tiled=True)
    even, odd, stats = [pltpu.with_memory_space_constraint(x, pltpu.VMEM) for x in (even, odd, stats)]
    cur, aux = pl.pallas_call(
        functools.partial(prep_kernel, sizes),
        name="lay_out",
        cost_estimate=pl.CostEstimate(flops=1 << 24, transcendentals=1 << 16, bytes_accessed=1 << 24),
        out_shape=(
            jax.ShapeDtypeStruct((30, blocks, LANES), f32),
            jax.ShapeDtypeStruct((7, blocks, LANES), f32),
        ),
        in_specs=[HBM] * 5,
        out_specs=(VMEM,) * 2,
        scratch_shapes=[
            pltpu.VMEM(state.shape, f32),
            *dense,
            pltpu.VMEM((8 * blocks, LANES), f32),
            pltpu.VMEM((LAID * blocks, LANES), f32),
            pltpu.SemaphoreType.DMA((5,)),
        ],
        compiler_params=PARAMS,
    )(state, depth, metric, partner, refine)
    cur, rates, twice, weights, ends, lines = pl.pallas_call(
        functools.partial(first_kernel, sizes),
        name="rates_twice",
        cost_estimate=pl.CostEstimate(flops=1024, transcendentals=0, bytes_accessed=1024),
        out_shape=(
            jax.ShapeDtypeStruct((30, sizes.tall, LANES), f32),
            jax.ShapeDtypeStruct((30, sizes.tall, LANES), f32),
            jax.ShapeDtypeStruct((30, slots, LANES), f32),
            jax.ShapeDtypeStruct((3 * PACK, 3 * WIDE), jnp.bfloat16),
            jax.ShapeDtypeStruct((2, slots, LANES), f32),
            jax.ShapeDtypeStruct((3, 8, LANES), f32),
        ),
        in_specs=[VMEM] * 4 + [HBM] * 3,
        out_specs=(VMEM,) * 6,
        scratch_shapes=[
            pltpu.VMEM((15, rows, LANES), f32),
            pltpu.VMEM((7, sizes.tall, LANES), f32),
            pltpu.SMEM(diff_ops.shape, f32),
            pltpu.SMEM(lift.shape, f32),
            pltpu.VMEM(prolong.shape, f32),
            pltpu.SemaphoreType.DMA((3,)),
        ],
        compiler_params=PARAMS,
    )(cur, aux, odd, even, diff_ops, lift, prolong)
    refined = pl.pallas_call(
        functools.partial(refine_kernel, sizes),
        name="sum_and_refine",
        out_shape=jax.ShapeDtypeStruct((10, 3, LANES * slots), f32),
        in_specs=[VMEM] * 7,
        out_specs=HBM,
        scratch_shapes=[
            pltpu.VMEM((10, 3, LANES * slots), f32),
            pltpu.VMEM((8, LANES), i32),
            pltpu.SMEM((8, LANES), i32),
            pltpu.VMEM((STEP * (slots + 1), LANES), f32),
            pltpu.VMEM((3, slots, LANES), f32),
            pltpu.SemaphoreType.DMA((slots // 8,)),
            pltpu.SemaphoreType.DMA,
        ],
        compiler_params=PARAMS,
    )(cur, rates, twice, weights, ends, lines, stats)
    return jnp.transpose(refined, (1, 0, 2))


def solution(mesh):
    return jax.shard_map(
        shards,
        mesh=mesh,
        in_specs=(
            P(None, None, AXES),
            P(AXES),
            P(None, AXES),
            P(AXES),
            P(AXES),
            P(),
            P(),
            P(),
        ),
        out_specs=P(None, None, AXES),
        check_vma=False,
    )
```

```python
import functools

import jax
import jax.numpy as jnp
from jax import lax
from jax.experimental import pallas as pl
from jax.experimental.pallas import tpu as pltpu
from jax.sharding import PartitionSpec as P

GRAVITY = 9.81
COURANT = 0.5
HIGH = lax.Precision.HIGHEST
LANES = 128
AXES = ("row", "col")
FACES = ((0, 1, 2, 3), (3, 6, 8, 9), (9, 7, 4, 0))
PACK = 40
LAID = 41
SENT = 37
WIDE = 32
STEP = 33
TALL = 16
PAD = 8

VMEM = pl.BlockSpec(memory_space=pltpu.VMEM)
HBM = pl.BlockSpec(memory_space=pltpu.HBM)
PARAMS = pltpu.CompilerParams(vmem_limit_bytes=48 * 1024 * 1024)


class Sizes:
    def __init__(self, cells):
        self.cells = cells
        self.blocks = cells // LANES
        self.margin = cells // 4 // LANES
        self.halo = self.margin + 1
        self.rows = -(-(self.blocks + 2 * self.halo) // 8) * 8
        self.tall = self.rows + 2 * PAD
        self.slots = 3 * self.blocks // 2
        self.keep = self.halo - self.margin


def fetch_all(pairs, sems):
    copies = [pltpu.make_async_copy(src, dst, sems.at[num]) for num, (src, dst) in enumerate(pairs)]
    for copy in copies:
        copy.start()
    return copies


def split_metric(metric_ref, spread, blocks):
    for block in range(blocks):
        spread[8 * block : 8 * block + 4, :] = metric_ref[:, LANES * block : LANES * (block + 1)]
    return [spread[pl.ds(comp, blocks, stride=8), :] for comp in range(4)]


def pack_kernel(
    sizes, state_hbm, depth_hbm, metric_hbm, partner_hbm, refine_hbm, stats_ref, even_ref, odd_ref,
    state_even, state_odd, depth_ref, metric_ref, partner_ref, refine_ref, spread, sems,
):
    blocks, halo = sizes.blocks, sizes.halo
    wide = LANES * halo
    late = blocks - halo
    even = (lax.axis_index(AXES) + 1) % 2 * late
    odd = late - even
    copies = fetch_all(
        (
            (depth_hbm, depth_ref),
            (metric_hbm, metric_ref),
            (refine_hbm, refine_ref),
            (partner_hbm, partner_ref),
            (state_hbm.at[:, :, pl.ds(pl.multiple_of(LANES * even, LANES), wide)], state_even),
            (state_hbm.at[:, :, pl.ds(pl.multiple_of(LANES * odd, LANES), wide)], state_odd),
        ),
        sems,
    )
    for copy in copies[:3]:
        copy.wait()
    rx, ry, sx, sy = split_metric(metric_ref, spread, blocks)
    depth = depth_ref[...]
    refine = refine_ref[...].astype(jnp.float32)
    faces = ((sx, sy), (rx + sx, ry + sy), (rx, ry))
    lengths = [jnp.sqrt(vx * vx + vy * vy) for vx, vy in faces]
    rate = jnp.sqrt(GRAVITY * depth) * jnp.maximum(jnp.maximum(lengths[0], lengths[1]), lengths[2])
    top = jnp.max(jnp.max(rate, axis=0, keepdims=True), axis=1, keepdims=True)
    extra = jnp.sum(jnp.sum(refine, axis=0, keepdims=True), axis=1, keepdims=True)
    shape = stats_ref.shape
    lane = lax.broadcasted_iota(jnp.int32, shape, 1)
    stats_ref[...] = jnp.where(
        lane < LANES // 2, jnp.broadcast_to(top, shape), jnp.broadcast_to(extra, shape)
    )
    for copy in copies[3:]:
        copy.wait()
    for ref, source, start in ((even_ref, state_even, even), (odd_ref, state_odd, odd)):
        pack_state(source, ref, halo, SENT, 3)
        at = pl.ds(start, halo)
        dense = [depth_ref[at, :]]
        dense += [spread[pl.ds(8 * start + comp, halo, stride=8), :] for comp in range(4)]
        dense += [partner_ref[at, :].astype(jnp.float32), refine_ref[at, :].astype(jnp.float32)]
        for num, value in enumerate(dense):
            ref[pl.ds(30 + num, halo, stride=SENT), :] = value


def pack_state(source, target, blocks, height, width):
    for block in range(blocks):
        for node in range(10):
            at = height * block + width * node
            target[at : at + 3, :] = source[node, :, LANES * block : LANES * (block + 1)]


def pair_index(partner):
    lane = lax.broadcasted_iota(jnp.int32, partner.shape, 1)
    target = lane + partner.astype(jnp.int32)
    return target & (LANES - 1), (target >= 0) & (target < LANES)


def lane_gather(values, index):
    return jnp.take_along_axis(values, index, axis=1, mode="promise_in_bounds")


def outer_values(load, index, inside):
    shape = index.shape
    lane = lax.broadcasted_iota(jnp.int32, shape, 1)

    def prev(item):
        return pltpu.roll(jnp.where(lane == LANES - 1, load(item, -1), load(item, 0)), 1, 1)

    def after(item):
        return pltpu.roll(jnp.where(lane == 0, load(item, 1), load(item, 0)), LANES - 1, 1)

    def across(item):
        other = jnp.where(lane < LANES // 2, load(item, 1), load(item, -1))
        return jnp.where(inside, lane_gather(load(item, 0), index), lane_gather(other, index))

    return prev, after, across


def wall_masks(sizes, start, place, count, partner):
    shape = partner.shape
    lane = lax.broadcasted_iota(jnp.int32, shape, 1)
    row = lax.broadcasted_iota(jnp.int32, shape, 0) + start
    first = (lane == 0) & (row == sizes.halo) & (place == 0)
    last = (lane == LANES - 1) & (row == sizes.halo + sizes.blocks - 1) & (place == count - 1)
    return first, last, partner == 0


def tendency(load, geo, walls, index, inside, diff_ref, lift_ref):
    speed_sq, rx, ry, sx, sy = geo[:5]
    outer_sq, waves, ghosts = geo[5:8], geo[8:11], geo[11:14]
    own = [[load(10 * field + node, 0) for node in range(10)] for field in range(3)]
    eta, mom_x, mom_y = own
    flow_r = [-(rx * mom_x[b] + ry * mom_y[b]) for b in range(10)]
    flow_s = [-(sx * mom_x[b] + sy * mom_y[b]) for b in range(10)]
    half_r = (0.5 * rx, 0.5 * ry)
    half_s = (0.5 * sx, 0.5 * sy)
    vectors = (
        (-half_s[0], -half_s[1]),
        (half_r[0] + half_s[0], half_r[1] + half_s[1]),
        (-half_r[0], -half_r[1]),
    )
    fetch = outer_values(load, index, inside)
    jumps = ([], [], [])
    for face in range(3):
        vec_x, vec_y = vectors[face]
        theirs = FACES[(1, 0, 2)[face]]
        wall = walls[face]
        for j in range(4):
            node, match = FACES[face][j], theirs[3 - j]
            in_eta, in_x, in_y = eta[node], mom_x[node], mom_y[node]
            ext_eta, ext_x, ext_y = [fetch[face](10 * field + match) for field in range(3)]
            bounce = (in_x * vec_x + in_y * vec_y) * ghosts[face]
            d_eta = jnp.where(wall, 0.0, in_eta - ext_eta)
            d_x = jnp.where(wall, bounce * vec_x, in_x - ext_x)
            d_y = jnp.where(wall, bounce * vec_y, in_y - ext_y)
            head = jnp.where(wall, 0.0, speed_sq * in_eta - outer_sq[face] * ext_eta)
            jumps[0].append(d_x * vec_x + d_y * vec_y - waves[face] * d_eta)
            jumps[1].append(head * vec_x - waves[face] * d_x)
            jumps[2].append(head * vec_y - waves[face] * d_y)
    pull = (-speed_sq * rx, -speed_sq * ry)
    push = (-speed_sq * sx, -speed_sq * sy)
    out = [[None] * 10 for _ in range(3)]
    for a in range(10):
        total = along_r = along_s = None
        for b in range(10):
            d_r, d_s = diff_ref[a, 0, b], diff_ref[a, 1, b]
            term = d_r * flow_r[b] + d_s * flow_s[b]
            total = term if b == 0 else total + term
            along_r = d_r * eta[b] if b == 0 else along_r + d_r * eta[b]
            along_s = d_s * eta[b] if b == 0 else along_s + d_s * eta[b]
        sums = [total, pull[0] * along_r + push[0] * along_s, pull[1] * along_r + push[1] * along_s]
        for q in range(12):
            weight = lift_ref[a, q]
            for field in range(3):
                sums[field] = sums[field] + weight * jumps[field][q]
        for field in range(3):
            out[field][a] = sums[field]
    return [out[field][a] for field in range(3) for a in range(10)]


def child_matrix(prolong_ref):
    f32 = jnp.float32
    node_r = lax.broadcasted_iota(jnp.int32, (PACK, 10), 0) // 4
    spread_r = (node_r == lax.broadcasted_iota(jnp.int32, (PACK, 10), 1)).astype(f32)
    item_c = lax.broadcasted_iota(jnp.int32, (10, WIDE), 1)
    spread_c = (item_c % 10 == lax.broadcasted_iota(jnp.int32, (10, WIDE), 0)).astype(f32)
    row = lax.broadcasted_iota(jnp.int32, (PACK, WIDE), 0)
    col = lax.broadcasted_iota(jnp.int32, (PACK, WIDE), 1)
    same = row % 4 == col // 10
    parts = []
    for child in range(2):
        left = jnp.dot(spread_r, prolong_ref[:, child, :], precision=HIGH, preferred_element_type=f32)
        full = jnp.dot(left, spread_c, precision=HIGH, preferred_element_type=f32)
        parts.append(jnp.where(same, full, 0.0))
    parts.append((same & (row // 4 == col % 10)).astype(f32))
    whole = jnp.concatenate(parts, axis=0)
    rounded = whole.astype(jnp.bfloat16)
    rest = (whole - rounded.astype(f32)).astype(jnp.bfloat16)
    return jnp.concatenate([rounded, rounded, rest], axis=1)


def sum_children(sizes, refine, ends_ref, lines_ref):
    slots, f32 = sizes.slots, jnp.float32
    counts = (1.0 + refine).astype(jnp.bfloat16)
    row_i = lax.broadcasted_iota(jnp.int32, (LANES, LANES), 0)
    col_i = lax.broadcasted_iota(jnp.int32, (LANES, LANES), 1)
    upper = (row_i <= col_i).astype(jnp.bfloat16)
    within = jnp.dot(counts, upper, preferred_element_type=f32)
    whole = jnp.dot(counts, jnp.ones((LANES, LANES), jnp.bfloat16), preferred_element_type=f32)
    row_s = lax.broadcasted_iota(jnp.int32, (slots, slots), 0)
    col_s = lax.broadcasted_iota(jnp.int32, (slots, slots), 1)
    lower = (col_s < row_s).astype(jnp.bfloat16)
    before = jnp.dot(lower, whole.astype(jnp.bfloat16), preferred_element_type=f32)
    before = before - before[sizes.margin : sizes.margin + 1, :]
    ends_ref[0] = 2.0 * (within + before) + refine
    ends_ref[1] = before + whole
    ones = jnp.ones((8, LANES), jnp.bfloat16)
    sums = lax.dot_general(ones, counts, (((1,), (1,)), ((), ())), preferred_element_type=f32)
    gap = lax.broadcasted_iota(jnp.int32, (slots, LANES), 1) - lax.broadcasted_iota(jnp.int32, (slots, LANES), 0)
    lines = [
        jnp.dot(sums.astype(jnp.bfloat16), (gap >= least).astype(jnp.bfloat16), preferred_element_type=f32)
        for least in (2, 1, 0)
    ]
    own = lines[1][:, sizes.margin : sizes.margin + 1]
    for num in range(3):
        lines_ref[num] = lines[num] - own


def prep_kernel(
    sizes, state_hbm, depth_hbm, metric_hbm, partner_hbm, refine_hbm, diff_hbm, lift_hbm, prolong_hbm,
    cur, aux, weights, diff_ref, lift_ref,
    state_ref, depth_ref, metric_ref, partner_ref, refine_ref, prolong_ref, spread, wide, sems,
):
    blocks = sizes.blocks
    copies = fetch_all(
        (
            (metric_hbm, metric_ref),
            (state_hbm, state_ref),
            (depth_hbm, depth_ref),
            (partner_hbm, partner_ref),
            (refine_hbm, refine_ref),
            (prolong_hbm, prolong_ref),
            (diff_hbm, diff_ref),
            (lift_hbm, lift_ref),
        ),
        sems,
    )
    for copy in copies:
        copy.wait()
    weights[...] = child_matrix(prolong_ref)
    metric = split_metric(metric_ref, spread, blocks)
    dense = [depth_ref[...], *metric, partner_ref[...].astype(jnp.float32), refine_ref[...].astype(jnp.float32)]
    for num in range(7):
        aux[num] = dense[num]
    pack_state(state_ref, wide, blocks, LAID, 4)
    for field in range(3):
        for node in range(10):
            cur[10 * field + node] = wide[pl.ds(4 * node + field, blocks, stride=LAID), :]


def first_kernel(
    sizes, cur_own, aux_own, weights_in, diff_in, lift_in, odd_ref, even_ref,
    cur, rate_ref, twice_ref, weights, ends_ref, lines_ref,
    geo_ref, aux, diff_ref, lift_ref, sems,
):
    blocks, halo = sizes.blocks, sizes.halo
    top, bottom = PAD + halo, PAD + halo + blocks
    place = lax.axis_index(AXES)
    count = lax.axis_size(AXES)
    copies = fetch_all(((diff_in, diff_ref), (lift_in, lift_ref)), sems)
    even = place % 2 == 0

    def set_halo(target, num, row):
        by_even = even_ref[pl.ds(row, halo, stride=SENT), :]
        by_odd = odd_ref[pl.ds(row, halo, stride=SENT), :]
        target[num, top - halo : top, :] = jnp.where(even, by_odd, by_even)
        target[num, bottom : bottom + halo, :] = jnp.where(even, by_even, by_odd)

    for num in range(7):
        set_halo(aux, num, 30 + num)
        aux[num, top:bottom, :] = aux_own[num]
    for field in range(3):
        for node in range(10):
            item = 10 * field + node
            set_halo(cur, item, 3 * node + field)
            cur[item, top:bottom, :] = cur_own[item]

    weights[...] = weights_in[...]
    begin = PAD + sizes.keep
    sum_children(sizes, aux[6, begin : begin + sizes.slots, :], ends_ref, lines_ref)
    for copy in copies:
        copy.wait()

    def step(start, height):
        base = PAD + start

        def load_aux(item, shift):
            return aux[item, pl.ds(base + shift, height), :]

        def load(item, shift):
            return cur[item, pl.ds(base + shift, height), :]

        depth, rx, ry, sx, sy, partner = [load_aux(num, 0) for num in range(6)]
        index, inside = pair_index(partner)
        fetch = outer_values(load_aux, index, inside)
        walls = wall_masks(sizes, start, place, count, partner)
        speed_sq = GRAVITY * depth
        outer_sq = [jnp.where(walls[k], speed_sq, GRAVITY * fetch[k](0)) for k in range(3)]
        faces = ((sx, sy), (rx + sx, ry + sy), (rx, ry))
        squares = [vx * vx + vy * vy for vx, vy in faces]
        waves = [
            0.5 * jnp.sqrt(squares[k]) * jnp.sqrt(jnp.maximum(speed_sq, outer_sq[k])) for k in range(3)
        ]
        ghosts = [8.0 / squares[k] for k in range(3)]
        geo = [speed_sq, rx, ry, sx, sy, *outer_sq, *waves, *ghosts]
        rates = tendency(load, geo, walls, index, inside, diff_ref, lift_ref)
        for num, value in enumerate([*geo, partner]):
            geo_ref[num, pl.ds(start, height), :] = value
        for item in range(30):
            rate_ref[item, pl.ds(base, height), :] = rates[item]

    def again(start, height):
        row = start + sizes.keep
        at = pl.ds(row, height)

        def load(item, shift):
            return rate_ref[item, pl.ds(PAD + row + shift, height), :]

        geo = [geo_ref[num, at, :] for num in range(14)]
        partner = geo_ref[14, at, :]
        index, inside = pair_index(partner)
        walls = wall_masks(sizes, row, place, count, partner)
        rates = tendency(load, geo, walls, index, inside, diff_ref, lift_ref)
        for item in range(30):
            twice_ref[item, pl.ds(start, height), :] = rates[item]

    def sweep(work, rows):
        def body(num, carry):
            work(pl.multiple_of(TALL * num, TALL), TALL)
            return carry

        lax.fori_loop(0, rows // TALL, body, 0)

    for start in range(sizes.rows // TALL * TALL, sizes.rows, 8):
        step(start, 8)
    sweep(step, sizes.rows)
    for start in range(sizes.slots // TALL * TALL, sizes.slots, 8):
        again(start, 8)
    sweep(again, sizes.slots)


def refine_kernel(
    sizes, cur, rate_ref, twice_ref, weights, base_ref, lines_ref, stats_ref, out_hbm,
    out_ref, place_v, place_s, wide, index_ref, out_sems, sem,
):
    slots, keep = sizes.slots, sizes.keep
    place = lax.axis_index(AXES)
    stats = stats_ref[...]
    half = LANES // 2
    row_n = lax.broadcasted_iota(jnp.int32, stats.shape, 0)
    top = jnp.max(stats, axis=0, keepdims=True)
    earlier = jnp.sum(jnp.where(row_n < place, stats, 0.0), axis=0, keepdims=True)
    left = lax.broadcasted_iota(jnp.int32, (1, LANES), 1) < half
    top = jnp.where(left, top, pltpu.roll(top, half, 1))
    earlier = jnp.where(left, pltpu.roll(earlier, half, 1), earlier)
    step = COURANT / top
    half_square = 0.5 * step * step
    start = earlier - (place * (sizes.cells // 2)).astype(jnp.float32)
    first_slot = LANES * lax.broadcasted_iota(jnp.int32, (slots, LANES), 1).astype(jnp.float32)
    lead = jnp.sum((base_ref[1] + start <= first_slot).astype(jnp.float32), axis=0, keepdims=True)
    lead = jnp.clip(lead.astype(jnp.int32), 0, slots - 1)
    place_v[...] = jnp.broadcast_to(lead, (8, LANES))
    copy = pltpu.make_async_copy(place_v, place_s, sem)
    copy.start()
    for item in range(30):
        now = slice(PAD + keep, PAD + keep + slots)
        value = cur[item, now, :] + step * rate_ref[item, now, :] + half_square * twice_ref[item]
        wide[pl.ds(item, slots, stride=STEP), :] = value
    for item in (30, 31):
        wide[pl.ds(item, slots + 1, stride=STEP), :] = jnp.zeros((slots + 1, LANES), jnp.float32)
    slot_start = LANES * lax.broadcasted_iota(jnp.int32, (slots, LANES), 0).astype(jnp.float32)
    begun = [lines_ref[num, 0:1, :] + start <= slot_start for num in range(3)]
    near, far = [
        2.0 * start
        + jnp.dot(
            (begun[num] & ~begun[num + 1]).astype(jnp.float32)[:, :slots],
            base_ref[0],
            precision=HIGH,
            preferred_element_type=jnp.float32,
        )
        for num in (1, 0)
    ]
    lane = lax.broadcasted_iota(jnp.int32, (slots, LANES), 1)
    slot_no = LANES * lax.broadcasted_iota(jnp.int32, (slots, LANES), 0) + lane
    goal = (2 * slot_no + 1).astype(jnp.float32)
    beyond = jnp.broadcast_to(near[:, LANES - 1 :], (slots, LANES)) <= goal

    def pick(index):
        return jnp.where(beyond, lane_gather(far, index), lane_gather(near, index))

    found = jnp.zeros((slots, LANES), jnp.int32)
    size = LANES // 2
    while size:
        passed = pick(found + (size - 1)) <= goal
        found = jnp.where(passed, found + size, found)
        size //= 2
    mine = pick(found).astype(jnp.int32)
    split = mine & 1
    begin = (mine >> 1) - 1 - split
    kind = split * (1 + slot_no - begin)
    index_ref[0] = found.astype(jnp.float32)
    index_ref[1] = kind.astype(jnp.float32)
    index_ref[2] = (lane < jnp.broadcast_to(found[:, 0:1], (slots, LANES))).astype(jnp.float32)
    copy.wait()
    matrix = weights[...]
    chunk = 8 * LANES
    results = []
    for part in range(slots // 8):
        span = slice(chunk * part, chunk * (part + 1))
        columns = []
        for slot in range(8 * part, 8 * part + 8):
            lead_at = place_s[0, slot] * STEP
            lane_idx = jnp.broadcast_to(index_ref[0, slot : slot + 1, :], (8, LANES)).astype(jnp.int32)
            ahead = jnp.broadcast_to(index_ref[2, slot : slot + 1, :], (8, LANES)) > 0.5
            tiles = []
            for row in range(0, WIDE, 8):
                one = wide[pl.ds(lead_at + row, 8), :]
                two = wide[pl.ds(lead_at + STEP + row, 8), :]
                tiles.append(lane_gather(jnp.where(ahead, two, one), lane_idx))
            columns.append(jnp.concatenate(tiles, axis=0))
        values = jnp.concatenate(columns, axis=1)
        high = values.astype(jnp.bfloat16)
        low = (values - high.astype(jnp.float32)).astype(jnp.bfloat16)
        stack = jnp.concatenate([high, low, high], axis=0)
        children = jnp.dot(matrix, stack, preferred_element_type=jnp.float32)
        for sub in range(8):
            slot = 8 * part + sub
            cut = slice(LANES * sub, LANES * (sub + 1))
            tag = jnp.broadcast_to(index_ref[1, slot : slot + 1, :], (PACK, LANES))
            value = jnp.where(
                tag < 0.5,
                children[2 * PACK :, cut],
                jnp.where(tag < 1.5, children[:PACK, cut], children[PACK : 2 * PACK, cut]),
            )
            for node in range(10):
                out_ref[node, :, LANES * slot : LANES * (slot + 1)] = value[4 * node : 4 * node + 3]
        result = pltpu.make_async_copy(out_ref.at[:, :, span], out_hbm.at[:, :, span], out_sems.at[part])
        result.start()
        results.append(result)
    for result in results:
        result.wait()


def swaps(start, count):
    pairs = [(i, i + 1) for i in range(start, count - 1, 2)]
    return pairs + [(j, i) for i, j in pairs]


def shards(state, depth, metric, partner, refine, diff_ops, lift, prolong):
    sizes = Sizes(state.shape[2])
    count = lax.axis_size(AXES)
    blocks, rows, slots, halo = sizes.blocks, sizes.rows, sizes.slots, sizes.halo
    depth, partner, refine = [x.reshape(blocks, LANES) for x in (depth, partner, refine)]
    state, diff_ops, prolong = [jnp.transpose(x, (1, 0, 2)) for x in (state, diff_ops, prolong)]
    state, depth, metric, partner, refine, diff_ops, lift, prolong = [
        pltpu.with_memory_space_constraint(x, pltpu.HBM)
        for x in (state, depth, metric, partner, refine, diff_ops, lift, prolong)
    ]
    f32, i32 = jnp.float32, jnp.int32
    packed = jax.ShapeDtypeStruct((SENT * halo, LANES), f32)
    dense = [
        pltpu.VMEM((blocks, LANES), f32),
        pltpu.VMEM(metric.shape, f32),
        pltpu.VMEM((blocks, LANES), i32),
        pltpu.VMEM((blocks, LANES), i32),
    ]
    stats, even, odd = pl.pallas_call(
        functools.partial(pack_kernel, sizes),
        name="pack",
        out_shape=(pltpu.VMEM((count, LANES), f32), packed, packed),
        in_specs=[HBM] * 5,
        out_specs=(VMEM,) * 3,
        scratch_shapes=[
            pltpu.VMEM((10, 3, LANES * halo), f32),
            pltpu.VMEM((10, 3, LANES * halo), f32),
            *dense,
            pltpu.VMEM((8 * blocks, LANES), f32),
            pltpu.SemaphoreType.DMA((6,)),
        ],
        compiler_params=PARAMS,
    )(state, depth, metric, partner, refine)
    odd = lax.ppermute(odd, AXES, swaps(1, count))
    even = lax.ppermute(even, AXES, swaps(0, count))
    stats = lax.all_to_all(stats, AXES, 0, 0, tiled=True)
    even, odd, stats = [pltpu.with_memory_space_constraint(x, pltpu.VMEM) for x in (even, odd, stats)]
    cur, aux, weights, diff_near, lift_near = pl.pallas_call(
        functools.partial(prep_kernel, sizes),
        name="lay_out",
        cost_estimate=pl.CostEstimate(flops=1 << 24, transcendentals=1 << 16, bytes_accessed=1 << 24),
        out_shape=(
            jax.ShapeDtypeStruct((30, blocks, LANES), f32),
            jax.ShapeDtypeStruct((7, blocks, LANES), f32),
            jax.ShapeDtypeStruct((3 * PACK, 3 * WIDE), jnp.bfloat16),
            jax.ShapeDtypeStruct(diff_ops.shape, f32),
            jax.ShapeDtypeStruct(lift.shape, f32),
        ),
        in_specs=[HBM] * 8,
        out_specs=(VMEM,) * 5,
        scratch_shapes=[
            pltpu.VMEM(state.shape, f32),
            *dense,
            pltpu.VMEM(prolong.shape, f32),
            pltpu.VMEM((8 * blocks, LANES), f32),
            pltpu.VMEM((LAID * blocks, LANES), f32),
            pltpu.SemaphoreType.DMA((8,)),
        ],
        compiler_params=PARAMS,
    )(state, depth, metric, partner, refine, diff_ops, lift, prolong)
    cur, rates, twice, weights, ends, lines = pl.pallas_call(
        functools.partial(first_kernel, sizes),
        name="rates_twice",
        cost_estimate=pl.CostEstimate(flops=1024, transcendentals=0, bytes_accessed=1024),
        out_shape=(
            jax.ShapeDtypeStruct((30, sizes.tall, LANES), f32),
            jax.ShapeDtypeStruct((30, sizes.tall, LANES), f32),
            jax.ShapeDtypeStruct((30, slots, LANES), f32),
            jax.ShapeDtypeStruct((3 * PACK, 3 * WIDE), jnp.bfloat16),
            jax.ShapeDtypeStruct((2, slots, LANES), f32),
            jax.ShapeDtypeStruct((3, 8, LANES), f32),
        ),
        in_specs=[VMEM] * 7,
        out_specs=(VMEM,) * 6,
        scratch_shapes=[
            pltpu.VMEM((15, rows, LANES), f32),
            pltpu.VMEM((7, sizes.tall, LANES), f32),
            pltpu.SMEM(diff_ops.shape, f32),
            pltpu.SMEM(lift.shape, f32),
            pltpu.SemaphoreType.DMA((2,)),
        ],
        compiler_params=PARAMS,
    )(cur, aux, weights, diff_near, lift_near, odd, even)
    refined = pl.pallas_call(
        functools.partial(refine_kernel, sizes),
        name="sum_and_refine",
        out_shape=jax.ShapeDtypeStruct((10, 3, LANES * slots), f32),
        in_specs=[VMEM] * 7,
        out_specs=HBM,
        scratch_shapes=[
            pltpu.VMEM((10, 3, LANES * slots), f32),
            pltpu.VMEM((8, LANES), i32),
            pltpu.SMEM((8, LANES), i32),
            pltpu.VMEM((STEP * (slots + 1), LANES), f32),
            pltpu.VMEM((3, slots, LANES), f32),
            pltpu.SemaphoreType.DMA((slots // 8,)),
            pltpu.SemaphoreType.DMA,
        ],
        compiler_params=PARAMS,
    )(cur, rates, twice, weights, ends, lines, stats)
    return jnp.transpose(refined, (1, 0, 2))


def solution(mesh):
    return jax.shard_map(
        shards,
        mesh=mesh,
        in_specs=(
            P(None, None, AXES),
            P(AXES),
            P(None, AXES),
            P(AXES),
            P(AXES),
            P(),
            P(),
            P(),
        ),
        out_specs=P(None, None, AXES),
        check_vma=False,
    )
```

```python
import functools

import jax
import jax.numpy as jnp
from jax import lax
from jax.experimental import pallas as pl
from jax.experimental.pallas import tpu as pltpu
from jax.sharding import PartitionSpec as P

GRAVITY = 9.81
COURANT = 0.5
HIGH = lax.Precision.HIGHEST
LANES = 128
AXES = ("row", "col")
FACES = ((0, 1, 2, 3), (3, 6, 8, 9), (9, 7, 4, 0))
PACK = 40
LAID = 41
SENT = 37
WIDE = 32
STEP = 33
TALL = 16
PAD = 8

VMEM = pl.BlockSpec(memory_space=pltpu.VMEM)
HBM = pl.BlockSpec(memory_space=pltpu.HBM)
PARAMS = pltpu.CompilerParams(vmem_limit_bytes=48 * 1024 * 1024)


class Sizes:
    def __init__(self, cells):
        self.cells = cells
        self.blocks = cells // LANES
        self.margin = cells // 4 // LANES
        self.halo = self.margin + 1
        self.rows = -(-(self.blocks + 2 * self.halo) // 8) * 8
        self.tall = self.rows + 2 * PAD
        self.slots = 3 * self.blocks // 2
        self.keep = self.halo - self.margin


def fetch_all(pairs, sems):
    copies = [pltpu.make_async_copy(src, dst, sems.at[num]) for num, (src, dst) in enumerate(pairs)]
    for copy in copies:
        copy.start()
    return copies


def split_metric(metric_ref, spread, blocks):
    for block in range(blocks):
        spread[8 * block : 8 * block + 4, :] = metric_ref[:, LANES * block : LANES * (block + 1)]
    return [spread[pl.ds(comp, blocks, stride=8), :] for comp in range(4)]


def pack_kernel(
    sizes, state_hbm, depth_hbm, metric_hbm, partner_hbm, refine_hbm, stats_hbm, even_ref, odd_ref,
    stats_ref, state_even, state_odd, depth_ref, metric_ref, partner_ref, refine_ref, spread, sems, sem,
):
    blocks, halo = sizes.blocks, sizes.halo
    wide = LANES * halo
    late = blocks - halo
    even = (lax.axis_index(AXES) + 1) % 2 * late
    odd = late - even
    copies = fetch_all(
        (
            (depth_hbm, depth_ref),
            (metric_hbm, metric_ref),
            (refine_hbm, refine_ref),
            (partner_hbm, partner_ref),
            (state_hbm.at[:, :, pl.ds(pl.multiple_of(LANES * even, LANES), wide)], state_even),
            (state_hbm.at[:, :, pl.ds(pl.multiple_of(LANES * odd, LANES), wide)], state_odd),
        ),
        sems,
    )
    for copy in copies[:3]:
        copy.wait()
    rx, ry, sx, sy = split_metric(metric_ref, spread, blocks)
    depth = depth_ref[...]
    refine = refine_ref[...].astype(jnp.float32)
    faces = ((sx, sy), (rx + sx, ry + sy), (rx, ry))
    lengths = [jnp.sqrt(vx * vx + vy * vy) for vx, vy in faces]
    rate = jnp.sqrt(GRAVITY * depth) * jnp.maximum(jnp.maximum(lengths[0], lengths[1]), lengths[2])
    top = jnp.max(jnp.max(rate, axis=0, keepdims=True), axis=1, keepdims=True)
    extra = jnp.sum(jnp.sum(refine, axis=0, keepdims=True), axis=1, keepdims=True)
    shape = stats_ref.shape
    lane = lax.broadcasted_iota(jnp.int32, shape, 1)
    stats_ref[...] = jnp.where(
        lane < LANES // 2, jnp.broadcast_to(top, shape), jnp.broadcast_to(extra, shape)
    )
    sent = pltpu.make_async_copy(stats_ref, stats_hbm, sem)
    sent.start()
    for copy in copies[3:]:
        copy.wait()
    for ref, source, start in ((even_ref, state_even, even), (odd_ref, state_odd, odd)):
        pack_state(source, ref, halo, SENT, 3)
        at = pl.ds(start, halo)
        dense = [depth_ref[at, :]]
        dense += [spread[pl.ds(8 * start + comp, halo, stride=8), :] for comp in range(4)]
        dense += [partner_ref[at, :].astype(jnp.float32), refine_ref[at, :].astype(jnp.float32)]
        for num, value in enumerate(dense):
            ref[pl.ds(30 + num, halo, stride=SENT), :] = value
    sent.wait()


def pack_state(source, target, blocks, height, width):
    for block in range(blocks):
        for node in range(10):
            at = height * block + width * node
            target[at : at + 3, :] = source[node, :, LANES * block : LANES * (block + 1)]


def pair_index(partner):
    lane = lax.broadcasted_iota(jnp.int32, partner.shape, 1)
    target = lane + partner.astype(jnp.int32)
    return target & (LANES - 1), (target >= 0) & (target < LANES)


def lane_gather(values, index):
    return jnp.take_along_axis(values, index, axis=1, mode="promise_in_bounds")


def outer_values(load, index, inside):
    shape = index.shape
    lane = lax.broadcasted_iota(jnp.int32, shape, 1)

    def prev(item):
        return pltpu.roll(jnp.where(lane == LANES - 1, load(item, -1), load(item, 0)), 1, 1)

    def after(item):
        return pltpu.roll(jnp.where(lane == 0, load(item, 1), load(item, 0)), LANES - 1, 1)

    def across(item):
        other = jnp.where(lane < LANES // 2, load(item, 1), load(item, -1))
        return jnp.where(inside, lane_gather(load(item, 0), index), lane_gather(other, index))

    return prev, after, across


def wall_masks(sizes, start, place, count, partner):
    shape = partner.shape
    lane = lax.broadcasted_iota(jnp.int32, shape, 1)
    row = lax.broadcasted_iota(jnp.int32, shape, 0) + start
    first = (lane == 0) & (row == sizes.halo) & (place == 0)
    last = (lane == LANES - 1) & (row == sizes.halo + sizes.blocks - 1) & (place == count - 1)
    return first, last, partner == 0


def tendency(load, geo, walls, index, inside, diff_ref, lift_ref):
    speed_sq, rx, ry, sx, sy = geo[:5]
    outer_sq, waves, ghosts = geo[5:8], geo[8:11], geo[11:14]
    own = [[load(10 * field + node, 0) for node in range(10)] for field in range(3)]
    eta, mom_x, mom_y = own
    flow_r = [-(rx * mom_x[b] + ry * mom_y[b]) for b in range(10)]
    flow_s = [-(sx * mom_x[b] + sy * mom_y[b]) for b in range(10)]
    half_r = (0.5 * rx, 0.5 * ry)
    half_s = (0.5 * sx, 0.5 * sy)
    vectors = (
        (-half_s[0], -half_s[1]),
        (half_r[0] + half_s[0], half_r[1] + half_s[1]),
        (-half_r[0], -half_r[1]),
    )
    fetch = outer_values(load, index, inside)
    jumps = ([], [], [])
    for face in range(3):
        vec_x, vec_y = vectors[face]
        theirs = FACES[(1, 0, 2)[face]]
        wall = walls[face]
        for j in range(4):
            node, match = FACES[face][j], theirs[3 - j]
            in_eta, in_x, in_y = eta[node], mom_x[node], mom_y[node]
            ext_eta, ext_x, ext_y = [fetch[face](10 * field + match) for field in range(3)]
            bounce = (in_x * vec_x + in_y * vec_y) * ghosts[face]
            d_eta = jnp.where(wall, 0.0, in_eta - ext_eta)
            d_x = jnp.where(wall, bounce * vec_x, in_x - ext_x)
            d_y = jnp.where(wall, bounce * vec_y, in_y - ext_y)
            head = jnp.where(wall, 0.0, speed_sq * in_eta - outer_sq[face] * ext_eta)
            jumps[0].append(d_x * vec_x + d_y * vec_y - waves[face] * d_eta)
            jumps[1].append(head * vec_x - waves[face] * d_x)
            jumps[2].append(head * vec_y - waves[face] * d_y)
    pull = (-speed_sq * rx, -speed_sq * ry)
    push = (-speed_sq * sx, -speed_sq * sy)
    out = [[None] * 10 for _ in range(3)]
    for a in range(10):
        total = along_r = along_s = None
        for b in range(10):
            d_r, d_s = diff_ref[a, 0, b], diff_ref[a, 1, b]
            term = d_r * flow_r[b] + d_s * flow_s[b]
            total = term if b == 0 else total + term
            along_r = d_r * eta[b] if b == 0 else along_r + d_r * eta[b]
            along_s = d_s * eta[b] if b == 0 else along_s + d_s * eta[b]
        sums = [total, pull[0] * along_r + push[0] * along_s, pull[1] * along_r + push[1] * along_s]
        for q in range(12):
            weight = lift_ref[a, q]
            for field in range(3):
                sums[field] = sums[field] + weight * jumps[field][q]
        for field in range(3):
            out[field][a] = sums[field]
    return [out[field][a] for field in range(3) for a in range(10)]


def child_matrix(prolong_ref):
    f32, bf16 = jnp.float32, jnp.bfloat16

    def number(shape, axis):
        return lax.broadcasted_iota(jnp.int32, shape, axis)

    both = jnp.concatenate([prolong_ref[:, 0, :], prolong_ref[:, 1, :]], axis=0)
    rounded = both.astype(bf16)
    rest = (both - rounded.astype(f32)).astype(bf16)
    shape = (10, WIDE)
    columns = (number(shape, 1) % 10 == number(shape, 0)).astype(bf16)
    shape = (2 * PACK, 20)
    rows = (number(shape, 0) // 4 == number(shape, 1)).astype(bf16)
    shape = (2 * PACK, WIDE)
    same = number(shape, 0) % 4 == number(shape, 1) // 10
    parts = []
    for matrix in (rounded, rest):
        spread = jnp.dot(matrix, columns, preferred_element_type=f32).astype(bf16)
        full = jnp.dot(rows, spread, preferred_element_type=f32)
        parts.append(jnp.where(same, full, 0.0))
    shape = (PACK, WIDE)
    same = (number(shape, 0) % 4 == number(shape, 1) // 10) & (number(shape, 0) // 4 == number(shape, 1) % 10)
    first = jnp.concatenate([parts[0], same.astype(f32)], axis=0)
    last = jnp.concatenate([parts[1], jnp.zeros(shape, f32)], axis=0)
    return jnp.concatenate([first, first, last], axis=1).astype(bf16)


def sum_children(sizes, refine, ends_ref, lines_ref):
    slots, f32 = sizes.slots, jnp.float32
    counts = (1.0 + refine).astype(jnp.bfloat16)
    row_i = lax.broadcasted_iota(jnp.int32, (LANES, LANES), 0)
    col_i = lax.broadcasted_iota(jnp.int32, (LANES, LANES), 1)
    upper = (row_i <= col_i).astype(jnp.bfloat16)
    within = jnp.dot(counts, upper, preferred_element_type=f32)
    whole = jnp.dot(counts, jnp.ones((LANES, LANES), jnp.bfloat16), preferred_element_type=f32)
    row_s = lax.broadcasted_iota(jnp.int32, (slots, slots), 0)
    col_s = lax.broadcasted_iota(jnp.int32, (slots, slots), 1)
    lower = (col_s < row_s).astype(jnp.bfloat16)
    before = jnp.dot(lower, whole.astype(jnp.bfloat16), preferred_element_type=f32)
    before = before - before[sizes.margin : sizes.margin + 1, :]
    ends_ref[0] = 2.0 * (within + before) + refine
    ends_ref[1] = before + whole
    ones = jnp.ones((8, LANES), jnp.bfloat16)
    sums = lax.dot_general(ones, counts, (((1,), (1,)), ((), ())), preferred_element_type=f32)
    gap = lax.broadcasted_iota(jnp.int32, (slots, LANES), 1) - lax.broadcasted_iota(jnp.int32, (slots, LANES), 0)
    lines = [
        jnp.dot(sums.astype(jnp.bfloat16), (gap >= least).astype(jnp.bfloat16), preferred_element_type=f32)
        for least in (2, 1, 0)
    ]
    own = lines[1][:, sizes.margin : sizes.margin + 1]
    for num in range(3):
        lines_ref[num] = lines[num] - own


def prep_kernel(
    sizes, state_hbm, depth_hbm, metric_hbm, partner_hbm, refine_hbm, diff_hbm, lift_hbm, prolong_hbm,
    cur, aux, weights, diff_ref, lift_ref,
    state_ref, depth_ref, metric_ref, partner_ref, refine_ref, prolong_ref, spread, wide, sems,
):
    blocks = sizes.blocks
    copies = fetch_all(
        (
            (metric_hbm, metric_ref),
            (state_hbm, state_ref),
            (depth_hbm, depth_ref),
            (partner_hbm, partner_ref),
            (refine_hbm, refine_ref),
            (prolong_hbm, prolong_ref),
            (diff_hbm, diff_ref),
            (lift_hbm, lift_ref),
        ),
        sems,
    )
    for copy in copies:
        copy.wait()
    weights[...] = child_matrix(prolong_ref)
    metric = split_metric(metric_ref, spread, blocks)
    dense = [depth_ref[...], *metric, partner_ref[...].astype(jnp.float32), refine_ref[...].astype(jnp.float32)]
    for num in range(7):
        aux[num] = dense[num]
    pack_state(state_ref, wide, blocks, LAID, 4)
    for field in range(3):
        for node in range(10):
            cur[10 * field + node] = wide[pl.ds(4 * node + field, blocks, stride=LAID), :]


def first_kernel(
    sizes, cur_own, aux_own, weights_in, diff_in, lift_in, odd_ref, even_ref,
    cur, rate_ref, twice_ref, weights, ends_ref, lines_ref,
    geo_ref, aux, diff_ref, lift_ref, sems,
):
    blocks, halo = sizes.blocks, sizes.halo
    top, bottom = PAD + halo, PAD + halo + blocks
    place = lax.axis_index(AXES)
    count = lax.axis_size(AXES)
    copies = fetch_all(((diff_in, diff_ref), (lift_in, lift_ref)), sems)
    even = place % 2 == 0

    def set_halo(target, num, row):
        by_even = even_ref[pl.ds(row, halo, stride=SENT), :]
        by_odd = odd_ref[pl.ds(row, halo, stride=SENT), :]
        target[num, top - halo : top, :] = jnp.where(even, by_odd, by_even)
        target[num, bottom : bottom + halo, :] = jnp.where(even, by_even, by_odd)

    for num in range(7):
        set_halo(aux, num, 30 + num)
        aux[num, top:bottom, :] = aux_own[num]
    for field in range(3):
        for node in range(10):
            item = 10 * field + node
            set_halo(cur, item, 3 * node + field)
            cur[item, top:bottom, :] = cur_own[item]

    weights[...] = weights_in[...]
    begin = PAD + sizes.keep
    sum_children(sizes, aux[6, begin : begin + sizes.slots, :], ends_ref, lines_ref)
    for copy in copies:
        copy.wait()

    def step(start, height):
        base = PAD + start

        def load_aux(item, shift):
            return aux[item, pl.ds(base + shift, height), :]

        def load(item, shift):
            return cur[item, pl.ds(base + shift, height), :]

        depth, rx, ry, sx, sy, partner = [load_aux(num, 0) for num in range(6)]
        index, inside = pair_index(partner)
        fetch = outer_values(load_aux, index, inside)
        walls = wall_masks(sizes, start, place, count, partner)
        speed_sq = GRAVITY * depth
        outer_sq = [jnp.where(walls[k], speed_sq, GRAVITY * fetch[k](0)) for k in range(3)]
        faces = ((sx, sy), (rx + sx, ry + sy), (rx, ry))
        squares = [vx * vx + vy * vy for vx, vy in faces]
        waves = [
            0.5 * jnp.sqrt(squares[k]) * jnp.sqrt(jnp.maximum(speed_sq, outer_sq[k])) for k in range(3)
        ]
        ghosts = [8.0 / squares[k] for k in range(3)]
        geo = [speed_sq, rx, ry, sx, sy, *outer_sq, *waves, *ghosts]
        rates = tendency(load, geo, walls, index, inside, diff_ref, lift_ref)
        for num, value in enumerate([*geo, partner]):
            geo_ref[num, pl.ds(start, height), :] = value
        for item in range(30):
            rate_ref[item, pl.ds(base, height), :] = rates[item]

    def again(start, height):
        row = start + sizes.keep
        at = pl.ds(row, height)

        def load(item, shift):
            return rate_ref[item, pl.ds(PAD + row + shift, height), :]

        geo = [geo_ref[num, at, :] for num in range(14)]
        partner = geo_ref[14, at, :]
        index, inside = pair_index(partner)
        walls = wall_masks(sizes, row, place, count, partner)
        rates = tendency(load, geo, walls, index, inside, diff_ref, lift_ref)
        for item in range(30):
            twice_ref[item, pl.ds(start, height), :] = rates[item]

    def sweep(work, rows):
        def body(num, carry):
            work(pl.multiple_of(TALL * num, TALL), TALL)
            return carry

        lax.fori_loop(0, rows // TALL, body, 0)

    for start in range(sizes.rows // TALL * TALL, sizes.rows, 8):
        step(start, 8)
    sweep(step, sizes.rows)
    for start in range(sizes.slots // TALL * TALL, sizes.slots, 8):
        again(start, 8)
    sweep(again, sizes.slots)


def refine_kernel(
    sizes, cur, rate_ref, twice_ref, weights, base_ref, lines_ref, stats_ref, out_hbm,
    out_ref, place_v, place_s, wide, index_ref, out_sems, sem,
):
    slots, keep = sizes.slots, sizes.keep
    place = lax.axis_index(AXES)
    stats = stats_ref[...]
    half = LANES // 2
    row_n = lax.broadcasted_iota(jnp.int32, stats.shape, 0)
    top = jnp.max(stats, axis=0, keepdims=True)
    earlier = jnp.sum(jnp.where(row_n < place, stats, 0.0), axis=0, keepdims=True)
    left = lax.broadcasted_iota(jnp.int32, (1, LANES), 1) < half
    top = jnp.where(left, top, pltpu.roll(top, half, 1))
    earlier = jnp.where(left, pltpu.roll(earlier, half, 1), earlier)
    step = COURANT / top
    half_square = 0.5 * step * step
    start = earlier - (place * (sizes.cells // 2)).astype(jnp.float32)
    first_slot = LANES * lax.broadcasted_iota(jnp.int32, (slots, LANES), 1).astype(jnp.float32)
    lead = jnp.sum((base_ref[1] + start <= first_slot).astype(jnp.float32), axis=0, keepdims=True)
    lead = jnp.clip(lead.astype(jnp.int32), 0, slots - 1)
    place_v[...] = jnp.broadcast_to(lead, (8, LANES))
    copy = pltpu.make_async_copy(place_v, place_s, sem)
    copy.start()
    for item in range(30):
        now = slice(PAD + keep, PAD + keep + slots)
        value = cur[item, now, :] + step * rate_ref[item, now, :] + half_square * twice_ref[item]
        wide[pl.ds(item, slots, stride=STEP), :] = value
    for item in (30, 31):
        wide[pl.ds(item, slots + 1, stride=STEP), :] = jnp.zeros((slots + 1, LANES), jnp.float32)
    slot_start = LANES * lax.broadcasted_iota(jnp.int32, (slots, LANES), 0).astype(jnp.float32)
    begun = [lines_ref[num, 0:1, :] + start <= slot_start for num in range(3)]
    near, far = [
        2.0 * start
        + jnp.dot(
            (begun[num] & ~begun[num + 1]).astype(jnp.float32)[:, :slots],
            base_ref[0],
            precision=HIGH,
            preferred_element_type=jnp.float32,
        )
        for num in (1, 0)
    ]
    lane = lax.broadcasted_iota(jnp.int32, (slots, LANES), 1)
    slot_no = LANES * lax.broadcasted_iota(jnp.int32, (slots, LANES), 0) + lane
    goal = (2 * slot_no + 1).astype(jnp.float32)
    beyond = jnp.broadcast_to(near[:, LANES - 1 :], (slots, LANES)) <= goal

    def pick(index):
        return jnp.where(beyond, lane_gather(far, index), lane_gather(near, index))

    found = jnp.zeros((slots, LANES), jnp.int32)
    size = LANES // 2
    while size:
        passed = pick(found + (size - 1)) <= goal
        found = jnp.where(passed, found + size, found)
        size //= 2
    mine = pick(found).astype(jnp.int32)
    split = mine & 1
    begin = (mine >> 1) - 1 - split
    kind = split * (1 + slot_no - begin)
    index_ref[0] = found.astype(jnp.float32)
    index_ref[1] = kind.astype(jnp.float32)
    index_ref[2] = (lane < jnp.broadcast_to(found[:, 0:1], (slots, LANES))).astype(jnp.float32)
    copy.wait()
    matrix = weights[...]
    chunk = 8 * LANES
    results = []
    for part in range(slots // 8):
        span = slice(chunk * part, chunk * (part + 1))
        columns = []
        for slot in range(8 * part, 8 * part + 8):
            lead_at = place_s[0, slot] * STEP
            lane_idx = jnp.broadcast_to(index_ref[0, slot : slot + 1, :], (8, LANES)).astype(jnp.int32)
            ahead = jnp.broadcast_to(index_ref[2, slot : slot + 1, :], (8, LANES)) > 0.5
            tiles = []
            for row in range(0, WIDE, 8):
                one = wide[pl.ds(lead_at + row, 8), :]
                two = wide[pl.ds(lead_at + STEP + row, 8), :]
                tiles.append(lane_gather(jnp.where(ahead, two, one), lane_idx))
            columns.append(jnp.concatenate(tiles, axis=0))
        values = jnp.concatenate(columns, axis=1)
        high = values.astype(jnp.bfloat16)
        low = (values - high.astype(jnp.float32)).astype(jnp.bfloat16)
        stack = jnp.concatenate([high, low, high], axis=0)
        children = jnp.dot(matrix, stack, preferred_element_type=jnp.float32)
        for sub in range(8):
            slot = 8 * part + sub
            cut = slice(LANES * sub, LANES * (sub + 1))
            tag = jnp.broadcast_to(index_ref[1, slot : slot + 1, :], (PACK, LANES))
            value = jnp.where(
                tag < 0.5,
                children[2 * PACK :, cut],
                jnp.where(tag < 1.5, children[:PACK, cut], children[PACK : 2 * PACK, cut]),
            )
            for node in range(10):
                out_ref[node, :, LANES * slot : LANES * (slot + 1)] = value[4 * node : 4 * node + 3]
        result = pltpu.make_async_copy(out_ref.at[:, :, span], out_hbm.at[:, :, span], out_sems.at[part])
        result.start()
        results.append(result)
    for result in results:
        result.wait()


def swaps(start, count):
    pairs = [(i, i + 1) for i in range(start, count - 1, 2)]
    return pairs + [(j, i) for i, j in pairs]


def shards(state, depth, metric, partner, refine, diff_ops, lift, prolong):
    sizes = Sizes(state.shape[2])
    count = lax.axis_size(AXES)
    blocks, rows, slots, halo = sizes.blocks, sizes.rows, sizes.slots, sizes.halo
    depth, partner, refine = [x.reshape(blocks, LANES) for x in (depth, partner, refine)]
    state, diff_ops, prolong = [jnp.transpose(x, (1, 0, 2)) for x in (state, diff_ops, prolong)]
    state, depth, metric, partner, refine, diff_ops, lift, prolong = [
        pltpu.with_memory_space_constraint(x, pltpu.HBM)
        for x in (state, depth, metric, partner, refine, diff_ops, lift, prolong)
    ]
    f32, i32 = jnp.float32, jnp.int32
    packed = jax.ShapeDtypeStruct((SENT * halo, LANES), f32)
    dense = [
        pltpu.VMEM((blocks, LANES), f32),
        pltpu.VMEM(metric.shape, f32),
        pltpu.VMEM((blocks, LANES), i32),
        pltpu.VMEM((blocks, LANES), i32),
    ]
    stats, even, odd = pl.pallas_call(
        functools.partial(pack_kernel, sizes),
        name="pack",
        out_shape=(jax.ShapeDtypeStruct((count, LANES), f32), packed, packed),
        in_specs=[HBM] * 5,
        out_specs=(HBM, VMEM, VMEM),
        scratch_shapes=[
            pltpu.VMEM((count, LANES), f32),
            pltpu.VMEM((10, 3, LANES * halo), f32),
            pltpu.VMEM((10, 3, LANES * halo), f32),
            *dense,
            pltpu.VMEM((8 * blocks, LANES), f32),
            pltpu.SemaphoreType.DMA((6,)),
            pltpu.SemaphoreType.DMA,
        ],
        compiler_params=PARAMS,
    )(state, depth, metric, partner, refine)
    odd = lax.ppermute(odd, AXES, swaps(1, count))
    even = lax.ppermute(even, AXES, swaps(0, count))
    stats = lax.all_to_all(stats, AXES, 0, 0, tiled=True)
    even, odd, stats = [pltpu.with_memory_space_constraint(x, pltpu.VMEM) for x in (even, odd, stats)]
    cur, aux, weights, diff_near, lift_near = pl.pallas_call(
        functools.partial(prep_kernel, sizes),
        name="lay_out",
        cost_estimate=pl.CostEstimate(flops=1 << 24, transcendentals=1 << 16, bytes_accessed=1 << 24),
        out_shape=(
            jax.ShapeDtypeStruct((30, blocks, LANES), f32),
            jax.ShapeDtypeStruct((7, blocks, LANES), f32),
            jax.ShapeDtypeStruct((3 * PACK, 3 * WIDE), jnp.bfloat16),
            jax.ShapeDtypeStruct(diff_ops.shape, f32),
            jax.ShapeDtypeStruct(lift.shape, f32),
        ),
        in_specs=[HBM] * 8,
        out_specs=(VMEM,) * 5,
        scratch_shapes=[
            pltpu.VMEM(state.shape, f32),
            *dense,
            pltpu.VMEM(prolong.shape, f32),
            pltpu.VMEM((8 * blocks, LANES), f32),
            pltpu.VMEM((LAID * blocks, LANES), f32),
            pltpu.SemaphoreType.DMA((8,)),
        ],
        compiler_params=PARAMS,
    )(state, depth, metric, partner, refine, diff_ops, lift, prolong)
    cur, rates, twice, weights, ends, lines = pl.pallas_call(
        functools.partial(first_kernel, sizes),
        name="rates_twice",
        cost_estimate=pl.CostEstimate(flops=1024, transcendentals=0, bytes_accessed=1024),
        out_shape=(
            jax.ShapeDtypeStruct((30, sizes.tall, LANES), f32),
            jax.ShapeDtypeStruct((30, sizes.tall, LANES), f32),
            jax.ShapeDtypeStruct((30, slots, LANES), f32),
            jax.ShapeDtypeStruct((3 * PACK, 3 * WIDE), jnp.bfloat16),
            jax.ShapeDtypeStruct((2, slots, LANES), f32),
            jax.ShapeDtypeStruct((3, 8, LANES), f32),
        ),
        in_specs=[VMEM] * 7,
        out_specs=(VMEM,) * 6,
        scratch_shapes=[
            pltpu.VMEM((15, rows, LANES), f32),
            pltpu.VMEM((7, sizes.tall, LANES), f32),
            pltpu.SMEM(diff_ops.shape, f32),
            pltpu.SMEM(lift.shape, f32),
            pltpu.SemaphoreType.DMA((2,)),
        ],
        compiler_params=PARAMS,
    )(cur, aux, weights, diff_near, lift_near, odd, even)
    refined = pl.pallas_call(
        functools.partial(refine_kernel, sizes),
        name="sum_and_refine",
        out_shape=jax.ShapeDtypeStruct((10, 3, LANES * slots), f32),
        in_specs=[VMEM] * 7,
        out_specs=HBM,
        scratch_shapes=[
            pltpu.VMEM((10, 3, LANES * slots), f32),
            pltpu.VMEM((8, LANES), i32),
            pltpu.SMEM((8, LANES), i32),
            pltpu.VMEM((STEP * (slots + 1), LANES), f32),
            pltpu.VMEM((3, slots, LANES), f32),
            pltpu.SemaphoreType.DMA((slots // 8,)),
            pltpu.SemaphoreType.DMA,
        ],
        compiler_params=PARAMS,
    )(cur, rates, twice, weights, ends, lines, stats)
    return jnp.transpose(refined, (1, 0, 2))


def solution(mesh):
    return jax.shard_map(
        shards,
        mesh=mesh,
        in_specs=(
            P(None, None, AXES),
            P(AXES),
            P(None, AXES),
            P(AXES),
            P(AXES),
            P(),
            P(),
            P(),
        ),
        out_specs=P(None, None, AXES),
        check_vma=False,
    )
```

```python
import functools

import jax
import jax.numpy as jnp
from jax import lax
from jax.experimental import pallas as pl
from jax.experimental.pallas import tpu as pltpu
from jax.sharding import PartitionSpec as P

GRAVITY = 9.81
COURANT = 0.5
HIGH = lax.Precision.HIGHEST
LANES = 128
AXES = ("row", "col")
FACES = ((0, 1, 2, 3), (3, 6, 8, 9), (9, 7, 4, 0))
PACK = 40
LAID = 41
SENT = 37
WIDE = 32
STEP = 33
TALL = 16
PAD = 8

VMEM = pl.BlockSpec(memory_space=pltpu.VMEM)
HBM = pl.BlockSpec(memory_space=pltpu.HBM)
PARAMS = pltpu.CompilerParams(vmem_limit_bytes=48 * 1024 * 1024)


class Sizes:
    def __init__(self, cells):
        self.cells = cells
        self.blocks = cells // LANES
        self.margin = cells // 4 // LANES
        self.halo = self.margin + 1
        self.rows = -(-(self.blocks + 2 * self.halo) // 8) * 8
        self.tall = self.rows + 2 * PAD
        self.slots = 3 * self.blocks // 2
        self.children = self.slots + 2 * self.margin
        self.keep = self.halo - self.margin


def fetch_all(pairs, sems):
    copies = [pltpu.make_async_copy(src, dst, sems.at[num]) for num, (src, dst) in enumerate(pairs)]
    for copy in copies:
        copy.start()
    return copies


def split_metric(metric_ref, spread, blocks):
    for block in range(blocks):
        spread[8 * block : 8 * block + 4, :] = metric_ref[:, LANES * block : LANES * (block + 1)]
    return [spread[pl.ds(comp, blocks, stride=8), :] for comp in range(4)]


def pack_kernel(
    sizes, state_hbm, depth_hbm, metric_hbm, partner_hbm, refine_hbm, stats_hbm, even_ref, odd_ref,
    stats_ref, state_even, state_odd, depth_ref, metric_ref, partner_ref, refine_ref, spread, sems, sem,
):
    blocks, halo = sizes.blocks, sizes.halo
    wide = LANES * halo
    late = blocks - halo
    even = (lax.axis_index(AXES) + 1) % 2 * late
    odd = late - even
    copies = fetch_all(
        (
            (depth_hbm, depth_ref),
            (metric_hbm, metric_ref),
            (refine_hbm, refine_ref),
            (partner_hbm, partner_ref),
            (state_hbm.at[:, :, pl.ds(pl.multiple_of(LANES * even, LANES), wide)], state_even),
            (state_hbm.at[:, :, pl.ds(pl.multiple_of(LANES * odd, LANES), wide)], state_odd),
        ),
        sems,
    )
    for copy in copies[:3]:
        copy.wait()
    rx, ry, sx, sy = split_metric(metric_ref, spread, blocks)
    depth = depth_ref[...]
    refine = refine_ref[...].astype(jnp.float32)
    faces = ((sx, sy), (rx + sx, ry + sy), (rx, ry))
    lengths = [jnp.sqrt(vx * vx + vy * vy) for vx, vy in faces]
    rate = jnp.sqrt(GRAVITY * depth) * jnp.maximum(jnp.maximum(lengths[0], lengths[1]), lengths[2])
    top = jnp.max(jnp.max(rate, axis=0, keepdims=True), axis=1, keepdims=True)
    extra = jnp.sum(jnp.sum(refine, axis=0, keepdims=True), axis=1, keepdims=True)
    shape = stats_ref.shape
    lane = lax.broadcasted_iota(jnp.int32, shape, 1)
    stats_ref[...] = jnp.where(
        lane < LANES // 2, jnp.broadcast_to(top, shape), jnp.broadcast_to(extra, shape)
    )
    sent = pltpu.make_async_copy(stats_ref, stats_hbm, sem)
    sent.start()
    for copy in copies[3:]:
        copy.wait()
    for ref, source, start in ((even_ref, state_even, even), (odd_ref, state_odd, odd)):
        pack_state(source, ref, halo, SENT, 3)
        at = pl.ds(start, halo)
        dense = [depth_ref[at, :]]
        dense += [spread[pl.ds(8 * start + comp, halo, stride=8), :] for comp in range(4)]
        dense += [partner_ref[at, :].astype(jnp.float32), refine_ref[at, :].astype(jnp.float32)]
        for num, value in enumerate(dense):
            ref[pl.ds(30 + num, halo, stride=SENT), :] = value
    sent.wait()


def pack_state(source, target, blocks, height, width):
    for block in range(blocks):
        for node in range(10):
            at = height * block + width * node
            target[at : at + 3, :] = source[node, :, LANES * block : LANES * (block + 1)]


def pair_index(partner):
    lane = lax.broadcasted_iota(jnp.int32, partner.shape, 1)
    target = lane + partner.astype(jnp.int32)
    return target & (LANES - 1), (target >= 0) & (target < LANES)


def lane_gather(values, index):
    return jnp.take_along_axis(values, index, axis=1, mode="promise_in_bounds")


def outer_values(load, index, inside):
    shape = index.shape
    lane = lax.broadcasted_iota(jnp.int32, shape, 1)

    def prev(item):
        return pltpu.roll(jnp.where(lane == LANES - 1, load(item, -1), load(item, 0)), 1, 1)

    def after(item):
        return pltpu.roll(jnp.where(lane == 0, load(item, 1), load(item, 0)), LANES - 1, 1)

    def across(item):
        other = jnp.where(lane < LANES // 2, load(item, 1), load(item, -1))
        return jnp.where(inside, lane_gather(load(item, 0), index), lane_gather(other, index))

    return prev, after, across


def wall_masks(sizes, start, place, count, partner):
    shape = partner.shape
    lane = lax.broadcasted_iota(jnp.int32, shape, 1)
    row = lax.broadcasted_iota(jnp.int32, shape, 0) + start
    first = (lane == 0) & (row == sizes.halo) & (place == 0)
    last = (lane == LANES - 1) & (row == sizes.halo + sizes.blocks - 1) & (place == count - 1)
    return first, last, partner == 0


def tendency(load, geo, walls, index, inside, diff_ref, lift_ref):
    speed_sq, rx, ry, sx, sy = geo[:5]
    outer_sq, waves, ghosts = geo[5:8], geo[8:11], geo[11:14]
    own = [[load(10 * field + node, 0) for node in range(10)] for field in range(3)]
    eta, mom_x, mom_y = own
    flow_r = [-(rx * mom_x[b] + ry * mom_y[b]) for b in range(10)]
    flow_s = [-(sx * mom_x[b] + sy * mom_y[b]) for b in range(10)]
    half_r = (0.5 * rx, 0.5 * ry)
    half_s = (0.5 * sx, 0.5 * sy)
    vectors = (
        (-half_s[0], -half_s[1]),
        (half_r[0] + half_s[0], half_r[1] + half_s[1]),
        (-half_r[0], -half_r[1]),
    )
    fetch = outer_values(load, index, inside)
    jumps = ([], [], [])
    for face in range(3):
        vec_x, vec_y = vectors[face]
        theirs = FACES[(1, 0, 2)[face]]
        wall = walls[face]
        for j in range(4):
            node, match = FACES[face][j], theirs[3 - j]
            in_eta, in_x, in_y = eta[node], mom_x[node], mom_y[node]
            ext_eta, ext_x, ext_y = [fetch[face](10 * field + match) for field in range(3)]
            bounce = (in_x * vec_x + in_y * vec_y) * ghosts[face]
            d_eta = jnp.where(wall, 0.0, in_eta - ext_eta)
            d_x = jnp.where(wall, bounce * vec_x, in_x - ext_x)
            d_y = jnp.where(wall, bounce * vec_y, in_y - ext_y)
            head = jnp.where(wall, 0.0, speed_sq * in_eta - outer_sq[face] * ext_eta)
            jumps[0].append(d_x * vec_x + d_y * vec_y - waves[face] * d_eta)
            jumps[1].append(head * vec_x - waves[face] * d_x)
            jumps[2].append(head * vec_y - waves[face] * d_y)
    pull = (-speed_sq * rx, -speed_sq * ry)
    push = (-speed_sq * sx, -speed_sq * sy)
    out = [[None] * 10 for _ in range(3)]
    for a in range(10):
        total = along_r = along_s = None
        for b in range(10):
            d_r, d_s = diff_ref[a, 0, b], diff_ref[a, 1, b]
            term = d_r * flow_r[b] + d_s * flow_s[b]
            total = term if b == 0 else total + term
            along_r = d_r * eta[b] if b == 0 else along_r + d_r * eta[b]
            along_s = d_s * eta[b] if b == 0 else along_s + d_s * eta[b]
        sums = [total, pull[0] * along_r + push[0] * along_s, pull[1] * along_r + push[1] * along_s]
        for q in range(12):
            weight = lift_ref[a, q]
            for field in range(3):
                sums[field] = sums[field] + weight * jumps[field][q]
        for field in range(3):
            out[field][a] = sums[field]
    return [out[field][a] for field in range(3) for a in range(10)]


def child_matrix(prolong_ref):
    f32, bf16 = jnp.float32, jnp.bfloat16

    def number(shape, axis):
        return lax.broadcasted_iota(jnp.int32, shape, axis)

    both = jnp.concatenate([prolong_ref[:, 0, :], prolong_ref[:, 1, :]], axis=0)
    rounded = both.astype(bf16)
    rest = (both - rounded.astype(f32)).astype(bf16)
    shape = (10, WIDE)
    columns = (number(shape, 1) % 10 == number(shape, 0)).astype(bf16)
    shape = (2 * PACK, 20)
    rows = (number(shape, 0) // 4 == number(shape, 1)).astype(bf16)
    shape = (2 * PACK, WIDE)
    same = number(shape, 0) % 4 == number(shape, 1) // 10
    parts = []
    for matrix in (rounded, rest):
        spread = jnp.dot(matrix, columns, preferred_element_type=f32).astype(bf16)
        full = jnp.dot(rows, spread, preferred_element_type=f32)
        parts.append(jnp.where(same, full, 0.0))
    shape = (PACK, WIDE)
    same = (number(shape, 0) % 4 == number(shape, 1) // 10) & (number(shape, 0) // 4 == number(shape, 1) % 10)
    first = jnp.concatenate([parts[0], same.astype(f32)], axis=0)
    last = jnp.concatenate([parts[1], jnp.zeros(shape, f32)], axis=0)
    return jnp.concatenate([first, first, last], axis=1).astype(bf16)


def find_parents(sizes, refine, code_ref, parent_ref):
    slots, margin, f32, bf16 = sizes.slots, sizes.margin, jnp.float32, jnp.bfloat16
    counts = (1.0 + refine).astype(bf16)
    row_i = lax.broadcasted_iota(jnp.int32, (LANES, LANES), 0)
    col_i = lax.broadcasted_iota(jnp.int32, (LANES, LANES), 1)
    within = jnp.dot(counts, (row_i <= col_i).astype(bf16), preferred_element_type=f32)
    whole = jnp.dot(counts, jnp.ones((LANES, LANES), bf16), preferred_element_type=f32)
    row_s = lax.broadcasted_iota(jnp.int32, (slots, slots), 0)
    col_s = lax.broadcasted_iota(jnp.int32, (slots, slots), 1)
    before = jnp.dot((col_s < row_s).astype(bf16), whole.astype(bf16), preferred_element_type=f32)
    ends = 2.0 * (within + before - before[margin : margin + 1, :]) + refine
    sums = lax.dot_general(
        jnp.ones((8, LANES), bf16), counts, (((1,), (1,)), ((), ())), preferred_element_type=f32
    ).astype(bf16)
    gap = lax.broadcasted_iota(jnp.int32, (slots, LANES), 1) - lax.broadcasted_iota(jnp.int32, (slots, LANES), 0)
    lines = [jnp.dot(sums, (gap >= least).astype(bf16), preferred_element_type=f32)[0:1] for least in (2, 1, 0)]
    own = lines[1][:, margin : margin + 1]
    shape = (sizes.children, LANES)
    lane = lax.broadcasted_iota(jnp.int32, shape, 1)
    row_start = LANES * (lax.broadcasted_iota(jnp.int32, shape, 0) - margin)
    begun = [line - own <= row_start.astype(f32) for line in lines]
    high = jnp.floor(ends * (1.0 / 256.0))
    rows = lax.broadcasted_iota(jnp.int32, (slots, LANES), 0).astype(f32)
    stack = jnp.concatenate([high, ends - 256.0 * high, rows], axis=1).astype(bf16)
    found_rows = [
        jnp.dot((begun[k] & ~begun[k + 1]).astype(bf16)[:, :slots], stack, preferred_element_type=f32)
        for k in (1, 0)
    ]
    near, far = [256.0 * x[:, :LANES] + x[:, LANES : 2 * LANES] for x in found_rows]
    child = row_start + lane
    goal = (2 * child + 1).astype(f32)
    beyond = jnp.broadcast_to(near[:, LANES - 1 :], shape) <= goal

    def pick(index):
        return jnp.where(beyond, lane_gather(far, index), lane_gather(near, index))

    found = jnp.zeros(shape, jnp.int32)
    size = LANES // 2
    while size:
        passed = pick(found + (size - 1)) <= goal
        found = jnp.where(passed, found + size, found)
        size //= 2
    mine = pick(found).astype(jnp.int32)
    split = mine & 1
    begin = (mine >> 1) - 1 - split
    code_ref[: sizes.children, :] = (found + LANES * split * (1 + child - begin)).astype(f32)
    code_ref[sizes.children :, :] = jnp.zeros((8, LANES), f32)
    parent_ref[...] = found_rows[0][:, 2 * LANES :].astype(jnp.int32) + beyond.astype(jnp.int32)


def prep_kernel(
    sizes, state_hbm, depth_hbm, metric_hbm, partner_hbm, refine_hbm, diff_hbm, lift_hbm, prolong_hbm,
    cur, aux, weights, diff_ref, lift_ref,
    state_ref, depth_ref, metric_ref, partner_ref, refine_ref, prolong_ref, spread, wide, sems,
):
    blocks = sizes.blocks
    copies = fetch_all(
        (
            (metric_hbm, metric_ref),
            (state_hbm, state_ref),
            (depth_hbm, depth_ref),
            (partner_hbm, partner_ref),
            (refine_hbm, refine_ref),
            (prolong_hbm, prolong_ref),
            (diff_hbm, diff_ref),
            (lift_hbm, lift_ref),
        ),
        sems,
    )
    for copy in copies:
        copy.wait()
    weights[...] = child_matrix(prolong_ref)
    metric = split_metric(metric_ref, spread, blocks)
    dense = [depth_ref[...], *metric, partner_ref[...].astype(jnp.float32), refine_ref[...].astype(jnp.float32)]
    for num in range(7):
        aux[num] = dense[num]
    pack_state(state_ref, wide, blocks, LAID, 4)
    for field in range(3):
        for node in range(10):
            cur[10 * field + node] = wide[pl.ds(4 * node + field, blocks, stride=LAID), :]


def first_kernel(
    sizes, cur_own, aux_own, weights_in, diff_in, lift_in, odd_ref, even_ref,
    cur, rate_ref, twice_ref, weights, code_ref, parent_ref,
    geo_ref, aux, diff_ref, lift_ref, sems,
):
    blocks, halo = sizes.blocks, sizes.halo
    top, bottom = PAD + halo, PAD + halo + blocks
    place = lax.axis_index(AXES)
    count = lax.axis_size(AXES)
    copies = fetch_all(((diff_in, diff_ref), (lift_in, lift_ref)), sems)
    even = place % 2 == 0

    def set_halo(target, num, row):
        by_even = even_ref[pl.ds(row, halo, stride=SENT), :]
        by_odd = odd_ref[pl.ds(row, halo, stride=SENT), :]
        target[num, top - halo : top, :] = jnp.where(even, by_odd, by_even)
        target[num, bottom : bottom + halo, :] = jnp.where(even, by_even, by_odd)

    for num in range(7):
        set_halo(aux, num, 30 + num)
        aux[num, top:bottom, :] = aux_own[num]
    for field in range(3):
        for node in range(10):
            item = 10 * field + node
            set_halo(cur, item, 3 * node + field)
            cur[item, top:bottom, :] = cur_own[item]

    weights[...] = weights_in[...]
    begin = PAD + sizes.keep
    for copy in copies:
        copy.wait()
    find_parents(sizes, aux[6, begin : begin + sizes.slots, :], code_ref, parent_ref)

    def step(start, height):
        base = PAD + start

        def load_aux(item, shift):
            return aux[item, pl.ds(base + shift, height), :]

        def load(item, shift):
            return cur[item, pl.ds(base + shift, height), :]

        depth, rx, ry, sx, sy, partner = [load_aux(num, 0) for num in range(6)]
        index, inside = pair_index(partner)
        fetch = outer_values(load_aux, index, inside)
        walls = wall_masks(sizes, start, place, count, partner)
        speed_sq = GRAVITY * depth
        outer_sq = [jnp.where(walls[k], speed_sq, GRAVITY * fetch[k](0)) for k in range(3)]
        faces = ((sx, sy), (rx + sx, ry + sy), (rx, ry))
        squares = [vx * vx + vy * vy for vx, vy in faces]
        waves = [
            0.5 * jnp.sqrt(squares[k]) * jnp.sqrt(jnp.maximum(speed_sq, outer_sq[k])) for k in range(3)
        ]
        ghosts = [8.0 / squares[k] for k in range(3)]
        geo = [speed_sq, rx, ry, sx, sy, *outer_sq, *waves, *ghosts]
        rates = tendency(load, geo, walls, index, inside, diff_ref, lift_ref)
        for num, value in enumerate([*geo, partner]):
            geo_ref[num, pl.ds(start, height), :] = value
        for item in range(30):
            rate_ref[item, pl.ds(base, height), :] = rates[item]

    def again(start, height):
        row = start + sizes.keep
        at = pl.ds(row, height)

        def load(item, shift):
            return rate_ref[item, pl.ds(PAD + row + shift, height), :]

        geo = [geo_ref[num, at, :] for num in range(14)]
        partner = geo_ref[14, at, :]
        index, inside = pair_index(partner)
        walls = wall_masks(sizes, row, place, count, partner)
        rates = tendency(load, geo, walls, index, inside, diff_ref, lift_ref)
        for item in range(30):
            twice_ref[item, pl.ds(start, height), :] = rates[item]

    def sweep(work, rows):
        def body(num, carry):
            work(pl.multiple_of(TALL * num, TALL), TALL)
            return carry

        lax.fori_loop(0, rows // TALL, body, 0)

    for start in range(sizes.rows // TALL * TALL, sizes.rows, 8):
        step(start, 8)
    sweep(step, sizes.rows)
    for start in range(sizes.slots // TALL * TALL, sizes.slots, 8):
        again(start, 8)
    sweep(again, sizes.slots)


def refine_kernel(
    sizes, cur, rate_ref, twice_ref, weights, code_ref, parent_ref, stats_ref, out_hbm,
    out_ref, parents, wide, index_ref, out_sems, sem,
):
    slots, keep, margin = sizes.slots, sizes.keep, LANES * sizes.margin
    place = lax.axis_index(AXES)
    copy = pltpu.make_async_copy(parent_ref, parents, sem)
    copy.start()
    stats = stats_ref[...]
    half = LANES // 2
    row_n = lax.broadcasted_iota(jnp.int32, stats.shape, 0)
    lane_n = lax.broadcasted_iota(jnp.int32, stats.shape, 1)
    top = jnp.max(stats, axis=0, keepdims=True)
    left = lax.broadcasted_iota(jnp.int32, (1, LANES), 1) < half
    step = COURANT / jnp.where(left, top, pltpu.roll(top, half, 1))
    half_square = 0.5 * step * step
    earlier = jnp.sum(jnp.where((row_n < place) & (lane_n == LANES - 1), stats, 0.0))
    shift = margin - (earlier.astype(jnp.int32) - place * (sizes.cells // 2))
    shift = jnp.clip(shift, 0, 2 * margin)
    row_shift, lane_shift = shift // LANES, shift % LANES
    lane = lax.broadcasted_iota(jnp.int32, (slots, LANES), 1)
    code = jnp.where(
        lane < lane_shift, code_ref[pl.ds(row_shift + 1, slots), :], code_ref[pl.ds(row_shift, slots), :]
    )
    code = pltpu.roll(code, (LANES - lane_shift) % LANES, 1).astype(jnp.int32)
    found = code & (LANES - 1)
    index_ref[0] = found
    index_ref[1] = code >> 7
    index_ref[2] = jnp.broadcast_to(found[:, 0:1], (slots, LANES))
    for item in range(30):
        now = slice(PAD + keep, PAD + keep + slots)
        value = cur[item, now, :] + step * rate_ref[item, now, :] + half_square * twice_ref[item]
        wide[pl.ds(item, slots, stride=STEP), :] = value
    for item in (30, 31):
        wide[pl.ds(item, slots + 1, stride=STEP), :] = jnp.zeros((slots + 1, LANES), jnp.float32)
    copy.wait()
    lane8 = lax.broadcasted_iota(jnp.int32, (8, LANES), 1)
    matrix = weights[...]
    chunk = 8 * LANES
    results = []
    for part in range(slots // 8):
        span = slice(chunk * part, chunk * (part + 1))
        columns = []
        for slot in range(8 * part, 8 * part + 8):
            lead_at = jnp.clip(parents[slot + row_shift, lane_shift], 0, slots - 1) * STEP
            lane_idx = jnp.broadcast_to(index_ref[0, slot : slot + 1, :], (8, LANES))
            ahead = lane8 < jnp.broadcast_to(index_ref[2, slot : slot + 1, :], (8, LANES))
            tiles = []
            for row in range(0, WIDE, 8):
                one = wide[pl.ds(lead_at + row, 8), :]
                two = wide[pl.ds(lead_at + STEP + row, 8), :]
                tiles.append(lane_gather(jnp.where(ahead, two, one), lane_idx))
            columns.append(jnp.concatenate(tiles, axis=0))
        values = jnp.concatenate(columns, axis=1)
        high = values.astype(jnp.bfloat16)
        low = (values - high.astype(jnp.float32)).astype(jnp.bfloat16)
        stack = jnp.concatenate([high, low, high], axis=0)
        children = jnp.dot(matrix, stack, preferred_element_type=jnp.float32)
        for sub in range(8):
            slot = 8 * part + sub
            cut = slice(LANES * sub, LANES * (sub + 1))
            tag = jnp.broadcast_to(index_ref[1, slot : slot + 1, :], (PACK, LANES))
            value = jnp.where(
                tag == 0,
                children[2 * PACK :, cut],
                jnp.where(tag == 1, children[:PACK, cut], children[PACK : 2 * PACK, cut]),
            )
            for node in range(10):
                out_ref[node, :, LANES * slot : LANES * (slot + 1)] = value[4 * node : 4 * node + 3]
        result = pltpu.make_async_copy(out_ref.at[:, :, span], out_hbm.at[:, :, span], out_sems.at[part])
        result.start()
        results.append(result)
    for result in results:
        result.wait()


def swaps(start, count):
    pairs = [(i, i + 1) for i in range(start, count - 1, 2)]
    return pairs + [(j, i) for i, j in pairs]


def shards(state, depth, metric, partner, refine, diff_ops, lift, prolong):
    sizes = Sizes(state.shape[2])
    count = lax.axis_size(AXES)
    blocks, rows, slots, halo = sizes.blocks, sizes.rows, sizes.slots, sizes.halo
    depth, partner, refine = [x.reshape(blocks, LANES) for x in (depth, partner, refine)]
    state, diff_ops, prolong = [jnp.transpose(x, (1, 0, 2)) for x in (state, diff_ops, prolong)]
    state, depth, metric, partner, refine, diff_ops, lift, prolong = [
        pltpu.with_memory_space_constraint(x, pltpu.HBM)
        for x in (state, depth, metric, partner, refine, diff_ops, lift, prolong)
    ]
    f32, i32 = jnp.float32, jnp.int32
    packed = jax.ShapeDtypeStruct((SENT * halo, LANES), f32)
    dense = [
        pltpu.VMEM((blocks, LANES), f32),
        pltpu.VMEM(metric.shape, f32),
        pltpu.VMEM((blocks, LANES), i32),
        pltpu.VMEM((blocks, LANES), i32),
    ]
    stats, even, odd = pl.pallas_call(
        functools.partial(pack_kernel, sizes),
        name="pack",
        out_shape=(jax.ShapeDtypeStruct((count, LANES), f32), packed, packed),
        in_specs=[HBM] * 5,
        out_specs=(HBM, VMEM, VMEM),
        scratch_shapes=[
            pltpu.VMEM((count, LANES), f32),
            pltpu.VMEM((10, 3, LANES * halo), f32),
            pltpu.VMEM((10, 3, LANES * halo), f32),
            *dense,
            pltpu.VMEM((8 * blocks, LANES), f32),
            pltpu.SemaphoreType.DMA((6,)),
            pltpu.SemaphoreType.DMA,
        ],
        compiler_params=PARAMS,
    )(state, depth, metric, partner, refine)
    odd = lax.ppermute(odd, AXES, swaps(1, count))
    even = lax.ppermute(even, AXES, swaps(0, count))
    stats = lax.all_to_all(stats, AXES, 0, 0, tiled=True)
    even, odd, stats = [pltpu.with_memory_space_constraint(x, pltpu.VMEM) for x in (even, odd, stats)]
    cur, aux, weights, diff_near, lift_near = pl.pallas_call(
        functools.partial(prep_kernel, sizes),
        name="lay_out",
        cost_estimate=pl.CostEstimate(flops=1 << 24, transcendentals=1 << 16, bytes_accessed=1 << 24),
        out_shape=(
            jax.ShapeDtypeStruct((30, blocks, LANES), f32),
            jax.ShapeDtypeStruct((7, blocks, LANES), f32),
            jax.ShapeDtypeStruct((3 * PACK, 3 * WIDE), jnp.bfloat16),
            jax.ShapeDtypeStruct(diff_ops.shape, f32),
            jax.ShapeDtypeStruct(lift.shape, f32),
        ),
        in_specs=[HBM] * 8,
        out_specs=(VMEM,) * 5,
        scratch_shapes=[
            pltpu.VMEM(state.shape, f32),
            *dense,
            pltpu.VMEM(prolong.shape, f32),
            pltpu.VMEM((8 * blocks, LANES), f32),
            pltpu.VMEM((LAID * blocks, LANES), f32),
            pltpu.SemaphoreType.DMA((8,)),
        ],
        compiler_params=PARAMS,
    )(state, depth, metric, partner, refine, diff_ops, lift, prolong)
    cur, rates, twice, weights, codes, parents = pl.pallas_call(
        functools.partial(first_kernel, sizes),
        name="rates_twice",
        cost_estimate=pl.CostEstimate(flops=1024, transcendentals=0, bytes_accessed=1024),
        out_shape=(
            jax.ShapeDtypeStruct((30, sizes.tall, LANES), f32),
            jax.ShapeDtypeStruct((30, sizes.tall, LANES), f32),
            jax.ShapeDtypeStruct((30, slots, LANES), f32),
            jax.ShapeDtypeStruct((3 * PACK, 3 * WIDE), jnp.bfloat16),
            jax.ShapeDtypeStruct((sizes.children + 8, LANES), f32),
            jax.ShapeDtypeStruct((sizes.children, LANES), i32),
        ),
        in_specs=[VMEM] * 7,
        out_specs=(VMEM,) * 6,
        scratch_shapes=[
            pltpu.VMEM((15, rows, LANES), f32),
            pltpu.VMEM((7, sizes.tall, LANES), f32),
            pltpu.SMEM(diff_ops.shape, f32),
            pltpu.SMEM(lift.shape, f32),
            pltpu.SemaphoreType.DMA((2,)),
        ],
        compiler_params=PARAMS,
    )(cur, aux, weights, diff_near, lift_near, odd, even)
    refined = pl.pallas_call(
        functools.partial(refine_kernel, sizes),
        name="sum_and_refine",
        out_shape=jax.ShapeDtypeStruct((10, 3, LANES * slots), f32),
        in_specs=[VMEM] * 7,
        out_specs=HBM,
        scratch_shapes=[
            pltpu.VMEM((10, 3, LANES * slots), f32),
            pltpu.SMEM((sizes.children, LANES), i32),
            pltpu.VMEM((STEP * (slots + 1), LANES), f32),
            pltpu.VMEM((3, slots, LANES), i32),
            pltpu.SemaphoreType.DMA((slots // 8,)),
            pltpu.SemaphoreType.DMA,
        ],
        compiler_params=PARAMS,
    )(cur, rates, twice, weights, codes, parents, stats)
    return jnp.transpose(refined, (1, 0, 2))


def solution(mesh):
    return jax.shard_map(
        shards,
        mesh=mesh,
        in_specs=(
            P(None, None, AXES),
            P(AXES),
            P(None, AXES),
            P(AXES),
            P(AXES),
            P(),
            P(),
            P(),
        ),
        out_specs=P(None, None, AXES),
        check_vma=False,
    )
```

```python
import functools

import jax
import jax.numpy as jnp
from jax import lax
from jax.experimental import pallas as pl
from jax.experimental.pallas import tpu as pltpu
from jax.sharding import PartitionSpec as P

GRAVITY = 9.81
COURANT = 0.5
HIGH = lax.Precision.HIGHEST
LANES = 128
AXES = ("row", "col")
FACES = ((0, 1, 2, 3), (3, 6, 8, 9), (9, 7, 4, 0))
PACK = 40
LAID = 41
SENT = 37
WIDE = 32
STEP = 40
TALL = 16
PAD = 8

VMEM = pl.BlockSpec(memory_space=pltpu.VMEM)
HBM = pl.BlockSpec(memory_space=pltpu.HBM)
PARAMS = pltpu.CompilerParams(vmem_limit_bytes=48 * 1024 * 1024)


class Sizes:
    def __init__(self, cells):
        self.cells = cells
        self.blocks = cells // LANES
        self.margin = cells // 4 // LANES
        self.halo = self.margin + 1
        self.rows = -(-(self.blocks + 2 * self.halo) // 8) * 8
        self.tall = self.rows + 2 * PAD
        self.slots = 3 * self.blocks // 2
        self.keep = self.halo - self.margin


def fetch_all(pairs, sems):
    copies = [pltpu.make_async_copy(src, dst, sems.at[num]) for num, (src, dst) in enumerate(pairs)]
    for copy in copies:
        copy.start()
    return copies


def split_metric(metric_ref, spread, blocks):
    for block in range(blocks):
        spread[8 * block : 8 * block + 4, :] = metric_ref[:, LANES * block : LANES * (block + 1)]
    return [spread[pl.ds(comp, blocks, stride=8), :] for comp in range(4)]


def pack_kernel(
    sizes, state_hbm, depth_hbm, metric_hbm, partner_hbm, refine_hbm, stats_hbm, even_ref, odd_ref,
    stats_ref, state_even, state_odd, depth_ref, metric_ref, partner_ref, refine_ref, spread, sems, sem,
):
    blocks, halo = sizes.blocks, sizes.halo
    wide = LANES * halo
    late = blocks - halo
    even = (lax.axis_index(AXES) + 1) % 2 * late
    odd = late - even
    copies = fetch_all(
        (
            (depth_hbm, depth_ref),
            (metric_hbm, metric_ref),
            (refine_hbm, refine_ref),
            (partner_hbm, partner_ref),
            (state_hbm.at[:, :, pl.ds(pl.multiple_of(LANES * even, LANES), wide)], state_even),
            (state_hbm.at[:, :, pl.ds(pl.multiple_of(LANES * odd, LANES), wide)], state_odd),
        ),
        sems,
    )
    for copy in copies[:3]:
        copy.wait()
    rx, ry, sx, sy = split_metric(metric_ref, spread, blocks)
    depth = depth_ref[...]
    refine = refine_ref[...].astype(jnp.float32)
    faces = ((sx, sy), (rx + sx, ry + sy), (rx, ry))
    lengths = [jnp.sqrt(vx * vx + vy * vy) for vx, vy in faces]
    rate = jnp.sqrt(GRAVITY * depth) * jnp.maximum(jnp.maximum(lengths[0], lengths[1]), lengths[2])
    top = jnp.max(jnp.max(rate, axis=0, keepdims=True), axis=1, keepdims=True)
    extra = jnp.sum(jnp.sum(refine, axis=0, keepdims=True), axis=1, keepdims=True)
    shape = stats_ref.shape
    lane = lax.broadcasted_iota(jnp.int32, shape, 1)
    stats_ref[...] = jnp.where(
        lane < LANES // 2, jnp.broadcast_to(top, shape), jnp.broadcast_to(extra, shape)
    )
    sent = pltpu.make_async_copy(stats_ref, stats_hbm, sem)
    sent.start()
    for copy in copies[3:]:
        copy.wait()
    for ref, source, start in ((even_ref, state_even, even), (odd_ref, state_odd, odd)):
        pack_state(source, ref, halo, SENT, 3)
        at = pl.ds(start, halo)
        dense = [depth_ref[at, :]]
        dense += [spread[pl.ds(8 * start + comp, halo, stride=8), :] for comp in range(4)]
        dense += [partner_ref[at, :].astype(jnp.float32), refine_ref[at, :].astype(jnp.float32)]
        for num, value in enumerate(dense):
            ref[pl.ds(30 + num, halo, stride=SENT), :] = value
    sent.wait()


def pack_state(source, target, blocks, height, width):
    for block in range(blocks):
        for node in range(10):
            at = height * block + width * node
            target[at : at + 3, :] = source[node, :, LANES * block : LANES * (block + 1)]


def pair_index(partner):
    lane = lax.broadcasted_iota(jnp.int32, partner.shape, 1)
    target = lane + partner.astype(jnp.int32)
    return target & (LANES - 1), (target >= 0) & (target < LANES)


def lane_gather(values, index):
    return jnp.take_along_axis(values, index, axis=1, mode="promise_in_bounds")


def outer_values(load, index, inside):
    shape = index.shape
    lane = lax.broadcasted_iota(jnp.int32, shape, 1)

    def prev(item):
        return pltpu.roll(jnp.where(lane == LANES - 1, load(item, -1), load(item, 0)), 1, 1)

    def after(item):
        return pltpu.roll(jnp.where(lane == 0, load(item, 1), load(item, 0)), LANES - 1, 1)

    def across(item):
        other = jnp.where(lane < LANES // 2, load(item, 1), load(item, -1))
        return jnp.where(inside, lane_gather(load(item, 0), index), lane_gather(other, index))

    return prev, after, across


def wall_masks(sizes, start, place, count, partner):
    shape = partner.shape
    lane = lax.broadcasted_iota(jnp.int32, shape, 1)
    row = lax.broadcasted_iota(jnp.int32, shape, 0) + start
    first = (lane == 0) & (row == sizes.halo) & (place == 0)
    last = (lane == LANES - 1) & (row == sizes.halo + sizes.blocks - 1) & (place == count - 1)
    return first, last, partner == 0


def tendency(load, geo, walls, index, inside, operators):
    speed_sq, rx, ry, sx, sy = geo[:5]
    outer_sq, waves, ghosts = geo[5:8], geo[8:11], geo[11:14]
    own = [[load(10 * field + node, 0) for node in range(10)] for field in range(3)]
    eta, mom_x, mom_y = own
    flow_r = [-(rx * mom_x[b] + ry * mom_y[b]) for b in range(10)]
    flow_s = [-(sx * mom_x[b] + sy * mom_y[b]) for b in range(10)]
    half_r = (0.5 * rx, 0.5 * ry)
    half_s = (0.5 * sx, 0.5 * sy)
    vectors = (
        (-half_s[0], -half_s[1]),
        (half_r[0] + half_s[0], half_r[1] + half_s[1]),
        (-half_r[0], -half_r[1]),
    )
    fetch = outer_values(load, index, inside)
    jumps = ([], [], [])
    for face in range(3):
        vec_x, vec_y = vectors[face]
        theirs = FACES[(1, 0, 2)[face]]
        wall = walls[face]
        for j in range(4):
            node, match = FACES[face][j], theirs[3 - j]
            in_eta, in_x, in_y = eta[node], mom_x[node], mom_y[node]
            ext_eta, ext_x, ext_y = [fetch[face](10 * field + match) for field in range(3)]
            bounce = (in_x * vec_x + in_y * vec_y) * ghosts[face]
            d_eta = jnp.where(wall, 0.0, in_eta - ext_eta)
            d_x = jnp.where(wall, bounce * vec_x, in_x - ext_x)
            d_y = jnp.where(wall, bounce * vec_y, in_y - ext_y)
            head = jnp.where(wall, 0.0, speed_sq * in_eta - outer_sq[face] * ext_eta)
            jumps[0].append(d_x * vec_x + d_y * vec_y - waves[face] * d_eta)
            jumps[1].append(head * vec_x - waves[face] * d_x)
            jumps[2].append(head * vec_y - waves[face] * d_y)
    pull = (-speed_sq * rx, -speed_sq * ry)
    push = (-speed_sq * sx, -speed_sq * sy)
    out = [[None] * 10 for _ in range(3)]
    for a in range(10):
        total = along_r = along_s = None
        for b in range(10):
            d_r, d_s = operators[a // 4, a % 4 * 32 + b], operators[a // 4, a % 4 * 32 + 10 + b]
            term = d_r * flow_r[b] + d_s * flow_s[b]
            total = term if b == 0 else total + term
            along_r = d_r * eta[b] if b == 0 else along_r + d_r * eta[b]
            along_s = d_s * eta[b] if b == 0 else along_s + d_s * eta[b]
        sums = [total, pull[0] * along_r + push[0] * along_s, pull[1] * along_r + push[1] * along_s]
        for q in range(12):
            weight = operators[a // 4, a % 4 * 32 + 20 + q]
            for field in range(3):
                sums[field] = sums[field] + weight * jumps[field][q]
        for field in range(3):
            out[field][a] = sums[field]
    return [out[field][a] for field in range(3) for a in range(10)]


def child_matrix(prolong_ref):
    f32, bf16 = jnp.float32, jnp.bfloat16

    def number(shape, axis):
        return lax.broadcasted_iota(jnp.int32, shape, axis)

    both = jnp.concatenate([prolong_ref[:, 0, :], prolong_ref[:, 1, :]], axis=0)
    rounded = both.astype(bf16)
    rest = (both - rounded.astype(f32)).astype(bf16)
    shape = (10, WIDE)
    columns = (number(shape, 1) % 10 == number(shape, 0)).astype(bf16)
    shape = (2 * PACK, 20)
    rows = (number(shape, 0) // 4 == number(shape, 1)).astype(bf16)
    shape = (2 * PACK, WIDE)
    same = number(shape, 0) % 4 == number(shape, 1) // 10
    parts = []
    for matrix in (rounded, rest):
        spread = jnp.dot(matrix, columns, preferred_element_type=f32).astype(bf16)
        full = jnp.dot(rows, spread, preferred_element_type=f32)
        parts.append(jnp.where(same, full, 0.0))
    shape = (PACK, WIDE)
    same = (number(shape, 0) % 4 == number(shape, 1) // 10) & (number(shape, 0) // 4 == number(shape, 1) % 10)
    first = jnp.concatenate([parts[0], same.astype(f32)], axis=0)
    last = jnp.concatenate([parts[1], jnp.zeros(shape, f32)], axis=0)
    return jnp.concatenate([first, first, last], axis=1).astype(bf16)


def sum_children(sizes, refine, ends_ref, lines_ref):
    slots, f32 = sizes.slots, jnp.float32
    counts = (1.0 + refine).astype(jnp.bfloat16)
    row_i = lax.broadcasted_iota(jnp.int32, (LANES, LANES), 0)
    col_i = lax.broadcasted_iota(jnp.int32, (LANES, LANES), 1)
    upper = (row_i <= col_i).astype(jnp.bfloat16)
    within = jnp.dot(counts, upper, preferred_element_type=f32)
    whole = jnp.dot(counts, jnp.ones((LANES, LANES), jnp.bfloat16), preferred_element_type=f32)
    row_s = lax.broadcasted_iota(jnp.int32, (slots, slots), 0)
    col_s = lax.broadcasted_iota(jnp.int32, (slots, slots), 1)
    lower = (col_s < row_s).astype(jnp.bfloat16)
    before = jnp.dot(lower, whole.astype(jnp.bfloat16), preferred_element_type=f32)
    before = before - before[sizes.margin : sizes.margin + 1, :]
    ends_ref[0] = 2.0 * (within + before) + refine
    ends_ref[1] = before + whole
    ones = jnp.ones((8, LANES), jnp.bfloat16)
    sums = lax.dot_general(ones, counts, (((1,), (1,)), ((), ())), preferred_element_type=f32)
    gap = lax.broadcasted_iota(jnp.int32, (slots, LANES), 1) - lax.broadcasted_iota(jnp.int32, (slots, LANES), 0)
    lines = [
        jnp.dot(sums.astype(jnp.bfloat16), (gap >= least).astype(jnp.bfloat16), preferred_element_type=f32)
        for least in (2, 1, 0)
    ]
    own = lines[1][:, sizes.margin : sizes.margin + 1]
    for num in range(3):
        lines_ref[num] = lines[num] - own


def prep_kernel(
    sizes, state_hbm, depth_hbm, metric_hbm, partner_hbm, refine_hbm, diff_hbm, lift_hbm, prolong_hbm,
    cur, aux, weights, operators,
    state_ref, depth_ref, metric_ref, partner_ref, refine_ref, prolong_ref, diff_ref, lift_ref, spread, wide, sems,
):
    blocks = sizes.blocks
    copies = fetch_all(
        (
            (metric_hbm, metric_ref),
            (state_hbm, state_ref),
            (depth_hbm, depth_ref),
            (partner_hbm, partner_ref),
            (refine_hbm, refine_ref),
            (prolong_hbm, prolong_ref),
            (diff_hbm, diff_ref),
            (lift_hbm, lift_ref),
        ),
        sems,
    )
    for copy in copies:
        copy.wait()
    weights[...] = child_matrix(prolong_ref)
    rows = jnp.concatenate([diff_ref[:, 0, :], diff_ref[:, 1, :], lift_ref[...]], axis=1)
    rows = jnp.concatenate([rows, jnp.zeros((2, 32), jnp.float32)], axis=0)
    for row in range(3):
        for part in range(4):
            at = 4 * row + part
            operators[row : row + 1, 32 * part : 32 * part + 32] = rows[at : at + 1]
    metric = split_metric(metric_ref, spread, blocks)
    dense = [depth_ref[...], *metric, partner_ref[...].astype(jnp.float32), refine_ref[...].astype(jnp.float32)]
    for num in range(7):
        aux[num] = dense[num]
    pack_state(state_ref, wide, blocks, LAID, 4)
    for field in range(3):
        for node in range(10):
            cur[10 * field + node] = wide[pl.ds(4 * node + field, blocks, stride=LAID), :]


def first_kernel(
    sizes, cur_own, aux_own, weights_in, operators_in, odd_ref, even_ref,
    cur, rate_ref, twice_ref, weights, ends_ref, lines_ref,
    geo_ref, aux, operators, sems,
):
    blocks, halo = sizes.blocks, sizes.halo
    top, bottom = PAD + halo, PAD + halo + blocks
    place = lax.axis_index(AXES)
    count = lax.axis_size(AXES)
    copies = fetch_all(((operators_in, operators),), sems)
    even = place % 2 == 0

    def set_halo(target, num, row):
        by_even = even_ref[pl.ds(row, halo, stride=SENT), :]
        by_odd = odd_ref[pl.ds(row, halo, stride=SENT), :]
        target[num, top - halo : top, :] = jnp.where(even, by_odd, by_even)
        target[num, bottom : bottom + halo, :] = jnp.where(even, by_even, by_odd)

    for num in range(7):
        set_halo(aux, num, 30 + num)
        aux[num, top:bottom, :] = aux_own[num]
    for field in range(3):
        for node in range(10):
            item = 10 * field + node
            set_halo(cur, item, 3 * node + field)
            cur[item, top:bottom, :] = cur_own[item]

    weights[...] = weights_in[...]
    begin = PAD + sizes.keep
    sum_children(sizes, aux[6, begin : begin + sizes.slots, :], ends_ref, lines_ref)
    for copy in copies:
        copy.wait()

    def step(start, height):
        base = PAD + start

        def load_aux(item, shift):
            return aux[item, pl.ds(base + shift, height), :]

        def load(item, shift):
            return cur[item, pl.ds(base + shift, height), :]

        depth, rx, ry, sx, sy, partner = [load_aux(num, 0) for num in range(6)]
        index, inside = pair_index(partner)
        fetch = outer_values(load_aux, index, inside)
        walls = wall_masks(sizes, start, place, count, partner)
        speed_sq = GRAVITY * depth
        outer_sq = [jnp.where(walls[k], speed_sq, GRAVITY * fetch[k](0)) for k in range(3)]
        faces = ((sx, sy), (rx + sx, ry + sy), (rx, ry))
        squares = [vx * vx + vy * vy for vx, vy in faces]
        waves = [
            0.5 * jnp.sqrt(squares[k]) * jnp.sqrt(jnp.maximum(speed_sq, outer_sq[k])) for k in range(3)
        ]
        ghosts = [8.0 / squares[k] for k in range(3)]
        geo = [speed_sq, rx, ry, sx, sy, *outer_sq, *waves, *ghosts]
        rates = tendency(load, geo, walls, index, inside, operators)
        for num, value in enumerate([*geo, partner]):
            geo_ref[num, pl.ds(start, height), :] = value
        for item in range(30):
            rate_ref[item, pl.ds(base, height), :] = rates[item]

    def again(start, height):
        row = start + sizes.keep
        at = pl.ds(row, height)

        def load(item, shift):
            return rate_ref[item, pl.ds(PAD + row + shift, height), :]

        geo = [geo_ref[num, at, :] for num in range(14)]
        partner = geo_ref[14, at, :]
        index, inside = pair_index(partner)
        walls = wall_masks(sizes, row, place, count, partner)
        rates = tendency(load, geo, walls, index, inside, operators)
        for item in range(30):
            twice_ref[item, pl.ds(start, height), :] = rates[item]

    def sweep(work, rows):
        def body(num, carry):
            work(pl.multiple_of(TALL * num, TALL), TALL)
            return carry

        lax.fori_loop(0, rows // TALL, body, 0)

    for start in range(sizes.rows // TALL * TALL, sizes.rows, 8):
        step(start, 8)
    sweep(step, sizes.rows)
    for start in range(sizes.slots // TALL * TALL, sizes.slots, 8):
        again(start, 8)
    sweep(again, sizes.slots)


def refine_kernel(
    sizes, cur, rate_ref, twice_ref, weights, base_ref, lines_ref, stats_ref, out_hbm,
    out_ref, place_v, place_s, wide, index_ref, out_sems, sem,
):
    slots, keep = sizes.slots, sizes.keep
    place = lax.axis_index(AXES)
    stats = stats_ref[...]
    half = LANES // 2
    row_n = lax.broadcasted_iota(jnp.int32, stats.shape, 0)
    top = jnp.max(stats, axis=0, keepdims=True)
    earlier = jnp.sum(jnp.where(row_n < place, stats, 0.0), axis=0, keepdims=True)
    left = lax.broadcasted_iota(jnp.int32, (1, LANES), 1) < half
    top = jnp.where(left, top, pltpu.roll(top, half, 1))
    earlier = jnp.where(left, pltpu.roll(earlier, half, 1), earlier)
    step = COURANT / top
    half_square = 0.5 * step * step
    start = earlier - (place * (sizes.cells // 2)).astype(jnp.float32)
    first_slot = LANES * lax.broadcasted_iota(jnp.int32, (slots, LANES), 1).astype(jnp.float32)
    lead = jnp.sum((base_ref[1] + start <= first_slot).astype(jnp.float32), axis=0, keepdims=True)
    lead = jnp.clip(lead.astype(jnp.int32), 0, slots - 1)
    place_v[...] = lead
    copy = pltpu.make_async_copy(place_v, place_s, sem)
    copy.start()
    for item in range(30):
        now = slice(PAD + keep, PAD + keep + slots)
        value = cur[item, now, :] + step * rate_ref[item, now, :] + half_square * twice_ref[item]
        wide[pl.ds(item, slots, stride=STEP), :] = value
    for item in (30, 31):
        wide[pl.ds(item, slots + 1, stride=STEP), :] = jnp.zeros((slots + 1, LANES), jnp.float32)
    slot_start = LANES * lax.broadcasted_iota(jnp.int32, (slots, LANES), 0).astype(jnp.float32)
    begun = [lines_ref[num, 0:1, :] + start <= slot_start for num in range(3)]
    near, far = [
        2.0 * start
        + jnp.dot(
            (begun[num] & ~begun[num + 1]).astype(jnp.float32)[:, :slots],
            base_ref[0],
            precision=HIGH,
            preferred_element_type=jnp.float32,
        )
        for num in (1, 0)
    ]
    lane = lax.broadcasted_iota(jnp.int32, (slots, LANES), 1)
    slot_no = LANES * lax.broadcasted_iota(jnp.int32, (slots, LANES), 0) + lane
    goal = (2 * slot_no + 1).astype(jnp.float32)
    beyond = jnp.broadcast_to(near[:, LANES - 1 :], (slots, LANES)) <= goal

    def pick(index):
        return jnp.where(beyond, lane_gather(far, index), lane_gather(near, index))

    found = jnp.zeros((slots, LANES), jnp.int32)
    size = LANES // 2
    while size:
        passed = pick(found + (size - 1)) <= goal
        found = jnp.where(passed, found + size, found)
        size //= 2
    mine = pick(found).astype(jnp.int32)
    split = mine & 1
    begin = (mine >> 1) - 1 - split
    kind = split * (1 + slot_no - begin)
    index_ref[0] = found.astype(jnp.float32)
    index_ref[1] = kind.astype(jnp.float32)
    index_ref[2] = (lane < jnp.broadcast_to(found[:, 0:1], (slots, LANES))).astype(jnp.float32)
    copy.wait()
    matrix = weights[...]
    chunk = 8 * LANES
    results = []
    for part in range(slots // 8):
        span = slice(chunk * part, chunk * (part + 1))
        columns = []
        for slot in range(8 * part, 8 * part + 8):
            lead_at = place_s[0, slot] * STEP
            lane_idx = jnp.broadcast_to(index_ref[0, slot : slot + 1, :], (8, LANES)).astype(jnp.int32)
            ahead = jnp.broadcast_to(index_ref[2, slot : slot + 1, :], (8, LANES)) > 0.5
            tiles = []
            for row in range(0, WIDE, 8):
                one = wide[pl.ds(pl.multiple_of(lead_at + row, 8), 8), :]
                two = wide[pl.ds(pl.multiple_of(lead_at + STEP + row, 8), 8), :]
                tiles.append(lane_gather(jnp.where(ahead, two, one), lane_idx))
            columns.append(jnp.concatenate(tiles, axis=0))
        values = jnp.concatenate(columns, axis=1)
        high = values.astype(jnp.bfloat16)
        low = (values - high.astype(jnp.float32)).astype(jnp.bfloat16)
        stack = jnp.concatenate([high, low, high], axis=0)
        children = jnp.dot(matrix, stack, preferred_element_type=jnp.float32)
        for sub in range(8):
            slot = 8 * part + sub
            cut = slice(LANES * sub, LANES * (sub + 1))
            tag = jnp.broadcast_to(index_ref[1, slot : slot + 1, :], (PACK, LANES))
            value = jnp.where(
                tag < 0.5,
                children[2 * PACK :, cut],
                jnp.where(tag < 1.5, children[:PACK, cut], children[PACK : 2 * PACK, cut]),
            )
            for node in range(10):
                out_ref[node, :, LANES * slot : LANES * (slot + 1)] = value[4 * node : 4 * node + 3]
        result = pltpu.make_async_copy(out_ref.at[:, :, span], out_hbm.at[:, :, span], out_sems.at[part])
        result.start()
        results.append(result)
    for result in results:
        result.wait()


def swaps(start, count):
    pairs = [(i, i + 1) for i in range(start, count - 1, 2)]
    return pairs + [(j, i) for i, j in pairs]


def shards(state, depth, metric, partner, refine, diff_ops, lift, prolong):
    sizes = Sizes(state.shape[2])
    count = lax.axis_size(AXES)
    blocks, rows, slots, halo = sizes.blocks, sizes.rows, sizes.slots, sizes.halo
    depth, partner, refine = [x.reshape(blocks, LANES) for x in (depth, partner, refine)]
    state, diff_ops, prolong = [jnp.transpose(x, (1, 0, 2)) for x in (state, diff_ops, prolong)]
    state, depth, metric, partner, refine, diff_ops, lift, prolong = [
        pltpu.with_memory_space_constraint(x, pltpu.HBM)
        for x in (state, depth, metric, partner, refine, diff_ops, lift, prolong)
    ]
    f32, i32 = jnp.float32, jnp.int32
    packed = jax.ShapeDtypeStruct((SENT * halo, LANES), f32)
    dense = [
        pltpu.VMEM((blocks, LANES), f32),
        pltpu.VMEM(metric.shape, f32),
        pltpu.VMEM((blocks, LANES), i32),
        pltpu.VMEM((blocks, LANES), i32),
    ]
    stats, even, odd = pl.pallas_call(
        functools.partial(pack_kernel, sizes),
        name="pack",
        out_shape=(jax.ShapeDtypeStruct((count, LANES), f32), packed, packed),
        in_specs=[HBM] * 5,
        out_specs=(HBM, VMEM, VMEM),
        scratch_shapes=[
            pltpu.VMEM((count, LANES), f32),
            pltpu.VMEM((10, 3, LANES * halo), f32),
            pltpu.VMEM((10, 3, LANES * halo), f32),
            *dense,
            pltpu.VMEM((8 * blocks, LANES), f32),
            pltpu.SemaphoreType.DMA((6,)),
            pltpu.SemaphoreType.DMA,
        ],
        compiler_params=PARAMS,
    )(state, depth, metric, partner, refine)
    odd = lax.ppermute(odd, AXES, swaps(1, count))
    even = lax.ppermute(even, AXES, swaps(0, count))
    stats = lax.all_to_all(stats, AXES, 0, 0, tiled=True)
    even, odd, stats = [pltpu.with_memory_space_constraint(x, pltpu.VMEM) for x in (even, odd, stats)]
    cur, aux, weights, operators = pl.pallas_call(
        functools.partial(prep_kernel, sizes),
        name="lay_out",
        cost_estimate=pl.CostEstimate(flops=1 << 24, transcendentals=1 << 16, bytes_accessed=1 << 24),
        out_shape=(
            jax.ShapeDtypeStruct((30, blocks, LANES), f32),
            jax.ShapeDtypeStruct((7, blocks, LANES), f32),
            jax.ShapeDtypeStruct((3 * PACK, 3 * WIDE), jnp.bfloat16),
            jax.ShapeDtypeStruct((3, LANES), f32),
        ),
        in_specs=[HBM] * 8,
        out_specs=(VMEM,) * 4,
        scratch_shapes=[
            pltpu.VMEM(state.shape, f32),
            *dense,
            pltpu.VMEM(prolong.shape, f32),
            pltpu.VMEM(diff_ops.shape, f32),
            pltpu.VMEM(lift.shape, f32),
            pltpu.VMEM((8 * blocks, LANES), f32),
            pltpu.VMEM((LAID * blocks, LANES), f32),
            pltpu.SemaphoreType.DMA((8,)),
        ],
        compiler_params=PARAMS,
    )(state, depth, metric, partner, refine, diff_ops, lift, prolong)
    cur, rates, twice, weights, ends, lines = pl.pallas_call(
        functools.partial(first_kernel, sizes),
        name="rates_twice",
        cost_estimate=pl.CostEstimate(flops=1024, transcendentals=0, bytes_accessed=1024),
        out_shape=(
            jax.ShapeDtypeStruct((30, sizes.tall, LANES), f32),
            jax.ShapeDtypeStruct((30, sizes.tall, LANES), f32),
            jax.ShapeDtypeStruct((30, slots, LANES), f32),
            jax.ShapeDtypeStruct((3 * PACK, 3 * WIDE), jnp.bfloat16),
            jax.ShapeDtypeStruct((2, slots, LANES), f32),
            jax.ShapeDtypeStruct((3, 8, LANES), f32),
        ),
        in_specs=[VMEM] * 6,
        out_specs=(VMEM,) * 6,
        scratch_shapes=[
            pltpu.VMEM((15, rows, LANES), f32),
            pltpu.VMEM((7, sizes.tall, LANES), f32),
            pltpu.SMEM((3, LANES), f32),
            pltpu.SemaphoreType.DMA((1,)),
        ],
        compiler_params=PARAMS,
    )(cur, aux, weights, operators, odd, even)
    refined = pl.pallas_call(
        functools.partial(refine_kernel, sizes),
        name="sum_and_refine",
        out_shape=jax.ShapeDtypeStruct((10, 3, LANES * slots), f32),
        in_specs=[VMEM] * 7,
        out_specs=HBM,
        scratch_shapes=[
            pltpu.VMEM((10, 3, LANES * slots), f32),
            pltpu.VMEM((1, LANES), i32),
            pltpu.SMEM((1, LANES), i32),
            pltpu.VMEM((STEP * (slots + 1), LANES), f32),
            pltpu.VMEM((3, slots, LANES), f32),
            pltpu.SemaphoreType.DMA((slots // 8,)),
            pltpu.SemaphoreType.DMA,
        ],
        compiler_params=PARAMS,
    )(cur, rates, twice, weights, ends, lines, stats)
    return jnp.transpose(refined, (1, 0, 2))


def solution(mesh):
    return jax.shard_map(
        shards,
        mesh=mesh,
        in_specs=(
            P(None, None, AXES),
            P(AXES),
            P(None, AXES),
            P(AXES),
            P(AXES),
            P(),
            P(),
            P(),
        ),
        out_specs=P(None, None, AXES),
        check_vma=False,
    )
```

```python
import functools

import jax
import jax.numpy as jnp
from jax import lax
from jax.experimental import pallas as pl
from jax.experimental.pallas import tpu as pltpu
from jax.sharding import PartitionSpec as P

GRAVITY = 9.81
COURANT = 0.5
HIGH = lax.Precision.HIGHEST
LANES = 128
AXES = ("row", "col")
FACES = ((0, 1, 2, 3), (3, 6, 8, 9), (9, 7, 4, 0))
PACK = 40
LAID = 41
SENT = 37
WIDE = 32
STEP = 33
TALL = 16
PAD = 8

VMEM = pl.BlockSpec(memory_space=pltpu.VMEM)
HBM = pl.BlockSpec(memory_space=pltpu.HBM)
PARAMS = pltpu.CompilerParams(vmem_limit_bytes=48 * 1024 * 1024)


class Sizes:
    def __init__(self, cells):
        self.cells = cells
        self.blocks = cells // LANES
        self.margin = cells // 4 // LANES
        self.halo = self.margin + 1
        self.rows = -(-(self.blocks + 2 * self.halo) // 8) * 8
        self.tall = self.rows + 2 * PAD
        self.slots = 3 * self.blocks // 2
        self.keep = self.halo - self.margin


def fetch_all(pairs, sems):
    copies = [pltpu.make_async_copy(src, dst, sems.at[num]) for num, (src, dst) in enumerate(pairs)]
    for copy in copies:
        copy.start()
    return copies


def split_metric(metric_ref, spread, blocks):
    for block in range(blocks):
        spread[8 * block : 8 * block + 4, :] = metric_ref[:, LANES * block : LANES * (block + 1)]
    return [spread[pl.ds(comp, blocks, stride=8), :] for comp in range(4)]


def pack_kernel(
    sizes, state_hbm, depth_hbm, metric_hbm, partner_hbm, refine_hbm, stats_hbm, even_ref, odd_ref,
    stats_ref, state_even, state_odd, depth_ref, metric_ref, partner_ref, refine_ref, spread, sems, sem,
):
    blocks, halo = sizes.blocks, sizes.halo
    wide = LANES * halo
    late = blocks - halo
    even = (lax.axis_index(AXES) + 1) % 2 * late
    odd = late - even
    copies = fetch_all(
        (
            (depth_hbm, depth_ref),
            (metric_hbm, metric_ref),
            (refine_hbm, refine_ref),
            (partner_hbm, partner_ref),
            (state_hbm.at[:, :, pl.ds(pl.multiple_of(LANES * even, LANES), wide)], state_even),
            (state_hbm.at[:, :, pl.ds(pl.multiple_of(LANES * odd, LANES), wide)], state_odd),
        ),
        sems,
    )
    for copy in copies[:3]:
        copy.wait()
    rx, ry, sx, sy = split_metric(metric_ref, spread, blocks)
    depth = depth_ref[...]
    refine = refine_ref[...].astype(jnp.float32)
    faces = ((sx, sy), (rx + sx, ry + sy), (rx, ry))
    lengths = [jnp.sqrt(vx * vx + vy * vy) for vx, vy in faces]
    rate = jnp.sqrt(GRAVITY * depth) * jnp.maximum(jnp.maximum(lengths[0], lengths[1]), lengths[2])
    top = jnp.max(jnp.max(rate, axis=0, keepdims=True), axis=1, keepdims=True)
    extra = jnp.sum(jnp.sum(refine, axis=0, keepdims=True), axis=1, keepdims=True)
    shape = stats_ref.shape
    lane = lax.broadcasted_iota(jnp.int32, shape, 1)
    stats_ref[...] = jnp.where(
        lane < LANES // 2, jnp.broadcast_to(top, shape), jnp.broadcast_to(extra, shape)
    )
    sent = pltpu.make_async_copy(stats_ref, stats_hbm, sem)
    sent.start()
    for copy in copies[3:]:
        copy.wait()
    for ref, source, start in ((even_ref, state_even, even), (odd_ref, state_odd, odd)):
        pack_state(source, ref, halo, SENT, 3)
        at = pl.ds(start, halo)
        dense = [depth_ref[at, :]]
        dense += [spread[pl.ds(8 * start + comp, halo, stride=8), :] for comp in range(4)]
        dense += [partner_ref[at, :].astype(jnp.float32), refine_ref[at, :].astype(jnp.float32)]
        for num, value in enumerate(dense):
            ref[pl.ds(30 + num, halo, stride=SENT), :] = value
    sent.wait()


def pack_state(source, target, blocks, height, width):
    for block in range(blocks):
        for node in range(10):
            at = height * block + width * node
            target[at : at + 3, :] = source[node, :, LANES * block : LANES * (block + 1)]


def pair_index(partner):
    lane = lax.broadcasted_iota(jnp.int32, partner.shape, 1)
    target = lane + partner.astype(jnp.int32)
    return target & (LANES - 1), (target >= 0) & (target < LANES)


def lane_gather(values, index):
    return jnp.take_along_axis(values, index, axis=1, mode="promise_in_bounds")


def outer_values(load, index, inside):
    shape = index.shape
    lane = lax.broadcasted_iota(jnp.int32, shape, 1)

    def prev(item):
        return pltpu.roll(jnp.where(lane == LANES - 1, load(item, -1), load(item, 0)), 1, 1)

    def after(item):
        return pltpu.roll(jnp.where(lane == 0, load(item, 1), load(item, 0)), LANES - 1, 1)

    def across(item):
        other = jnp.where(lane < LANES // 2, load(item, 1), load(item, -1))
        return jnp.where(inside, lane_gather(load(item, 0), index), lane_gather(other, index))

    return prev, after, across


def wall_masks(sizes, start, place, count, partner):
    shape = partner.shape
    lane = lax.broadcasted_iota(jnp.int32, shape, 1)
    row = lax.broadcasted_iota(jnp.int32, shape, 0) + start
    first = (lane == 0) & (row == sizes.halo) & (place == 0)
    last = (lane == LANES - 1) & (row == sizes.halo + sizes.blocks - 1) & (place == count - 1)
    return first, last, partner == 0


def tendency(load, geo, walls, index, inside, operators):
    speed_sq, rx, ry, sx, sy = geo[:5]
    outer_sq, waves, ghosts = geo[5:8], geo[8:11], geo[11:14]
    own = [[load(10 * field + node, 0) for node in range(10)] for field in range(3)]
    eta, mom_x, mom_y = own
    flow_r = [-(rx * mom_x[b] + ry * mom_y[b]) for b in range(10)]
    flow_s = [-(sx * mom_x[b] + sy * mom_y[b]) for b in range(10)]
    half_r = (0.5 * rx, 0.5 * ry)
    half_s = (0.5 * sx, 0.5 * sy)
    vectors = (
        (-half_s[0], -half_s[1]),
        (half_r[0] + half_s[0], half_r[1] + half_s[1]),
        (-half_r[0], -half_r[1]),
    )
    fetch = outer_values(load, index, inside)
    jumps = ([], [], [])
    for face in range(3):
        vec_x, vec_y = vectors[face]
        theirs = FACES[(1, 0, 2)[face]]
        wall = walls[face]
        for j in range(4):
            node, match = FACES[face][j], theirs[3 - j]
            in_eta, in_x, in_y = eta[node], mom_x[node], mom_y[node]
            ext_eta, ext_x, ext_y = [fetch[face](10 * field + match) for field in range(3)]
            bounce = (in_x * vec_x + in_y * vec_y) * ghosts[face]
            d_eta = jnp.where(wall, 0.0, in_eta - ext_eta)
            d_x = jnp.where(wall, bounce * vec_x, in_x - ext_x)
            d_y = jnp.where(wall, bounce * vec_y, in_y - ext_y)
            head = jnp.where(wall, 0.0, speed_sq * in_eta - outer_sq[face] * ext_eta)
            jumps[0].append(d_x * vec_x + d_y * vec_y - waves[face] * d_eta)
            jumps[1].append(head * vec_x - waves[face] * d_x)
            jumps[2].append(head * vec_y - waves[face] * d_y)
    pull = (-speed_sq * rx, -speed_sq * ry)
    push = (-speed_sq * sx, -speed_sq * sy)
    out = [[None] * 10 for _ in range(3)]
    for a in range(10):
        total = along_r = along_s = None
        for b in range(10):
            d_r, d_s = operators[a // 4, a % 4 * 32 + b], operators[a // 4, a % 4 * 32 + 10 + b]
            term = d_r * flow_r[b] + d_s * flow_s[b]
            total = term if b == 0 else total + term
            along_r = d_r * eta[b] if b == 0 else along_r + d_r * eta[b]
            along_s = d_s * eta[b] if b == 0 else along_s + d_s * eta[b]
        sums = [total, pull[0] * along_r + push[0] * along_s, pull[1] * along_r + push[1] * along_s]
        for q in range(12):
            weight = operators[a // 4, a % 4 * 32 + 20 + q]
            for field in range(3):
                sums[field] = sums[field] + weight * jumps[field][q]
        for field in range(3):
            out[field][a] = sums[field]
    return [out[field][a] for field in range(3) for a in range(10)]


def child_matrix(prolong_ref):
    f32, bf16 = jnp.float32, jnp.bfloat16

    def number(shape, axis):
        return lax.broadcasted_iota(jnp.int32, shape, axis)

    both = jnp.concatenate([prolong_ref[:, 0, :], prolong_ref[:, 1, :]], axis=0)
    rounded = both.astype(bf16)
    rest = (both - rounded.astype(f32)).astype(bf16)
    shape = (10, WIDE)
    columns = (number(shape, 1) % 10 == number(shape, 0)).astype(bf16)
    shape = (2 * PACK, 20)
    rows = (number(shape, 0) // 4 == number(shape, 1)).astype(bf16)
    shape = (2 * PACK, WIDE)
    same = number(shape, 0) % 4 == number(shape, 1) // 10
    parts = []
    for matrix in (rounded, rest):
        spread = jnp.dot(matrix, columns, preferred_element_type=f32).astype(bf16)
        full = jnp.dot(rows, spread, preferred_element_type=f32)
        parts.append(jnp.where(same, full, 0.0))
    shape = (PACK, WIDE)
    same = (number(shape, 0) % 4 == number(shape, 1) // 10) & (number(shape, 0) // 4 == number(shape, 1) % 10)
    first = jnp.concatenate([parts[0], same.astype(f32)], axis=0)
    last = jnp.concatenate([parts[1], jnp.zeros(shape, f32)], axis=0)
    return jnp.concatenate([first, first, last], axis=1).astype(bf16)


def sum_children(sizes, refine, ends_ref, full_ref, lines_ref):
    slots, f32 = sizes.slots, jnp.float32
    counts = (1.0 + refine).astype(jnp.bfloat16)
    row_i = lax.broadcasted_iota(jnp.int32, (LANES, LANES), 0)
    col_i = lax.broadcasted_iota(jnp.int32, (LANES, LANES), 1)
    upper = (row_i <= col_i).astype(jnp.bfloat16)
    within = jnp.dot(counts, upper, preferred_element_type=f32)
    whole = jnp.dot(counts, jnp.ones((LANES, LANES), jnp.bfloat16), preferred_element_type=f32)
    row_s = lax.broadcasted_iota(jnp.int32, (slots, slots), 0)
    col_s = lax.broadcasted_iota(jnp.int32, (slots, slots), 1)
    lower = (col_s < row_s).astype(jnp.bfloat16)
    before = jnp.dot(lower, whole.astype(jnp.bfloat16), preferred_element_type=f32)
    before = before - before[sizes.margin : sizes.margin + 1, :]
    ends = 2.0 * (within + before) + refine
    high = jnp.floor(ends * (1.0 / 256.0))
    ends_ref[...] = jnp.concatenate([high, ends - 256.0 * high], axis=1).astype(jnp.bfloat16)
    full_ref[...] = before + whole
    ones = jnp.ones((8, LANES), jnp.bfloat16)
    sums = lax.dot_general(ones, counts, (((1,), (1,)), ((), ())), preferred_element_type=f32)
    gap = lax.broadcasted_iota(jnp.int32, (slots, LANES), 1) - lax.broadcasted_iota(jnp.int32, (slots, LANES), 0)
    lines = [
        jnp.dot(sums.astype(jnp.bfloat16), (gap >= least).astype(jnp.bfloat16), preferred_element_type=f32)
        for least in (2, 1, 0)
    ]
    own = lines[1][:, sizes.margin : sizes.margin + 1]
    for num in range(3):
        lines_ref[num] = lines[num] - own


def prep_kernel(
    sizes, state_hbm, depth_hbm, metric_hbm, partner_hbm, refine_hbm, diff_hbm, lift_hbm, prolong_hbm,
    cur, aux, weights, operators,
    state_ref, depth_ref, metric_ref, partner_ref, refine_ref, prolong_ref, diff_ref, lift_ref, spread, wide, sems,
):
    blocks = sizes.blocks
    copies = fetch_all(
        (
            (metric_hbm, metric_ref),
            (state_hbm, state_ref),
            (depth_hbm, depth_ref),
            (partner_hbm, partner_ref),
            (refine_hbm, refine_ref),
            (prolong_hbm, prolong_ref),
            (diff_hbm, diff_ref),
            (lift_hbm, lift_ref),
        ),
        sems,
    )
    for copy in copies:
        copy.wait()
    weights[...] = child_matrix(prolong_ref)
    rows = jnp.concatenate([diff_ref[:, 0, :], diff_ref[:, 1, :], lift_ref[...]], axis=1)
    rows = jnp.concatenate([rows, jnp.zeros((2, 32), jnp.float32)], axis=0)
    for row in range(3):
        for part in range(4):
            at = 4 * row + part
            operators[row : row + 1, 32 * part : 32 * part + 32] = rows[at : at + 1]
    metric = split_metric(metric_ref, spread, blocks)
    dense = [depth_ref[...], *metric, partner_ref[...].astype(jnp.float32), refine_ref[...].astype(jnp.float32)]
    for num in range(7):
        aux[num] = dense[num]
    pack_state(state_ref, wide, blocks, LAID, 4)
    for field in range(3):
        for node in range(10):
            cur[10 * field + node] = wide[pl.ds(4 * node + field, blocks, stride=LAID), :]


def first_kernel(
    sizes, cur_own, aux_own, weights_in, operators_in, odd_ref, even_ref,
    cur, rate_ref, twice_ref, weights, ends_ref, full_ref, lines_ref,
    geo_ref, aux, operators, sems,
):
    blocks, halo = sizes.blocks, sizes.halo
    top, bottom = PAD + halo, PAD + halo + blocks
    place = lax.axis_index(AXES)
    count = lax.axis_size(AXES)
    copies = fetch_all(((operators_in, operators),), sems)
    even = place % 2 == 0

    def set_halo(target, num, row):
        by_even = even_ref[pl.ds(row, halo, stride=SENT), :]
        by_odd = odd_ref[pl.ds(row, halo, stride=SENT), :]
        target[num, top - halo : top, :] = jnp.where(even, by_odd, by_even)
        target[num, bottom : bottom + halo, :] = jnp.where(even, by_even, by_odd)

    for num in range(7):
        set_halo(aux, num, 30 + num)
        aux[num, top:bottom, :] = aux_own[num]
    for field in range(3):
        for node in range(10):
            item = 10 * field + node
            set_halo(cur, item, 3 * node + field)
            cur[item, top:bottom, :] = cur_own[item]

    weights[...] = weights_in[...]
    begin = PAD + sizes.keep
    sum_children(sizes, aux[6, begin : begin + sizes.slots, :], ends_ref, full_ref, lines_ref)
    for copy in copies:
        copy.wait()

    def step(start, height):
        base = PAD + start

        def load_aux(item, shift):
            return aux[item, pl.ds(base + shift, height), :]

        def load(item, shift):
            return cur[item, pl.ds(base + shift, height), :]

        depth, rx, ry, sx, sy, partner = [load_aux(num, 0) for num in range(6)]
        index, inside = pair_index(partner)
        fetch = outer_values(load_aux, index, inside)
        walls = wall_masks(sizes, start, place, count, partner)
        speed_sq = GRAVITY * depth
        outer_sq = [jnp.where(walls[k], speed_sq, GRAVITY * fetch[k](0)) for k in range(3)]
        faces = ((sx, sy), (rx + sx, ry + sy), (rx, ry))
        squares = [vx * vx + vy * vy for vx, vy in faces]
        waves = [
            0.5 * jnp.sqrt(squares[k]) * jnp.sqrt(jnp.maximum(speed_sq, outer_sq[k])) for k in range(3)
        ]
        ghosts = [8.0 / squares[k] for k in range(3)]
        geo = [speed_sq, rx, ry, sx, sy, *outer_sq, *waves, *ghosts]
        rates = tendency(load, geo, walls, index, inside, operators)
        for num, value in enumerate([*geo, partner]):
            geo_ref[num, pl.ds(start, height), :] = value
        for item in range(30):
            rate_ref[item, pl.ds(base, height), :] = rates[item]

    def again(start, height):
        row = start + sizes.keep
        at = pl.ds(row, height)

        def load(item, shift):
            return rate_ref[item, pl.ds(PAD + row + shift, height), :]

        geo = [geo_ref[num, at, :] for num in range(14)]
        partner = geo_ref[14, at, :]
        index, inside = pair_index(partner)
        walls = wall_masks(sizes, row, place, count, partner)
        rates = tendency(load, geo, walls, index, inside, operators)
        for item in range(30):
            twice_ref[item, pl.ds(start, height), :] = rates[item]

    def sweep(work, rows):
        for start in range(0, rows // TALL * TALL, TALL):
            work(start, TALL)

    for start in range(sizes.rows // TALL * TALL, sizes.rows, 8):
        step(start, 8)
    sweep(step, sizes.rows)
    for start in range(sizes.slots // TALL * TALL, sizes.slots, 8):
        again(start, 8)
    sweep(again, sizes.slots)


def refine_kernel(
    sizes, cur, rate_ref, twice_ref, weights, base_ref, full_ref, lines_ref, stats_ref, out_hbm,
    out_ref, place_v, place_s, wide, index_ref, out_sems, sem,
):
    slots, keep = sizes.slots, sizes.keep
    place = lax.axis_index(AXES)
    stats = stats_ref[...]
    half = LANES // 2
    row_n = lax.broadcasted_iota(jnp.int32, stats.shape, 0)
    top = jnp.max(stats, axis=0, keepdims=True)
    earlier = jnp.sum(jnp.where(row_n < place, stats, 0.0), axis=0, keepdims=True)
    left = lax.broadcasted_iota(jnp.int32, (1, LANES), 1) < half
    top = jnp.where(left, top, pltpu.roll(top, half, 1))
    earlier = jnp.where(left, pltpu.roll(earlier, half, 1), earlier)
    step = COURANT / top
    half_square = 0.5 * step * step
    start = earlier - (place * (sizes.cells // 2)).astype(jnp.float32)
    first_slot = LANES * lax.broadcasted_iota(jnp.int32, (slots, LANES), 1).astype(jnp.float32)
    lead = jnp.sum((full_ref[...] + start <= first_slot).astype(jnp.float32), axis=0, keepdims=True)
    lead = jnp.clip(lead.astype(jnp.int32), 0, slots - 1)
    place_v[...] = lead
    copy = pltpu.make_async_copy(place_v, place_s, sem)
    copy.start()
    for item in range(30):
        now = slice(PAD + keep, PAD + keep + slots)
        value = cur[item, now, :] + step * rate_ref[item, now, :] + half_square * twice_ref[item]
        wide[pl.ds(item, slots, stride=STEP), :] = value
    for item in (30, 31):
        wide[pl.ds(item, slots + 1, stride=STEP), :] = jnp.zeros((slots + 1, LANES), jnp.float32)
    slot_start = LANES * lax.broadcasted_iota(jnp.int32, (slots, LANES), 0).astype(jnp.float32)
    begun = [lines_ref[num, 0:1, :] + start <= slot_start for num in range(3)]
    halves = [
        jnp.dot(
            (begun[num] & ~begun[num + 1]).astype(jnp.bfloat16)[:, :slots],
            base_ref[...],
            preferred_element_type=jnp.float32,
        )
        for num in (1, 0)
    ]
    near, far = [256.0 * x[:, :LANES] + (x[:, LANES:] + 2.0 * start) for x in halves]
    lane = lax.broadcasted_iota(jnp.int32, (slots, LANES), 1)
    slot_no = LANES * lax.broadcasted_iota(jnp.int32, (slots, LANES), 0) + lane
    goal = (2 * slot_no + 1).astype(jnp.float32)
    beyond = jnp.broadcast_to(near[:, LANES - 1 :], (slots, LANES)) <= goal

    def pick(index):
        return jnp.where(beyond, lane_gather(far, index), lane_gather(near, index))

    found = jnp.zeros((slots, LANES), jnp.int32)
    for size in (LANES // 4, LANES // 16, LANES // 64):
        passed = [(pick(found + (probe * size - 1)) <= goal).astype(jnp.int32) for probe in (1, 2, 3)]
        found = found + size * (passed[0] + passed[1] + passed[2])
    found = found + (pick(found) <= goal).astype(jnp.int32)
    mine = pick(found).astype(jnp.int32)
    split = mine & 1
    begin = (mine >> 1) - 1 - split
    kind = split * (1 + slot_no - begin)
    index_ref[0] = found.astype(jnp.float32)
    index_ref[1] = kind.astype(jnp.float32)
    index_ref[2] = (lane < jnp.broadcast_to(found[:, 0:1], (slots, LANES))).astype(jnp.float32)
    copy.wait()
    matrix = weights[...]
    results = []
    parts = [(at, 8) for at in range(0, slots - 8, 8)] + [(slots - 8, 4), (slots - 4, 4)]
    for part, (begin_at, height) in enumerate(parts):
        span = slice(LANES * begin_at, LANES * (begin_at + height))
        columns = []
        for slot in range(begin_at, begin_at + height):
            lead_at = place_s[0, slot] * STEP
            lane_idx = jnp.broadcast_to(index_ref[0, slot : slot + 1, :], (8, LANES)).astype(jnp.int32)
            ahead = jnp.broadcast_to(index_ref[2, slot : slot + 1, :], (8, LANES)) > 0.5
            tiles = []
            for row in range(0, WIDE, 8):
                one = wide[pl.ds(lead_at + row, 8), :]
                two = wide[pl.ds(lead_at + STEP + row, 8), :]
                tiles.append(lane_gather(jnp.where(ahead, two, one), lane_idx))
            columns.append(jnp.concatenate(tiles, axis=0))
        values = jnp.concatenate(columns, axis=1)
        high = values.astype(jnp.bfloat16)
        low = (values - high.astype(jnp.float32)).astype(jnp.bfloat16)
        stack = jnp.concatenate([high, low, high], axis=0)
        children = jnp.dot(matrix, stack, preferred_element_type=jnp.float32)
        for sub in range(height):
            slot = begin_at + sub
            cut = slice(LANES * sub, LANES * (sub + 1))
            tag = jnp.broadcast_to(index_ref[1, slot : slot + 1, :], (PACK, LANES))
            value = jnp.where(
                tag < 0.5,
                children[2 * PACK :, cut],
                jnp.where(tag < 1.5, children[:PACK, cut], children[PACK : 2 * PACK, cut]),
            )
            for node in range(10):
                out_ref[node, :, LANES * slot : LANES * (slot + 1)] = value[4 * node : 4 * node + 3]
        result = pltpu.make_async_copy(out_ref.at[:, :, span], out_hbm.at[:, :, span], out_sems.at[part])
        result.start()
        results.append(result)
    for result in results:
        result.wait()


def swaps(start, count):
    pairs = [(i, i + 1) for i in range(start, count - 1, 2)]
    return pairs + [(j, i) for i, j in pairs]


def shards(state, depth, metric, partner, refine, diff_ops, lift, prolong):
    sizes = Sizes(state.shape[2])
    count = lax.axis_size(AXES)
    blocks, rows, slots, halo = sizes.blocks, sizes.rows, sizes.slots, sizes.halo
    depth, partner, refine = [x.reshape(blocks, LANES) for x in (depth, partner, refine)]
    state, diff_ops, prolong = [jnp.transpose(x, (1, 0, 2)) for x in (state, diff_ops, prolong)]
    state, depth, metric, partner, refine, diff_ops, lift, prolong = [
        pltpu.with_memory_space_constraint(x, pltpu.HBM)
        for x in (state, depth, metric, partner, refine, diff_ops, lift, prolong)
    ]
    f32, i32 = jnp.float32, jnp.int32
    packed = jax.ShapeDtypeStruct((SENT * halo, LANES), f32)
    dense = [
        pltpu.VMEM((blocks, LANES), f32),
        pltpu.VMEM(metric.shape, f32),
        pltpu.VMEM((blocks, LANES), i32),
        pltpu.VMEM((blocks, LANES), i32),
    ]
    stats, even, odd = pl.pallas_call(
        functools.partial(pack_kernel, sizes),
        name="pack",
        out_shape=(jax.ShapeDtypeStruct((count, LANES), f32), packed, packed),
        in_specs=[HBM] * 5,
        out_specs=(HBM, VMEM, VMEM),
        scratch_shapes=[
            pltpu.VMEM((count, LANES), f32),
            pltpu.VMEM((10, 3, LANES * halo), f32),
            pltpu.VMEM((10, 3, LANES * halo), f32),
            *dense,
            pltpu.VMEM((8 * blocks, LANES), f32),
            pltpu.SemaphoreType.DMA((6,)),
            pltpu.SemaphoreType.DMA,
        ],
        compiler_params=PARAMS,
    )(state, depth, metric, partner, refine)
    odd = lax.ppermute(odd, AXES, swaps(1, count))
    even = lax.ppermute(even, AXES, swaps(0, count))
    stats = lax.all_to_all(stats, AXES, 0, 0, tiled=True)
    even, odd, stats = [pltpu.with_memory_space_constraint(x, pltpu.VMEM) for x in (even, odd, stats)]
    cur, aux, weights, operators = pl.pallas_call(
        functools.partial(prep_kernel, sizes),
        name="lay_out",
        cost_estimate=pl.CostEstimate(flops=1 << 24, transcendentals=1 << 16, bytes_accessed=1 << 24),
        out_shape=(
            jax.ShapeDtypeStruct((30, blocks, LANES), f32),
            jax.ShapeDtypeStruct((7, blocks, LANES), f32),
            jax.ShapeDtypeStruct((3 * PACK, 3 * WIDE), jnp.bfloat16),
            jax.ShapeDtypeStruct((3, LANES), f32),
        ),
        in_specs=[HBM] * 8,
        out_specs=(VMEM,) * 4,
        scratch_shapes=[
            pltpu.VMEM(state.shape, f32),
            *dense,
            pltpu.VMEM(prolong.shape, f32),
            pltpu.VMEM(diff_ops.shape, f32),
            pltpu.VMEM(lift.shape, f32),
            pltpu.VMEM((8 * blocks, LANES), f32),
            pltpu.VMEM((LAID * blocks, LANES), f32),
            pltpu.SemaphoreType.DMA((8,)),
        ],
        compiler_params=PARAMS,
    )(state, depth, metric, partner, refine, diff_ops, lift, prolong)
    cur, rates, twice, weights, ends, full, lines = pl.pallas_call(
        functools.partial(first_kernel, sizes),
        name="rates_twice",
        cost_estimate=pl.CostEstimate(flops=1024, transcendentals=0, bytes_accessed=1024),
        out_shape=(
            jax.ShapeDtypeStruct((30, sizes.tall, LANES), f32),
            jax.ShapeDtypeStruct((30, sizes.tall, LANES), f32),
            jax.ShapeDtypeStruct((30, slots, LANES), f32),
            jax.ShapeDtypeStruct((3 * PACK, 3 * WIDE), jnp.bfloat16),
            jax.ShapeDtypeStruct((slots, 2 * LANES), jnp.bfloat16),
            jax.ShapeDtypeStruct((slots, LANES), f32),
            jax.ShapeDtypeStruct((3, 8, LANES), f32),
        ),
        in_specs=[VMEM] * 6,
        out_specs=(VMEM,) * 7,
        scratch_shapes=[
            pltpu.VMEM((15, rows, LANES), f32),
            pltpu.VMEM((7, sizes.tall, LANES), f32),
            pltpu.SMEM((3, LANES), f32),
            pltpu.SemaphoreType.DMA((1,)),
        ],
        compiler_params=PARAMS,
    )(cur, aux, weights, operators, odd, even)
    refined = pl.pallas_call(
        functools.partial(refine_kernel, sizes),
        name="sum_and_refine",
        out_shape=jax.ShapeDtypeStruct((10, 3, LANES * slots), f32),
        in_specs=[VMEM] * 8,
        out_specs=HBM,
        scratch_shapes=[
            pltpu.VMEM((10, 3, LANES * slots), f32),
            pltpu.VMEM((1, LANES), i32),
            pltpu.SMEM((1, LANES), i32),
            pltpu.VMEM((STEP * (slots + 1), LANES), f32),
            pltpu.VMEM((3, slots, LANES), f32),
            pltpu.SemaphoreType.DMA((slots // 8 + 1,)),
            pltpu.SemaphoreType.DMA,
        ],
        compiler_params=PARAMS,
    )(cur, rates, twice, weights, ends, full, lines, stats)
    return jnp.transpose(refined, (1, 0, 2))


def solution(mesh):
    return jax.shard_map(
        shards,
        mesh=mesh,
        in_specs=(
            P(None, None, AXES),
            P(AXES),
            P(None, AXES),
            P(AXES),
            P(AXES),
            P(),
            P(),
            P(),
        ),
        out_specs=P(None, None, AXES),
        check_vma=False,
    )
```

```python
import functools

import jax
import jax.numpy as jnp
from jax import lax
from jax.experimental import pallas as pl
from jax.experimental.pallas import tpu as pltpu
from jax.sharding import PartitionSpec as P

GRAVITY = 9.81
COURANT = 0.5
HIGH = lax.Precision.HIGHEST
LANES = 128
AXES = ("row", "col")
FACES = ((0, 1, 2, 3), (3, 6, 8, 9), (9, 7, 4, 0))
PACK = 40
LAID = 41
SENT = 37
WIDE = 32
STEP = 33
TALL = 16
PAD = 8

VMEM = pl.BlockSpec(memory_space=pltpu.VMEM)
HBM = pl.BlockSpec(memory_space=pltpu.HBM)
PARAMS = pltpu.CompilerParams(vmem_limit_bytes=48 * 1024 * 1024)


class Sizes:
    def __init__(self, cells):
        self.cells = cells
        self.blocks = cells // LANES
        self.margin = cells // 4 // LANES
        self.halo = self.margin + 1
        self.rows = -(-(self.blocks + 2 * self.halo) // 8) * 8
        self.tall = self.rows + 2 * PAD
        self.slots = 3 * self.blocks // 2
        self.keep = self.halo - self.margin


def fetch_all(pairs, sems):
    copies = [pltpu.make_async_copy(src, dst, sems.at[num]) for num, (src, dst) in enumerate(pairs)]
    for copy in copies:
        copy.start()
    return copies


def split_metric(metric_ref, spread, blocks):
    for block in range(blocks):
        spread[8 * block : 8 * block + 4, :] = metric_ref[:, LANES * block : LANES * (block + 1)]
    return [spread[pl.ds(comp, blocks, stride=8), :] for comp in range(4)]


def pack_kernel(
    sizes, state_hbm, depth_hbm, metric_hbm, partner_hbm, refine_hbm, stats_hbm, even_ref, odd_ref,
    stats_ref, state_even, state_odd, depth_ref, metric_ref, partner_ref, refine_ref, spread, sems, sem,
):
    blocks, halo = sizes.blocks, sizes.halo
    wide = LANES * halo
    late = blocks - halo
    even = (lax.axis_index(AXES) + 1) % 2 * late
    odd = late - even
    copies = fetch_all(
        (
            (depth_hbm, depth_ref),
            (metric_hbm, metric_ref),
            (refine_hbm, refine_ref),
            (partner_hbm, partner_ref),
            (state_hbm.at[:, :, pl.ds(pl.multiple_of(LANES * even, LANES), wide)], state_even),
            (state_hbm.at[:, :, pl.ds(pl.multiple_of(LANES * odd, LANES), wide)], state_odd),
        ),
        sems,
    )
    for copy in copies[:3]:
        copy.wait()
    rx, ry, sx, sy = split_metric(metric_ref, spread, blocks)
    depth = depth_ref[...]
    refine = refine_ref[...].astype(jnp.float32)
    faces = ((sx, sy), (rx + sx, ry + sy), (rx, ry))
    lengths = [jnp.sqrt(vx * vx + vy * vy) for vx, vy in faces]
    rate = jnp.sqrt(GRAVITY * depth) * jnp.maximum(jnp.maximum(lengths[0], lengths[1]), lengths[2])
    top = jnp.max(jnp.max(rate, axis=0, keepdims=True), axis=1, keepdims=True)
    extra = jnp.sum(jnp.sum(refine, axis=0, keepdims=True), axis=1, keepdims=True)
    shape = stats_ref.shape
    lane = lax.broadcasted_iota(jnp.int32, shape, 1)
    stats_ref[...] = jnp.where(
        lane < LANES // 2, jnp.broadcast_to(top, shape), jnp.broadcast_to(extra, shape)
    )
    sent = pltpu.make_async_copy(stats_ref, stats_hbm, sem)
    sent.start()
    for copy in copies[3:]:
        copy.wait()
    for ref, source, start in ((even_ref, state_even, even), (odd_ref, state_odd, odd)):
        pack_state(source, ref, halo, SENT, 3)
        at = pl.ds(start, halo)
        dense = [depth_ref[at, :]]
        dense += [spread[pl.ds(8 * start + comp, halo, stride=8), :] for comp in range(4)]
        dense += [partner_ref[at, :].astype(jnp.float32), refine_ref[at, :].astype(jnp.float32)]
        for num, value in enumerate(dense):
            ref[pl.ds(30 + num, halo, stride=SENT), :] = value
    sent.wait()


def pack_state(source, target, blocks, height, width):
    for block in range(blocks):
        for node in range(10):
            at = height * block + width * node
            target[at : at + 3, :] = source[node, :, LANES * block : LANES * (block + 1)]


def pair_index(partner):
    lane = lax.broadcasted_iota(jnp.int32, partner.shape, 1)
    target = lane + partner.astype(jnp.int32)
    return target & (LANES - 1), (target >= 0) & (target < LANES)


def lane_gather(values, index):
    return jnp.take_along_axis(values, index, axis=1, mode="promise_in_bounds")


def outer_values(load, index, inside):
    shape = index.shape
    lane = lax.broadcasted_iota(jnp.int32, shape, 1)

    def prev(item):
        return pltpu.roll(jnp.where(lane == LANES - 1, load(item, -1), load(item, 0)), 1, 1)

    def after(item):
        return pltpu.roll(jnp.where(lane == 0, load(item, 1), load(item, 0)), LANES - 1, 1)

    def across(item):
        other = jnp.where(lane < LANES // 2, load(item, 1), load(item, -1))
        return jnp.where(inside, lane_gather(load(item, 0), index), lane_gather(other, index))

    return prev, after, across


def wall_masks(sizes, start, place, count, partner):
    shape = partner.shape
    lane = lax.broadcasted_iota(jnp.int32, shape, 1)
    row = lax.broadcasted_iota(jnp.int32, shape, 0) + start
    first = (lane == 0) & (row == sizes.halo) & (place == 0)
    last = (lane == LANES - 1) & (row == sizes.halo + sizes.blocks - 1) & (place == count - 1)
    return first, last, partner == 0


def tendency(load, geo, walls, index, inside, operators):
    speed_sq, rx, ry, sx, sy = geo[:5]
    outer_sq, waves, ghosts = geo[5:8], geo[8:11], geo[11:14]
    own = [[load(10 * field + node, 0) for node in range(10)] for field in range(3)]
    eta, mom_x, mom_y = own
    flow_r = [-(rx * mom_x[b] + ry * mom_y[b]) for b in range(10)]
    flow_s = [-(sx * mom_x[b] + sy * mom_y[b]) for b in range(10)]
    half_r = (0.5 * rx, 0.5 * ry)
    half_s = (0.5 * sx, 0.5 * sy)
    vectors = (
        (-half_s[0], -half_s[1]),
        (half_r[0] + half_s[0], half_r[1] + half_s[1]),
        (-half_r[0], -half_r[1]),
    )
    fetch = outer_values(load, index, inside)
    jumps = ([], [], [])
    for face in range(3):
        vec_x, vec_y = vectors[face]
        theirs = FACES[(1, 0, 2)[face]]
        wall = walls[face]
        for j in range(4):
            node, match = FACES[face][j], theirs[3 - j]
            in_eta, in_x, in_y = eta[node], mom_x[node], mom_y[node]
            ext_eta, ext_x, ext_y = [fetch[face](10 * field + match) for field in range(3)]
            bounce = (in_x * vec_x + in_y * vec_y) * ghosts[face]
            d_eta = jnp.where(wall, 0.0, in_eta - ext_eta)
            d_x = jnp.where(wall, bounce * vec_x, in_x - ext_x)
            d_y = jnp.where(wall, bounce * vec_y, in_y - ext_y)
            head = jnp.where(wall, 0.0, speed_sq * in_eta - outer_sq[face] * ext_eta)
            jumps[0].append(d_x * vec_x + d_y * vec_y - waves[face] * d_eta)
            jumps[1].append(head * vec_x - waves[face] * d_x)
            jumps[2].append(head * vec_y - waves[face] * d_y)
    pull = (-speed_sq * rx, -speed_sq * ry)
    push = (-speed_sq * sx, -speed_sq * sy)
    out = [[None] * 10 for _ in range(3)]
    for a in range(10):
        total = along_r = along_s = None
        for b in range(10):
            d_r, d_s = operators[a // 4, a % 4 * 32 + b], operators[a // 4, a % 4 * 32 + 10 + b]
            term = d_r * flow_r[b] + d_s * flow_s[b]
            total = term if b == 0 else total + term
            along_r = d_r * eta[b] if b == 0 else along_r + d_r * eta[b]
            along_s = d_s * eta[b] if b == 0 else along_s + d_s * eta[b]
        sums = [total, pull[0] * along_r + push[0] * along_s, pull[1] * along_r + push[1] * along_s]
        for q in range(12):
            weight = operators[a // 4, a % 4 * 32 + 20 + q]
            for field in range(3):
                sums[field] = sums[field] + weight * jumps[field][q]
        for field in range(3):
            out[field][a] = sums[field]
    return [out[field][a] for field in range(3) for a in range(10)]


def child_matrix(prolong_ref):
    f32, bf16 = jnp.float32, jnp.bfloat16

    def number(shape, axis):
        return lax.broadcasted_iota(jnp.int32, shape, axis)

    both = jnp.concatenate([prolong_ref[:, 0, :], prolong_ref[:, 1, :]], axis=0)
    rounded = both.astype(bf16)
    rest = (both - rounded.astype(f32)).astype(bf16)
    shape = (10, WIDE)
    columns = (number(shape, 1) % 10 == number(shape, 0)).astype(bf16)
    shape = (2 * PACK, 20)
    rows = (number(shape, 0) // 4 == number(shape, 1)).astype(bf16)
    shape = (2 * PACK, WIDE)
    same = number(shape, 0) % 4 == number(shape, 1) // 10
    parts = []
    for matrix in (rounded, rest):
        spread = jnp.dot(matrix, columns, preferred_element_type=f32).astype(bf16)
        full = jnp.dot(rows, spread, preferred_element_type=f32)
        parts.append(jnp.where(same, full, 0.0))
    shape = (PACK, WIDE)
    same = (number(shape, 0) % 4 == number(shape, 1) // 10) & (number(shape, 0) // 4 == number(shape, 1) % 10)
    first = jnp.concatenate([parts[0], same.astype(f32)], axis=0)
    last = jnp.concatenate([parts[1], jnp.zeros(shape, f32)], axis=0)
    return jnp.concatenate([first, first, last], axis=1).astype(bf16)


def sum_children(sizes, refine, ends_ref, full_ref, lines_ref):
    slots, f32 = sizes.slots, jnp.float32
    counts = (1.0 + refine).astype(jnp.bfloat16)
    row_i = lax.broadcasted_iota(jnp.int32, (LANES, LANES), 0)
    col_i = lax.broadcasted_iota(jnp.int32, (LANES, LANES), 1)
    upper = (row_i <= col_i).astype(jnp.bfloat16)
    within = jnp.dot(counts, upper, preferred_element_type=f32)
    whole = jnp.dot(counts, jnp.ones((LANES, LANES), jnp.bfloat16), preferred_element_type=f32)
    row_s = lax.broadcasted_iota(jnp.int32, (slots, slots), 0)
    col_s = lax.broadcasted_iota(jnp.int32, (slots, slots), 1)
    lower = (col_s < row_s).astype(jnp.bfloat16)
    before = jnp.dot(lower, whole.astype(jnp.bfloat16), preferred_element_type=f32)
    before = before - before[sizes.margin : sizes.margin + 1, :]
    ends = 2.0 * (within + before) + refine
    high = jnp.floor(ends * (1.0 / 256.0))
    ends_ref[...] = jnp.concatenate([high, ends - 256.0 * high], axis=1).astype(jnp.bfloat16)
    full_ref[...] = before + whole
    ones = jnp.ones((8, LANES), jnp.bfloat16)
    sums = lax.dot_general(ones, counts, (((1,), (1,)), ((), ())), preferred_element_type=f32)
    gap = lax.broadcasted_iota(jnp.int32, (slots, LANES), 1) - lax.broadcasted_iota(jnp.int32, (slots, LANES), 0)
    lines = [
        jnp.dot(sums.astype(jnp.bfloat16), (gap >= least).astype(jnp.bfloat16), preferred_element_type=f32)
        for least in (2, 1, 0)
    ]
    own = lines[1][:, sizes.margin : sizes.margin + 1]
    for num in range(3):
        lines_ref[num] = lines[num] - own


def prep_kernel(
    sizes, state_hbm, depth_hbm, metric_hbm, partner_hbm, refine_hbm, diff_hbm, lift_hbm, prolong_hbm,
    cur, aux, weights, operators,
    state_ref, depth_ref, metric_ref, partner_ref, refine_ref, prolong_ref, diff_ref, lift_ref, spread, wide, sems,
):
    blocks = sizes.blocks
    copies = fetch_all(
        (
            (metric_hbm, metric_ref),
            (state_hbm, state_ref),
            (depth_hbm, depth_ref),
            (partner_hbm, partner_ref),
            (refine_hbm, refine_ref),
            (prolong_hbm, prolong_ref),
            (diff_hbm, diff_ref),
            (lift_hbm, lift_ref),
        ),
        sems,
    )
    for copy in copies:
        copy.wait()
    weights[...] = child_matrix(prolong_ref)
    rows = jnp.concatenate([diff_ref[:, 0, :], diff_ref[:, 1, :], lift_ref[...]], axis=1)
    rows = jnp.concatenate([rows, jnp.zeros((2, 32), jnp.float32)], axis=0)
    for row in range(3):
        for part in range(4):
            at = 4 * row + part
            operators[row : row + 1, 32 * part : 32 * part + 32] = rows[at : at + 1]
    metric = split_metric(metric_ref, spread, blocks)
    dense = [depth_ref[...], *metric, partner_ref[...].astype(jnp.float32), refine_ref[...].astype(jnp.float32)]
    for num in range(7):
        aux[num] = dense[num]
    pack_state(state_ref, wide, blocks, LAID, 4)
    for field in range(3):
        for node in range(10):
            cur[10 * field + node] = wide[pl.ds(4 * node + field, blocks, stride=LAID), :]


def first_kernel(
    sizes, cur_own, aux_own, weights_in, operators_in, odd_ref, even_ref,
    cur, rate_ref, twice_ref, weights, ends_ref, full_ref, lines_ref,
    geo_ref, aux, operators, sems,
):
    blocks, halo = sizes.blocks, sizes.halo
    top, bottom = PAD + halo, PAD + halo + blocks
    place = lax.axis_index(AXES)
    count = lax.axis_size(AXES)
    copies = fetch_all(((operators_in, operators),), sems)
    even = place % 2 == 0
    zero = jnp.minimum(place, 0)

    def set_halo(target, num, row):
        by_even = even_ref[pl.ds(row, halo, stride=SENT), :]
        by_odd = odd_ref[pl.ds(row, halo, stride=SENT), :]
        target[num, top - halo : top, :] = jnp.where(even, by_odd, by_even)
        target[num, pl.ds(zero + bottom, halo), :] = jnp.where(even, by_even, by_odd)

    for num in range(7):
        set_halo(aux, num, 30 + num)
        aux[num, pl.ds(zero + top, blocks), :] = aux_own[num]
    for field in range(3):
        for node in range(10):
            item = 10 * field + node
            set_halo(cur, item, 3 * node + field)
            cur[item, pl.ds(zero + top, blocks), :] = cur_own[item]

    weights[...] = weights_in[...]
    begin = PAD + sizes.keep
    sum_children(sizes, aux[6, pl.ds(zero + begin, sizes.slots), :], ends_ref, full_ref, lines_ref)
    for copy in copies:
        copy.wait()

    def step(start, height):
        base = PAD + start

        def rows(shift):
            return pl.ds(zero + (base + shift) if shift else base, height)

        def load_aux(item, shift):
            return aux[item, rows(shift), :]

        def load(item, shift):
            return cur[item, rows(shift), :]

        depth, rx, ry, sx, sy, partner = [load_aux(num, 0) for num in range(6)]
        index, inside = pair_index(partner)
        fetch = outer_values(load_aux, index, inside)
        walls = wall_masks(sizes, start, place, count, partner)
        speed_sq = GRAVITY * depth
        outer_sq = [jnp.where(walls[k], speed_sq, GRAVITY * fetch[k](0)) for k in range(3)]
        faces = ((sx, sy), (rx + sx, ry + sy), (rx, ry))
        squares = [vx * vx + vy * vy for vx, vy in faces]
        waves = [
            0.5 * jnp.sqrt(squares[k]) * jnp.sqrt(jnp.maximum(speed_sq, outer_sq[k])) for k in range(3)
        ]
        ghosts = [8.0 / squares[k] for k in range(3)]
        geo = [speed_sq, rx, ry, sx, sy, *outer_sq, *waves, *ghosts]
        rates = tendency(load, geo, walls, index, inside, operators)
        for num, value in enumerate([*geo, partner]):
            geo_ref[num, pl.ds(start, height), :] = value
        for item in range(30):
            rate_ref[item, pl.ds(base, height), :] = rates[item]

    def again(start, height):
        row = start + sizes.keep
        at = pl.ds(zero + row, height)

        def load(item, shift):
            return rate_ref[item, pl.ds(zero + (PAD + row + shift), height), :]

        geo = [geo_ref[num, at, :] for num in range(14)]
        partner = geo_ref[14, at, :]
        index, inside = pair_index(partner)
        walls = wall_masks(sizes, row, place, count, partner)
        rates = tendency(load, geo, walls, index, inside, operators)
        for item in range(30):
            twice_ref[item, pl.ds(start, height), :] = rates[item]

    def sweep(work, rows):
        for start in range(0, rows // TALL * TALL, TALL):
            work(start, TALL)

    for start in range(sizes.rows // TALL * TALL, sizes.rows, 8):
        step(start, 8)
    sweep(step, sizes.rows)
    for start in range(sizes.slots // TALL * TALL, sizes.slots, 8):
        again(start, 8)
    sweep(again, sizes.slots)


def refine_kernel(
    sizes, cur, rate_ref, twice_ref, weights, base_ref, full_ref, lines_ref, stats_ref, out_hbm,
    out_ref, place_v, place_s, wide, index_ref, out_sems, sem,
):
    slots, keep = sizes.slots, sizes.keep
    place = lax.axis_index(AXES)
    zero = jnp.minimum(place, 0)
    stats = stats_ref[...]
    half = LANES // 2
    row_n = lax.broadcasted_iota(jnp.int32, stats.shape, 0)
    top = jnp.max(stats, axis=0, keepdims=True)
    earlier = jnp.sum(jnp.where(row_n < place, stats, 0.0), axis=0, keepdims=True)
    left = lax.broadcasted_iota(jnp.int32, (1, LANES), 1) < half
    top = jnp.where(left, top, pltpu.roll(top, half, 1))
    earlier = jnp.where(left, pltpu.roll(earlier, half, 1), earlier)
    step = COURANT / top
    half_square = 0.5 * step * step
    start = earlier - (place * (sizes.cells // 2)).astype(jnp.float32)
    first_slot = LANES * lax.broadcasted_iota(jnp.int32, (slots, LANES), 1).astype(jnp.float32)
    lead = jnp.sum((full_ref[...] + start <= first_slot).astype(jnp.float32), axis=0, keepdims=True)
    lead = jnp.clip(lead.astype(jnp.int32), 0, slots - 1)
    place_v[...] = lead
    copy = pltpu.make_async_copy(place_v, place_s, sem)
    copy.start()
    for item in range(30):
        now = pl.ds(zero + (PAD + keep), slots)
        value = cur[item, now, :] + step * rate_ref[item, now, :] + half_square * twice_ref[item]
        wide[pl.ds(item, slots, stride=STEP), :] = value
    for item in (30, 31):
        wide[pl.ds(item, slots + 1, stride=STEP), :] = jnp.zeros((slots + 1, LANES), jnp.float32)
    slot_start = LANES * lax.broadcasted_iota(jnp.int32, (slots, LANES), 0).astype(jnp.float32)
    begun = [lines_ref[num, 0:1, :] + start <= slot_start for num in range(3)]
    halves = [
        jnp.dot(
            (begun[num] & ~begun[num + 1]).astype(jnp.bfloat16)[:, :slots],
            base_ref[...],
            preferred_element_type=jnp.float32,
        )
        for num in (1, 0)
    ]
    near, far = [256.0 * x[:, :LANES] + (x[:, LANES:] + 2.0 * start) for x in halves]
    lane = lax.broadcasted_iota(jnp.int32, (slots, LANES), 1)
    slot_no = LANES * lax.broadcasted_iota(jnp.int32, (slots, LANES), 0) + lane
    goal = (2 * slot_no + 1).astype(jnp.float32)
    beyond = jnp.broadcast_to(near[:, LANES - 1 :], (slots, LANES)) <= goal

    def pick(index):
        return jnp.where(beyond, lane_gather(far, index), lane_gather(near, index))

    found = jnp.zeros((slots, LANES), jnp.int32)
    for size in (LANES // 4, LANES // 16, LANES // 64):
        passed = [(pick(found + (probe * size - 1)) <= goal).astype(jnp.int32) for probe in (1, 2, 3)]
        found = found + size * (passed[0] + passed[1] + passed[2])
    found = found + (pick(found) <= goal).astype(jnp.int32)
    mine = pick(found).astype(jnp.int32)
    split = mine & 1
    begin = (mine >> 1) - 1 - split
    kind = split * (1 + slot_no - begin)
    index_ref[0] = found.astype(jnp.float32)
    index_ref[1] = kind.astype(jnp.float32)
    index_ref[2] = (lane < jnp.broadcast_to(found[:, 0:1], (slots, LANES))).astype(jnp.float32)
    copy.wait()
    matrix = weights[...]
    results = []
    parts = [(at, 8) for at in range(0, slots - 8, 8)] + [(slots - 8, 4), (slots - 4, 4)]
    for part, (begin_at, height) in enumerate(parts):
        span = slice(LANES * begin_at, LANES * (begin_at + height))
        columns = []
        for slot in range(begin_at, begin_at + height):
            lead_at = place_s[0, slot] * STEP
            lane_idx = jnp.broadcast_to(index_ref[0, slot : slot + 1, :], (8, LANES)).astype(jnp.int32)
            ahead = jnp.broadcast_to(index_ref[2, slot : slot + 1, :], (8, LANES)) > 0.5
            tiles = []
            for row in range(0, WIDE, 8):
                one = wide[pl.ds(lead_at + row, 8), :]
                two = wide[pl.ds(lead_at + STEP + row, 8), :]
                tiles.append(lane_gather(jnp.where(ahead, two, one), lane_idx))
            columns.append(jnp.concatenate(tiles, axis=0))
        values = jnp.concatenate(columns, axis=1)
        high = values.astype(jnp.bfloat16)
        low = (values - high.astype(jnp.float32)).astype(jnp.bfloat16)
        stack = jnp.concatenate([high, low, high], axis=0)
        children = jnp.dot(matrix, stack, preferred_element_type=jnp.float32)
        for sub in range(height):
            slot = begin_at + sub
            cut = slice(LANES * sub, LANES * (sub + 1))
            tag = jnp.broadcast_to(index_ref[1, slot : slot + 1, :], (PACK, LANES))
            value = jnp.where(
                tag < 0.5,
                children[2 * PACK :, cut],
                jnp.where(tag < 1.5, children[:PACK, cut], children[PACK : 2 * PACK, cut]),
            )
            for node in range(10):
                out_ref[node, :, LANES * slot : LANES * (slot + 1)] = value[4 * node : 4 * node + 3]
        result = pltpu.make_async_copy(out_ref.at[:, :, span], out_hbm.at[:, :, span], out_sems.at[part])
        result.start()
        results.append(result)
    for result in results:
        result.wait()


def swaps(start, count):
    pairs = [(i, i + 1) for i in range(start, count - 1, 2)]
    return pairs + [(j, i) for i, j in pairs]


def shards(state, depth, metric, partner, refine, diff_ops, lift, prolong):
    sizes = Sizes(state.shape[2])
    count = lax.axis_size(AXES)
    blocks, rows, slots, halo = sizes.blocks, sizes.rows, sizes.slots, sizes.halo
    depth, partner, refine = [x.reshape(blocks, LANES) for x in (depth, partner, refine)]
    state, diff_ops, prolong = [jnp.transpose(x, (1, 0, 2)) for x in (state, diff_ops, prolong)]
    state, depth, metric, partner, refine, diff_ops, lift, prolong = [
        pltpu.with_memory_space_constraint(x, pltpu.HBM)
        for x in (state, depth, metric, partner, refine, diff_ops, lift, prolong)
    ]
    f32, i32 = jnp.float32, jnp.int32
    packed = jax.ShapeDtypeStruct((SENT * halo, LANES), f32)
    dense = [
        pltpu.VMEM((blocks, LANES), f32),
        pltpu.VMEM(metric.shape, f32),
        pltpu.VMEM((blocks, LANES), i32),
        pltpu.VMEM((blocks, LANES), i32),
    ]
    stats, even, odd = pl.pallas_call(
        functools.partial(pack_kernel, sizes),
        name="pack",
        out_shape=(jax.ShapeDtypeStruct((count, LANES), f32), packed, packed),
        in_specs=[HBM] * 5,
        out_specs=(HBM, VMEM, VMEM),
        scratch_shapes=[
            pltpu.VMEM((count, LANES), f32),
            pltpu.VMEM((10, 3, LANES * halo), f32),
            pltpu.VMEM((10, 3, LANES * halo), f32),
            *dense,
            pltpu.VMEM((8 * blocks, LANES), f32),
            pltpu.SemaphoreType.DMA((6,)),
            pltpu.SemaphoreType.DMA,
        ],
        compiler_params=PARAMS,
    )(state, depth, metric, partner, refine)
    odd = lax.ppermute(odd, AXES, swaps(1, count))
    even = lax.ppermute(even, AXES, swaps(0, count))
    stats = lax.all_to_all(stats, AXES, 0, 0, tiled=True)
    even, odd, stats = [pltpu.with_memory_space_constraint(x, pltpu.VMEM) for x in (even, odd, stats)]
    cur, aux, weights, operators = pl.pallas_call(
        functools.partial(prep_kernel, sizes),
        name="lay_out",
        cost_estimate=pl.CostEstimate(flops=1 << 24, transcendentals=1 << 16, bytes_accessed=1 << 24),
        out_shape=(
            jax.ShapeDtypeStruct((30, blocks, LANES), f32),
            jax.ShapeDtypeStruct((7, blocks, LANES), f32),
            jax.ShapeDtypeStruct((3 * PACK, 3 * WIDE), jnp.bfloat16),
            jax.ShapeDtypeStruct((3, LANES), f32),
        ),
        in_specs=[HBM] * 8,
        out_specs=(VMEM,) * 4,
        scratch_shapes=[
            pltpu.VMEM(state.shape, f32),
            *dense,
            pltpu.VMEM(prolong.shape, f32),
            pltpu.VMEM(diff_ops.shape, f32),
            pltpu.VMEM(lift.shape, f32),
            pltpu.VMEM((8 * blocks, LANES), f32),
            pltpu.VMEM((LAID * blocks, LANES), f32),
            pltpu.SemaphoreType.DMA((8,)),
        ],
        compiler_params=PARAMS,
    )(state, depth, metric, partner, refine, diff_ops, lift, prolong)
    cur, rates, twice, weights, ends, full, lines = pl.pallas_call(
        functools.partial(first_kernel, sizes),
        name="rates_twice",
        cost_estimate=pl.CostEstimate(flops=1024, transcendentals=0, bytes_accessed=1024),
        out_shape=(
            jax.ShapeDtypeStruct((30, sizes.tall, LANES), f32),
            jax.ShapeDtypeStruct((30, sizes.tall, LANES), f32),
            jax.ShapeDtypeStruct((30, slots, LANES), f32),
            jax.ShapeDtypeStruct((3 * PACK, 3 * WIDE), jnp.bfloat16),
            jax.ShapeDtypeStruct((slots, 2 * LANES), jnp.bfloat16),
            jax.ShapeDtypeStruct((slots, LANES), f32),
            jax.ShapeDtypeStruct((3, 8, LANES), f32),
        ),
        in_specs=[VMEM] * 6,
        out_specs=(VMEM,) * 7,
        scratch_shapes=[
            pltpu.VMEM((15, rows, LANES), f32),
            pltpu.VMEM((7, sizes.tall, LANES), f32),
            pltpu.SMEM((3, LANES), f32),
            pltpu.SemaphoreType.DMA((1,)),
        ],
        compiler_params=PARAMS,
    )(cur, aux, weights, operators, odd, even)
    refined = pl.pallas_call(
        functools.partial(refine_kernel, sizes),
        name="sum_and_refine",
        out_shape=jax.ShapeDtypeStruct((10, 3, LANES * slots), f32),
        in_specs=[VMEM] * 8,
        out_specs=HBM,
        scratch_shapes=[
            pltpu.VMEM((10, 3, LANES * slots), f32),
            pltpu.VMEM((1, LANES), i32),
            pltpu.SMEM((1, LANES), i32),
            pltpu.VMEM((STEP * (slots + 1), LANES), f32),
            pltpu.VMEM((3, slots, LANES), f32),
            pltpu.SemaphoreType.DMA((slots // 8 + 1,)),
            pltpu.SemaphoreType.DMA,
        ],
        compiler_params=PARAMS,
    )(cur, rates, twice, weights, ends, full, lines, stats)
    return jnp.transpose(refined, (1, 0, 2))


def solution(mesh):
    return jax.shard_map(
        shards,
        mesh=mesh,
        in_specs=(
            P(None, None, AXES),
            P(AXES),
            P(None, AXES),
            P(AXES),
            P(AXES),
            P(),
            P(),
            P(),
        ),
        out_specs=P(None, None, AXES),
        check_vma=False,
    )
```

```python
import functools

import jax
import jax.numpy as jnp
from jax import lax
from jax.experimental import pallas as pl
from jax.experimental.pallas import tpu as pltpu
from jax.sharding import PartitionSpec as P

GRAVITY = 9.81
COURANT = 0.5
HIGH = lax.Precision.HIGHEST
LANES = 128
AXES = ("row", "col")
FACES = ((0, 1, 2, 3), (3, 6, 8, 9), (9, 7, 4, 0))
PACK = 40
LAID = 41
SENT = 37
WIDE = 32
STEP = 33
TALL = 16
PAD = 8

VMEM = pl.BlockSpec(memory_space=pltpu.VMEM)
HBM = pl.BlockSpec(memory_space=pltpu.HBM)
PARAMS = pltpu.CompilerParams(vmem_limit_bytes=48 * 1024 * 1024)


class Sizes:
    def __init__(self, cells):
        self.cells = cells
        self.blocks = cells // LANES
        self.margin = cells // 4 // LANES
        self.halo = self.margin + 1
        self.rows = -(-(self.blocks + 2 * self.halo) // 8) * 8
        self.tall = self.rows + 2 * PAD
        self.slots = 3 * self.blocks // 2
        self.keep = self.halo - self.margin


def fetch_all(pairs, sems):
    copies = [pltpu.make_async_copy(src, dst, sems.at[num]) for num, (src, dst) in enumerate(pairs)]
    for copy in copies:
        copy.start()
    return copies


def split_metric(metric_ref, spread, blocks):
    for block in range(blocks):
        spread[8 * block : 8 * block + 4, :] = metric_ref[:, LANES * block : LANES * (block + 1)]
    return [spread[pl.ds(comp, blocks, stride=8), :] for comp in range(4)]


def pack_kernel(
    sizes, state_hbm, depth_hbm, metric_hbm, partner_hbm, refine_hbm, stats_hbm, even_ref, odd_ref,
    stats_ref, state_even, state_odd, depth_ref, metric_ref, partner_ref, refine_ref, spread, sems, sem,
):
    blocks, halo = sizes.blocks, sizes.halo
    wide = LANES * halo
    late = blocks - halo
    even = (lax.axis_index(AXES) + 1) % 2 * late
    odd = late - even
    copies = fetch_all(
        (
            (depth_hbm, depth_ref),
            (metric_hbm, metric_ref),
            (refine_hbm, refine_ref),
            (partner_hbm, partner_ref),
            (state_hbm.at[:, :, pl.ds(pl.multiple_of(LANES * even, LANES), wide)], state_even),
            (state_hbm.at[:, :, pl.ds(pl.multiple_of(LANES * odd, LANES), wide)], state_odd),
        ),
        sems,
    )
    for copy in copies[:3]:
        copy.wait()
    rx, ry, sx, sy = split_metric(metric_ref, spread, blocks)
    depth = depth_ref[...]
    refine = refine_ref[...].astype(jnp.float32)
    faces = ((sx, sy), (rx + sx, ry + sy), (rx, ry))
    squares = [vx * vx + vy * vy for vx, vy in faces]
    rate = (GRAVITY * depth) * jnp.maximum(jnp.maximum(squares[0], squares[1]), squares[2])
    top = jnp.sqrt(jnp.max(jnp.max(rate, axis=0, keepdims=True), axis=1, keepdims=True))
    extra = jnp.sum(jnp.sum(refine, axis=0, keepdims=True), axis=1, keepdims=True)
    shape = stats_ref.shape
    lane = lax.broadcasted_iota(jnp.int32, shape, 1)
    stats_ref[...] = jnp.where(
        lane < LANES // 2, jnp.broadcast_to(top, shape), jnp.broadcast_to(extra, shape)
    )
    sent = pltpu.make_async_copy(stats_ref, stats_hbm, sem)
    sent.start()
    for copy in copies[3:]:
        copy.wait()
    for ref, source, start in ((even_ref, state_even, even), (odd_ref, state_odd, odd)):
        pack_state(source, ref, halo, SENT, 3)
        at = pl.ds(start, halo)
        dense = [depth_ref[at, :]]
        dense += [spread[pl.ds(8 * start + comp, halo, stride=8), :] for comp in range(4)]
        dense += [partner_ref[at, :].astype(jnp.float32), refine_ref[at, :].astype(jnp.float32)]
        for num, value in enumerate(dense):
            ref[pl.ds(30 + num, halo, stride=SENT), :] = value
    sent.wait()


def pack_state(source, target, blocks, height, width):
    zero = jnp.minimum(lax.axis_index(AXES), 0)
    for block in range(blocks):
        for node in range(10):
            at = zero + (height * block + width * node)
            target[pl.ds(at, 3), :] = source[node, :, LANES * block : LANES * (block + 1)]


def pair_index(partner):
    lane = lax.broadcasted_iota(jnp.int32, partner.shape, 1)
    target = lane + partner.astype(jnp.int32)
    return target & (LANES - 1), (target >= 0) & (target < LANES)


def lane_gather(values, index):
    return jnp.take_along_axis(values, index, axis=1, mode="promise_in_bounds")


def outer_values(load, index, inside):
    shape = index.shape
    lane = lax.broadcasted_iota(jnp.int32, shape, 1)

    def prev(item):
        return pltpu.roll(jnp.where(lane == LANES - 1, load(item, -1), load(item, 0)), 1, 1)

    def after(item):
        return pltpu.roll(jnp.where(lane == 0, load(item, 1), load(item, 0)), LANES - 1, 1)

    def across(item):
        other = jnp.where(lane < LANES // 2, load(item, 1), load(item, -1))
        return jnp.where(inside, lane_gather(load(item, 0), index), lane_gather(other, index))

    return prev, after, across


def wall_masks(sizes, start, place, count, partner):
    shape = partner.shape
    lane = lax.broadcasted_iota(jnp.int32, shape, 1)
    row = lax.broadcasted_iota(jnp.int32, shape, 0) + start
    first = (lane == 0) & (row == sizes.halo) & (place == 0)
    last = (lane == LANES - 1) & (row == sizes.halo + sizes.blocks - 1) & (place == count - 1)
    return first, last, partner == 0


def tendency(load, geo, walls, index, inside, operators):
    speed_sq, rx, ry, sx, sy = geo[:5]
    outer_sq, waves, ghosts = geo[5:8], geo[8:11], geo[11:14]
    own = [[load(10 * field + node, 0) for node in range(10)] for field in range(3)]
    eta, mom_x, mom_y = own
    flow_r = [-(rx * mom_x[b] + ry * mom_y[b]) for b in range(10)]
    flow_s = [-(sx * mom_x[b] + sy * mom_y[b]) for b in range(10)]
    half_r = (0.5 * rx, 0.5 * ry)
    half_s = (0.5 * sx, 0.5 * sy)
    vectors = (
        (-half_s[0], -half_s[1]),
        (half_r[0] + half_s[0], half_r[1] + half_s[1]),
        (-half_r[0], -half_r[1]),
    )
    fetch = outer_values(load, index, inside)
    jumps = ([], [], [])
    for face in range(3):
        vec_x, vec_y = vectors[face]
        theirs = FACES[(1, 0, 2)[face]]
        wall = walls[face]
        for j in range(4):
            node, match = FACES[face][j], theirs[3 - j]
            in_eta, in_x, in_y = eta[node], mom_x[node], mom_y[node]
            ext_eta, ext_x, ext_y = [fetch[face](10 * field + match) for field in range(3)]
            bounce = (in_x * vec_x + in_y * vec_y) * ghosts[face]
            d_eta = jnp.where(wall, 0.0, in_eta - ext_eta)
            d_x = jnp.where(wall, bounce * vec_x, in_x - ext_x)
            d_y = jnp.where(wall, bounce * vec_y, in_y - ext_y)
            head = jnp.where(wall, 0.0, speed_sq * in_eta - outer_sq[face] * ext_eta)
            jumps[0].append(d_x * vec_x + d_y * vec_y - waves[face] * d_eta)
            jumps[1].append(head * vec_x - waves[face] * d_x)
            jumps[2].append(head * vec_y - waves[face] * d_y)
    pull = (-speed_sq * rx, -speed_sq * ry)
    push = (-speed_sq * sx, -speed_sq * sy)
    out = [[None] * 10 for _ in range(3)]
    for a in range(10):
        total = along_r = along_s = None
        for b in range(10):
            d_r, d_s = operators[a // 4, a % 4 * 32 + b], operators[a // 4, a % 4 * 32 + 10 + b]
            term = d_r * flow_r[b] + d_s * flow_s[b]
            total = term if b == 0 else total + term
            along_r = d_r * eta[b] if b == 0 else along_r + d_r * eta[b]
            along_s = d_s * eta[b] if b == 0 else along_s + d_s * eta[b]
        sums = [total, pull[0] * along_r + push[0] * along_s, pull[1] * along_r + push[1] * along_s]
        for q in range(12):
            weight = operators[a // 4, a % 4 * 32 + 20 + q]
            for field in range(3):
                sums[field] = sums[field] + weight * jumps[field][q]
        for field in range(3):
            out[field][a] = sums[field]
    return [out[field][a] for field in range(3) for a in range(10)]


def child_matrix(prolong_ref):
    f32, bf16 = jnp.float32, jnp.bfloat16

    def number(shape, axis):
        return lax.broadcasted_iota(jnp.int32, shape, axis)

    both = jnp.concatenate([prolong_ref[:, 0, :], prolong_ref[:, 1, :]], axis=0)
    rounded = both.astype(bf16)
    rest = (both - rounded.astype(f32)).astype(bf16)
    shape = (10, WIDE)
    columns = (number(shape, 1) % 10 == number(shape, 0)).astype(bf16)
    shape = (2 * PACK, 20)
    rows = (number(shape, 0) // 4 == number(shape, 1)).astype(bf16)
    shape = (2 * PACK, WIDE)
    same = number(shape, 0) % 4 == number(shape, 1) // 10
    parts = []
    for matrix in (rounded, rest):
        spread = jnp.dot(matrix, columns, preferred_element_type=f32).astype(bf16)
        full = jnp.dot(rows, spread, preferred_element_type=f32)
        parts.append(jnp.where(same, full, 0.0))
    shape = (PACK, WIDE)
    same = (number(shape, 0) % 4 == number(shape, 1) // 10) & (number(shape, 0) // 4 == number(shape, 1) % 10)
    first = jnp.concatenate([parts[0], same.astype(f32)], axis=0)
    last = jnp.concatenate([parts[1], jnp.zeros(shape, f32)], axis=0)
    return jnp.concatenate([first, first, last], axis=1).astype(bf16)


def sum_children(sizes, refine, ends_ref, full_ref, lines_ref):
    slots, f32 = sizes.slots, jnp.float32
    counts = (1.0 + refine).astype(jnp.bfloat16)
    row_i = lax.broadcasted_iota(jnp.int32, (LANES, LANES), 0)
    col_i = lax.broadcasted_iota(jnp.int32, (LANES, LANES), 1)
    upper = (row_i <= col_i).astype(jnp.bfloat16)
    within = jnp.dot(counts, upper, preferred_element_type=f32)
    whole = jnp.dot(counts, jnp.ones((LANES, LANES), jnp.bfloat16), preferred_element_type=f32)
    row_s = lax.broadcasted_iota(jnp.int32, (slots, slots), 0)
    col_s = lax.broadcasted_iota(jnp.int32, (slots, slots), 1)
    lower = (col_s < row_s).astype(jnp.bfloat16)
    before = jnp.dot(lower, whole.astype(jnp.bfloat16), preferred_element_type=f32)
    before = before - before[sizes.margin : sizes.margin + 1, :]
    ends = 2.0 * (within + before) + refine
    high = jnp.floor(ends * (1.0 / 256.0))
    ends_ref[...] = jnp.concatenate([high, ends - 256.0 * high], axis=1).astype(jnp.bfloat16)
    full_ref[...] = before + whole
    ones = jnp.ones((8, LANES), jnp.bfloat16)
    sums = lax.dot_general(ones, counts, (((1,), (1,)), ((), ())), preferred_element_type=f32)
    gap = lax.broadcasted_iota(jnp.int32, (slots, LANES), 1) - lax.broadcasted_iota(jnp.int32, (slots, LANES), 0)
    lines = [
        jnp.dot(sums.astype(jnp.bfloat16), (gap >= least).astype(jnp.bfloat16), preferred_element_type=f32)
        for least in (2, 1, 0)
    ]
    own = lines[1][:, sizes.margin : sizes.margin + 1]
    for num in range(3):
        lines_ref[num] = lines[num] - own


def prep_kernel(
    sizes, state_hbm, depth_hbm, metric_hbm, partner_hbm, refine_hbm, diff_hbm, lift_hbm, prolong_hbm,
    cur, aux, weights, operators,
    state_ref, depth_ref, metric_ref, partner_ref, refine_ref, prolong_ref, diff_ref, lift_ref, spread, wide, sems,
):
    blocks = sizes.blocks
    copies = fetch_all(
        (
            (metric_hbm, metric_ref),
            (state_hbm, state_ref),
            (depth_hbm, depth_ref),
            (partner_hbm, partner_ref),
            (refine_hbm, refine_ref),
            (prolong_hbm, prolong_ref),
            (diff_hbm, diff_ref),
            (lift_hbm, lift_ref),
        ),
        sems,
    )
    for copy in copies:
        copy.wait()
    weights[...] = child_matrix(prolong_ref)
    rows = jnp.concatenate([diff_ref[:, 0, :], diff_ref[:, 1, :], lift_ref[...]], axis=1)
    rows = jnp.concatenate([rows, jnp.zeros((2, 32), jnp.float32)], axis=0)
    for row in range(3):
        for part in range(4):
            at = 4 * row + part
            operators[row : row + 1, 32 * part : 32 * part + 32] = rows[at : at + 1]
    metric = split_metric(metric_ref, spread, blocks)
    dense = [depth_ref[...], *metric, partner_ref[...].astype(jnp.float32), refine_ref[...].astype(jnp.float32)]
    for num in range(7):
        aux[num] = dense[num]
    pack_state(state_ref, wide, blocks, LAID, 4)
    for field in range(3):
        for node in range(10):
            cur[10 * field + node] = wide[pl.ds(4 * node + field, blocks, stride=LAID), :]


def first_kernel(
    sizes, cur_own, aux_own, weights_in, operators_in, odd_ref, even_ref,
    cur, rate_ref, twice_ref, weights, ends_ref, full_ref, lines_ref,
    geo_ref, aux, operators, sems,
):
    blocks, halo = sizes.blocks, sizes.halo
    top, bottom = PAD + halo, PAD + halo + blocks
    place = lax.axis_index(AXES)
    count = lax.axis_size(AXES)
    copies = fetch_all(((operators_in, operators),), sems)
    even = place % 2 == 0
    zero = jnp.minimum(place, 0)

    def set_halo(target, num, row):
        by_even = even_ref[pl.ds(row, halo, stride=SENT), :]
        by_odd = odd_ref[pl.ds(row, halo, stride=SENT), :]
        target[num, top - halo : top, :] = jnp.where(even, by_odd, by_even)
        target[num, pl.ds(zero + bottom, halo), :] = jnp.where(even, by_even, by_odd)

    for num in range(7):
        set_halo(aux, num, 30 + num)
        aux[num, pl.ds(zero + top, blocks), :] = aux_own[num]
    for field in range(3):
        for node in range(10):
            item = 10 * field + node
            set_halo(cur, item, 3 * node + field)
            cur[item, pl.ds(zero + top, blocks), :] = cur_own[item]

    weights[...] = weights_in[...]
    begin = PAD + sizes.keep
    sum_children(sizes, aux[6, pl.ds(zero + begin, sizes.slots), :], ends_ref, full_ref, lines_ref)
    for copy in copies:
        copy.wait()

    def step(start, height):
        base = PAD + start

        def rows(shift):
            return pl.ds(zero + (base + shift) if shift else base, height)

        def load_aux(item, shift):
            return aux[item, rows(shift), :]

        def load(item, shift):
            return cur[item, rows(shift), :]

        depth, rx, ry, sx, sy, partner = [load_aux(num, 0) for num in range(6)]
        index, inside = pair_index(partner)
        fetch = outer_values(load_aux, index, inside)
        walls = wall_masks(sizes, start, place, count, partner)
        speed_sq = GRAVITY * depth
        outer_sq = [jnp.where(walls[k], speed_sq, GRAVITY * fetch[k](0)) for k in range(3)]
        faces = ((sx, sy), (rx + sx, ry + sy), (rx, ry))
        squares = [vx * vx + vy * vy for vx, vy in faces]
        waves = [
            0.5 * jnp.sqrt(squares[k]) * jnp.sqrt(jnp.maximum(speed_sq, outer_sq[k])) for k in range(3)
        ]
        ghosts = [8.0 / squares[k] for k in range(3)]
        geo = [speed_sq, rx, ry, sx, sy, *outer_sq, *waves, *ghosts]
        rates = tendency(load, geo, walls, index, inside, operators)
        for num, value in enumerate([*geo, partner]):
            geo_ref[num, pl.ds(start, height), :] = value
        for item in range(30):
            rate_ref[item, pl.ds(base, height), :] = rates[item]

    def again(start, height):
        row = start + sizes.keep
        at = pl.ds(zero + row, height)

        def load(item, shift):
            return rate_ref[item, pl.ds(zero + (PAD + row + shift), height), :]

        geo = [geo_ref[num, at, :] for num in range(14)]
        partner = geo_ref[14, at, :]
        index, inside = pair_index(partner)
        walls = wall_masks(sizes, row, place, count, partner)
        rates = tendency(load, geo, walls, index, inside, operators)
        for item in range(30):
            twice_ref[item, pl.ds(start, height), :] = rates[item]

    def sweep(work, rows):
        for start in range(0, rows // TALL * TALL, TALL):
            work(start, TALL)

    for start in range(sizes.rows // TALL * TALL, sizes.rows, 8):
        step(start, 8)
    sweep(step, sizes.rows)
    for start in range(sizes.slots // TALL * TALL, sizes.slots, 8):
        again(start, 8)
    sweep(again, sizes.slots)


def refine_kernel(
    sizes, cur, rate_ref, twice_ref, weights, base_ref, full_ref, lines_ref, stats_ref, out_hbm,
    out_ref, place_v, place_s, wide, index_ref, out_sems, sem,
):
    slots, keep = sizes.slots, sizes.keep
    place = lax.axis_index(AXES)
    zero = jnp.minimum(place, 0)
    stats = stats_ref[...]
    half = LANES // 2
    row_n = lax.broadcasted_iota(jnp.int32, stats.shape, 0)
    top = jnp.max(stats, axis=0, keepdims=True)
    earlier = jnp.sum(jnp.where(row_n < place, stats, 0.0), axis=0, keepdims=True)
    left = lax.broadcasted_iota(jnp.int32, (1, LANES), 1) < half
    top = jnp.where(left, top, pltpu.roll(top, half, 1))
    earlier = jnp.where(left, pltpu.roll(earlier, half, 1), earlier)
    step = COURANT / top
    half_square = 0.5 * step * step
    start = earlier - (place * (sizes.cells // 2)).astype(jnp.float32)
    first_slot = LANES * lax.broadcasted_iota(jnp.int32, (slots, LANES), 1).astype(jnp.float32)
    lead = jnp.sum((full_ref[...] + start <= first_slot).astype(jnp.float32), axis=0, keepdims=True)
    lead = jnp.clip(lead.astype(jnp.int32), 0, slots - 1)
    place_v[...] = lead
    copy = pltpu.make_async_copy(place_v, place_s, sem)
    copy.start()
    for item in range(30):
        now = pl.ds(zero + (PAD + keep), slots)
        value = cur[item, now, :] + step * rate_ref[item, now, :] + half_square * twice_ref[item]
        wide[pl.ds(item, slots, stride=STEP), :] = value
    for item in (30, 31):
        wide[pl.ds(item, slots + 1, stride=STEP), :] = jnp.zeros((slots + 1, LANES), jnp.float32)
    slot_start = LANES * lax.broadcasted_iota(jnp.int32, (slots, LANES), 0).astype(jnp.float32)
    begun = [lines_ref[num, 0:1, :] + start <= slot_start for num in range(3)]
    halves = [
        jnp.dot(
            (begun[num] & ~begun[num + 1]).astype(jnp.bfloat16)[:, :slots],
            base_ref[...],
            preferred_element_type=jnp.float32,
        )
        for num in (1, 0)
    ]
    near, far = [256.0 * x[:, :LANES] + (x[:, LANES:] + 2.0 * start) for x in halves]
    lane = lax.broadcasted_iota(jnp.int32, (slots, LANES), 1)
    slot_no = LANES * lax.broadcasted_iota(jnp.int32, (slots, LANES), 0) + lane
    goal = (2 * slot_no + 1).astype(jnp.float32)
    beyond = jnp.broadcast_to(near[:, LANES - 1 :], (slots, LANES)) <= goal

    def pick(index):
        return jnp.where(beyond, lane_gather(far, index), lane_gather(near, index))

    found = jnp.zeros((slots, LANES), jnp.int32)
    for size in (LANES // 4, LANES // 16, LANES // 64):
        passed = [(pick(found + (probe * size - 1)) <= goal).astype(jnp.int32) for probe in (1, 2, 3)]
        found = found + size * (passed[0] + passed[1] + passed[2])
    found = found + (pick(found) <= goal).astype(jnp.int32)
    mine = pick(found).astype(jnp.int32)
    split = mine & 1
    begin = (mine >> 1) - 1 - split
    kind = split * (1 + slot_no - begin)
    index_ref[0] = found.astype(jnp.float32)
    index_ref[1] = kind.astype(jnp.float32)
    index_ref[2] = (lane < jnp.broadcast_to(found[:, 0:1], (slots, LANES))).astype(jnp.float32)
    copy.wait()
    matrix = weights[...]
    results = []
    parts = [(at, 4) for at in range(0, slots, 4)]
    for part, (begin_at, height) in enumerate(parts):
        span = slice(LANES * begin_at, LANES * (begin_at + height))
        columns = []
        for slot in range(begin_at, begin_at + height):
            lead_at = place_s[0, slot] * STEP
            lane_idx = jnp.broadcast_to(index_ref[0, slot : slot + 1, :], (8, LANES)).astype(jnp.int32)
            ahead = jnp.broadcast_to(index_ref[2, slot : slot + 1, :], (8, LANES)) > 0.5
            tiles = []
            for row in range(0, WIDE, 8):
                one = wide[pl.ds(lead_at + row, 8), :]
                two = wide[pl.ds(lead_at + STEP + row, 8), :]
                tiles.append(lane_gather(jnp.where(ahead, two, one), lane_idx))
            columns.append(jnp.concatenate(tiles, axis=0))
        values = jnp.concatenate(columns, axis=1)
        high = values.astype(jnp.bfloat16)
        low = (values - high.astype(jnp.float32)).astype(jnp.bfloat16)
        stack = jnp.concatenate([high, low, high], axis=0)
        children = jnp.dot(matrix, stack, preferred_element_type=jnp.float32)
        for sub in range(height):
            slot = begin_at + sub
            cut = slice(LANES * sub, LANES * (sub + 1))
            tag = jnp.broadcast_to(index_ref[1, slot : slot + 1, :], (PACK, LANES))
            value = jnp.where(
                tag < 0.5,
                children[2 * PACK :, cut],
                jnp.where(tag < 1.5, children[:PACK, cut], children[PACK : 2 * PACK, cut]),
            )
            for node in range(10):
                out_ref[node, :, LANES * slot : LANES * (slot + 1)] = value[4 * node : 4 * node + 3]
        result = pltpu.make_async_copy(out_ref.at[:, :, span], out_hbm.at[:, :, span], out_sems.at[part])
        result.start()
        results.append(result)
    for result in results:
        result.wait()


def swaps(start, count):
    pairs = [(i, i + 1) for i in range(start, count - 1, 2)]
    return pairs + [(j, i) for i, j in pairs]


def shards(state, depth, metric, partner, refine, diff_ops, lift, prolong):
    sizes = Sizes(state.shape[2])
    count = lax.axis_size(AXES)
    blocks, rows, slots, halo = sizes.blocks, sizes.rows, sizes.slots, sizes.halo
    depth, partner, refine = [x.reshape(blocks, LANES) for x in (depth, partner, refine)]
    state, diff_ops, prolong = [jnp.transpose(x, (1, 0, 2)) for x in (state, diff_ops, prolong)]
    state, depth, metric, partner, refine, diff_ops, lift, prolong = [
        pltpu.with_memory_space_constraint(x, pltpu.HBM)
        for x in (state, depth, metric, partner, refine, diff_ops, lift, prolong)
    ]
    f32, i32 = jnp.float32, jnp.int32
    packed = jax.ShapeDtypeStruct((SENT * halo, LANES), f32)
    dense = [
        pltpu.VMEM((blocks, LANES), f32),
        pltpu.VMEM(metric.shape, f32),
        pltpu.VMEM((blocks, LANES), i32),
        pltpu.VMEM((blocks, LANES), i32),
    ]
    stats, even, odd = pl.pallas_call(
        functools.partial(pack_kernel, sizes),
        name="pack",
        out_shape=(jax.ShapeDtypeStruct((count, LANES), f32), packed, packed),
        in_specs=[HBM] * 5,
        out_specs=(HBM, VMEM, VMEM),
        scratch_shapes=[
            pltpu.VMEM((count, LANES), f32),
            pltpu.VMEM((10, 3, LANES * halo), f32),
            pltpu.VMEM((10, 3, LANES * halo), f32),
            *dense,
            pltpu.VMEM((8 * blocks, LANES), f32),
            pltpu.SemaphoreType.DMA((6,)),
            pltpu.SemaphoreType.DMA,
        ],
        compiler_params=PARAMS,
    )(state, depth, metric, partner, refine)
    odd = lax.ppermute(odd, AXES, swaps(1, count))
    even = lax.ppermute(even, AXES, swaps(0, count))
    stats = lax.all_to_all(stats, AXES, 0, 0, tiled=True)
    even, odd, stats = [pltpu.with_memory_space_constraint(x, pltpu.VMEM) for x in (even, odd, stats)]
    cur, aux, weights, operators = pl.pallas_call(
        functools.partial(prep_kernel, sizes),
        name="lay_out",
        cost_estimate=pl.CostEstimate(flops=1 << 24, transcendentals=1 << 16, bytes_accessed=1 << 24),
        out_shape=(
            jax.ShapeDtypeStruct((30, blocks, LANES), f32),
            jax.ShapeDtypeStruct((7, blocks, LANES), f32),
            jax.ShapeDtypeStruct((3 * PACK, 3 * WIDE), jnp.bfloat16),
            jax.ShapeDtypeStruct((3, LANES), f32),
        ),
        in_specs=[HBM] * 8,
        out_specs=(VMEM,) * 4,
        scratch_shapes=[
            pltpu.VMEM(state.shape, f32),
            *dense,
            pltpu.VMEM(prolong.shape, f32),
            pltpu.VMEM(diff_ops.shape, f32),
            pltpu.VMEM(lift.shape, f32),
            pltpu.VMEM((8 * blocks, LANES), f32),
            pltpu.VMEM((LAID * blocks, LANES), f32),
            pltpu.SemaphoreType.DMA((8,)),
        ],
        compiler_params=PARAMS,
    )(state, depth, metric, partner, refine, diff_ops, lift, prolong)
    cur, rates, twice, weights, ends, full, lines = pl.pallas_call(
        functools.partial(first_kernel, sizes),
        name="rates_twice",
        cost_estimate=pl.CostEstimate(flops=1024, transcendentals=0, bytes_accessed=1024),
        out_shape=(
            jax.ShapeDtypeStruct((30, sizes.tall, LANES), f32),
            jax.ShapeDtypeStruct((30, sizes.tall, LANES), f32),
            jax.ShapeDtypeStruct((30, slots, LANES), f32),
            jax.ShapeDtypeStruct((3 * PACK, 3 * WIDE), jnp.bfloat16),
            jax.ShapeDtypeStruct((slots, 2 * LANES), jnp.bfloat16),
            jax.ShapeDtypeStruct((slots, LANES), f32),
            jax.ShapeDtypeStruct((3, 8, LANES), f32),
        ),
        in_specs=[VMEM] * 6,
        out_specs=(VMEM,) * 7,
        scratch_shapes=[
            pltpu.VMEM((15, rows, LANES), f32),
            pltpu.VMEM((7, sizes.tall, LANES), f32),
            pltpu.SMEM((3, LANES), f32),
            pltpu.SemaphoreType.DMA((1,)),
        ],
        compiler_params=PARAMS,
    )(cur, aux, weights, operators, odd, even)
    refined = pl.pallas_call(
        functools.partial(refine_kernel, sizes),
        name="sum_and_refine",
        out_shape=jax.ShapeDtypeStruct((10, 3, LANES * slots), f32),
        in_specs=[VMEM] * 8,
        out_specs=HBM,
        scratch_shapes=[
            pltpu.VMEM((10, 3, LANES * slots), f32),
            pltpu.VMEM((1, LANES), i32),
            pltpu.SMEM((1, LANES), i32),
            pltpu.VMEM((STEP * (slots + 1), LANES), f32),
            pltpu.VMEM((3, slots, LANES), f32),
            pltpu.SemaphoreType.DMA((slots // 4,)),
            pltpu.SemaphoreType.DMA,
        ],
        compiler_params=PARAMS,
    )(cur, rates, twice, weights, ends, full, lines, stats)
    return jnp.transpose(refined, (1, 0, 2))


def solution(mesh):
    return jax.shard_map(
        shards,
        mesh=mesh,
        in_specs=(
            P(None, None, AXES),
            P(AXES),
            P(None, AXES),
            P(AXES),
            P(AXES),
            P(),
            P(),
            P(),
        ),
        out_specs=P(None, None, AXES),
        check_vma=False,
    )
```

```python
import functools

import jax
import jax.numpy as jnp
from jax import lax
from jax.experimental import pallas as pl
from jax.experimental.pallas import tpu as pltpu
from jax.sharding import PartitionSpec as P

GRAVITY = 9.81
COURANT = 0.5
HIGH = lax.Precision.HIGHEST
LANES = 128
AXES = ("row", "col")
FACES = ((0, 1, 2, 3), (3, 6, 8, 9), (9, 7, 4, 0))
PACK = 40
LAID = 41
SENT = 37
WIDE = 32
TALL = 16
PAD = 8

VMEM = pl.BlockSpec(memory_space=pltpu.VMEM)
HBM = pl.BlockSpec(memory_space=pltpu.HBM)
PARAMS = pltpu.CompilerParams(vmem_limit_bytes=48 * 1024 * 1024)


class Sizes:
    def __init__(self, cells):
        self.cells = cells
        self.blocks = cells // LANES
        self.margin = cells // 4 // LANES
        self.halo = self.margin + 1
        self.rows = -(-(self.blocks + 2 * self.halo) // 8) * 8
        self.tall = self.rows + 2 * PAD
        self.slots = 3 * self.blocks // 2
        self.keep = self.halo - self.margin


def fetch_all(pairs, sems):
    copies = [pltpu.make_async_copy(src, dst, sems.at[num]) for num, (src, dst) in enumerate(pairs)]
    for copy in copies:
        copy.start()
    return copies


def split_metric(metric_ref, spread, blocks):
    for block in range(blocks):
        spread[8 * block : 8 * block + 4, :] = metric_ref[:, LANES * block : LANES * (block + 1)]
    return [spread[pl.ds(comp, blocks, stride=8), :] for comp in range(4)]


def pack_kernel(
    sizes, state_hbm, depth_hbm, metric_hbm, partner_hbm, refine_hbm, stats_hbm, even_ref, odd_ref,
    stats_ref, state_even, state_odd, depth_ref, metric_ref, partner_ref, refine_ref, spread, sems, sem,
):
    blocks, halo = sizes.blocks, sizes.halo
    wide = LANES * halo
    late = blocks - halo
    even = (lax.axis_index(AXES) + 1) % 2 * late
    odd = late - even
    copies = fetch_all(
        (
            (depth_hbm, depth_ref),
            (metric_hbm, metric_ref),
            (refine_hbm, refine_ref),
            (partner_hbm, partner_ref),
            (state_hbm.at[:, :, pl.ds(pl.multiple_of(LANES * even, LANES), wide)], state_even),
            (state_hbm.at[:, :, pl.ds(pl.multiple_of(LANES * odd, LANES), wide)], state_odd),
        ),
        sems,
    )
    for copy in copies[:3]:
        copy.wait()
    rx, ry, sx, sy = split_metric(metric_ref, spread, blocks)
    depth = depth_ref[...]
    refine = refine_ref[...].astype(jnp.float32)
    faces = ((sx, sy), (rx + sx, ry + sy), (rx, ry))
    lengths = [jnp.sqrt(vx * vx + vy * vy) for vx, vy in faces]
    rate = jnp.sqrt(GRAVITY * depth) * jnp.maximum(jnp.maximum(lengths[0], lengths[1]), lengths[2])
    top = jnp.max(jnp.max(rate, axis=0, keepdims=True), axis=1, keepdims=True)
    extra = jnp.sum(jnp.sum(refine, axis=0, keepdims=True), axis=1, keepdims=True)
    shape = stats_ref.shape
    lane = lax.broadcasted_iota(jnp.int32, shape, 1)
    stats_ref[...] = jnp.where(
        lane < LANES // 2, jnp.broadcast_to(top, shape), jnp.broadcast_to(extra, shape)
    )
    sent = pltpu.make_async_copy(stats_ref, stats_hbm, sem)
    sent.start()
    for copy in copies[3:]:
        copy.wait()
    for ref, source, start in ((even_ref, state_even, even), (odd_ref, state_odd, odd)):
        pack_state(source, ref, halo, SENT, 3)
        at = pl.ds(start, halo)
        dense = [depth_ref[at, :]]
        dense += [spread[pl.ds(8 * start + comp, halo, stride=8), :] for comp in range(4)]
        dense += [partner_ref[at, :].astype(jnp.float32), refine_ref[at, :].astype(jnp.float32)]
        for num, value in enumerate(dense):
            ref[pl.ds(30 + num, halo, stride=SENT), :] = value
    sent.wait()


def pack_state(source, target, blocks, height, width):
    for block in range(blocks):
        for node in range(10):
            at = height * block + width * node
            target[at : at + 3, :] = source[node, :, LANES * block : LANES * (block + 1)]


def pair_index(partner):
    lane = lax.broadcasted_iota(jnp.int32, partner.shape, 1)
    target = lane + partner.astype(jnp.int32)
    return target & (LANES - 1), (target >= 0) & (target < LANES)


def lane_gather(values, index):
    return jnp.take_along_axis(values, index, axis=1, mode="promise_in_bounds")


def outer_values(load, index, inside):
    shape = index.shape
    lane = lax.broadcasted_iota(jnp.int32, shape, 1)

    def prev(item):
        return pltpu.roll(jnp.where(lane == LANES - 1, load(item, -1), load(item, 0)), 1, 1)

    def after(item):
        return pltpu.roll(jnp.where(lane == 0, load(item, 1), load(item, 0)), LANES - 1, 1)

    def across(item):
        other = jnp.where(lane < LANES // 2, load(item, 1), load(item, -1))
        return jnp.where(inside, lane_gather(load(item, 0), index), lane_gather(other, index))

    return prev, after, across


def wall_masks(sizes, start, place, count, partner):
    shape = partner.shape
    lane = lax.broadcasted_iota(jnp.int32, shape, 1)
    row = lax.broadcasted_iota(jnp.int32, shape, 0) + start
    first = (lane == 0) & (row == sizes.halo) & (place == 0)
    last = (lane == LANES - 1) & (row == sizes.halo + sizes.blocks - 1) & (place == count - 1)
    return first, last, partner == 0


def tendency(load, geo, walls, index, inside, operators):
    speed_sq, rx, ry, sx, sy = geo[:5]
    outer_sq, waves, ghosts = geo[5:8], geo[8:11], geo[11:14]
    own = [[load(10 * field + node, 0) for node in range(10)] for field in range(3)]
    eta, mom_x, mom_y = own
    flow_r = [-(rx * mom_x[b] + ry * mom_y[b]) for b in range(10)]
    flow_s = [-(sx * mom_x[b] + sy * mom_y[b]) for b in range(10)]
    half_r = (0.5 * rx, 0.5 * ry)
    half_s = (0.5 * sx, 0.5 * sy)
    vectors = (
        (-half_s[0], -half_s[1]),
        (half_r[0] + half_s[0], half_r[1] + half_s[1]),
        (-half_r[0], -half_r[1]),
    )
    fetch = outer_values(load, index, inside)
    jumps = ([], [], [])
    for face in range(3):
        vec_x, vec_y = vectors[face]
        theirs = FACES[(1, 0, 2)[face]]
        wall = walls[face]
        for j in range(4):
            node, match = FACES[face][j], theirs[3 - j]
            in_eta, in_x, in_y = eta[node], mom_x[node], mom_y[node]
            ext_eta, ext_x, ext_y = [fetch[face](10 * field + match) for field in range(3)]
            bounce = (in_x * vec_x + in_y * vec_y) * ghosts[face]
            d_eta = jnp.where(wall, 0.0, in_eta - ext_eta)
            d_x = jnp.where(wall, bounce * vec_x, in_x - ext_x)
            d_y = jnp.where(wall, bounce * vec_y, in_y - ext_y)
            head = jnp.where(wall, 0.0, speed_sq * in_eta - outer_sq[face] * ext_eta)
            jumps[0].append(d_x * vec_x + d_y * vec_y - waves[face] * d_eta)
            jumps[1].append(head * vec_x - waves[face] * d_x)
            jumps[2].append(head * vec_y - waves[face] * d_y)
    pull = (-speed_sq * rx, -speed_sq * ry)
    push = (-speed_sq * sx, -speed_sq * sy)
    out = [[None] * 10 for _ in range(3)]
    for a in range(10):
        total = along_r = along_s = None
        for b in range(10):
            d_r, d_s = operators[a // 4, a % 4 * 32 + b], operators[a // 4, a % 4 * 32 + 10 + b]
            term = d_r * flow_r[b] + d_s * flow_s[b]
            total = term if b == 0 else total + term
            along_r = d_r * eta[b] if b == 0 else along_r + d_r * eta[b]
            along_s = d_s * eta[b] if b == 0 else along_s + d_s * eta[b]
        sums = [total, pull[0] * along_r + push[0] * along_s, pull[1] * along_r + push[1] * along_s]
        for q in range(12):
            weight = operators[a // 4, a % 4 * 32 + 20 + q]
            for field in range(3):
                sums[field] = sums[field] + weight * jumps[field][q]
        for field in range(3):
            out[field][a] = sums[field]
    return [out[field][a] for field in range(3) for a in range(10)]


def child_matrix(prolong_ref):
    f32, bf16 = jnp.float32, jnp.bfloat16

    def number(shape, axis):
        return lax.broadcasted_iota(jnp.int32, shape, axis)

    both = jnp.concatenate([prolong_ref[:, 0, :], prolong_ref[:, 1, :]], axis=0)
    rounded = both.astype(bf16)
    rest = (both - rounded.astype(f32)).astype(bf16)
    shape = (10, WIDE)
    columns = (number(shape, 1) % 10 == number(shape, 0)).astype(bf16)
    shape = (2 * PACK, 20)
    rows = (number(shape, 0) // 4 == number(shape, 1)).astype(bf16)
    shape = (2 * PACK, WIDE)
    same = number(shape, 0) % 4 == number(shape, 1) // 10
    parts = []
    for matrix in (rounded, rest):
        spread = jnp.dot(matrix, columns, preferred_element_type=f32).astype(bf16)
        full = jnp.dot(rows, spread, preferred_element_type=f32)
        parts.append(jnp.where(same, full, 0.0))
    shape = (PACK, WIDE)
    same = (number(shape, 0) % 4 == number(shape, 1) // 10) & (number(shape, 0) // 4 == number(shape, 1) % 10)
    first = jnp.concatenate([parts[0], same.astype(f32)], axis=0)
    last = jnp.concatenate([parts[1], jnp.zeros(shape, f32)], axis=0)
    return jnp.concatenate([first, first, last], axis=1).astype(bf16)


def sum_children(sizes, refine, ends_ref, full_ref, lines_ref):
    slots, f32 = sizes.slots, jnp.float32
    counts = (1.0 + refine).astype(jnp.bfloat16)
    row_i = lax.broadcasted_iota(jnp.int32, (LANES, LANES), 0)
    col_i = lax.broadcasted_iota(jnp.int32, (LANES, LANES), 1)
    upper = (row_i <= col_i).astype(jnp.bfloat16)
    within = jnp.dot(counts, upper, preferred_element_type=f32)
    whole = jnp.dot(counts, jnp.ones((LANES, LANES), jnp.bfloat16), preferred_element_type=f32)
    row_s = lax.broadcasted_iota(jnp.int32, (slots, slots), 0)
    col_s = lax.broadcasted_iota(jnp.int32, (slots, slots), 1)
    lower = (col_s < row_s).astype(jnp.bfloat16)
    before = jnp.dot(lower, whole.astype(jnp.bfloat16), preferred_element_type=f32)
    before = before - before[sizes.margin : sizes.margin + 1, :]
    ends = 2.0 * (within + before) + refine
    high = jnp.floor(ends * (1.0 / 256.0))
    ends_ref[...] = jnp.concatenate([high, ends - 256.0 * high], axis=1).astype(jnp.bfloat16)
    full_ref[...] = before + whole
    ones = jnp.ones((8, LANES), jnp.bfloat16)
    sums = lax.dot_general(ones, counts, (((1,), (1,)), ((), ())), preferred_element_type=f32)
    gap = lax.broadcasted_iota(jnp.int32, (slots, LANES), 1) - lax.broadcasted_iota(jnp.int32, (slots, LANES), 0)
    lines = [
        jnp.dot(sums.astype(jnp.bfloat16), (gap >= least).astype(jnp.bfloat16), preferred_element_type=f32)
        for least in (2, 1, 0)
    ]
    own = lines[1][:, sizes.margin : sizes.margin + 1]
    for num in range(3):
        lines_ref[num] = lines[num] - own


def prep_kernel(
    sizes, state_hbm, depth_hbm, metric_hbm, partner_hbm, refine_hbm, diff_hbm, lift_hbm, prolong_hbm,
    cur, aux, weights, operators,
    state_ref, depth_ref, metric_ref, partner_ref, refine_ref, prolong_ref, diff_ref, lift_ref, spread, wide, sems,
):
    blocks = sizes.blocks
    copies = fetch_all(
        (
            (metric_hbm, metric_ref),
            (state_hbm, state_ref),
            (depth_hbm, depth_ref),
            (partner_hbm, partner_ref),
            (refine_hbm, refine_ref),
            (prolong_hbm, prolong_ref),
            (diff_hbm, diff_ref),
            (lift_hbm, lift_ref),
        ),
        sems,
    )
    for copy in copies:
        copy.wait()
    weights[...] = child_matrix(prolong_ref)
    rows = jnp.concatenate([diff_ref[:, 0, :], diff_ref[:, 1, :], lift_ref[...]], axis=1)
    rows = jnp.concatenate([rows, jnp.zeros((2, 32), jnp.float32)], axis=0)
    for row in range(3):
        for part in range(4):
            at = 4 * row + part
            operators[row : row + 1, 32 * part : 32 * part + 32] = rows[at : at + 1]
    metric = split_metric(metric_ref, spread, blocks)
    dense = [depth_ref[...], *metric, partner_ref[...].astype(jnp.float32), refine_ref[...].astype(jnp.float32)]
    for num in range(7):
        aux[num] = dense[num]
    pack_state(state_ref, wide, blocks, LAID, 4)
    for field in range(3):
        for node in range(10):
            cur[10 * field + node] = wide[pl.ds(4 * node + field, blocks, stride=LAID), :]


def first_kernel(
    sizes, cur_own, aux_own, weights_in, operators_in, odd_ref, even_ref,
    cur, rate_ref, twice_ref, weights, ends_ref, full_ref, lines_ref,
    geo_ref, aux, operators, sems,
):
    blocks, halo = sizes.blocks, sizes.halo
    top, bottom = PAD + halo, PAD + halo + blocks
    place = lax.axis_index(AXES)
    count = lax.axis_size(AXES)
    copies = fetch_all(((operators_in, operators),), sems)
    even = place % 2 == 0
    zero = jnp.minimum(place, 0)

    def set_halo(target, num, row):
        by_even = even_ref[pl.ds(row, halo, stride=SENT), :]
        by_odd = odd_ref[pl.ds(row, halo, stride=SENT), :]
        target[num, top - halo : top, :] = jnp.where(even, by_odd, by_even)
        target[num, pl.ds(zero + bottom, halo), :] = jnp.where(even, by_even, by_odd)

    for num in range(7):
        set_halo(aux, num, 30 + num)
        aux[num, pl.ds(zero + top, blocks), :] = aux_own[num]
    for field in range(3):
        for node in range(10):
            item = 10 * field + node
            set_halo(cur, item, 3 * node + field)
            cur[item, pl.ds(zero + top, blocks), :] = cur_own[item]

    weights[...] = weights_in[...]
    begin = PAD + sizes.keep
    sum_children(sizes, aux[6, pl.ds(zero + begin, sizes.slots), :], ends_ref, full_ref, lines_ref)
    for copy in copies:
        copy.wait()

    def step(start, height):
        base = PAD + start

        def rows(shift):
            return pl.ds(zero + (base + shift) if shift else base, height)

        def load_aux(item, shift):
            return aux[item, rows(shift), :]

        def load(item, shift):
            return cur[item, rows(shift), :]

        depth, rx, ry, sx, sy, partner = [load_aux(num, 0) for num in range(6)]
        index, inside = pair_index(partner)
        fetch = outer_values(load_aux, index, inside)
        walls = wall_masks(sizes, start, place, count, partner)
        speed_sq = GRAVITY * depth
        outer_sq = [jnp.where(walls[k], speed_sq, GRAVITY * fetch[k](0)) for k in range(3)]
        faces = ((sx, sy), (rx + sx, ry + sy), (rx, ry))
        squares = [vx * vx + vy * vy for vx, vy in faces]
        waves = [
            0.5 * jnp.sqrt(squares[k]) * jnp.sqrt(jnp.maximum(speed_sq, outer_sq[k])) for k in range(3)
        ]
        ghosts = [8.0 / squares[k] for k in range(3)]
        geo = [speed_sq, rx, ry, sx, sy, *outer_sq, *waves, *ghosts]
        rates = tendency(load, geo, walls, index, inside, operators)
        for num, value in enumerate([*geo, partner]):
            geo_ref[num, pl.ds(start, height), :] = value
        for item in range(30):
            rate_ref[item, pl.ds(base, height), :] = rates[item]

    def again(start, height):
        row = start + sizes.keep
        at = pl.ds(zero + row, height)

        def load(item, shift):
            return rate_ref[item, pl.ds(zero + (PAD + row + shift), height), :]

        geo = [geo_ref[num, at, :] for num in range(14)]
        partner = geo_ref[14, at, :]
        index, inside = pair_index(partner)
        walls = wall_masks(sizes, row, place, count, partner)
        rates = tendency(load, geo, walls, index, inside, operators)
        for item in range(30):
            twice_ref[item, pl.ds(start, height), :] = rates[item]

    def sweep(work, rows):
        for start in range(0, rows // TALL * TALL, TALL):
            work(start, TALL)

    for start in range(sizes.rows // TALL * TALL, sizes.rows, 8):
        step(start, 8)
    sweep(step, sizes.rows)
    for start in range(sizes.slots // TALL * TALL, sizes.slots, 8):
        again(start, 8)
    sweep(again, sizes.slots)


def refine_kernel(
    sizes, cur, rate_ref, twice_ref, weights, base_ref, full_ref, lines_ref, stats_ref, out_hbm,
    out_ref, place_v, place_s, wide, index_ref, out_sems, sem,
):
    slots, keep = sizes.slots, sizes.keep
    place = lax.axis_index(AXES)
    zero = jnp.minimum(place, 0)
    stats = stats_ref[...]
    half = LANES // 2
    row_n = lax.broadcasted_iota(jnp.int32, stats.shape, 0)
    top = jnp.max(stats, axis=0, keepdims=True)
    earlier = jnp.sum(jnp.where(row_n < place, stats, 0.0), axis=0, keepdims=True)
    left = lax.broadcasted_iota(jnp.int32, (1, LANES), 1) < half
    top = jnp.where(left, top, pltpu.roll(top, half, 1))
    earlier = jnp.where(left, pltpu.roll(earlier, half, 1), earlier)
    step = COURANT / top
    half_square = 0.5 * step * step
    start = earlier - (place * (sizes.cells // 2)).astype(jnp.float32)
    first_slot = LANES * lax.broadcasted_iota(jnp.int32, (slots, LANES), 1).astype(jnp.float32)
    lead = jnp.sum((full_ref[...] + start <= first_slot).astype(jnp.float32), axis=0, keepdims=True)
    lead = jnp.clip(lead.astype(jnp.int32), 0, slots - 1)
    place_v[...] = lead
    copy = pltpu.make_async_copy(place_v, place_s, sem)
    copy.start()
    now = pl.ds(zero + (PAD + keep), slots)
    for first in range(0, WIDE, 8):
        values = []
        for item in range(first, first + 8):
            if item < 30:
                once = cur[item, now, :] + step * rate_ref[item, now, :]
                values.append(once + half_square * twice_ref[item])
            else:
                values.append(jnp.zeros((slots, LANES), jnp.float32))
        wide[:slots, first : first + 8, :] = jnp.swapaxes(jnp.stack(values, axis=0), 0, 1)
    slot_start = LANES * lax.broadcasted_iota(jnp.int32, (slots, LANES), 0).astype(jnp.float32)
    begun = [lines_ref[num, 0:1, :] + start <= slot_start for num in range(3)]
    halves = [
        jnp.dot(
            (begun[num] & ~begun[num + 1]).astype(jnp.bfloat16)[:, :slots],
            base_ref[...],
            preferred_element_type=jnp.float32,
        )
        for num in (1, 0)
    ]
    near, far = [256.0 * x[:, :LANES] + (x[:, LANES:] + 2.0 * start) for x in halves]
    lane = lax.broadcasted_iota(jnp.int32, (slots, LANES), 1)
    slot_no = LANES * lax.broadcasted_iota(jnp.int32, (slots, LANES), 0) + lane
    goal = (2 * slot_no + 1).astype(jnp.float32)
    beyond = jnp.broadcast_to(near[:, LANES - 1 :], (slots, LANES)) <= goal

    def pick(index):
        return jnp.where(beyond, lane_gather(far, index), lane_gather(near, index))

    found = jnp.zeros((slots, LANES), jnp.int32)
    for size in (LANES // 4, LANES // 16, LANES // 64):
        passed = [(pick(found + (probe * size - 1)) <= goal).astype(jnp.int32) for probe in (1, 2, 3)]
        found = found + size * (passed[0] + passed[1] + passed[2])
    found = found + (pick(found) <= goal).astype(jnp.int32)
    mine = pick(found).astype(jnp.int32)
    split = mine & 1
    begin = (mine >> 1) - 1 - split
    kind = split * (1 + slot_no - begin)
    index_ref[0] = found.astype(jnp.float32)
    index_ref[1] = kind.astype(jnp.float32)
    index_ref[2] = (lane < jnp.broadcast_to(found[:, 0:1], (slots, LANES))).astype(jnp.float32)
    copy.wait()
    matrix = weights[...]
    results = []
    parts = [(at, 8) for at in range(0, slots - 8, 8)] + [(slots - 8, 4), (slots - 4, 4)]
    for part, (begin_at, height) in enumerate(parts):
        span = slice(LANES * begin_at, LANES * (begin_at + height))
        columns = []
        for slot in range(begin_at, begin_at + height):
            lead_at = place_s[0, slot]
            lane_idx = jnp.broadcast_to(index_ref[0, slot : slot + 1, :], (8, LANES)).astype(jnp.int32)
            ahead = jnp.broadcast_to(index_ref[2, slot : slot + 1, :], (8, LANES)) > 0.5
            tiles = []
            for row in range(0, WIDE, 8):
                one = wide[lead_at, row : row + 8, :]
                two = wide[lead_at + 1, row : row + 8, :]
                tiles.append(lane_gather(jnp.where(ahead, two, one), lane_idx))
            columns.append(jnp.concatenate(tiles, axis=0))
        values = jnp.concatenate(columns, axis=1)
        high = values.astype(jnp.bfloat16)
        low = (values - high.astype(jnp.float32)).astype(jnp.bfloat16)
        stack = jnp.concatenate([high, low, high], axis=0)
        children = jnp.dot(matrix, stack, preferred_element_type=jnp.float32)
        for sub in range(height):
            slot = begin_at + sub
            cut = slice(LANES * sub, LANES * (sub + 1))
            tag = jnp.broadcast_to(index_ref[1, slot : slot + 1, :], (PACK, LANES))
            value = jnp.where(
                tag < 0.5,
                children[2 * PACK :, cut],
                jnp.where(tag < 1.5, children[:PACK, cut], children[PACK : 2 * PACK, cut]),
            )
            for node in range(10):
                out_ref[node, :, LANES * slot : LANES * (slot + 1)] = value[4 * node : 4 * node + 3]
        result = pltpu.make_async_copy(out_ref.at[:, :, span], out_hbm.at[:, :, span], out_sems.at[part])
        result.start()
        results.append(result)
    for result in results:
        result.wait()


def swaps(start, count):
    pairs = [(i, i + 1) for i in range(start, count - 1, 2)]
    return pairs + [(j, i) for i, j in pairs]


def shards(state, depth, metric, partner, refine, diff_ops, lift, prolong):
    sizes = Sizes(state.shape[2])
    count = lax.axis_size(AXES)
    blocks, rows, slots, halo = sizes.blocks, sizes.rows, sizes.slots, sizes.halo
    depth, partner, refine = [x.reshape(blocks, LANES) for x in (depth, partner, refine)]
    state, diff_ops, prolong = [jnp.transpose(x, (1, 0, 2)) for x in (state, diff_ops, prolong)]
    state, depth, metric, partner, refine, diff_ops, lift, prolong = [
        pltpu.with_memory_space_constraint(x, pltpu.HBM)
        for x in (state, depth, metric, partner, refine, diff_ops, lift, prolong)
    ]
    f32, i32 = jnp.float32, jnp.int32
    packed = jax.ShapeDtypeStruct((SENT * halo, LANES), f32)
    dense = [
        pltpu.VMEM((blocks, LANES), f32),
        pltpu.VMEM(metric.shape, f32),
        pltpu.VMEM((blocks, LANES), i32),
        pltpu.VMEM((blocks, LANES), i32),
    ]
    stats, even, odd = pl.pallas_call(
        functools.partial(pack_kernel, sizes),
        name="pack",
        out_shape=(jax.ShapeDtypeStruct((count, LANES), f32), packed, packed),
        in_specs=[HBM] * 5,
        out_specs=(HBM, VMEM, VMEM),
        scratch_shapes=[
            pltpu.VMEM((count, LANES), f32),
            pltpu.VMEM((10, 3, LANES * halo), f32),
            pltpu.VMEM((10, 3, LANES * halo), f32),
            *dense,
            pltpu.VMEM((8 * blocks, LANES), f32),
            pltpu.SemaphoreType.DMA((6,)),
            pltpu.SemaphoreType.DMA,
        ],
        compiler_params=PARAMS,
    )(state, depth, metric, partner, refine)
    odd = lax.ppermute(odd, AXES, swaps(1, count))
    even = lax.ppermute(even, AXES, swaps(0, count))
    stats = lax.all_to_all(stats, AXES, 0, 0, tiled=True)
    even, odd, stats = [pltpu.with_memory_space_constraint(x, pltpu.VMEM) for x in (even, odd, stats)]
    cur, aux, weights, operators = pl.pallas_call(
        functools.partial(prep_kernel, sizes),
        name="lay_out",
        cost_estimate=pl.CostEstimate(flops=1 << 24, transcendentals=1 << 16, bytes_accessed=1 << 24),
        out_shape=(
            jax.ShapeDtypeStruct((30, blocks, LANES), f32),
            jax.ShapeDtypeStruct((7, blocks, LANES), f32),
            jax.ShapeDtypeStruct((3 * PACK, 3 * WIDE), jnp.bfloat16),
            jax.ShapeDtypeStruct((3, LANES), f32),
        ),
        in_specs=[HBM] * 8,
        out_specs=(VMEM,) * 4,
        scratch_shapes=[
            pltpu.VMEM(state.shape, f32),
            *dense,
            pltpu.VMEM(prolong.shape, f32),
            pltpu.VMEM(diff_ops.shape, f32),
            pltpu.VMEM(lift.shape, f32),
            pltpu.VMEM((8 * blocks, LANES), f32),
            pltpu.VMEM((LAID * blocks, LANES), f32),
            pltpu.SemaphoreType.DMA((8,)),
        ],
        compiler_params=PARAMS,
    )(state, depth, metric, partner, refine, diff_ops, lift, prolong)
    cur, rates, twice, weights, ends, full, lines = pl.pallas_call(
        functools.partial(first_kernel, sizes),
        name="rates_twice",
        cost_estimate=pl.CostEstimate(flops=1024, transcendentals=0, bytes_accessed=1024),
        out_shape=(
            jax.ShapeDtypeStruct((30, sizes.tall, LANES), f32),
            jax.ShapeDtypeStruct((30, sizes.tall, LANES), f32),
            jax.ShapeDtypeStruct((30, slots, LANES), f32),
            jax.ShapeDtypeStruct((3 * PACK, 3 * WIDE), jnp.bfloat16),
            jax.ShapeDtypeStruct((slots, 2 * LANES), jnp.bfloat16),
            jax.ShapeDtypeStruct((slots, LANES), f32),
            jax.ShapeDtypeStruct((3, 8, LANES), f32),
        ),
        in_specs=[VMEM] * 6,
        out_specs=(VMEM,) * 7,
        scratch_shapes=[
            pltpu.VMEM((15, rows, LANES), f32),
            pltpu.VMEM((7, sizes.tall, LANES), f32),
            pltpu.SMEM((3, LANES), f32),
            pltpu.SemaphoreType.DMA((1,)),
        ],
        compiler_params=PARAMS,
    )(cur, aux, weights, operators, odd, even)
    refined = pl.pallas_call(
        functools.partial(refine_kernel, sizes),
        name="sum_and_refine",
        out_shape=jax.ShapeDtypeStruct((10, 3, LANES * slots), f32),
        in_specs=[VMEM] * 8,
        out_specs=HBM,
        scratch_shapes=[
            pltpu.VMEM((10, 3, LANES * slots), f32),
            pltpu.VMEM((1, LANES), i32),
            pltpu.SMEM((1, LANES), i32),
            pltpu.VMEM((slots + 1, WIDE, LANES), f32),
            pltpu.VMEM((3, slots, LANES), f32),
            pltpu.SemaphoreType.DMA((slots // 8 + 1,)),
            pltpu.SemaphoreType.DMA,
        ],
        compiler_params=PARAMS,
    )(cur, rates, twice, weights, ends, full, lines, stats)
    return jnp.transpose(refined, (1, 0, 2))


def solution(mesh):
    return jax.shard_map(
        shards,
        mesh=mesh,
        in_specs=(
            P(None, None, AXES),
            P(AXES),
            P(None, AXES),
            P(AXES),
            P(AXES),
            P(),
            P(),
            P(),
        ),
        out_specs=P(None, None, AXES),
        check_vma=False,
    )
```

```python
import functools

import jax
import jax.numpy as jnp
from jax import lax
from jax.experimental import pallas as pl
from jax.experimental.pallas import tpu as pltpu
from jax.sharding import PartitionSpec as P

GRAVITY = 9.81
COURANT = 0.5
HIGH = lax.Precision.HIGHEST
LANES = 128
AXES = ("row", "col")
FACES = ((0, 1, 2, 3), (3, 6, 8, 9), (9, 7, 4, 0))
PACK = 40
LAID = 41
SENT = 37
WIDE = 32
STEP = 33
TALL = 16
PAD = 8

VMEM = pl.BlockSpec(memory_space=pltpu.VMEM)
HBM = pl.BlockSpec(memory_space=pltpu.HBM)
PARAMS = pltpu.CompilerParams(vmem_limit_bytes=48 * 1024 * 1024)


class Sizes:
    def __init__(self, cells):
        self.cells = cells
        self.blocks = cells // LANES
        self.margin = cells // 4 // LANES
        self.halo = self.margin + 1
        self.rows = -(-(self.blocks + 2 * self.halo) // 8) * 8
        self.tall = self.rows + 2 * PAD
        self.slots = 3 * self.blocks // 2
        self.keep = self.halo - self.margin


def fetch_all(pairs, sems):
    copies = [pltpu.make_async_copy(src, dst, sems.at[num]) for num, (src, dst) in enumerate(pairs)]
    for copy in copies:
        copy.start()
    return copies


def split_metric(metric_ref, spread, blocks):
    for block in range(blocks):
        spread[8 * block : 8 * block + 4, :] = metric_ref[:, LANES * block : LANES * (block + 1)]
    return [spread[pl.ds(comp, blocks, stride=8), :] for comp in range(4)]


def pack_kernel(
    sizes, state_hbm, depth_hbm, metric_hbm, partner_hbm, refine_hbm, stats_hbm, even_ref, odd_ref,
    stats_ref, state_even, state_odd, depth_ref, metric_ref, partner_ref, refine_ref, spread, sems, sem,
):
    blocks, halo = sizes.blocks, sizes.halo
    wide = LANES * halo
    late = blocks - halo
    even = (lax.axis_index(AXES) + 1) % 2 * late
    odd = late - even
    copies = fetch_all(
        (
            (depth_hbm, depth_ref),
            (metric_hbm, metric_ref),
            (refine_hbm, refine_ref),
            (partner_hbm, partner_ref),
            (state_hbm.at[:, :, pl.ds(pl.multiple_of(LANES * even, LANES), wide)], state_even),
            (state_hbm.at[:, :, pl.ds(pl.multiple_of(LANES * odd, LANES), wide)], state_odd),
        ),
        sems,
    )
    for copy in copies[:3]:
        copy.wait()
    rx, ry, sx, sy = split_metric(metric_ref, spread, blocks)
    depth = depth_ref[...]
    refine = refine_ref[...].astype(jnp.float32)
    faces = ((sx, sy), (rx + sx, ry + sy), (rx, ry))
    lengths = [jnp.sqrt(vx * vx + vy * vy) for vx, vy in faces]
    rate = jnp.sqrt(GRAVITY * depth) * jnp.maximum(jnp.maximum(lengths[0], lengths[1]), lengths[2])
    top = jnp.max(jnp.max(rate, axis=0, keepdims=True), axis=1, keepdims=True)
    extra = jnp.sum(jnp.sum(refine, axis=0, keepdims=True), axis=1, keepdims=True)
    shape = stats_ref.shape
    lane = lax.broadcasted_iota(jnp.int32, shape, 1)
    stats_ref[...] = jnp.where(
        lane < LANES // 2, jnp.broadcast_to(top, shape), jnp.broadcast_to(extra, shape)
    )
    sent = pltpu.make_async_copy(stats_ref, stats_hbm, sem)
    sent.start()
    for copy in copies[3:]:
        copy.wait()
    for ref, source, start in ((even_ref, state_even, even), (odd_ref, state_odd, odd)):
        pack_state(source, ref, halo, SENT, 3)
        at = pl.ds(start, halo)
        dense = [depth_ref[at, :]]
        dense += [spread[pl.ds(8 * start + comp, halo, stride=8), :] for comp in range(4)]
        dense += [partner_ref[at, :].astype(jnp.float32), refine_ref[at, :].astype(jnp.float32)]
        for num, value in enumerate(dense):
            ref[pl.ds(30 + num, halo, stride=SENT), :] = value
    sent.wait()


def pack_state(source, target, blocks, height, width):
    for block in range(blocks):
        for node in range(10):
            at = height * block + width * node
            target[at : at + 3, :] = source[node, :, LANES * block : LANES * (block + 1)]


def pair_index(partner):
    lane = lax.broadcasted_iota(jnp.int32, partner.shape, 1)
    target = lane + partner.astype(jnp.int32)
    return target & (LANES - 1), (target >= 0) & (target < LANES)


def lane_gather(values, index):
    return jnp.take_along_axis(values, index, axis=1, mode="promise_in_bounds")


def outer_values(load, index, inside):
    shape = index.shape
    lane = lax.broadcasted_iota(jnp.int32, shape, 1)

    def prev(item):
        return pltpu.roll(jnp.where(lane == LANES - 1, load(item, -1), load(item, 0)), 1, 1)

    def after(item):
        return pltpu.roll(jnp.where(lane == 0, load(item, 1), load(item, 0)), LANES - 1, 1)

    def across(item):
        other = jnp.where(lane < LANES // 2, load(item, 1), load(item, -1))
        return jnp.where(inside, lane_gather(load(item, 0), index), lane_gather(other, index))

    return prev, after, across


def wall_masks(sizes, start, place, count, partner):
    shape = partner.shape
    lane = lax.broadcasted_iota(jnp.int32, shape, 1)
    row = lax.broadcasted_iota(jnp.int32, shape, 0) + start
    first = (lane == 0) & (row == sizes.halo) & (place == 0)
    last = (lane == LANES - 1) & (row == sizes.halo + sizes.blocks - 1) & (place == count - 1)
    return first, last, partner == 0


def tendency(load, geo, walls, index, inside, operators):
    speed_sq, rx, ry, sx, sy = geo[:5]
    outer_sq, waves, ghosts = geo[5:8], geo[8:11], geo[11:14]
    own = [[load(10 * field + node, 0) for node in range(10)] for field in range(3)]
    eta, mom_x, mom_y = own
    flow_r = [-(rx * mom_x[b] + ry * mom_y[b]) for b in range(10)]
    flow_s = [-(sx * mom_x[b] + sy * mom_y[b]) for b in range(10)]
    half_r = (0.5 * rx, 0.5 * ry)
    half_s = (0.5 * sx, 0.5 * sy)
    vectors = (
        (-half_s[0], -half_s[1]),
        (half_r[0] + half_s[0], half_r[1] + half_s[1]),
        (-half_r[0], -half_r[1]),
    )
    fetch = outer_values(load, index, inside)
    jumps = ([], [], [])
    for face in range(3):
        vec_x, vec_y = vectors[face]
        theirs = FACES[(1, 0, 2)[face]]
        wall = walls[face]
        for j in range(4):
            node, match = FACES[face][j], theirs[3 - j]
            in_eta, in_x, in_y = eta[node], mom_x[node], mom_y[node]
            ext_eta, ext_x, ext_y = [fetch[face](10 * field + match) for field in range(3)]
            bounce = (in_x * vec_x + in_y * vec_y) * ghosts[face]
            d_eta = jnp.where(wall, 0.0, in_eta - ext_eta)
            d_x = jnp.where(wall, bounce * vec_x, in_x - ext_x)
            d_y = jnp.where(wall, bounce * vec_y, in_y - ext_y)
            head = jnp.where(wall, 0.0, speed_sq * in_eta - outer_sq[face] * ext_eta)
            jumps[0].append(d_x * vec_x + d_y * vec_y - waves[face] * d_eta)
            jumps[1].append(head * vec_x - waves[face] * d_x)
            jumps[2].append(head * vec_y - waves[face] * d_y)
    pull = (-speed_sq * rx, -speed_sq * ry)
    push = (-speed_sq * sx, -speed_sq * sy)
    out = [[None] * 10 for _ in range(3)]
    for a in range(10):
        total = along_r = along_s = None
        for b in range(10):
            d_r, d_s = operators[a // 4, a % 4 * 32 + b], operators[a // 4, a % 4 * 32 + 10 + b]
            term = d_r * flow_r[b] + d_s * flow_s[b]
            total = term if b == 0 else total + term
            along_r = d_r * eta[b] if b == 0 else along_r + d_r * eta[b]
            along_s = d_s * eta[b] if b == 0 else along_s + d_s * eta[b]
        sums = [total, pull[0] * along_r + push[0] * along_s, pull[1] * along_r + push[1] * along_s]
        for q in range(12):
            weight = operators[a // 4, a % 4 * 32 + 20 + q]
            for field in range(3):
                sums[field] = sums[field] + weight * jumps[field][q]
        for field in range(3):
            out[field][a] = sums[field]
    return [out[field][a] for field in range(3) for a in range(10)]


def child_matrix(prolong_ref):
    f32, bf16 = jnp.float32, jnp.bfloat16

    def number(shape, axis):
        return lax.broadcasted_iota(jnp.int32, shape, axis)

    both = jnp.concatenate([prolong_ref[:, 0, :], prolong_ref[:, 1, :]], axis=0)
    rounded = both.astype(bf16)
    rest = (both - rounded.astype(f32)).astype(bf16)
    shape = (10, WIDE)
    columns = (number(shape, 1) % 10 == number(shape, 0)).astype(bf16)
    shape = (2 * PACK, 20)
    rows = (number(shape, 0) // 4 == number(shape, 1)).astype(bf16)
    shape = (2 * PACK, WIDE)
    same = number(shape, 0) % 4 == number(shape, 1) // 10
    parts = []
    for matrix in (rounded, rest):
        spread = jnp.dot(matrix, columns, preferred_element_type=f32).astype(bf16)
        full = jnp.dot(rows, spread, preferred_element_type=f32)
        parts.append(jnp.where(same, full, 0.0))
    shape = (PACK, WIDE)
    same = (number(shape, 0) % 4 == number(shape, 1) // 10) & (number(shape, 0) // 4 == number(shape, 1) % 10)
    first = jnp.concatenate([parts[0], same.astype(f32)], axis=0)
    last = jnp.concatenate([parts[1], jnp.zeros(shape, f32)], axis=0)
    return jnp.concatenate([first, first, last], axis=1).astype(bf16)


def sum_children(sizes, refine, ends_ref, full_ref, lines_ref):
    slots, f32 = sizes.slots, jnp.float32
    counts = (1.0 + refine).astype(jnp.bfloat16)
    row_i = lax.broadcasted_iota(jnp.int32, (LANES, LANES), 0)
    col_i = lax.broadcasted_iota(jnp.int32, (LANES, LANES), 1)
    upper = (row_i <= col_i).astype(jnp.bfloat16)
    within = jnp.dot(counts, upper, preferred_element_type=f32)
    whole = jnp.dot(counts, jnp.ones((LANES, LANES), jnp.bfloat16), preferred_element_type=f32)
    row_s = lax.broadcasted_iota(jnp.int32, (slots, slots), 0)
    col_s = lax.broadcasted_iota(jnp.int32, (slots, slots), 1)
    lower = (col_s < row_s).astype(jnp.bfloat16)
    before = jnp.dot(lower, whole.astype(jnp.bfloat16), preferred_element_type=f32)
    before = before - before[sizes.margin : sizes.margin + 1, :]
    ends = 2.0 * (within + before) + refine
    high = jnp.floor(ends * (1.0 / 256.0))
    ends_ref[...] = jnp.concatenate([high, ends - 256.0 * high], axis=1).astype(jnp.bfloat16)
    full_ref[...] = before + whole
    ones = jnp.ones((8, LANES), jnp.bfloat16)
    sums = lax.dot_general(ones, counts, (((1,), (1,)), ((), ())), preferred_element_type=f32)
    gap = lax.broadcasted_iota(jnp.int32, (slots, LANES), 1) - lax.broadcasted_iota(jnp.int32, (slots, LANES), 0)
    lines = [
        jnp.dot(sums.astype(jnp.bfloat16), (gap >= least).astype(jnp.bfloat16), preferred_element_type=f32)
        for least in (2, 1, 0)
    ]
    own = lines[1][:, sizes.margin : sizes.margin + 1]
    for num in range(3):
        lines_ref[num] = lines[num] - own


def prep_kernel(
    sizes, state_hbm, depth_hbm, metric_hbm, partner_hbm, refine_hbm, diff_hbm, lift_hbm, prolong_hbm,
    cur, aux, weights, operators,
    state_ref, depth_ref, metric_ref, partner_ref, refine_ref, prolong_ref, diff_ref, lift_ref, spread, wide, sems,
):
    blocks = sizes.blocks
    copies = fetch_all(
        (
            (metric_hbm, metric_ref),
            (state_hbm, state_ref),
            (depth_hbm, depth_ref),
            (partner_hbm, partner_ref),
            (refine_hbm, refine_ref),
            (prolong_hbm, prolong_ref),
            (diff_hbm, diff_ref),
            (lift_hbm, lift_ref),
        ),
        sems,
    )
    for copy in copies:
        copy.wait()
    weights[...] = child_matrix(prolong_ref)
    rows = jnp.concatenate([diff_ref[:, 0, :], diff_ref[:, 1, :], lift_ref[...]], axis=1)
    rows = jnp.concatenate([rows, jnp.zeros((2, 32), jnp.float32)], axis=0)
    for row in range(3):
        for part in range(4):
            at = 4 * row + part
            operators[row : row + 1, 32 * part : 32 * part + 32] = rows[at : at + 1]
    metric = split_metric(metric_ref, spread, blocks)
    dense = [depth_ref[...], *metric, partner_ref[...].astype(jnp.float32), refine_ref[...].astype(jnp.float32)]
    for num in range(7):
        aux[num] = dense[num]
    pack_state(state_ref, wide, blocks, LAID, 4)
    for field in range(3):
        for node in range(10):
            cur[10 * field + node] = wide[pl.ds(4 * node + field, blocks, stride=LAID), :]


def first_kernel(
    sizes, cur_own, aux_own, weights_in, operators_in, odd_ref, even_ref,
    cur, rate_ref, twice_ref, weights, ends_ref, full_ref, lines_ref,
    geo_ref, aux, operators, sems,
):
    blocks, halo = sizes.blocks, sizes.halo
    top, bottom = PAD + halo, PAD + halo + blocks
    place = lax.axis_index(AXES)
    count = lax.axis_size(AXES)
    copies = fetch_all(((operators_in, operators),), sems)
    even = place % 2 == 0
    zero = jnp.minimum(place, 0)

    def set_halo(target, num, row):
        by_even = even_ref[pl.ds(row, halo, stride=SENT), :]
        by_odd = odd_ref[pl.ds(row, halo, stride=SENT), :]
        target[num, top - halo : top, :] = jnp.where(even, by_odd, by_even)
        target[num, pl.ds(zero + bottom, halo), :] = jnp.where(even, by_even, by_odd)

    for num in range(7):
        set_halo(aux, num, 30 + num)
        aux[num, pl.ds(zero + top, blocks), :] = aux_own[num]
    for field in range(3):
        for node in range(10):
            item = 10 * field + node
            set_halo(cur, item, 3 * node + field)
            cur[item, pl.ds(zero + top, blocks), :] = cur_own[item]

    weights[...] = weights_in[...]
    begin = PAD + sizes.keep
    sum_children(sizes, aux[6, pl.ds(zero + begin, sizes.slots), :], ends_ref, full_ref, lines_ref)
    for copy in copies:
        copy.wait()

    def step(start, height):
        base = PAD + start

        def rows(shift):
            return pl.ds(zero + (base + shift) if shift else base, height)

        def load_aux(item, shift):
            return aux[item, rows(shift), :]

        def load(item, shift):
            return cur[item, rows(shift), :]

        depth, rx, ry, sx, sy, partner = [load_aux(num, 0) for num in range(6)]
        index, inside = pair_index(partner)
        fetch = outer_values(load_aux, index, inside)
        walls = wall_masks(sizes, start, place, count, partner)
        speed_sq = GRAVITY * depth
        outer_sq = [jnp.where(walls[k], speed_sq, GRAVITY * fetch[k](0)) for k in range(3)]
        faces = ((sx, sy), (rx + sx, ry + sy), (rx, ry))
        squares = [vx * vx + vy * vy for vx, vy in faces]
        waves = [
            0.5 * jnp.sqrt(squares[k]) * jnp.sqrt(jnp.maximum(speed_sq, outer_sq[k])) for k in range(3)
        ]
        ghosts = [8.0 / squares[k] for k in range(3)]
        geo = [speed_sq, rx, ry, sx, sy, *outer_sq, *waves, *ghosts]
        rates = tendency(load, geo, walls, index, inside, operators)
        for num, value in enumerate([*geo, partner]):
            geo_ref[num, pl.ds(start, height), :] = value
        for item in range(30):
            rate_ref[item, pl.ds(base, height), :] = rates[item]

    def again(start, height):
        row = start + sizes.keep
        at = pl.ds(zero + row, height)

        def load(item, shift):
            return rate_ref[item, pl.ds(zero + (PAD + row + shift), height), :]

        geo = [geo_ref[num, at, :] for num in range(14)]
        partner = geo_ref[14, at, :]
        index, inside = pair_index(partner)
        walls = wall_masks(sizes, row, place, count, partner)
        rates = tendency(load, geo, walls, index, inside, operators)
        for item in range(30):
            twice_ref[item, pl.ds(start, height), :] = rates[item]

    def sweep(work, rows):
        for start in range(0, rows // TALL * TALL, TALL):
            work(start, TALL)

    for start in range(sizes.rows // TALL * TALL, sizes.rows, 8):
        step(start, 8)
    sweep(step, sizes.rows)
    for start in range(sizes.slots // TALL * TALL, sizes.slots, 8):
        again(start, 8)
    sweep(again, sizes.slots)


def refine_kernel(
    sizes, cur, rate_ref, twice_ref, weights, base_ref, full_ref, lines_ref, stats_ref, out_hbm,
    out_ref, place_v, place_s, wide, index_ref, out_sems, sem,
):
    slots, keep = sizes.slots, sizes.keep
    place = lax.axis_index(AXES)
    zero = jnp.minimum(place, 0)
    stats = stats_ref[...]
    half = LANES // 2
    row_n = lax.broadcasted_iota(jnp.int32, stats.shape, 0)
    top = jnp.max(stats, axis=0, keepdims=True)
    earlier = jnp.sum(jnp.where(row_n < place, stats, 0.0), axis=0, keepdims=True)
    left = lax.broadcasted_iota(jnp.int32, (1, LANES), 1) < half
    top = jnp.where(left, top, pltpu.roll(top, half, 1))
    earlier = jnp.where(left, pltpu.roll(earlier, half, 1), earlier)
    step = COURANT / top
    half_square = 0.5 * step * step
    start = earlier - (place * (sizes.cells // 2)).astype(jnp.float32)
    first_slot = LANES * lax.broadcasted_iota(jnp.int32, (slots, LANES), 1).astype(jnp.float32)
    lead = jnp.sum((full_ref[...] + start <= first_slot).astype(jnp.float32), axis=0, keepdims=True)
    lead = jnp.clip(lead.astype(jnp.int32), 0, slots - 1)
    place_v[...] = lead
    copy = pltpu.make_async_copy(place_v, place_s, sem)
    copy.start()
    for item in range(30):
        now = pl.ds(zero + (PAD + keep), slots)
        value = cur[item, now, :] + step * rate_ref[item, now, :] + half_square * twice_ref[item]
        wide[pl.ds(item, slots, stride=STEP), :] = value
    for item in (30, 31):
        wide[pl.ds(item, slots + 1, stride=STEP), :] = jnp.zeros((slots + 1, LANES), jnp.float32)
    slot_start = LANES * lax.broadcasted_iota(jnp.int32, (slots, LANES), 0).astype(jnp.float32)
    begun = [lines_ref[num, 0:1, :] + start <= slot_start for num in range(3)]
    halves = [
        jnp.dot(
            (begun[num] & ~begun[num + 1]).astype(jnp.bfloat16)[:, :slots],
            base_ref[...],
            preferred_element_type=jnp.float32,
        )
        for num in (1, 0)
    ]
    near, far = [256.0 * x[:, :LANES] + (x[:, LANES:] + 2.0 * start) for x in halves]
    lane = lax.broadcasted_iota(jnp.int32, (slots, LANES), 1)
    slot_no = LANES * lax.broadcasted_iota(jnp.int32, (slots, LANES), 0) + lane
    goal = (2 * slot_no + 1).astype(jnp.float32)
    beyond = jnp.broadcast_to(near[:, LANES - 1 :], (slots, LANES)) <= goal

    def pick(index):
        return jnp.where(beyond, lane_gather(far, index), lane_gather(near, index))

    found = jnp.zeros((slots, LANES), jnp.int32)
    for ways, size in ((8, LANES // 8), (4, LANES // 32), (4, LANES // 128)):
        passed = [(pick(found + (probe * size - 1)) <= goal).astype(jnp.int32) for probe in range(1, ways)]
        found = found + size * sum(passed)
    mine = pick(found).astype(jnp.int32)
    split = mine & 1
    begin = (mine >> 1) - 1 - split
    kind = split * (1 + slot_no - begin)
    index_ref[0] = found.astype(jnp.float32)
    index_ref[1] = kind.astype(jnp.float32)
    index_ref[2] = (lane < jnp.broadcast_to(found[:, 0:1], (slots, LANES))).astype(jnp.float32)
    copy.wait()
    matrix = weights[...]
    results = []
    parts = [(at, 16) for at in range(0, slots - 16, 16)]
    parts += [(slots - 16, 8), (slots - 8, 4), (slots - 4, 4)]
    for part, (begin_at, height) in enumerate(parts):
        span = slice(LANES * begin_at, LANES * (begin_at + height))
        columns = []
        for slot in range(begin_at, begin_at + height):
            lead_at = place_s[0, slot] * STEP
            lane_idx = jnp.broadcast_to(index_ref[0, slot : slot + 1, :], (8, LANES)).astype(jnp.int32)
            ahead = jnp.broadcast_to(index_ref[2, slot : slot + 1, :], (8, LANES)) > 0.5
            tiles = []
            for row in range(0, WIDE, 8):
                one = wide[pl.ds(lead_at + row, 8), :]
                two = wide[pl.ds(lead_at + STEP + row, 8), :]
                tiles.append(lane_gather(jnp.where(ahead, two, one), lane_idx))
            columns.append(jnp.concatenate(tiles, axis=0))
        values = jnp.concatenate(columns, axis=1)
        high = values.astype(jnp.bfloat16)
        low = (values - high.astype(jnp.float32)).astype(jnp.bfloat16)
        stack = jnp.concatenate([high, low, high], axis=0)
        children = jnp.dot(matrix, stack, preferred_element_type=jnp.float32)
        for sub in range(height):
            slot = begin_at + sub
            cut = slice(LANES * sub, LANES * (sub + 1))
            tag = jnp.broadcast_to(index_ref[1, slot : slot + 1, :], (PACK, LANES))
            value = jnp.where(
                tag < 0.5,
                children[2 * PACK :, cut],
                jnp.where(tag < 1.5, children[:PACK, cut], children[PACK : 2 * PACK, cut]),
            )
            for node in range(10):
                out_ref[node, :, LANES * slot : LANES * (slot + 1)] = value[4 * node : 4 * node + 3]
        result = pltpu.make_async_copy(out_ref.at[:, :, span], out_hbm.at[:, :, span], out_sems.at[part])
        result.start()
        results.append(result)
    for result in results:
        result.wait()


def swaps(start, count):
    pairs = [(i, i + 1) for i in range(start, count - 1, 2)]
    return pairs + [(j, i) for i, j in pairs]


def shards(state, depth, metric, partner, refine, diff_ops, lift, prolong):
    sizes = Sizes(state.shape[2])
    count = lax.axis_size(AXES)
    blocks, rows, slots, halo = sizes.blocks, sizes.rows, sizes.slots, sizes.halo
    depth, partner, refine = [x.reshape(blocks, LANES) for x in (depth, partner, refine)]
    state, diff_ops, prolong = [jnp.transpose(x, (1, 0, 2)) for x in (state, diff_ops, prolong)]
    state, depth, metric, partner, refine, diff_ops, lift, prolong = [
        pltpu.with_memory_space_constraint(x, pltpu.HBM)
        for x in (state, depth, metric, partner, refine, diff_ops, lift, prolong)
    ]
    f32, i32 = jnp.float32, jnp.int32
    packed = jax.ShapeDtypeStruct((SENT * halo, LANES), f32)
    dense = [
        pltpu.VMEM((blocks, LANES), f32),
        pltpu.VMEM(metric.shape, f32),
        pltpu.VMEM((blocks, LANES), i32),
        pltpu.VMEM((blocks, LANES), i32),
    ]
    stats, even, odd = pl.pallas_call(
        functools.partial(pack_kernel, sizes),
        name="pack",
        out_shape=(jax.ShapeDtypeStruct((count, LANES), f32), packed, packed),
        in_specs=[HBM] * 5,
        out_specs=(HBM, VMEM, VMEM),
        scratch_shapes=[
            pltpu.VMEM((count, LANES), f32),
            pltpu.VMEM((10, 3, LANES * halo), f32),
            pltpu.VMEM((10, 3, LANES * halo), f32),
            *dense,
            pltpu.VMEM((8 * blocks, LANES), f32),
            pltpu.SemaphoreType.DMA((6,)),
            pltpu.SemaphoreType.DMA,
        ],
        compiler_params=PARAMS,
    )(state, depth, metric, partner, refine)
    odd = lax.ppermute(odd, AXES, swaps(1, count))
    even = lax.ppermute(even, AXES, swaps(0, count))
    stats = lax.all_to_all(stats, AXES, 0, 0, tiled=True)
    even, odd, stats = [pltpu.with_memory_space_constraint(x, pltpu.VMEM) for x in (even, odd, stats)]
    cur, aux, weights, operators = pl.pallas_call(
        functools.partial(prep_kernel, sizes),
        name="lay_out",
        cost_estimate=pl.CostEstimate(flops=1 << 24, transcendentals=1 << 16, bytes_accessed=1 << 24),
        out_shape=(
            jax.ShapeDtypeStruct((30, blocks, LANES), f32),
            jax.ShapeDtypeStruct((7, blocks, LANES), f32),
            jax.ShapeDtypeStruct((3 * PACK, 3 * WIDE), jnp.bfloat16),
            jax.ShapeDtypeStruct((3, LANES), f32),
        ),
        in_specs=[HBM] * 8,
        out_specs=(VMEM,) * 4,
        scratch_shapes=[
            pltpu.VMEM(state.shape, f32),
            *dense,
            pltpu.VMEM(prolong.shape, f32),
            pltpu.VMEM(diff_ops.shape, f32),
            pltpu.VMEM(lift.shape, f32),
            pltpu.VMEM((8 * blocks, LANES), f32),
            pltpu.VMEM((LAID * blocks, LANES), f32),
            pltpu.SemaphoreType.DMA((8,)),
        ],
        compiler_params=PARAMS,
    )(state, depth, metric, partner, refine, diff_ops, lift, prolong)
    cur, rates, twice, weights, ends, full, lines = pl.pallas_call(
        functools.partial(first_kernel, sizes),
        name="rates_twice",
        cost_estimate=pl.CostEstimate(flops=1024, transcendentals=0, bytes_accessed=1024),
        out_shape=(
            jax.ShapeDtypeStruct((30, sizes.tall, LANES), f32),
            jax.ShapeDtypeStruct((30, sizes.tall, LANES), f32),
            jax.ShapeDtypeStruct((30, slots, LANES), f32),
            jax.ShapeDtypeStruct((3 * PACK, 3 * WIDE), jnp.bfloat16),
            jax.ShapeDtypeStruct((slots, 2 * LANES), jnp.bfloat16),
            jax.ShapeDtypeStruct((slots, LANES), f32),
            jax.ShapeDtypeStruct((3, 8, LANES), f32),
        ),
        in_specs=[VMEM] * 6,
        out_specs=(VMEM,) * 7,
        scratch_shapes=[
            pltpu.VMEM((15, rows, LANES), f32),
            pltpu.VMEM((7, sizes.tall, LANES), f32),
            pltpu.SMEM((3, LANES), f32),
            pltpu.SemaphoreType.DMA((1,)),
        ],
        compiler_params=PARAMS,
    )(cur, aux, weights, operators, odd, even)
    refined = pl.pallas_call(
        functools.partial(refine_kernel, sizes),
        name="sum_and_refine",
        out_shape=jax.ShapeDtypeStruct((10, 3, LANES * slots), f32),
        in_specs=[VMEM] * 8,
        out_specs=HBM,
        scratch_shapes=[
            pltpu.VMEM((10, 3, LANES * slots), f32),
            pltpu.VMEM((1, LANES), i32),
            pltpu.SMEM((1, LANES), i32),
            pltpu.VMEM((STEP * (slots + 1), LANES), f32),
            pltpu.VMEM((3, slots, LANES), f32),
            pltpu.SemaphoreType.DMA((slots // 8 + 1,)),
            pltpu.SemaphoreType.DMA,
        ],
        compiler_params=PARAMS,
    )(cur, rates, twice, weights, ends, full, lines, stats)
    return jnp.transpose(refined, (1, 0, 2))


def solution(mesh):
    return jax.shard_map(
        shards,
        mesh=mesh,
        in_specs=(
            P(None, None, AXES),
            P(AXES),
            P(None, AXES),
            P(AXES),
            P(AXES),
            P(),
            P(),
            P(),
        ),
        out_specs=P(None, None, AXES),
        check_vma=False,
    )
```

```python
import functools

import jax
import jax.numpy as jnp
from jax import lax
from jax.experimental import pallas as pl
from jax.experimental.pallas import tpu as pltpu
from jax.sharding import PartitionSpec as P

GRAVITY = 9.81
COURANT = 0.5
HIGH = lax.Precision.HIGHEST
LANES = 128
AXES = ("row", "col")
FACES = ((0, 1, 2, 3), (3, 6, 8, 9), (9, 7, 4, 0))
PACK = 40
LAID = 41
SENT = 37
WIDE = 32
STEP = 33
TALL = 16
PAD = 8

VMEM = pl.BlockSpec(memory_space=pltpu.VMEM)
HBM = pl.BlockSpec(memory_space=pltpu.HBM)
PARAMS = pltpu.CompilerParams(vmem_limit_bytes=48 * 1024 * 1024)


class Sizes:
    def __init__(self, cells):
        self.cells = cells
        self.blocks = cells // LANES
        self.margin = cells // 4 // LANES
        self.halo = self.margin + 1
        self.rows = -(-(self.blocks + 2 * self.halo) // 8) * 8
        self.tall = self.rows + 2 * PAD
        self.slots = 3 * self.blocks // 2
        self.keep = self.halo - self.margin


def fetch_all(pairs, sems):
    copies = [pltpu.make_async_copy(src, dst, sems.at[num]) for num, (src, dst) in enumerate(pairs)]
    for copy in copies:
        copy.start()
    return copies


def split_metric(metric_ref, spread, blocks):
    for block in range(blocks):
        spread[8 * block : 8 * block + 4, :] = metric_ref[:, LANES * block : LANES * (block + 1)]
    return [spread[pl.ds(comp, blocks, stride=8), :] for comp in range(4)]


def pack_kernel(
    sizes, state_hbm, depth_hbm, metric_hbm, partner_hbm, refine_hbm, stats_hbm, even_ref, odd_ref,
    stats_ref, state_even, state_odd, depth_ref, metric_ref, partner_ref, refine_ref, spread, sems, sem,
):
    blocks, halo = sizes.blocks, sizes.halo
    wide = LANES * halo
    late = blocks - halo
    even = (lax.axis_index(AXES) + 1) % 2 * late
    odd = late - even
    copies = fetch_all(
        (
            (depth_hbm, depth_ref),
            (metric_hbm, metric_ref),
            (refine_hbm, refine_ref),
            (partner_hbm, partner_ref),
            (state_hbm.at[:, :, pl.ds(pl.multiple_of(LANES * even, LANES), wide)], state_even),
            (state_hbm.at[:, :, pl.ds(pl.multiple_of(LANES * odd, LANES), wide)], state_odd),
        ),
        sems,
    )
    for copy in copies[:3]:
        copy.wait()
    rx, ry, sx, sy = split_metric(metric_ref, spread, blocks)
    depth = depth_ref[...]
    refine = refine_ref[...].astype(jnp.float32)
    faces = ((sx, sy), (rx + sx, ry + sy), (rx, ry))
    lengths = [jnp.sqrt(vx * vx + vy * vy) for vx, vy in faces]
    rate = jnp.sqrt(GRAVITY * depth) * jnp.maximum(jnp.maximum(lengths[0], lengths[1]), lengths[2])
    top = jnp.max(jnp.max(rate, axis=0, keepdims=True), axis=1, keepdims=True)
    extra = jnp.sum(jnp.sum(refine, axis=0, keepdims=True), axis=1, keepdims=True)
    shape = stats_ref.shape
    lane = lax.broadcasted_iota(jnp.int32, shape, 1)
    stats_ref[...] = jnp.where(
        lane < LANES // 2, jnp.broadcast_to(top, shape), jnp.broadcast_to(extra, shape)
    )
    sent = pltpu.make_async_copy(stats_ref, stats_hbm, sem)
    sent.start()
    for copy in copies[3:]:
        copy.wait()
    for ref, source, start in ((even_ref, state_even, even), (odd_ref, state_odd, odd)):
        pack_state(source, ref, halo, SENT, 3)
        at = pl.ds(start, halo)
        dense = [depth_ref[at, :]]
        dense += [spread[pl.ds(8 * start + comp, halo, stride=8), :] for comp in range(4)]
        dense += [partner_ref[at, :].astype(jnp.float32), refine_ref[at, :].astype(jnp.float32)]
        for num, value in enumerate(dense):
            ref[pl.ds(30 + num, halo, stride=SENT), :] = value
    sent.wait()


def pack_state(source, target, blocks, height, width):
    for block in range(blocks):
        for node in range(10):
            at = height * block + width * node
            target[at : at + 3, :] = source[node, :, LANES * block : LANES * (block + 1)]


def pair_index(partner):
    lane = lax.broadcasted_iota(jnp.int32, partner.shape, 1)
    target = lane + partner.astype(jnp.int32)
    return target & (LANES - 1), (target >= 0) & (target < LANES)


def lane_gather(values, index):
    return jnp.take_along_axis(values, index, axis=1, mode="promise_in_bounds")


def outer_values(load, index, inside):
    shape = index.shape
    lane = lax.broadcasted_iota(jnp.int32, shape, 1)

    def prev(item):
        return pltpu.roll(jnp.where(lane == LANES - 1, load(item, -1), load(item, 0)), 1, 1)

    def after(item):
        return pltpu.roll(jnp.where(lane == 0, load(item, 1), load(item, 0)), LANES - 1, 1)

    def across(item):
        other = jnp.where(lane < LANES // 2, load(item, 1), load(item, -1))
        return jnp.where(inside, lane_gather(load(item, 0), index), lane_gather(other, index))

    return prev, after, across


def wall_masks(sizes, start, place, count, partner):
    shape = partner.shape
    lane = lax.broadcasted_iota(jnp.int32, shape, 1)
    row = lax.broadcasted_iota(jnp.int32, shape, 0) + start
    first = (lane == 0) & (row == sizes.halo) & (place == 0)
    last = (lane == LANES - 1) & (row == sizes.halo + sizes.blocks - 1) & (place == count - 1)
    return first, last, partner == 0


def tendency(load, geo, walls, index, inside, operators):
    speed_sq, rx, ry, sx, sy = geo[:5]
    outer_sq, waves, ghosts = geo[5:8], geo[8:11], geo[11:14]
    own = [[load(10 * field + node, 0) for node in range(10)] for field in range(3)]
    eta, mom_x, mom_y = own
    flow_r = [-(rx * mom_x[b] + ry * mom_y[b]) for b in range(10)]
    flow_s = [-(sx * mom_x[b] + sy * mom_y[b]) for b in range(10)]
    half_r = (0.5 * rx, 0.5 * ry)
    half_s = (0.5 * sx, 0.5 * sy)
    vectors = (
        (-half_s[0], -half_s[1]),
        (half_r[0] + half_s[0], half_r[1] + half_s[1]),
        (-half_r[0], -half_r[1]),
    )
    fetch = outer_values(load, index, inside)
    jumps = ([], [], [])
    for face in range(3):
        vec_x, vec_y = vectors[face]
        theirs = FACES[(1, 0, 2)[face]]
        wall = walls[face]
        for j in range(4):
            node, match = FACES[face][j], theirs[3 - j]
            in_eta, in_x, in_y = eta[node], mom_x[node], mom_y[node]
            ext_eta, ext_x, ext_y = [fetch[face](10 * field + match) for field in range(3)]
            bounce = (in_x * vec_x + in_y * vec_y) * ghosts[face]
            d_eta = jnp.where(wall, 0.0, in_eta - ext_eta)
            d_x = jnp.where(wall, bounce * vec_x, in_x - ext_x)
            d_y = jnp.where(wall, bounce * vec_y, in_y - ext_y)
            head = jnp.where(wall, 0.0, speed_sq * in_eta - outer_sq[face] * ext_eta)
            jumps[0].append(d_x * vec_x + d_y * vec_y - waves[face] * d_eta)
            jumps[1].append(head * vec_x - waves[face] * d_x)
            jumps[2].append(head * vec_y - waves[face] * d_y)
    pull = (-speed_sq * rx, -speed_sq * ry)
    push = (-speed_sq * sx, -speed_sq * sy)
    out = [[None] * 10 for _ in range(3)]
    for a in range(10):
        total = along_r = along_s = None
        for b in range(10):
            d_r, d_s = operators[a // 4, a % 4 * 32 + b], operators[a // 4, a % 4 * 32 + 10 + b]
            term = d_r * flow_r[b] + d_s * flow_s[b]
            total = term if b == 0 else total + term
            along_r = d_r * eta[b] if b == 0 else along_r + d_r * eta[b]
            along_s = d_s * eta[b] if b == 0 else along_s + d_s * eta[b]
        sums = [total, pull[0] * along_r + push[0] * along_s, pull[1] * along_r + push[1] * along_s]
        for q in range(12):
            weight = operators[a // 4, a % 4 * 32 + 20 + q]
            for field in range(3):
                sums[field] = sums[field] + weight * jumps[field][q]
        for field in range(3):
            out[field][a] = sums[field]
    return [out[field][a] for field in range(3) for a in range(10)]


def child_matrix(prolong_ref):
    f32, bf16 = jnp.float32, jnp.bfloat16

    def number(shape, axis):
        return lax.broadcasted_iota(jnp.int32, shape, axis)

    both = jnp.concatenate([prolong_ref[:, 0, :], prolong_ref[:, 1, :]], axis=0)
    rounded = both.astype(bf16)
    rest = (both - rounded.astype(f32)).astype(bf16)
    shape = (10, WIDE)
    columns = (number(shape, 1) % 10 == number(shape, 0)).astype(bf16)
    shape = (2 * PACK, 20)
    rows = (number(shape, 0) // 4 == number(shape, 1)).astype(bf16)
    shape = (2 * PACK, WIDE)
    same = number(shape, 0) % 4 == number(shape, 1) // 10
    parts = []
    for matrix in (rounded, rest):
        spread = jnp.dot(matrix, columns, preferred_element_type=f32).astype(bf16)
        full = jnp.dot(rows, spread, preferred_element_type=f32)
        parts.append(jnp.where(same, full, 0.0))
    shape = (PACK, WIDE)
    same = (number(shape, 0) % 4 == number(shape, 1) // 10) & (number(shape, 0) // 4 == number(shape, 1) % 10)
    first = jnp.concatenate([parts[0], same.astype(f32)], axis=0)
    last = jnp.concatenate([parts[1], jnp.zeros(shape, f32)], axis=0)
    return jnp.concatenate([first, first, last], axis=1).astype(bf16)


def sum_children(sizes, refine, ends_ref, full_ref, lines_ref):
    slots, f32 = sizes.slots, jnp.float32
    counts = (1.0 + refine).astype(jnp.bfloat16)
    row_i = lax.broadcasted_iota(jnp.int32, (LANES, LANES), 0)
    col_i = lax.broadcasted_iota(jnp.int32, (LANES, LANES), 1)
    upper = (row_i <= col_i).astype(jnp.bfloat16)
    within = jnp.dot(counts, upper, preferred_element_type=f32)
    whole = jnp.dot(counts, jnp.ones((LANES, LANES), jnp.bfloat16), preferred_element_type=f32)
    row_s = lax.broadcasted_iota(jnp.int32, (slots, slots), 0)
    col_s = lax.broadcasted_iota(jnp.int32, (slots, slots), 1)
    lower = (col_s < row_s).astype(jnp.bfloat16)
    before = jnp.dot(lower, whole.astype(jnp.bfloat16), preferred_element_type=f32)
    before = before - before[sizes.margin : sizes.margin + 1, :]
    ends = 2.0 * (within + before) + refine
    high = jnp.floor(ends * (1.0 / 256.0))
    ends_ref[...] = jnp.concatenate([high, ends - 256.0 * high], axis=1).astype(jnp.bfloat16)
    full_ref[...] = before + whole
    ones = jnp.ones((8, LANES), jnp.bfloat16)
    sums = lax.dot_general(ones, counts, (((1,), (1,)), ((), ())), preferred_element_type=f32)
    gap = lax.broadcasted_iota(jnp.int32, (slots, LANES), 1) - lax.broadcasted_iota(jnp.int32, (slots, LANES), 0)
    lines = [
        jnp.dot(sums.astype(jnp.bfloat16), (gap >= least).astype(jnp.bfloat16), preferred_element_type=f32)
        for least in (2, 1, 0)
    ]
    own = lines[1][:, sizes.margin : sizes.margin + 1]
    for num in range(3):
        lines_ref[num] = lines[num] - own


def prep_kernel(
    sizes, state_hbm, depth_hbm, metric_hbm, partner_hbm, refine_hbm, diff_hbm, lift_hbm, prolong_hbm,
    cur, aux, weights, operators,
    state_ref, depth_ref, metric_ref, partner_ref, refine_ref, prolong_ref, diff_ref, lift_ref, spread, wide, sems,
):
    blocks = sizes.blocks
    copies = fetch_all(
        (
            (metric_hbm, metric_ref),
            (state_hbm, state_ref),
            (depth_hbm, depth_ref),
            (partner_hbm, partner_ref),
            (refine_hbm, refine_ref),
            (prolong_hbm, prolong_ref),
            (diff_hbm, diff_ref),
            (lift_hbm, lift_ref),
        ),
        sems,
    )
    for copy in copies:
        copy.wait()
    weights[...] = child_matrix(prolong_ref)
    rows = jnp.concatenate([diff_ref[:, 0, :], diff_ref[:, 1, :], lift_ref[...]], axis=1)
    rows = jnp.concatenate([rows, jnp.zeros((2, 32), jnp.float32)], axis=0)
    for row in range(3):
        for part in range(4):
            at = 4 * row + part
            operators[row : row + 1, 32 * part : 32 * part + 32] = rows[at : at + 1]
    metric = split_metric(metric_ref, spread, blocks)
    dense = [depth_ref[...], *metric, partner_ref[...].astype(jnp.float32), refine_ref[...].astype(jnp.float32)]
    for num in range(7):
        aux[num] = dense[num]
    pack_state(state_ref, wide, blocks, LAID, 4)
    for field in range(3):
        for node in range(10):
            cur[10 * field + node] = wide[pl.ds(4 * node + field, blocks, stride=LAID), :]


def first_kernel(
    sizes, cur_own, aux_own, weights_in, operators_in, odd_ref, even_ref,
    cur, rate_ref, twice_ref, weights, ends_ref, full_ref, lines_ref,
    geo_ref, aux, operators, sems,
):
    blocks, halo = sizes.blocks, sizes.halo
    top, bottom = PAD + halo, PAD + halo + blocks
    place = lax.axis_index(AXES)
    count = lax.axis_size(AXES)
    copies = fetch_all(((operators_in, operators),), sems)
    even = place % 2 == 0
    zero = jnp.minimum(place, 0)

    def set_halo(target, num, row):
        by_even = even_ref[pl.ds(row, halo, stride=SENT), :]
        by_odd = odd_ref[pl.ds(row, halo, stride=SENT), :]
        target[num, top - halo : top, :] = jnp.where(even, by_odd, by_even)
        target[num, pl.ds(zero + bottom, halo), :] = jnp.where(even, by_even, by_odd)

    for num in range(7):
        set_halo(aux, num, 30 + num)
        aux[num, pl.ds(zero + top, blocks), :] = aux_own[num]
    for field in range(3):
        for node in range(10):
            item = 10 * field + node
            set_halo(cur, item, 3 * node + field)
            cur[item, pl.ds(zero + top, blocks), :] = cur_own[item]

    weights[...] = weights_in[...]
    begin = PAD + sizes.keep
    sum_children(sizes, aux[6, pl.ds(zero + begin, sizes.slots), :], ends_ref, full_ref, lines_ref)
    for copy in copies:
        copy.wait()

    def step(start, height):
        base = PAD + start

        def rows(shift):
            return pl.ds(zero + (base + shift) if shift else base, height)

        def load_aux(item, shift):
            return aux[item, rows(shift), :]

        def load(item, shift):
            return cur[item, rows(shift), :]

        depth, rx, ry, sx, sy, partner = [load_aux(num, 0) for num in range(6)]
        index, inside = pair_index(partner)
        fetch = outer_values(load_aux, index, inside)
        walls = wall_masks(sizes, start, place, count, partner)
        speed_sq = GRAVITY * depth
        outer_sq = [jnp.where(walls[k], speed_sq, GRAVITY * fetch[k](0)) for k in range(3)]
        faces = ((sx, sy), (rx + sx, ry + sy), (rx, ry))
        squares = [vx * vx + vy * vy for vx, vy in faces]
        waves = [
            0.5 * jnp.sqrt(squares[k]) * jnp.sqrt(jnp.maximum(speed_sq, outer_sq[k])) for k in range(3)
        ]
        ghosts = [8.0 / squares[k] for k in range(3)]
        geo = [speed_sq, rx, ry, sx, sy, *outer_sq, *waves, *ghosts]
        rates = tendency(load, geo, walls, index, inside, operators)
        for num, value in enumerate([*geo, partner]):
            geo_ref[num, pl.ds(start, height), :] = value
        for item in range(30):
            rate_ref[item, pl.ds(base, height), :] = rates[item]

    def again(start, height):
        row = start + sizes.keep
        at = pl.ds(zero + row, height)

        def load(item, shift):
            return rate_ref[item, pl.ds(zero + (PAD + row + shift), height), :]

        geo = [geo_ref[num, at, :] for num in range(14)]
        partner = geo_ref[14, at, :]
        index, inside = pair_index(partner)
        walls = wall_masks(sizes, row, place, count, partner)
        rates = tendency(load, geo, walls, index, inside, operators)
        for item in range(30):
            twice_ref[item, pl.ds(start, height), :] = rates[item]

    def sweep(work, rows):
        for start in range(0, rows // TALL * TALL, TALL):
            work(start, TALL)

    for start in range(sizes.rows // TALL * TALL, sizes.rows, 8):
        step(start, 8)
    sweep(step, sizes.rows)
    for start in range(sizes.slots // TALL * TALL, sizes.slots, 8):
        again(start, 8)
    sweep(again, sizes.slots)


def refine_kernel(
    sizes, cur, rate_ref, twice_ref, weights, base_ref, full_ref, lines_ref, stats_ref, out_hbm,
    out_ref, place_v, place_s, wide, index_ref, out_sems, sem,
):
    slots, keep = sizes.slots, sizes.keep
    place = lax.axis_index(AXES)
    zero = jnp.minimum(place, 0)
    stats = stats_ref[...]
    half = LANES // 2
    row_n = lax.broadcasted_iota(jnp.int32, stats.shape, 0)
    top = jnp.max(stats, axis=0, keepdims=True)
    earlier = jnp.sum(jnp.where(row_n < place, stats, 0.0), axis=0, keepdims=True)
    left = lax.broadcasted_iota(jnp.int32, (1, LANES), 1) < half
    top = jnp.where(left, top, pltpu.roll(top, half, 1))
    earlier = jnp.where(left, pltpu.roll(earlier, half, 1), earlier)
    step = COURANT / top
    half_square = 0.5 * step * step
    start = earlier - (place * (sizes.cells // 2)).astype(jnp.float32)
    first_slot = LANES * lax.broadcasted_iota(jnp.int32, (slots, LANES), 1).astype(jnp.float32)
    lead = jnp.sum((full_ref[...] + start <= first_slot).astype(jnp.float32), axis=0, keepdims=True)
    lead = jnp.clip(lead.astype(jnp.int32), 0, slots - 1)
    place_v[...] = lead
    copy = pltpu.make_async_copy(place_v, place_s, sem)
    copy.start()
    for item in range(30):
        now = pl.ds(zero + (PAD + keep), slots)
        value = cur[item, now, :] + step * rate_ref[item, now, :] + half_square * twice_ref[item]
        wide[pl.ds(item, slots, stride=STEP), :] = value
    for item in (30, 31):
        wide[pl.ds(item, slots + 1, stride=STEP), :] = jnp.zeros((slots + 1, LANES), jnp.float32)
    slot_start = LANES * lax.broadcasted_iota(jnp.int32, (slots, LANES), 0).astype(jnp.float32)
    begun = [lines_ref[num, 0:1, :] + start <= slot_start for num in range(3)]
    halves = [
        jnp.dot(
            (begun[num] & ~begun[num + 1]).astype(jnp.bfloat16)[:, :slots],
            base_ref[...],
            preferred_element_type=jnp.float32,
        )
        for num in (1, 0)
    ]
    near, far = [256.0 * x[:, :LANES] + (x[:, LANES:] + 2.0 * start) for x in halves]
    lane = lax.broadcasted_iota(jnp.int32, (slots, LANES), 1)
    slot_no = LANES * lax.broadcasted_iota(jnp.int32, (slots, LANES), 0) + lane
    goal = (2 * slot_no + 1).astype(jnp.float32)
    beyond = jnp.broadcast_to(near[:, LANES - 1 :], (slots, LANES)) <= goal

    def pick(index):
        return jnp.where(beyond, lane_gather(far, index), lane_gather(near, index))

    found = jnp.zeros((slots, LANES), jnp.int32)
    for ways, size in ((8, LANES // 8), (4, LANES // 32), (4, LANES // 128)):
        passed = [(pick(found + (probe * size - 1)) <= goal).astype(jnp.int32) for probe in range(1, ways)]
        found = found + size * sum(passed)
    mine = pick(found).astype(jnp.int32)
    split = mine & 1
    begin = (mine >> 1) - 1 - split
    kind = split * (1 + slot_no - begin)
    index_ref[0] = found.astype(jnp.float32)
    index_ref[1] = kind.astype(jnp.float32)
    index_ref[2] = (lane < jnp.broadcast_to(found[:, 0:1], (slots, LANES))).astype(jnp.float32)
    copy.wait()
    matrix = weights[...]
    results = []
    parts = [(at, 16) for at in range(0, slots - 16, 16)]
    parts += [(slots - 16, 8), (slots - 8, 4), (slots - 4, 4)]
    for part, (begin_at, height) in enumerate(parts):
        span = slice(LANES * begin_at, LANES * (begin_at + height))
        columns = []
        for slot in range(begin_at, begin_at + height):
            lead_at = place_s[0, slot] * STEP
            lane_idx = jnp.broadcast_to(index_ref[0, slot : slot + 1, :], (8, LANES)).astype(jnp.int32)
            ahead = jnp.broadcast_to(index_ref[2, slot : slot + 1, :], (8, LANES)) > 0.5
            tiles = []
            for row in range(0, WIDE, 8):
                one = wide[pl.ds(lead_at + row, 8), :]
                two = wide[pl.ds(lead_at + STEP + row, 8), :]
                tiles.append(lane_gather(jnp.where(ahead, two, one), lane_idx))
            columns.append(jnp.concatenate(tiles, axis=0))
        values = jnp.concatenate(columns, axis=1)
        high = values.astype(jnp.bfloat16)
        low = (values - high.astype(jnp.float32)).astype(jnp.bfloat16)
        stack = jnp.concatenate([high, low, high], axis=0)
        children = jnp.dot(matrix, stack, preferred_element_type=jnp.float32)
        for sub in range(height):
            slot = begin_at + sub
            cut = slice(LANES * sub, LANES * (sub + 1))
            tag = jnp.broadcast_to(index_ref[1, slot : slot + 1, :], (8, LANES))
            plain, earlier_child = tag < 0.5, tag < 1.5
            for row in range(0, PACK, 8):
                one, two, copied = [children[PACK * k + row : PACK * k + row + 8, cut] for k in range(3)]
                value = jnp.where(plain, copied, jnp.where(earlier_child, one, two))
                for half_row in range(2):
                    node = row // 4 + half_row
                    out_ref[node, :, LANES * slot : LANES * (slot + 1)] = value[4 * half_row : 4 * half_row + 3]
        result = pltpu.make_async_copy(out_ref.at[:, :, span], out_hbm.at[:, :, span], out_sems.at[part])
        result.start()
        results.append(result)
    for result in results:
        result.wait()


def swaps(start, count):
    pairs = [(i, i + 1) for i in range(start, count - 1, 2)]
    return pairs + [(j, i) for i, j in pairs]


def shards(state, depth, metric, partner, refine, diff_ops, lift, prolong):
    sizes = Sizes(state.shape[2])
    count = lax.axis_size(AXES)
    blocks, rows, slots, halo = sizes.blocks, sizes.rows, sizes.slots, sizes.halo
    depth, partner, refine = [x.reshape(blocks, LANES) for x in (depth, partner, refine)]
    state, diff_ops, prolong = [jnp.transpose(x, (1, 0, 2)) for x in (state, diff_ops, prolong)]
    state, depth, metric, partner, refine, diff_ops, lift, prolong = [
        pltpu.with_memory_space_constraint(x, pltpu.HBM)
        for x in (state, depth, metric, partner, refine, diff_ops, lift, prolong)
    ]
    f32, i32 = jnp.float32, jnp.int32
    packed = jax.ShapeDtypeStruct((SENT * halo, LANES), f32)
    dense = [
        pltpu.VMEM((blocks, LANES), f32),
        pltpu.VMEM(metric.shape, f32),
        pltpu.VMEM((blocks, LANES), i32),
        pltpu.VMEM((blocks, LANES), i32),
    ]
    stats, even, odd = pl.pallas_call(
        functools.partial(pack_kernel, sizes),
        name="pack",
        out_shape=(jax.ShapeDtypeStruct((count, LANES), f32), packed, packed),
        in_specs=[HBM] * 5,
        out_specs=(HBM, VMEM, VMEM),
        scratch_shapes=[
            pltpu.VMEM((count, LANES), f32),
            pltpu.VMEM((10, 3, LANES * halo), f32),
            pltpu.VMEM((10, 3, LANES * halo), f32),
            *dense,
            pltpu.VMEM((8 * blocks, LANES), f32),
            pltpu.SemaphoreType.DMA((6,)),
            pltpu.SemaphoreType.DMA,
        ],
        compiler_params=PARAMS,
    )(state, depth, metric, partner, refine)
    odd = lax.ppermute(odd, AXES, swaps(1, count))
    even = lax.ppermute(even, AXES, swaps(0, count))
    stats = lax.all_to_all(stats, AXES, 0, 0, tiled=True)
    even, odd, stats = [pltpu.with_memory_space_constraint(x, pltpu.VMEM) for x in (even, odd, stats)]
    cur, aux, weights, operators = pl.pallas_call(
        functools.partial(prep_kernel, sizes),
        name="lay_out",
        cost_estimate=pl.CostEstimate(flops=1 << 24, transcendentals=1 << 16, bytes_accessed=1 << 24),
        out_shape=(
            jax.ShapeDtypeStruct((30, blocks, LANES), f32),
            jax.ShapeDtypeStruct((7, blocks, LANES), f32),
            jax.ShapeDtypeStruct((3 * PACK, 3 * WIDE), jnp.bfloat16),
            jax.ShapeDtypeStruct((3, LANES), f32),
        ),
        in_specs=[HBM] * 8,
        out_specs=(VMEM,) * 4,
        scratch_shapes=[
            pltpu.VMEM(state.shape, f32),
            *dense,
            pltpu.VMEM(prolong.shape, f32),
            pltpu.VMEM(diff_ops.shape, f32),
            pltpu.VMEM(lift.shape, f32),
            pltpu.VMEM((8 * blocks, LANES), f32),
            pltpu.VMEM((LAID * blocks, LANES), f32),
            pltpu.SemaphoreType.DMA((8,)),
        ],
        compiler_params=PARAMS,
    )(state, depth, metric, partner, refine, diff_ops, lift, prolong)
    cur, rates, twice, weights, ends, full, lines = pl.pallas_call(
        functools.partial(first_kernel, sizes),
        name="rates_twice",
        cost_estimate=pl.CostEstimate(flops=1024, transcendentals=0, bytes_accessed=1024),
        out_shape=(
            jax.ShapeDtypeStruct((30, sizes.tall, LANES), f32),
            jax.ShapeDtypeStruct((30, sizes.tall, LANES), f32),
            jax.ShapeDtypeStruct((30, slots, LANES), f32),
            jax.ShapeDtypeStruct((3 * PACK, 3 * WIDE), jnp.bfloat16),
            jax.ShapeDtypeStruct((slots, 2 * LANES), jnp.bfloat16),
            jax.ShapeDtypeStruct((slots, LANES), f32),
            jax.ShapeDtypeStruct((3, 8, LANES), f32),
        ),
        in_specs=[VMEM] * 6,
        out_specs=(VMEM,) * 7,
        scratch_shapes=[
            pltpu.VMEM((15, rows, LANES), f32),
            pltpu.VMEM((7, sizes.tall, LANES), f32),
            pltpu.SMEM((3, LANES), f32),
            pltpu.SemaphoreType.DMA((1,)),
        ],
        compiler_params=PARAMS,
    )(cur, aux, weights, operators, odd, even)
    refined = pl.pallas_call(
        functools.partial(refine_kernel, sizes),
        name="sum_and_refine",
        out_shape=jax.ShapeDtypeStruct((10, 3, LANES * slots), f32),
        in_specs=[VMEM] * 8,
        out_specs=HBM,
        scratch_shapes=[
            pltpu.VMEM((10, 3, LANES * slots), f32),
            pltpu.VMEM((1, LANES), i32),
            pltpu.SMEM((1, LANES), i32),
            pltpu.VMEM((STEP * (slots + 1), LANES), f32),
            pltpu.VMEM((3, slots, LANES), f32),
            pltpu.SemaphoreType.DMA((slots // 8 + 1,)),
            pltpu.SemaphoreType.DMA,
        ],
        compiler_params=PARAMS,
    )(cur, rates, twice, weights, ends, full, lines, stats)
    return jnp.transpose(refined, (1, 0, 2))


def solution(mesh):
    return jax.shard_map(
        shards,
        mesh=mesh,
        in_specs=(
            P(None, None, AXES),
            P(AXES),
            P(None, AXES),
            P(AXES),
            P(AXES),
            P(),
            P(),
            P(),
        ),
        out_specs=P(None, None, AXES),
        check_vma=False,
    )
```
